32 devices in a mesh: mod: 2 (over x), dp: 16 (over z, y, core).
Axes of the slice: x: 2, y: 2, z: 4, core: 2. Of those that a mesh axis runs over, the one named last changes fastest.
Arguments:
- layer_rows: bfloat16 [2, 16384, 768], P('mod', 'dp'), may hold values from -6 to 6
- cotangent: bfloat16 [2, 16384, 768], P('mod', 'dp'), may hold values from -6 to 6
- row_live: int32 [2, 16384], P(None, 'dp'), may hold values from 0 to 1, as said below
- partner: int32 [16, 16], P('dp'), may hold values from 0 to 15, as said below
- w_qkv: bfloat16 [768, 2304], replicated, may hold values from -0.21875 to 0.21875
- b_qv: float32 [2, 768], replicated, may hold values from -1.8 to 1.8
- w_out: bfloat16 [768, 768], replicated, may hold values from -0.875 to 0.875
- norm_gains: float32 [2, 768], replicated, may hold values from 0.5 to 1.5
- bias_rows: float32 [4, 768], replicated, may hold values from -1.8 to 1.8
- w_in: bfloat16 [768, 3072], replicated, may hold values from -0.21875 to 0.21875
- b_in: float32 [3072], replicated, may hold values from -1.8 to 1.8
- w_back: bfloat16 [3072, 768], replicated, may hold values from -0.15625 to 0.15625
Outputs:
- output: bfloat16 [2, 16384, 768], P('mod', 'dp')
- grad_rows: bfloat16 [2, 16384, 768], P('mod', 'dp')
- grad_w_qkv: float32 [768, 2304], P('dp')
- grad_b_qv: float32 [2, 768], P(None, 'dp')
- grad_w_out: float32 [768, 768], P('dp')
- grad_gains: float32 [2, 768], P(None, 'dp')
- grad_biases: float32 [4, 768], P(None, 'dp')
- grad_w_in: float32 [768, 3072], P('dp')
- grad_b_in: float32 [3072], P('dp')
- grad_w_back: float32 [3072, 768], P('dp')
The draws below stay inside these ranges and needn't reach their ends.
Inputs may be any that keep to these rules, and one draw needn't show every extreme that they name: `row_live`: within each pair and modality the live rows are the first ones of its 64 slots, at least one; the first pair of every index of dp is live in all its rows of both modalities. Each row partner[g] is a permutation of the 16 region slots of index g of dp.
All inputs are finite; a program needn't handle non-finite values.
Results may differ from the reference program's by a relative error of at most 0.015.
Values may be sent and summed in bfloat16 or wider, within the bound.
No kernel may reach another device: no remote copies, remote signals or barrier semaphores. Data moves between devices by JAX's collectives and lax.ppermute only.
A program may use at most 192 MiB of HBM per device.

```python
import jax
import jax.numpy as jnp
from jax import lax

D = 768
HEADS = 12
FF = 3072
SLOT = 64
PAIRS_DEV = 16
GROUPS = 16
ROWS = 16384
N_DP = 16


def draw_row_live(key, part):
    key = jax.random.fold_in(key, 11)
    pair_total = GROUPS * PAIRS_DEV
    counts = jax.random.randint(key, (2, pair_total), 1, SLOT + 1)
    leading = jnp.arange(pair_total) % PAIRS_DEV == 0
    counts = jnp.where(leading[None, :], SLOT, counts)
    places = jnp.arange(SLOT)
    filled = places[None, None, :] < counts[:, :, None]
    return filled.astype(jnp.int32).reshape(2, pair_total * SLOT)


def draw_partner(key, part):
    key = jax.random.fold_in(key, 23)
    ranks = jax.random.randint(key, (GROUPS, PAIRS_DEV), 0, 1 << 20)
    ranks = ranks * PAIRS_DEV + jnp.arange(PAIRS_DEV)[None, :]
    return jnp.argsort(ranks, axis=1, stable=True).astype(jnp.int32)


def block_levels(own_key, extent, shards, low, top_value):
    gain = 1.0
    for dim, shards_of in shards:
        steps = jax.random.uniform(jax.random.fold_in(jax.random.fold_in(own_key, 6), dim), (shards_of,), jnp.float32, low / len(shards), top_value / len(shards))
        gain = gain * jnp.repeat(jnp.exp(steps), extent[dim] // shards_of).reshape((-1,) + (1,) * (len(extent) - 1 - dim))
    return gain


def bell_draw(own_key, extent, scale, limit, split=(), kind=jnp.bfloat16):
    gain = block_levels(own_key, extent, split, -0.22, 0.18) if split else 1.0
    drawn = jax.random.normal(own_key, extent, jnp.float32) * scale * gain
    return jnp.minimum(jnp.maximum(drawn, -limit), limit).astype(kind)


def setup_inputs(seed: int = 0) -> dict:
    keys = jax.random.split(jax.random.key(seed), 13)
    layer_rows = bell_draw(keys[0], (2, ROWS, D), 1.0, 6.0, ((0, 2), (1, 16)))
    cotangent = bell_draw(keys[1], (2, ROWS, D), 1.0, 6.0, ((0, 2), (1, 16)))
    row_live = draw_row_live(jax.random.fold_in(keys[12], 71), 0)
    partner = draw_partner(jax.random.fold_in(keys[12], 71), 0)
    w_qkv = bell_draw(keys[4], (D, 3 * D), D ** -0.5, 0.21875)
    b_qv = bell_draw(keys[5], (2, D), 0.3, 1.8, (), jnp.float32)
    w_out = bell_draw(keys[6], (D, D), (D // 16) ** -0.5, 0.875)
    norm_gains = jnp.clip(1.0 + 0.1 * jax.random.normal(keys[7], (2, D), jnp.float32), 0.5, 1.5)
    bias_rows = bell_draw(keys[8], (4, D), 0.3, 1.8, (), jnp.float32)
    w_in = bell_draw(keys[9], (D, FF), D ** -0.5, 0.21875)
    b_in = bell_draw(keys[10], (FF,), 0.3, 1.8, (), jnp.float32)
    w_back = bell_draw(keys[11], (FF, D), (FF // 2) ** -0.5, 0.15625)
    return dict(layer_rows=layer_rows, cotangent=cotangent, row_live=row_live, partner=partner, w_qkv=w_qkv, b_qv=b_qv, w_out=w_out, norm_gains=norm_gains, bias_rows=bias_rows, w_in=w_in, b_in=b_in, w_back=w_back)


@jax.custom_vjp
def low(v):
    return lax.optimization_barrier(v.astype(jnp.bfloat16)).astype(jnp.float32)

@jax.custom_vjp
def low_back(v):
    return v

def low_keep(v):
    return (low(v), None)

def low_pass(kept, grad):
    return (grad,)

def back_keep(v):
    return (v, None)

def back_low(kept, grad):
    return (low(grad),)
low.defvjp(low_keep, low_pass)
low_back.defvjp(back_keep, back_low)

def hi_dot(left_side, right_side):
    return jnp.dot(left_side, right_side, precision=lax.Precision.HIGHEST, preferred_element_type=jnp.float32)

def layer_norm(values_in, gain_row, bias_row):
    centered = values_in - lax.optimization_barrier(jnp.mean(values_in, axis=-1, keepdims=True))
    spread = lax.optimization_barrier(jnp.mean(centered * centered, axis=-1, keepdims=True))
    return centered * lax.rsqrt(spread + 1e-12) * gain_row + bias_row

def mirror(values_in, pair_count):
    shaped = values_in.reshape((pair_count, 2) + values_in.shape[1:])
    return jnp.flip(shaped, 1).reshape(values_in.shape)

def block_forward(rows_in, live_in, w_qkv, b_qv, w_out, norm_gains, bias_rows, w_in, b_in, w_back):
    pair_count, length, model_width = rows_in.shape
    slot_rows = length // 2
    head_size = model_width // HEADS
    score_scale = head_size ** (-0.5)
    flat_rows = rows_in.reshape(pair_count * length, model_width)
    mixed_rows = hi_dot(flat_rows, w_qkv)
    queries = low_back(low(mixed_rows[:, :model_width] + b_qv[0]))
    keys_low = low_back(low(mixed_rows[:, model_width:2 * model_width]))
    values_low = low_back(low(mixed_rows[:, 2 * model_width:] + b_qv[1]))
    halves = (pair_count * 2, slot_rows, HEADS, head_size)
    queries = queries.reshape(halves)
    keys_low = keys_low.reshape(halves)
    values_low = values_low.reshape(halves)
    all_keys = jnp.concatenate([keys_low, mirror(low_back(keys_low), pair_count)], 1)
    all_values = jnp.concatenate([values_low, mirror(low_back(values_low), pair_count)], 1)
    seen_own = live_in.reshape(pair_count * 2, slot_rows)
    seen_keys = jnp.concatenate([seen_own, mirror(seen_own, pair_count)], 1) > 0
    scores = jnp.einsum('pqhe,pkhe->phqk', queries, all_keys, precision=lax.Precision.HIGHEST)
    scores = low_back(scores * score_scale)
    scores = jnp.where(seen_keys[:, None, None, :], scores, -1e+30)
    softmaxed = jax.nn.softmax(scores, axis=-1)
    context = jnp.einsum('phqk,pkhe->pqhe', low(softmaxed), all_values, precision=lax.Precision.HIGHEST)
    context = low_back(low(context)).reshape(pair_count * length, model_width)
    pre_one = flat_rows + low_back(hi_dot(context, w_out)) + bias_rows[0]
    hidden = layer_norm(pre_one, norm_gains[0], bias_rows[1])
    inner_pre = low_back(hi_dot(low(hidden), w_in)) + b_in
    low_act = low(jax.nn.gelu(inner_pre, approximate=False))
    pre_two = hidden + low_back(hi_dot(low_act, w_back)) + bias_rows[2]
    return layer_norm(pre_two, norm_gains[1], bias_rows[3]).reshape(pair_count, length, model_width)

def reference(layer_rows, cotangent, row_live, partner, w_qkv, b_qv, w_out, norm_gains, bias_rows, w_in, b_in, w_back):
    pairs_all = N_DP * PAIRS_DEV
    region_of = (partner + PAIRS_DEV * jnp.arange(N_DP, dtype=jnp.int32)[:, None]).reshape(pairs_all).astype(jnp.int32)

    def joined_pairs(values_in):
        tail = values_in.shape[2:]
        words = values_in[0].reshape((pairs_all, SLOT) + tail)
        regions = values_in[1].reshape((pairs_all, SLOT) + tail)[region_of]
        joined = jnp.concatenate([words, regions], 1)
        return joined.reshape((N_DP, PAIRS_DEV, 2 * SLOT) + tail)
    data_rows = joined_pairs(layer_rows).astype(jnp.float32)
    data_cot = joined_pairs(cotangent).astype(jnp.float32)
    data_live = joined_pairs(row_live)
    params = (w_qkv.astype(jnp.float32), b_qv.astype(jnp.float32), w_out.astype(jnp.float32), norm_gains.astype(jnp.float32), bias_rows.astype(jnp.float32), w_in.astype(jnp.float32), b_in.astype(jnp.float32), w_back.astype(jnp.float32))

    def scan_step(running, item_in):
        block_rows, block_cot, block_live = item_in

        def forward_block(rows_in, *params_in):
            return block_forward(rows_in, block_live, *params_in)
        result, pullback = jax.vjp(forward_block, block_rows, *params)
        grads = pullback(block_cot)
        running = jax.tree.map(jnp.add, running, tuple(grads[1:]))
        return (running, (result, grads[0]))
    start = tuple((jnp.zeros(item.shape, jnp.float32) for item in params))
    totals, (outputs, d_rows) = lax.scan(scan_step, start, (data_rows, data_cot, data_live))

    def parted(values_in):
        values_in = values_in.reshape(pairs_all, 2 * SLOT, D)
        regions = jnp.zeros((pairs_all, SLOT, D), jnp.float32).at[region_of].set(values_in[:, SLOT:])
        return jnp.stack([values_in[:, :SLOT].reshape(-1, D), regions.reshape(-1, D)]).astype(jnp.bfloat16)
    return (parted(outputs), parted(d_rows), totals[0], totals[1], totals[2], totals[3], totals[4], totals[5], totals[6], totals[7])
```

```python
import functools

import jax
import jax.numpy as jnp
from jax import lax
from jax.experimental import pallas as pl
from jax.experimental.pallas import tpu as pltpu
from jax.sharding import PartitionSpec as P

HEADS = 12
EPSILON = 1e-12
F32 = jnp.float32
BF16 = jnp.bfloat16
VMEM_LIMIT = 56 * 2**20


def dot(left, right, left_dim=1, right_dim=0):
    return lax.dot_general(
        left, right, (((left_dim,), (right_dim,)), ((), ())), preferred_element_type=F32
    )


def flipped(value, axis, mask):
    pairs = [(source, source ^ mask) for source in range(lax.axis_size(axis))]
    return lax.ppermute(value, axis, pairs)


def params(limit=VMEM_LIMIT):
    return pltpu.CompilerParams(vmem_limit_bytes=limit)


def kept_slot(scalars, pair, half):
    groups = 2 * half
    side = scalars[groups]
    place = side * half + pair
    return jnp.where(side == 0, place, scalars[place])


def sent_slot(scalars, pair, half):
    groups = 2 * half
    side = scalars[groups]
    place = (1 - side) * half + pair
    return jnp.where(side == 0, place, scalars[place])


def gather_sent(scalars, rows, half, cuts):
    slot_rows, width = rows.shape[1:]
    sizes = [cuts[i + 1] - cuts[i] for i in range(len(cuts) - 1)]

    def kernel(scalars_ref, rows_ref, *rest):
        outs, sems = rest[:-1], rest[-1]
        copies = []
        for part, out in enumerate(outs):
            for i in range(sizes[part]):
                pair = cuts[part] + i
                copies.append(
                    pltpu.make_async_copy(
                        rows_ref.at[sent_slot(scalars_ref, pair, half)], out.at[i], sems.at[pair]
                    )
                )
        for copy in copies:
            copy.start()
        for copy in copies:
            copy.wait()

    return pl.pallas_call(
        kernel,
        grid_spec=pltpu.PrefetchScalarGridSpec(
            num_scalar_prefetch=1,
            grid=(1,),
            in_specs=[pl.BlockSpec(memory_space=pl.ANY)],
            out_specs=[pl.BlockSpec(memory_space=pl.ANY)] * len(sizes),
            scratch_shapes=[pltpu.SemaphoreType.DMA((half,))],
        ),
        out_shape=[jax.ShapeDtypeStruct((size, slot_rows, width), rows.dtype) for size in sizes],
        compiler_params=params(),
        name="gather_sent",
    )(scalars, rows)


def scatter_home(scalars, kept, back, half):
    slot_rows, width = kept.shape[1:]

    def kernel(scalars_ref, kept_ref, back_ref, out, sems):
        copies = []
        for i in range(half):
            copies.append(
                pltpu.make_async_copy(
                    kept_ref.at[i], out.at[kept_slot(scalars_ref, i, half)], sems.at[0, i]
                )
            )
            copies.append(
                pltpu.make_async_copy(
                    back_ref.at[i], out.at[sent_slot(scalars_ref, i, half)], sems.at[1, i]
                )
            )
        for copy in copies:
            copy.start()
        for copy in copies:
            copy.wait()

    return pl.pallas_call(
        kernel,
        grid_spec=pltpu.PrefetchScalarGridSpec(
            num_scalar_prefetch=1,
            grid=(1,),
            in_specs=[pl.BlockSpec(memory_space=pl.ANY)] * 2,
            out_specs=pl.BlockSpec(memory_space=pl.ANY),
            scratch_shapes=[pltpu.SemaphoreType.DMA((2, half))],
        ),
        out_shape=jax.ShapeDtypeStruct((2 * half, slot_rows, width), kept.dtype),
        compiler_params=params(),
        name="scatter_home",
    )(scalars, kept, back)


def split_heads(value):
    low = lax.broadcasted_iota(jnp.int32, value.shape, 1) < value.shape[1] // 2
    zero = jnp.zeros_like(value)
    return jnp.concatenate([jnp.where(low, value, zero), jnp.where(low, zero, value)], 0)


def side_by_side(value):
    rows = value.shape[0] // 2
    return jnp.concatenate([value[:rows], value[rows:]], 1)


def attention_forward(
    scalars, rows, received, live, w_qkv, b_qv, w_out, norm_gains, bias_rows, first, half
):
    slot_rows, width = rows.shape[1:]
    pairs = received.shape[0]
    length = 2 * slot_rows
    duo = 2 * width // HEADS
    blocks = width // duo
    score_scale = (width // HEADS) ** (-0.5)

    def kernel(
        scalars_ref,
        kept_a,
        kept_b,
        got,
        live_ref,
        w_qkv_ref,
        b_qv_ref,
        w_out_ref,
        gains_ref,
        biases_ref,
        joined_out,
        mixed_out,
        probs_out,
        context_out,
        normed_out,
        root_out,
        hidden_out,
    ):
        joined = jnp.concatenate([kept_a[0], got[0], kept_b[0], got[1]], 0)
        joined_out[...] = joined
        mixed = dot(joined, w_qkv_ref[...])
        queries = ((mixed[:, :width] + b_qv_ref[0:1, :]).astype(BF16).astype(F32) * score_scale).astype(BF16)
        keys = mixed[:, width : 2 * width].astype(BF16)
        values = (mixed[:, 2 * width :] + b_qv_ref[1:2, :]).astype(BF16)
        mixed_out[:, :width] = queries
        mixed_out[:, width : 2 * width] = keys
        mixed_out[:, 2 * width :] = values
        contexts = []
        for pair in range(2):
            seen = live_ref[pair] > 0
            span = slice(pair * length, (pair + 1) * length)
            heads = []
            for block in range(blocks):
                cols = slice(block * duo, (block + 1) * duo)
                scores = dot(split_heads(queries[span, cols]), keys[span, cols], 1, 1)
                scores = jnp.where(seen, scores, -1e30)
                powered = jnp.exp(scores - jnp.max(scores, axis=-1, keepdims=True))
                low_probs = (powered / jnp.sum(powered, axis=-1, keepdims=True)).astype(BF16)
                probs_out[pair, block] = low_probs
                heads.append(
                    dot(side_by_side(low_probs), split_heads(values[span, cols])).astype(BF16)
                )
            contexts.append(jnp.concatenate(heads, 1))
        context = jnp.concatenate(contexts, 0)
        context_out[...] = context
        pre_one = joined.astype(F32) + dot(context, w_out_ref[...]) + biases_ref[0:1, :]
        centered = pre_one - jnp.mean(pre_one, axis=-1, keepdims=True)
        root = lax.rsqrt(jnp.mean(centered * centered, axis=-1, keepdims=True) + EPSILON)
        normed = centered * root
        normed_out[...] = normed
        root_out[...] = jnp.broadcast_to(root, root_out.shape)
        hidden_out[...] = (normed * gains_ref[0:1, :] + biases_ref[1:2, :]).astype(BF16)

    def whole(array):
        return pl.BlockSpec(array.shape, lambda i, s: (0,) * array.ndim)

    def by_rows(columns):
        return pl.BlockSpec((2 * length, columns), lambda i, s: (i, 0))

    slot = (1, slot_rows, width)
    total = pairs * length
    return pl.pallas_call(
        kernel,
        grid_spec=pltpu.PrefetchScalarGridSpec(
            num_scalar_prefetch=1,
            grid=(pairs // 2,),
            in_specs=[
                pl.BlockSpec(slot, lambda i, s: (kept_slot(s, first + 2 * i, half), 0, 0)),
                pl.BlockSpec(slot, lambda i, s: (kept_slot(s, first + 2 * i + 1, half), 0, 0)),
                pl.BlockSpec((2, slot_rows, width), lambda i, s: (i, 0, 0)),
                pl.BlockSpec((2, 1, length), lambda i, s: (first // 2 + i, 0, 0)),
                whole(w_qkv),
                whole(b_qv),
                whole(w_out),
                whole(norm_gains),
                whole(bias_rows),
            ],
            out_specs=[
                by_rows(width),
                by_rows(3 * width),
                pl.BlockSpec((2, blocks, 2 * length, length), lambda i, s: (i, 0, 0, 0)),
                by_rows(width),
                by_rows(width),
                by_rows(128),
                by_rows(width),
            ],
        ),
        out_shape=[
            jax.ShapeDtypeStruct((total, width), BF16),
            jax.ShapeDtypeStruct((total, 3 * width), BF16),
            jax.ShapeDtypeStruct((pairs, blocks, 2 * length, length), BF16),
            jax.ShapeDtypeStruct((total, width), BF16),
            jax.ShapeDtypeStruct((total, width), F32),
            jax.ShapeDtypeStruct((total, 128), F32),
            jax.ShapeDtypeStruct((total, width), BF16),
        ],
        compiler_params=params(),
        cost_estimate=pl.CostEstimate(
            flops=2 * total * width * width * 5, bytes_accessed=20 * 2**20, transcendentals=0
        ),
        name="attention_forward",
    )(scalars, rows, rows, received, live, w_qkv, b_qv, w_out, norm_gains, bias_rows)


def row_sum(value):
    return jnp.sum(value, axis=0, keepdims=True)


def feed_forward(
    scalars, low_hidden, normed, cotangent, far_cot, w_in, b_in, w_back, norm_gains, bias_rows, half
):
    slot_rows, width = cotangent.shape[1:]
    total = normed.shape[0]
    inner_width = w_in.shape[1]
    length = 2 * slot_rows
    chunk = 768

    def kernel(
        scalars_ref,
        hidden_ref,
        normed_ref,
        cot_a,
        cot_b,
        cot_far,
        w_in_ref,
        b_in_ref,
        w_back_ref,
        gains_ref,
        biases_ref,
        act_out,
        slope_out,
        branch_out,
        d_two_out,
        kept_out,
        far_out,
        sums_out,
    ):
        @pl.when(pl.program_id(0) == 0)
        def _():
            sums_out[...] = jnp.zeros_like(sums_out)

        low_hidden = hidden_ref[...]
        pre_two = normed_ref[...] * gains_ref[0:1, :] + biases_ref[1:2, :] + biases_ref[2:3, :]
        for start in range(0, inner_width, chunk):
            cols = slice(start, start + chunk)
            inner = dot(low_hidden, w_in_ref[:, cols]) + b_in_ref[:, cols]
            normal = 0.5 + 0.5 * lax.erf(inner * (0.5**0.5))
            low_act = (inner * normal).astype(BF16)
            density = jnp.exp(inner * inner * -0.5) * 0.3989422804014327
            act_out[:, cols] = low_act
            slope_out[:, cols] = (normal + inner * density).astype(BF16)
            pre_two = pre_two + dot(low_act, w_back_ref[cols, :])
        centered = pre_two - jnp.mean(pre_two, axis=-1, keepdims=True)
        root = lax.rsqrt(jnp.mean(centered * centered, axis=-1, keepdims=True) + EPSILON)
        scaled = centered * root
        output = (scaled * gains_ref[1:2, :] + biases_ref[3:4, :]).astype(BF16)
        for i in range(2):
            kept_out[i] = output[i * length : i * length + slot_rows]
            far_out[i] = output[i * length + slot_rows : (i + 1) * length]
        cot = jnp.concatenate([cot_a[0], cot_far[0], cot_b[0], cot_far[1]], 0).astype(F32)
        lifted = cot * gains_ref[1:2, :]
        d_two = root * (
            lifted
            - jnp.mean(lifted, axis=-1, keepdims=True)
            - scaled * jnp.mean(lifted * scaled, axis=-1, keepdims=True)
        )
        d_two_out[...] = d_two
        branch_out[...] = d_two.astype(BF16)
        sums_out[0:1, :] += row_sum(cot * scaled)
        sums_out[1:2, :] += row_sum(cot)
        sums_out[2:3, :] += row_sum(d_two)

    def whole(array):
        return pl.BlockSpec(
            array.shape, lambda i, s: (0,) * array.ndim, pipeline_mode=pl.Buffered(1)
        )

    def by_rows(columns):
        return pl.BlockSpec((2 * length, columns), lambda i, s: (i, 0))

    slot = (1, slot_rows, width)
    duo = pl.BlockSpec((2, slot_rows, width), lambda i, s: (i, 0, 0))
    return pl.pallas_call(
        kernel,
        grid_spec=pltpu.PrefetchScalarGridSpec(
            num_scalar_prefetch=1,
            grid=(total // (2 * length),),
            in_specs=[
                by_rows(width),
                by_rows(width),
                pl.BlockSpec(slot, lambda i, s: (kept_slot(s, 2 * i, half), 0, 0)),
                pl.BlockSpec(slot, lambda i, s: (kept_slot(s, 2 * i + 1, half), 0, 0)),
                duo,
                whole(w_in),
                whole(b_in),
                whole(w_back),
                whole(norm_gains),
                whole(bias_rows),
            ],
            out_specs=[
                by_rows(inner_width),
                by_rows(inner_width),
                by_rows(width),
                by_rows(width),
                duo,
                duo,
                pl.BlockSpec((8, width), lambda i, s: (0, 0)),
            ],
        ),
        out_shape=[
            jax.ShapeDtypeStruct((total, inner_width), BF16),
            jax.ShapeDtypeStruct((total, inner_width), BF16),
            jax.ShapeDtypeStruct((total, width), BF16),
            jax.ShapeDtypeStruct((total, width), F32),
            jax.ShapeDtypeStruct((half, slot_rows, width), BF16),
            jax.ShapeDtypeStruct((half, slot_rows, width), BF16),
            jax.ShapeDtypeStruct((8, width), F32),
        ],
        compiler_params=params(),
        cost_estimate=pl.CostEstimate(
            flops=2 * total * width * inner_width * 4, bytes_accessed=30 * 2**20, transcendentals=0
        ),
        name="feed_forward",
    )(
        scalars,
        low_hidden,
        normed,
        cotangent,
        cotangent,
        far_cot,
        w_in,
        b_in,
        w_back,
        norm_gains,
        bias_rows,
    )


def feed_backward(branch, slope, d_two, normed, root, w_in, w_back, norm_gains):
    total, width = branch.shape
    inner_width = slope.shape[1]
    step = 256
    chunk = 768

    def kernel(
        branch_ref,
        slope_ref,
        d_two_ref,
        normed_ref,
        root_ref,
        w_in_ref,
        w_back_ref,
        gains_ref,
        low_inner_out,
        d_one_out,
        low_attn_out,
        sums_out,
        inner_sum_out,
    ):
        @pl.when(pl.program_id(0) == 0)
        def _():
            sums_out[...] = jnp.zeros_like(sums_out)
            inner_sum_out[...] = jnp.zeros_like(inner_sum_out)

        low_branch = branch_ref[...]
        d_hidden = d_two_ref[...]
        for start in range(0, inner_width, chunk):
            cols = slice(start, start + chunk)
            d_inner = dot(low_branch, w_back_ref[cols, :], 1, 1) * slope_ref[:, cols].astype(F32)
            low_inner = d_inner.astype(BF16)
            low_inner_out[:, cols] = low_inner
            inner_sum_out[0:1, cols] += row_sum(d_inner)
            d_hidden = d_hidden + dot(low_inner, w_in_ref[:, cols], 1, 1)
        normed = normed_ref[...]
        lifted = d_hidden * gains_ref[0:1, :]
        d_one = root_ref[:, 0:1] * (
            lifted
            - jnp.mean(lifted, axis=-1, keepdims=True)
            - normed * jnp.mean(lifted * normed, axis=-1, keepdims=True)
        )
        d_one_out[...] = d_one
        low_attn_out[...] = d_one.astype(BF16)
        sums_out[0:1, :] += row_sum(d_hidden * normed)
        sums_out[1:2, :] += row_sum(d_hidden)
        sums_out[2:3, :] += row_sum(d_one)

    def whole(array):
        return pl.BlockSpec(array.shape, lambda i: (0,) * array.ndim, pipeline_mode=pl.Buffered(1))

    def by_rows(columns):
        return pl.BlockSpec((step, columns), lambda i: (i, 0))

    return pl.pallas_call(
        kernel,
        grid=(total // step,),
        in_specs=[
            by_rows(width),
            by_rows(inner_width),
            by_rows(width),
            by_rows(width),
            by_rows(128),
            whole(w_in),
            whole(w_back),
            whole(norm_gains),
        ],
        out_specs=[
            by_rows(inner_width),
            by_rows(width),
            by_rows(width),
            pl.BlockSpec((8, width), lambda i: (0, 0)),
            pl.BlockSpec((8, inner_width), lambda i: (0, 0)),
        ],
        out_shape=[
            jax.ShapeDtypeStruct((total, inner_width), BF16),
            jax.ShapeDtypeStruct((total, width), F32),
            jax.ShapeDtypeStruct((total, width), BF16),
            jax.ShapeDtypeStruct((8, width), F32),
            jax.ShapeDtypeStruct((8, inner_width), F32),
        ],
        compiler_params=params(),
        cost_estimate=pl.CostEstimate(
            flops=2 * total * width * inner_width * 3, bytes_accessed=30 * 2**20, transcendentals=0
        ),
        name="feed_backward",
    )(branch, slope, d_two, normed, root, w_in, w_back, norm_gains)


def attention_backward(low_attn, mixed, probs, d_one, w_out, w_qkv):
    total, width = low_attn.shape
    pairs, blocks, _, length = probs.shape
    duo = width // blocks
    slot_rows = length // 2
    score_scale = (width // HEADS) ** (-0.5)

    def kernel(
        low_attn_ref,
        mixed_ref,
        probs_ref,
        d_one_ref,
        w_out_ref,
        w_qkv_ref,
        d_mixed_out,
        kept_out,
        far_out,
        sums_out,
    ):
        @pl.when(pl.program_id(0) == 0)
        def _():
            sums_out[...] = jnp.zeros_like(sums_out)

        d_context = dot(low_attn_ref[...], w_out_ref[...], 1, 1).astype(BF16)
        low = lax.broadcasted_iota(jnp.int32, (length, duo), 1) < duo // 2
        for pair in range(2):
            span = slice(pair * length, (pair + 1) * length)
            for block in range(blocks):
                cols = slice(block * duo, (block + 1) * duo)
                queries = split_heads(mixed_ref[span, cols])
                keys = mixed_ref[span, width + block * duo : width + (block + 1) * duo]
                values = mixed_ref[span, 2 * width + block * duo : 2 * width + (block + 1) * duo]
                d_heads = split_heads(d_context[span, cols])
                low_probs = probs_ref[pair, block]
                wide = low_probs.astype(F32)
                d_probs = dot(d_heads, values, 1, 1)
                d_scores = wide * (d_probs - jnp.sum(wide * d_probs, axis=-1, keepdims=True))
                d_scores = d_scores.astype(BF16)
                d_queries = dot(side_by_side(d_scores), split_heads(keys)) * score_scale
                d_mixed_out[span, cols] = d_queries.astype(BF16)
                d_mixed_out[span, width + block * duo : width + (block + 1) * duo] = dot(
                    d_scores, queries, 0, 0
                ).astype(BF16)
                d_mixed_out[span, 2 * width + block * duo : 2 * width + (block + 1) * duo] = dot(
                    low_probs, d_heads, 0, 0
                ).astype(BF16)
        d_mixed = d_mixed_out[...]
        sums_out[0:1, :] += row_sum(d_mixed[:, :width].astype(F32))
        sums_out[1:2, :] += row_sum(d_mixed[:, 2 * width :].astype(F32))
        d_rows = (d_one_ref[...] + dot(d_mixed, w_qkv_ref[...], 1, 1)).astype(BF16)
        for i in range(2):
            kept_out[i] = d_rows[i * length : i * length + slot_rows]
            far_out[i] = d_rows[i * length + slot_rows : (i + 1) * length]

    def whole(array):
        return pl.BlockSpec(array.shape, lambda i: (0,) * array.ndim, pipeline_mode=pl.Buffered(1))

    def by_rows(columns):
        return pl.BlockSpec((2 * length, columns), lambda i: (i, 0))

    two = pl.BlockSpec((2, slot_rows, width), lambda i: (i, 0, 0))
    return pl.pallas_call(
        kernel,
        grid=(pairs // 2,),
        in_specs=[
            by_rows(width),
            by_rows(3 * width),
            pl.BlockSpec((2, blocks, 2 * length, length), lambda i: (i, 0, 0, 0)),
            by_rows(width),
            whole(w_out),
            whole(w_qkv),
        ],
        out_specs=[by_rows(3 * width), two, two, pl.BlockSpec((8, width), lambda i: (0, 0))],
        out_shape=[
            jax.ShapeDtypeStruct((total, 3 * width), BF16),
            jax.ShapeDtypeStruct((pairs, slot_rows, width), BF16),
            jax.ShapeDtypeStruct((pairs, slot_rows, width), BF16),
            jax.ShapeDtypeStruct((8, width), F32),
        ],
        compiler_params=params(),
        cost_estimate=pl.CostEstimate(
            flops=2 * total * width * width * 10, bytes_accessed=20 * 2**20, transcendentals=0
        ),
        name="attention_backward",
    )(low_attn, mixed, probs, d_one, w_out, w_qkv)


def grad_by_columns(scalars, left, right, shards, chunk, base):
    total, height = left.shape
    width = right.shape[1]
    shard = height // shards
    places = shards // 2

    def kernel(scalars_ref, left_ref, right_ref, send_out, keep_out, held):
        core, place = scalars_ref[base + 1], scalars_ref[base + 2]
        held[...] = dot(left_ref[...], right_ref[...], 0, 0).astype(BF16)
        for j in range(places):
            row = (place ^ j) * 2
            send_out[j] = held[pl.ds(pl.multiple_of((row + 1 - core) * shard, 16), shard), :]
            keep_out[j] = held[pl.ds(pl.multiple_of((row + core) * shard, 16), shard), :]

    out = pl.BlockSpec((places, shard, chunk), lambda i, s: (0, 0, i))
    shape = jax.ShapeDtypeStruct((places, shard, width), BF16)
    return pl.pallas_call(
        kernel,
        grid_spec=pltpu.PrefetchScalarGridSpec(
            num_scalar_prefetch=1,
            grid=(width // chunk,),
            in_specs=[
                pl.BlockSpec((total, height), lambda i, s: (0, 0), pipeline_mode=pl.Buffered(1)),
                pl.BlockSpec((total, chunk), lambda i, s: (0, i)),
            ],
            out_specs=[out, out],
            scratch_shapes=[pltpu.VMEM((height, chunk), BF16)],
        ),
        out_shape=[shape, shape],
        compiler_params=params(),
        cost_estimate=pl.CostEstimate(
            flops=2 * total * width * height, bytes_accessed=12 * 2**20, transcendentals=0
        ),
        name="grad_by_columns",
    )(scalars, left, right)


def grad_by_rows(scalars, left, right, shards, base):
    total, height = left.shape
    width = right.shape[1]
    shard = height // shards
    places = shards // 2
    chunk = 4 * shard

    def kernel(scalars_ref, left_ref, right_ref, send_out, keep_out, held):
        core, place = scalars_ref[base + 1], scalars_ref[base + 2]
        held[...] = dot(left_ref[...], right_ref[...], 0, 0).astype(BF16)
        for j in range(2):
            row = ((place & 1) ^ j) * 2
            send_out[j] = held[pl.ds(pl.multiple_of((row + 1 - core) * shard, 16), shard), :]
            keep_out[j] = held[pl.ds(pl.multiple_of((row + core) * shard, 16), shard), :]

    out = pl.BlockSpec((2, shard, width), lambda i, s: ((s[base + 2] >> 1) ^ i, 0, 0))
    shape = jax.ShapeDtypeStruct((places, shard, width), BF16)
    return pl.pallas_call(
        kernel,
        grid_spec=pltpu.PrefetchScalarGridSpec(
            num_scalar_prefetch=1,
            grid=(height // chunk,),
            in_specs=[
                pl.BlockSpec((total, chunk), lambda i, s: (0, i)),
                pl.BlockSpec((total, width), lambda i, s: (0, 0), pipeline_mode=pl.Buffered(1)),
            ],
            out_specs=[out, out],
            scratch_shapes=[pltpu.VMEM((chunk, width), BF16)],
        ),
        out_shape=[shape, shape],
        compiler_params=params(),
        cost_estimate=pl.CostEstimate(
            flops=2 * total * width * height, bytes_accessed=12 * 2**20, transcendentals=0
        ),
        name="grad_by_rows",
    )(scalars, left, right)


def added(parts):
    total = parts[0].astype(F32)
    for part in parts[1:]:
        total = total + part.astype(F32)
    return total.astype(BF16)


def reduce_shards(send, keep, order):
    places, shard, width = send.shape
    bits = places.bit_length() - 1
    shape = (2,) * bits + (shard, width)
    held = [keep.reshape(shape), flipped(send, "dp", 1).reshape(shape)]
    left = list(range(bits))[::-1]
    for bit in order:
        dim = left.index(bit)
        away = added([lax.index_in_dim(part, 1, dim, keepdims=False) for part in held])
        held = [lax.index_in_dim(part, 0, dim, keepdims=False) for part in held]
        held.append(flipped(away, "dp", 2 << bit))
        left.remove(bit)
    mine = lax.optimization_barrier(added(held))
    return mine.astype(F32) + flipped(mine, "mod", 1).astype(F32)


def reduce_plain(left, right):
    share = lax.psum_scatter(dot(left, right, 0, 0), "dp", scatter_dimension=0, tiled=True)
    return lax.psum(share.astype(BF16), "mod").astype(F32)


def body(
    layer_rows,
    cotangent,
    row_live,
    partner,
    w_qkv,
    b_qv,
    w_out,
    norm_gains,
    bias_rows,
    w_in,
    b_in,
    w_back,
):
    side = lax.axis_index("mod")
    place = lax.axis_index("dp")
    shards = lax.axis_size("dp")
    groups = partner.shape[1]
    half = groups // 2
    width = layer_rows.shape[2]
    slot_rows = layer_rows.shape[1] // groups
    inner_width = w_in.shape[1]
    slots = (groups, slot_rows, width)
    rows = layer_rows[0].reshape(slots)
    cot = cotangent[0].reshape(slots)
    scalars = jnp.concatenate(
        [partner[0], jnp.stack([side, place & 1, place >> 1]).astype(jnp.int32)]
    )
    cut = half // 2
    sent_a, sent_b = gather_sent(scalars, rows, half, (0, cut, half))
    got_a = flipped(sent_a, "mod", 1)
    got_b = flipped(sent_b, "mod", 1)
    cot, got_b = lax.optimization_barrier((cot, got_b))
    (sent_cot,) = gather_sent(scalars, cot, half, (0, half))
    far_cot = flipped(sent_cot, "mod", 1)

    live = row_live.reshape(2, groups, slot_rows)
    words_live = lax.dynamic_slice_in_dim(live[0], side * half, half, 0)
    region_live = live[1][lax.dynamic_slice_in_dim(partner[0], side * half, half, 0)]
    is_first = side == 0
    seen = jnp.concatenate(
        [
            jnp.where(is_first, words_live, region_live),
            jnp.where(is_first, region_live, words_live),
        ],
        1,
    )[:, None, :]

    parts = [
        attention_forward(
            scalars, rows, got, seen, w_qkv, b_qv, w_out, norm_gains, bias_rows, first, half
        )
        for got, first in ((got_a, 0), (got_b, cut))
    ]
    joined, mixed, probs, context, normed, root, low_hidden = [
        jnp.concatenate([a, b], 0) for a, b in zip(*parts)
    ]
    b_in_row = b_in.reshape(1, inner_width)
    act, slope, branch, d_two, out_kept, out_far, sums_two = feed_forward(
        scalars,
        low_hidden,
        normed,
        cot,
        far_cot,
        w_in,
        b_in_row,
        w_back,
        norm_gains,
        bias_rows,
        half,
    )
    out_back = flipped(out_far, "mod", 1)
    low_inner, d_one, low_attn, sums_one, inner_sum = feed_backward(
        branch, slope, d_two, normed, root, w_in, w_back, norm_gains
    )
    d_mixed, d_kept, d_far, sums_qv = attention_backward(
        low_attn, mixed, probs, d_one, w_out, w_qkv
    )
    d_back = flipped(d_far, "mod", 1)

    aligned = shards % 4 == 0 and shards & (shards - 1) == 0 and (width // shards) % 16 == 0
    if aligned:
        bits = (shards // 2).bit_length() - 1
        order = list(range(bits))
        grad_back = reduce_shards(*grad_by_rows(scalars, act, branch, shards, groups), order)
        grad_in = reduce_shards(
            *grad_by_columns(scalars, low_hidden, low_inner, shards, 768, groups), order
        )
        grad_out = reduce_shards(
            *grad_by_columns(scalars, context, low_attn, shards, 768, groups), order
        )
        grad_qkv = reduce_shards(
            *grad_by_columns(scalars, joined, d_mixed, shards, 768, groups), order
        )
    else:
        grad_back = reduce_plain(act, branch)
        grad_in = reduce_plain(low_hidden, low_inner)
        grad_out = reduce_plain(context, low_attn)
        grad_qkv = reduce_plain(joined, d_mixed)

    small = jnp.concatenate(
        [
            sums_qv[0:2],
            sums_one[0:1],
            sums_two[0:1],
            sums_one[2:3],
            sums_one[1:2],
            sums_two[2:3],
            sums_two[1:2],
            inner_sum[0].reshape(-1, width),
        ],
        0,
    )
    small = lax.psum(small, ("mod", "dp"))
    shard = width // shards
    rows_small = lax.dynamic_slice_in_dim(small[:8], place * shard, shard, 1)
    inner_shard = inner_width // shards
    grad_b_in = lax.dynamic_slice_in_dim(small[8:].reshape(-1), place * inner_shard, inner_shard)

    out_rows = scatter_home(scalars, out_kept, out_back, half).reshape(1, -1, width)
    grad_rows = scatter_home(scalars, d_kept, d_back, half).reshape(1, -1, width)
    return (
        out_rows,
        grad_rows,
        grad_qkv,
        rows_small[0:2],
        grad_out,
        rows_small[2:4],
        rows_small[4:8],
        grad_in,
        grad_b_in,
        grad_back,
    )


def solution(mesh):
    return jax.shard_map(
        body,
        mesh=mesh,
        in_specs=(
            P("mod", "dp", None),
            P("mod", "dp", None),
            P(None, "dp"),
            P("dp", None),
            P(),
            P(),
            P(),
            P(),
            P(),
            P(),
            P(),
            P(),
        ),
        out_specs=(
            P("mod", "dp", None),
            P("mod", "dp", None),
            P("dp", None),
            P(None, "dp"),
            P("dp", None),
            P(None, "dp"),
            P(None, "dp"),
            P("dp", None),
            P("dp"),
            P("dp", None),
        ),
        check_vma=False,
    )
```

```python
import functools

import jax
import jax.numpy as jnp
from jax import lax
from jax.experimental import pallas as pl
from jax.experimental.pallas import tpu as pltpu
from jax.sharding import PartitionSpec as P

HEADS = 12
EPSILON = 1e-12
F32 = jnp.float32
BF16 = jnp.bfloat16
VMEM_LIMIT = 56 * 2**20


def dot(left, right, left_dim=1, right_dim=0):
    return lax.dot_general(
        left, right, (((left_dim,), (right_dim,)), ((), ())), preferred_element_type=F32
    )


def flipped(value, axis, mask):
    pairs = [(source, source ^ mask) for source in range(lax.axis_size(axis))]
    return lax.ppermute(value, axis, pairs)


def params(limit=VMEM_LIMIT):
    return pltpu.CompilerParams(vmem_limit_bytes=limit)


def kept_slot(scalars, pair, half):
    groups = 2 * half
    side = scalars[groups]
    place = side * half + pair
    return jnp.where(side == 0, place, scalars[place])


def sent_slot(scalars, pair, half):
    groups = 2 * half
    side = scalars[groups]
    place = (1 - side) * half + pair
    return jnp.where(side == 0, place, scalars[place])


ANY = pl.BlockSpec(memory_space=pl.ANY)


def call(kernel, scalars, operands, in_specs, out_specs, out_shape, grid, name, work, **more):
    after = list(more.get("after", ()))
    into = list(more.get("into", ()))
    scratch = list(more.get("scratch", ()))
    taken, spare = len(operands), len(into) + len(after)

    def wrapped(scalars_ref, *refs):
        kernel(scalars_ref, *refs[:taken], *refs[taken + spare :])

    return pl.pallas_call(
        wrapped,
        grid_spec=pltpu.PrefetchScalarGridSpec(
            num_scalar_prefetch=1,
            grid=grid,
            in_specs=list(in_specs) + [ANY] * spare,
            out_specs=out_specs,
            scratch_shapes=scratch,
        ),
        out_shape=out_shape,
        input_output_aliases={1 + taken + i: i for i in range(len(into))},
        compiler_params=params(more.get("limit", VMEM_LIMIT)),
        cost_estimate=pl.CostEstimate(
            flops=int(work), bytes_accessed=more.get("moved", 2**20), transcendentals=0
        ),
        name=name,
    )(scalars, *operands, *into, *after)


def gather_sent(scalars, rows, half, first, count, after=()):
    slot_rows, width = rows.shape[1:]

    def kernel(scalars_ref, rows_ref, out, sems):
        copies = [
            pltpu.make_async_copy(
                rows_ref.at[sent_slot(scalars_ref, first + i, half)], out.at[i], sems.at[i]
            )
            for i in range(count)
        ]
        for copy in copies:
            copy.start()
        for copy in copies:
            copy.wait()

    shape = (count, slot_rows, width)
    return call(
        kernel,
        scalars,
        [rows],
        [ANY],
        pl.BlockSpec(shape, lambda i, s: (0, 0, 0)),
        jax.ShapeDtypeStruct(shape, rows.dtype),
        (1,),
        "gather_sent",
        1e6,
        scratch=[pltpu.SemaphoreType.DMA((count,))],
        after=after,
        limit=8 * 2**20,
    )


def scatter_home(scalars, kept, back, half, after=()):
    slot_rows, width = kept.shape[1:]

    def kernel(scalars_ref, kept_ref, back_ref, out, sems):
        copies = []
        for i in range(half):
            copies.append(
                pltpu.make_async_copy(
                    kept_ref.at[i], out.at[kept_slot(scalars_ref, i, half)], sems.at[0, i]
                )
            )
            copies.append(
                pltpu.make_async_copy(
                    back_ref.at[i], out.at[sent_slot(scalars_ref, i, half)], sems.at[1, i]
                )
            )
        for copy in copies:
            copy.start()
        for copy in copies:
            copy.wait()

    shape = (2 * half, slot_rows, width)
    return call(
        kernel,
        scalars,
        [kept, back],
        [ANY, ANY],
        pl.BlockSpec(shape, lambda i, s: (0, 0, 0)),
        jax.ShapeDtypeStruct(shape, kept.dtype),
        (1,),
        "scatter_home",
        1e6,
        scratch=[pltpu.SemaphoreType.DMA((2, half))],
        after=after,
        limit=8 * 2**20,
    )


def split_heads(value):
    low = lax.broadcasted_iota(jnp.int32, value.shape, 1) < value.shape[1] // 2
    zero = jnp.zeros_like(value)
    return jnp.concatenate([jnp.where(low, value, zero), jnp.where(low, zero, value)], 0)


def side_by_side(value):
    rows = value.shape[0] // 2
    return jnp.concatenate([value[:rows], value[rows:]], 1)


def row_sum(value):
    return jnp.sum(value, axis=0, keepdims=True)


def normal_form(value):
    centered = value - jnp.mean(value, axis=-1, keepdims=True)
    root = lax.rsqrt(jnp.mean(centered * centered, axis=-1, keepdims=True) + EPSILON)
    return centered * root, root


def normal_back(lifted, normed, root):
    return root * (
        lifted
        - jnp.mean(lifted, axis=-1, keepdims=True)
        - normed * jnp.mean(lifted * normed, axis=-1, keepdims=True)
    )


def whole(array):
    return pl.BlockSpec(
        array.shape, lambda *_: (0,) * array.ndim, pipeline_mode=pl.Buffered(1)
    )


def attention_forward(
    scalars, rows, received, live, weights, first, half, into=(), after=()
):
    w_qkv, b_qv, w_out, norm_gains, bias_rows = weights
    slot_rows, width = rows.shape[1:]
    pairs = received.shape[0]
    length = 2 * slot_rows
    duo = 2 * width // HEADS
    blocks = width // duo
    score_scale = (width // HEADS) ** (-0.5)

    def kernel(
        scalars_ref,
        kept_a,
        kept_b,
        got,
        live_ref,
        w_qkv_ref,
        b_qv_ref,
        w_out_ref,
        gains_ref,
        biases_ref,
        joined_out,
        mixed_out,
        probs_out,
        context_out,
        normed_out,
        root_out,
        hidden_out,
    ):
        joined = jnp.concatenate([kept_a[0], got[0], kept_b[0], got[1]], 0)
        joined_out[...] = joined
        mixed = dot(joined, w_qkv_ref[...])
        queries = (mixed[:, :width] + b_qv_ref[0:1, :]).astype(BF16)
        queries = (queries.astype(F32) * score_scale).astype(BF16)
        keys = mixed[:, width : 2 * width].astype(BF16)
        values = (mixed[:, 2 * width :] + b_qv_ref[1:2, :]).astype(BF16)
        mixed_out[:, :width] = queries
        mixed_out[:, width : 2 * width] = keys
        mixed_out[:, 2 * width :] = values
        contexts = []
        for pair in range(2):
            seen = live_ref[pair] > 0
            span = slice(pair * length, (pair + 1) * length)
            heads = []
            for block in range(blocks):
                cols = slice(block * duo, (block + 1) * duo)
                scores = dot(split_heads(queries[span, cols]), keys[span, cols], 1, 1)
                scores = jnp.where(seen, scores, -1e30)
                powered = jnp.exp(scores - jnp.max(scores, axis=-1, keepdims=True))
                low_probs = powered * (1.0 / jnp.sum(powered, axis=-1, keepdims=True))
                low_probs = low_probs.astype(BF16)
                probs_out[pair, block] = low_probs
                heads.append(
                    dot(side_by_side(low_probs), split_heads(values[span, cols])).astype(BF16)
                )
            contexts.append(jnp.concatenate(heads, 1))
        context = jnp.concatenate(contexts, 0)
        context_out[...] = context
        pre_one = joined.astype(F32) + dot(context, w_out_ref[...]) + biases_ref[0:1, :]
        normed, root = normal_form(pre_one)
        normed_out[...] = normed
        root_out[...] = jnp.broadcast_to(root, root_out.shape)
        hidden_out[...] = (normed * gains_ref[0:1, :] + biases_ref[1:2, :]).astype(BF16)

    start = first // 2

    def by_rows(columns):
        return pl.BlockSpec((2 * length, columns), lambda i, s: (start + i, 0))

    slot = (1, slot_rows, width)
    total = half * length
    return call(
        kernel,
        scalars,
        [rows, rows, received, live, w_qkv, b_qv, w_out, norm_gains, bias_rows],
        [
            pl.BlockSpec(slot, lambda i, s: (kept_slot(s, first + 2 * i, half), 0, 0)),
            pl.BlockSpec(slot, lambda i, s: (kept_slot(s, first + 2 * i + 1, half), 0, 0)),
            pl.BlockSpec((2, slot_rows, width), lambda i, s: (i, 0, 0)),
            pl.BlockSpec((2, 1, length), lambda i, s: (start + i, 0, 0)),
            whole(w_qkv),
            whole(b_qv),
            whole(w_out),
            whole(norm_gains),
            whole(bias_rows),
        ],
        [
            by_rows(width),
            by_rows(3 * width),
            pl.BlockSpec((2, blocks, 2 * length, length), lambda i, s: (start + i, 0, 0, 0)),
            by_rows(width),
            by_rows(width),
            by_rows(128),
            by_rows(width),
        ],
        [
            jax.ShapeDtypeStruct((total, width), BF16),
            jax.ShapeDtypeStruct((total, 3 * width), BF16),
            jax.ShapeDtypeStruct((half, blocks, 2 * length, length), BF16),
            jax.ShapeDtypeStruct((total, width), BF16),
            jax.ShapeDtypeStruct((total, width), F32),
            jax.ShapeDtypeStruct((total, 128), F32),
            jax.ShapeDtypeStruct((total, width), BF16),
        ],
        (pairs // 2,),
        "attention_forward",
        pairs * length * width * width * 10,
        into=into,
        after=after,
        moved=12 * 2**20,
    )


def feed_forward(scalars, low_hidden, normed, cot, far_cot, weights, first, half, into=(), after=()):
    w_in, b_in, w_back, norm_gains, bias_rows = weights
    slot_rows, width = cot.shape[1:]
    pairs = far_cot.shape[0]
    inner_width = w_in.shape[1]
    length = 2 * slot_rows
    chunk = 768
    steps = inner_width // chunk

    def kernel(scalars_ref, *refs):
        hidden_ref, normed_ref = refs[:2]
        cots = refs[2 : 2 + pairs]
        cot_far, w_in_ref, b_in_ref, w_back_ref, gains_ref, biases_ref = refs[2 + pairs : 8 + pairs]
        act_out, slope_out, branch_out, d_two_out, kept_out, far_out, sums_out, held = refs[
            8 + pairs :
        ]
        step = pl.program_id(0)
        inner = dot(hidden_ref[...], w_in_ref[...]) + b_in_ref[...]
        normal = 0.5 + 0.5 * lax.erf(inner * (0.5**0.5))
        low_act = (inner * normal).astype(BF16)
        density = jnp.exp(inner * inner * -0.5) * 0.3989422804014327
        act_out[...] = low_act
        slope_out[...] = (normal + inner * density).astype(BF16)
        share = dot(low_act, w_back_ref[...])

        @pl.when(step == 0)
        def _():
            held[...] = (
                normed_ref[...] * gains_ref[0:1, :]
                + (biases_ref[1:2, :] + biases_ref[2:3, :])
                + share
            )

        @pl.when(step > 0)
        def _():
            held[...] += share

        @pl.when(step == steps - 1)
        def _():
            sums = [jnp.zeros((1, width), F32)] * 3
            for i in range(pairs):
                span = slice(i * length, (i + 1) * length)
                scaled, root = normal_form(held[span])
                output = (scaled * gains_ref[1:2, :] + biases_ref[3:4, :]).astype(BF16)
                kept_out[i] = output[:slot_rows]
                far_out[i] = output[slot_rows:]
                here = jnp.concatenate([cots[i][0], cot_far[i]], 0).astype(F32)
                d_two = normal_back(here * gains_ref[1:2, :], scaled, root)
                d_two_out[span] = d_two
                branch_out[span] = d_two.astype(BF16)
                for j, part in enumerate((here * scaled, here, d_two)):
                    sums[j] = sums[j] + row_sum(part)
            sums_out[...] = jnp.concatenate(sums + [jnp.zeros((5, width), F32)], 0)

    part = first // pairs
    height = pairs * length

    def by_rows(columns):
        return pl.BlockSpec((height, columns), lambda i, s: (part, 0))

    def slot(j):
        return pl.BlockSpec(
            (1, slot_rows, width), lambda i, s: (kept_slot(s, first + j, half), 0, 0)
        )

    def by_chunk():
        return pl.BlockSpec((height, chunk), lambda i, s: (part, i))

    total = half * length
    pair_block = pl.BlockSpec((pairs, slot_rows, width), lambda i, s: (part, 0, 0))
    return call(
        kernel,
        scalars,
        [low_hidden, normed]
        + [cot] * pairs
        + [far_cot, w_in, b_in, w_back, norm_gains, bias_rows],
        [by_rows(width), by_rows(width)]
        + [slot(j) for j in range(pairs)]
        + [
            whole(far_cot),
            pl.BlockSpec((width, chunk), lambda i, s: (0, i)),
            pl.BlockSpec((1, chunk), lambda i, s: (0, i)),
            pl.BlockSpec((chunk, width), lambda i, s: (i, 0)),
            whole(norm_gains),
            whole(bias_rows),
        ],
        [
            by_chunk(),
            by_chunk(),
            by_rows(width),
            by_rows(width),
            pair_block,
            pair_block,
            pl.BlockSpec((8, width), lambda i, s: (0, 0)),
        ],
        [
            jax.ShapeDtypeStruct((total, inner_width), BF16),
            jax.ShapeDtypeStruct((total, inner_width), BF16),
            jax.ShapeDtypeStruct((total, width), BF16),
            jax.ShapeDtypeStruct((total, width), F32),
            jax.ShapeDtypeStruct((half, slot_rows, width), BF16),
            jax.ShapeDtypeStruct((half, slot_rows, width), BF16),
            jax.ShapeDtypeStruct((8, width), F32),
        ],
        (steps,),
        "feed_forward",
        height * width * inner_width * 6,
        into=into,
        after=after,
        scratch=[pltpu.VMEM((height, width), F32)],
        moved=20 * 2**20,
    )


def feed_backward(scalars, kept, weights, part, parts, into=(), after=()):
    branch, slope, d_two, normed, root = kept
    w_in, w_back, norm_gains = weights
    total, width = branch.shape
    inner_width = slope.shape[1]
    chunk = 768
    steps = inner_width // chunk
    height = total // parts

    def kernel(
        scalars_ref,
        branch_ref,
        slope_ref,
        d_two_ref,
        normed_ref,
        root_ref,
        w_in_ref,
        w_back_ref,
        gains_ref,
        low_inner_out,
        d_one_out,
        low_attn_out,
        sums_out,
        inner_sum_out,
        held,
    ):
        step = pl.program_id(0)
        d_inner = dot(branch_ref[...], w_back_ref[...], 1, 1) * slope_ref[...].astype(F32)
        low_inner = d_inner.astype(BF16)
        low_inner_out[...] = low_inner
        inner_sum_out[...] = jnp.broadcast_to(row_sum(d_inner), inner_sum_out.shape)
        share = dot(low_inner, w_in_ref[...], 1, 1)

        @pl.when(step == 0)
        def _():
            held[...] = d_two_ref[...] + share

        @pl.when(step > 0)
        def _():
            held[...] += share

        @pl.when(step == steps - 1)
        def _():
            sums = [jnp.zeros((1, width), F32)] * 3
            piece = 128
            for i in range(height // piece):
                span = slice(i * piece, (i + 1) * piece)
                d_hidden, scaled = held[span], normed_ref[span]
                d_one = normal_back(d_hidden * gains_ref[0:1, :], scaled, root_ref[span, 0:1])
                d_one_out[span] = d_one
                low_attn_out[span] = d_one.astype(BF16)
                for j, term in enumerate((d_hidden * scaled, d_hidden, d_one)):
                    sums[j] = sums[j] + row_sum(term)
            sums_out[...] = jnp.concatenate(sums + [jnp.zeros((5, width), F32)], 0)

    def by_rows(columns):
        return pl.BlockSpec((height, columns), lambda i, s: (part, 0))

    by_chunk = pl.BlockSpec((height, chunk), lambda i, s: (part, i))
    return call(
        kernel,
        scalars,
        [branch, slope, d_two, normed, root, w_in, w_back, norm_gains],
        [
            by_rows(width),
            by_chunk,
            by_rows(width),
            by_rows(width),
            by_rows(128),
            pl.BlockSpec((width, chunk), lambda i, s: (0, i)),
            pl.BlockSpec((chunk, width), lambda i, s: (i, 0)),
            whole(norm_gains),
        ],
        [
            by_chunk,
            by_rows(width),
            by_rows(width),
            pl.BlockSpec((8, width), lambda i, s: (0, 0)),
            pl.BlockSpec((8, chunk), lambda i, s: (0, i)),
        ],
        [
            jax.ShapeDtypeStruct((total, inner_width), BF16),
            jax.ShapeDtypeStruct((total, width), F32),
            jax.ShapeDtypeStruct((total, width), BF16),
            jax.ShapeDtypeStruct((8, width), F32),
            jax.ShapeDtypeStruct((8, inner_width), F32),
        ],
        (steps,),
        "feed_backward",
        height * width * inner_width * 4,
        into=into,
        after=after,
        scratch=[pltpu.VMEM((height, width), F32)],
        moved=16 * 2**20,
    )


def attention_backward(scalars, kept, weights, part, parts, into=(), after=()):
    low_attn, mixed, probs, d_one = kept
    w_out, w_qkv = weights
    total, width = low_attn.shape
    pairs, blocks, _, length = probs.shape
    duo = width // blocks
    slot_rows = length // 2
    score_scale = (width // HEADS) ** (-0.5)

    def kernel(
        scalars_ref,
        low_attn_ref,
        mixed_ref,
        probs_ref,
        d_one_ref,
        w_out_ref,
        w_qkv_ref,
        d_mixed_out,
        kept_out,
        far_out,
        sums_out,
    ):
        @pl.when(pl.program_id(0) == 0)
        def _():
            sums_out[...] = jnp.zeros_like(sums_out)

        d_context = dot(low_attn_ref[...], w_out_ref[...], 1, 1).astype(BF16)
        for pair in range(2):
            span = slice(pair * length, (pair + 1) * length)
            for block in range(blocks):
                cols = slice(block * duo, (block + 1) * duo)
                key_cols = slice(width + block * duo, width + (block + 1) * duo)
                value_cols = slice(2 * width + block * duo, 2 * width + (block + 1) * duo)
                queries = split_heads(mixed_ref[span, cols])
                keys = mixed_ref[span, key_cols]
                values = mixed_ref[span, value_cols]
                d_heads = split_heads(d_context[span, cols])
                low_probs = probs_ref[pair, block]
                wide = low_probs.astype(F32)
                d_probs = dot(d_heads, values, 1, 1)
                d_scores = wide * (d_probs - jnp.sum(wide * d_probs, axis=-1, keepdims=True))
                d_scores = d_scores.astype(BF16)
                d_queries = dot(side_by_side(d_scores), split_heads(keys)) * score_scale
                d_mixed_out[span, cols] = d_queries.astype(BF16)
                d_mixed_out[span, key_cols] = dot(d_scores, queries, 0, 0).astype(BF16)
                d_mixed_out[span, value_cols] = dot(low_probs, d_heads, 0, 0).astype(BF16)
        d_mixed = d_mixed_out[...]
        sums_out[0:1, :] += row_sum(d_mixed[:, :width].astype(F32))
        sums_out[1:2, :] += row_sum(d_mixed[:, 2 * width :].astype(F32))
        d_rows = (d_one_ref[...] + dot(d_mixed, w_qkv_ref[...], 1, 1)).astype(BF16)
        for i in range(2):
            kept_out[i] = d_rows[i * length : i * length + slot_rows]
            far_out[i] = d_rows[i * length + slot_rows : (i + 1) * length]

    steps = pairs // 2 // parts
    start = part * steps

    def by_rows(columns):
        return pl.BlockSpec((2 * length, columns), lambda i, s: (start + i, 0))

    two = pl.BlockSpec((2, slot_rows, width), lambda i, s: (start + i, 0, 0))
    return call(
        kernel,
        scalars,
        [low_attn, mixed, probs, d_one, w_out, w_qkv],
        [
            by_rows(width),
            by_rows(3 * width),
            pl.BlockSpec((2, blocks, 2 * length, length), lambda i, s: (start + i, 0, 0, 0)),
            by_rows(width),
            whole(w_out),
            whole(w_qkv),
        ],
        [by_rows(3 * width), two, two, pl.BlockSpec((8, width), lambda i, s: (0, 0))],
        [
            jax.ShapeDtypeStruct((total, 3 * width), BF16),
            jax.ShapeDtypeStruct((pairs, slot_rows, width), BF16),
            jax.ShapeDtypeStruct((pairs, slot_rows, width), BF16),
            jax.ShapeDtypeStruct((8, width), F32),
        ],
        (steps,),
        "attention_backward",
        total // parts * width * width * 20,
        into=into,
        after=after,
        moved=12 * 2**20,
    )


def grad_by_columns(scalars, left, right, shards, first, count, chunk, base, after=()):
    total, height = left.shape
    shard = height // shards
    places = shards // 2

    def kernel(scalars_ref, left_ref, right_ref, send_out, keep_out, held):
        core, place = scalars_ref[base + 1], scalars_ref[base + 2]
        held[...] = dot(left_ref[...], right_ref[...], 0, 0).astype(BF16)
        for j in range(places):
            row = (place ^ j) * 2
            send_out[j] = held[pl.ds(pl.multiple_of((row + 1 - core) * shard, 16), shard), :]
            keep_out[j] = held[pl.ds(pl.multiple_of((row + core) * shard, 16), shard), :]

    out = pl.BlockSpec((places, shard, chunk), lambda i, s: (0, 0, i))
    shape = jax.ShapeDtypeStruct((places, shard, count * chunk), BF16)
    return call(
        kernel,
        scalars,
        [left, right],
        [whole(left), pl.BlockSpec((total, chunk), lambda i, s: (0, first + i))],
        [out, out],
        [shape, shape],
        (count,),
        "grad_by_columns",
        2 * total * height * count * chunk,
        after=after,
        scratch=[pltpu.VMEM((height, chunk), BF16)],
        moved=8 * 2**20,
    )


def grad_by_rows(scalars, left, right, shards, first, width, base, after=()):
    total, height = left.shape
    shard = height // shards
    places = shards // 2
    chunk = 4 * shard

    def kernel(scalars_ref, left_ref, right_ref, send_out, keep_out, held):
        core, place = scalars_ref[base + 1], scalars_ref[base + 2]
        held[...] = dot(left_ref[...], right_ref[:, first : first + width], 0, 0).astype(BF16)
        for j in range(2):
            row = ((place & 1) ^ j) * 2
            send_out[j] = held[pl.ds(pl.multiple_of((row + 1 - core) * shard, 16), shard), :]
            keep_out[j] = held[pl.ds(pl.multiple_of((row + core) * shard, 16), shard), :]

    out = pl.BlockSpec((2, shard, width), lambda i, s: ((s[base + 2] >> 1) ^ i, 0, 0))
    shape = jax.ShapeDtypeStruct((places, shard, width), BF16)
    return call(
        kernel,
        scalars,
        [left, right],
        [pl.BlockSpec((total, chunk), lambda i, s: (0, i)), whole(right)],
        [out, out],
        [shape, shape],
        (height // chunk,),
        "grad_by_rows",
        2 * total * height * width,
        after=after,
        scratch=[pltpu.VMEM((chunk, width), BF16)],
        moved=8 * 2**20,
    )


def added(parts):
    total = parts[0].astype(F32)
    for part in parts[1:]:
        total = total + part.astype(F32)
    return total.astype(BF16)


class Shards:
    def __init__(self, send, keep, order):
        places, self.shard, self.width = send.shape
        bits = places.bit_length() - 1
        self.shape = (2,) * bits + (self.shard, self.width)
        self.order = list(order)
        self.left = list(range(bits))[::-1]
        self.held = [keep.reshape(self.shape)]
        self.coming = flipped(send, "dp", 1).reshape(self.shape)

    def step(self, after=None):
        coming = self.coming
        if after is not None:
            coming, _ = lax.optimization_barrier((coming, after))
        self.held.append(coming)
        if not self.order:
            self.mine = lax.optimization_barrier(added(self.held))
            self.coming = flipped(self.mine, "mod", 1)
            return self.mine
        bit = self.order.pop(0)
        dim = self.left.index(bit)
        away = added([lax.index_in_dim(part, 1, dim, keepdims=False) for part in self.held])
        self.held = [lax.index_in_dim(part, 0, dim, keepdims=False) for part in self.held]
        self.left.remove(bit)
        self.coming = flipped(away, "dp", 2 << bit)
        return away

    def result(self):
        return self.mine.astype(F32) + self.coming.astype(F32)


def reduce_plain(left, right):
    share = lax.psum_scatter(dot(left, right, 0, 0), "dp", scatter_dimension=0, tiled=True)
    return lax.psum(share.astype(BF16), "mod").astype(F32)


def sum_everywhere(value):
    shards = lax.axis_size("dp")
    if shards & (shards - 1):
        return lax.psum(value, ("mod", "dp"))
    mask = 1
    while mask < shards:
        value = value + flipped(value, "dp", mask)
        mask *= 2
    return value + flipped(value, "mod", 1)


def body(
    layer_rows,
    cotangent,
    row_live,
    partner,
    w_qkv,
    b_qv,
    w_out,
    norm_gains,
    bias_rows,
    w_in,
    b_in,
    w_back,
):
    side = lax.axis_index("mod")
    place = lax.axis_index("dp")
    shards = lax.axis_size("dp")
    groups = partner.shape[1]
    half = groups // 2
    width = layer_rows.shape[2]
    slot_rows = layer_rows.shape[1] // groups
    inner_width = w_in.shape[1]
    slots = (groups, slot_rows, width)
    rows = layer_rows[0].reshape(slots)
    cot = cotangent[0].reshape(slots)
    scalars = jnp.concatenate(
        [partner[0], jnp.stack([side, place & 1, place >> 1]).astype(jnp.int32)]
    )
    cut = half // 2
    sent_a = gather_sent(scalars, rows, half, 0, cut)
    got_a = flipped(sent_a, "mod", 1)
    sent_b = gather_sent(scalars, rows, half, cut, cut, [sent_a])
    got_b = flipped(sent_b, "mod", 1)
    sent_cot_a = gather_sent(scalars, cot, half, 0, cut, [sent_b])
    cot_a = flipped(sent_cot_a, "mod", 1)
    sent_cot_b = gather_sent(scalars, cot, half, cut, cut, [sent_cot_a])
    cot_b = flipped(sent_cot_b, "mod", 1)

    live = row_live.reshape(2, groups, slot_rows)
    words_live = lax.dynamic_slice_in_dim(live[0], side * half, half, 0)
    region_live = live[1][lax.dynamic_slice_in_dim(partner[0], side * half, half, 0)]
    is_first = side == 0
    seen = jnp.concatenate(
        [
            jnp.where(is_first, words_live, region_live),
            jnp.where(is_first, region_live, words_live),
        ],
        1,
    )[:, None, :]

    heads_weights = (w_qkv, b_qv, w_out, norm_gains, bias_rows)
    first_part = attention_forward(
        scalars, rows, got_a, seen, heads_weights, 0, half, after=[sent_cot_b]
    )
    joined, mixed, probs, context, normed, root, low_hidden = attention_forward(
        scalars, rows, got_b, seen, heads_weights, cut, half, into=first_part
    )
    feed_weights = (w_in, b_in.reshape(1, inner_width), w_back, norm_gains, bias_rows)
    *first_part, sums_two_a = feed_forward(
        scalars, low_hidden, normed, cot, cot_a, feed_weights, 0, half
    )
    act, slope, branch, d_two, out_kept, out_far, sums_two_b = feed_forward(
        scalars, low_hidden, normed, cot, cot_b, feed_weights, cut, half, into=first_part
    )
    sums_two = sums_two_a + sums_two_b

    aligned = shards % 4 == 0 and shards & (shards - 1) == 0 and (width // shards) % 16 == 0
    back_kept = (branch, slope, d_two, normed, root)
    back_weights = (w_in, w_back, norm_gains)
    if aligned:
        bits = (shards // 2).bit_length() - 1
        order = list(range(bits))
        other = order[1:] + order[:1]
        back_a = Shards(*grad_by_rows(scalars, act, branch, shards, 0, 512, groups), order)
        back_b = Shards(
            *grad_by_rows(scalars, act, branch, shards, 512, width - 512, groups, [back_a.held[0]]),
            order,
        )
        sent = back_a.step(back_b.held[0])
        out_back = flipped(out_far, "mod", 1)
        *first_part, sums_one_a, inner_a = feed_backward(
            scalars, back_kept, back_weights, 0, 2, after=[sent]
        )
        sent = back_b.step(inner_a)
        low_inner, d_one, low_attn, sums_one_b, inner_b = feed_backward(
            scalars, back_kept, back_weights, 1, 2, into=first_part, after=[sent]
        )
        span = inner_width // 768 // 2
        in_a = Shards(
            *grad_by_columns(scalars, low_hidden, low_inner, shards, 0, span, 768, groups), order
        )
        in_b = Shards(
            *grad_by_columns(
                scalars, low_hidden, low_inner, shards, span, span, 768, groups, [in_a.held[0]]
            ),
            order,
        )
        sent = [in_a.step(in_b.held[0]), back_a.step(in_b.held[0])]
        out = Shards(
            *grad_by_columns(scalars, context, low_attn, shards, 0, 1, 768, groups, sent), other
        )
        sent = [in_b.step(out.held[0]), out_back]
        attn_kept = (low_attn, mixed, probs, d_one)
        *first_part, sums_qv_a = attention_backward(
            scalars, attn_kept, (w_out, w_qkv), 0, 2, after=sent
        )
        sent = [part.step(sums_qv_a) for part in (back_a, back_b, out)]
        d_mixed, d_kept, d_far, sums_qv_b = attention_backward(
            scalars, attn_kept, (w_out, w_qkv), 1, 2, into=first_part, after=sent
        )
        qkv = []
        sent = [part.step(sums_qv_b) for part in (back_a, back_b, in_a, out)]
        for i in range(3):
            qkv.append(
                Shards(
                    *grad_by_columns(
                        scalars, joined, d_mixed, shards, i, 1, 768, groups, sent
                    ),
                    other if i == 1 else order,
                )
            )
            if i:
                sent = [qkv[i - 1].step(qkv[i].held[0])]
            else:
                sent = [qkv[0].held[0]]
        d_back = flipped(d_far, "mod", 1)
        pieces = [back_a, back_b, in_a, in_b, out] + qkv
        while any(not hasattr(piece, "mine") for piece in pieces):
            for piece in pieces:
                if not hasattr(piece, "mine"):
                    piece.step()
        done = [piece.result() for piece in pieces]
        grad_back = jnp.concatenate(done[0:2], 1)
        grad_in = jnp.concatenate(done[2:4], 1)
        grad_out = done[4]
        grad_qkv = jnp.concatenate(done[5:], 1)
    else:
        out_back = flipped(out_far, "mod", 1)
        *first_part, sums_one_a, inner_a = feed_backward(scalars, back_kept, back_weights, 0, 2)
        low_inner, d_one, low_attn, sums_one_b, inner_b = feed_backward(
            scalars, back_kept, back_weights, 1, 2, into=first_part
        )
        attn_kept = (low_attn, mixed, probs, d_one)
        *first_part, sums_qv_a = attention_backward(scalars, attn_kept, (w_out, w_qkv), 0, 2)
        d_mixed, d_kept, d_far, sums_qv_b = attention_backward(
            scalars, attn_kept, (w_out, w_qkv), 1, 2, into=first_part
        )
        d_back = flipped(d_far, "mod", 1)
        grad_back = reduce_plain(act, branch)
        grad_in = reduce_plain(low_hidden, low_inner)
        grad_out = reduce_plain(context, low_attn)
        grad_qkv = reduce_plain(joined, d_mixed)

    sums_one = sums_one_a + sums_one_b
    sums_qv = sums_qv_a + sums_qv_b
    inner_sum = (inner_a + inner_b)[0]
    small = jnp.concatenate(
        [
            sums_qv[0:2],
            sums_one[0:1],
            sums_two[0:1],
            sums_one[2:3],
            sums_one[1:2],
            sums_two[2:3],
            sums_two[1:2],
            inner_sum.reshape(-1, width),
        ],
        0,
    )
    small = sum_everywhere(small)
    shard = width // shards
    rows_small = lax.dynamic_slice_in_dim(small[:8], place * shard, shard, 1)
    inner_shard = inner_width // shards
    grad_b_in = lax.dynamic_slice_in_dim(small[8:].reshape(-1), place * inner_shard, inner_shard)

    out_rows = scatter_home(scalars, out_kept, out_back, half).reshape(1, -1, width)
    grad_rows = scatter_home(scalars, d_kept, d_back, half).reshape(1, -1, width)
    return (
        out_rows,
        grad_rows,
        grad_qkv,
        rows_small[0:2],
        grad_out,
        rows_small[2:4],
        rows_small[4:8],
        grad_in,
        grad_b_in,
        grad_back,
    )


def solution(mesh):
    return jax.shard_map(
        body,
        mesh=mesh,
        in_specs=(
            P("mod", "dp", None),
            P("mod", "dp", None),
            P(None, "dp"),
            P("dp", None),
            P(),
            P(),
            P(),
            P(),
            P(),
            P(),
            P(),
            P(),
        ),
        out_specs=(
            P("mod", "dp", None),
            P("mod", "dp", None),
            P("dp", None),
            P(None, "dp"),
            P("dp", None),
            P(None, "dp"),
            P(None, "dp"),
            P("dp", None),
            P("dp"),
            P("dp", None),
        ),
        check_vma=False,
    )
```

```python
import functools

import jax
import jax.numpy as jnp
from jax import lax
from jax.experimental import pallas as pl
from jax.experimental.pallas import tpu as pltpu
from jax.sharding import PartitionSpec as P

HEADS = 12
EPSILON = 1e-12
F32 = jnp.float32
BF16 = jnp.bfloat16
VMEM_LIMIT = 56 * 2**20


def dot(left, right, left_dim=1, right_dim=0):
    return lax.dot_general(
        left, right, (((left_dim,), (right_dim,)), ((), ())), preferred_element_type=F32
    )


def flipped(value, axis, mask):
    pairs = [(source, source ^ mask) for source in range(lax.axis_size(axis))]
    return lax.ppermute(value, axis, pairs)


def params(limit=VMEM_LIMIT):
    return pltpu.CompilerParams(vmem_limit_bytes=limit)


def kept_slot(scalars, pair, half):
    groups = 2 * half
    side = scalars[groups]
    place = side * half + pair
    return jnp.where(side == 0, place, scalars[place])


def sent_slot(scalars, pair, half):
    groups = 2 * half
    side = scalars[groups]
    place = (1 - side) * half + pair
    return jnp.where(side == 0, place, scalars[place])


ANY = pl.BlockSpec(memory_space=pl.ANY)


def call(kernel, scalars, operands, in_specs, out_specs, out_shape, grid, name, work, **more):
    after = list(more.get("after", ()))
    into = list(more.get("into", ()))
    scratch = list(more.get("scratch", ()))
    taken, spare = len(operands), len(into) + len(after)

    def wrapped(scalars_ref, *refs):
        kernel(scalars_ref, *refs[:taken], *refs[taken + spare :])

    return pl.pallas_call(
        wrapped,
        grid_spec=pltpu.PrefetchScalarGridSpec(
            num_scalar_prefetch=1,
            grid=grid,
            in_specs=list(in_specs) + [ANY] * spare,
            out_specs=out_specs,
            scratch_shapes=scratch,
        ),
        out_shape=out_shape,
        input_output_aliases={
            1 + taken + i: i + more.get("into_first", 0) for i in range(len(into))
        },
        compiler_params=params(more.get("limit", VMEM_LIMIT)),
        cost_estimate=pl.CostEstimate(
            flops=int(work), bytes_accessed=more.get("moved", 2**20), transcendentals=0
        ),
        name=name,
    )(scalars, *operands, *into, *after)


def gather_sent(scalars, rows, half, first, count, after=()):
    slot_rows, width = rows.shape[1:]

    def kernel(scalars_ref, rows_ref, out, sems):
        copies = [
            pltpu.make_async_copy(
                rows_ref.at[sent_slot(scalars_ref, first + i, half)], out.at[i], sems.at[i]
            )
            for i in range(count)
        ]
        for copy in copies:
            copy.start()
        for copy in copies:
            copy.wait()

    shape = (count, slot_rows, width)
    return call(
        kernel,
        scalars,
        [rows],
        [ANY],
        pl.BlockSpec(shape, lambda i, s: (0, 0, 0)),
        jax.ShapeDtypeStruct(shape, rows.dtype),
        (1,),
        "gather_sent",
        1e6,
        scratch=[pltpu.SemaphoreType.DMA((count,))],
        after=after,
        limit=8 * 2**20,
    )


def scatter_home(scalars, kept, back, half, after=()):
    slot_rows, width = kept.shape[1:]

    def kernel(scalars_ref, kept_ref, back_ref, out, sems):
        copies = []
        for i in range(half):
            copies.append(
                pltpu.make_async_copy(
                    kept_ref.at[i], out.at[kept_slot(scalars_ref, i, half)], sems.at[0, i]
                )
            )
            copies.append(
                pltpu.make_async_copy(
                    back_ref.at[i], out.at[sent_slot(scalars_ref, i, half)], sems.at[1, i]
                )
            )
        for copy in copies:
            copy.start()
        for copy in copies:
            copy.wait()

    shape = (2 * half, slot_rows, width)
    return call(
        kernel,
        scalars,
        [kept, back],
        [ANY, ANY],
        pl.BlockSpec(shape, lambda i, s: (0, 0, 0)),
        jax.ShapeDtypeStruct(shape, kept.dtype),
        (1,),
        "scatter_home",
        1e6,
        scratch=[pltpu.SemaphoreType.DMA((2, half))],
        after=after,
        limit=8 * 2**20,
    )


def split_heads(value):
    low = lax.broadcasted_iota(jnp.int32, value.shape, 1) < value.shape[1] // 2
    zero = jnp.zeros_like(value)
    return jnp.concatenate([jnp.where(low, value, zero), jnp.where(low, zero, value)], 0)


def side_by_side(value):
    rows = value.shape[0] // 2
    return jnp.concatenate([value[:rows], value[rows:]], 1)


def row_sum(value):
    return jnp.sum(value, axis=0, keepdims=True)


def normal_form(value):
    centered = value - jnp.mean(value, axis=-1, keepdims=True)
    root = lax.rsqrt(jnp.mean(centered * centered, axis=-1, keepdims=True) + EPSILON)
    return centered * root, root


def normal_back(lifted, normed, root):
    return root * (
        lifted
        - jnp.mean(lifted, axis=-1, keepdims=True)
        - normed * jnp.mean(lifted * normed, axis=-1, keepdims=True)
    )


def whole(array):
    return pl.BlockSpec(
        array.shape, lambda *_: (0,) * array.ndim, pipeline_mode=pl.Buffered(1)
    )


def attention_forward(
    scalars, rows, received, live, weights, first, half, into=(), after=()
):
    w_qkv, b_qv, w_out, norm_gains, bias_rows = weights
    slot_rows, width = rows.shape[1:]
    pairs = received.shape[0]
    length = 2 * slot_rows
    duo = 2 * width // HEADS
    blocks = width // duo
    score_scale = (width // HEADS) ** (-0.5)

    def kernel(
        scalars_ref,
        kept_a,
        kept_b,
        got,
        live_ref,
        w_qkv_ref,
        b_qv_ref,
        w_out_ref,
        gains_ref,
        biases_ref,
        joined_out,
        mixed_out,
        probs_out,
        context_out,
        normed_out,
        root_out,
    ):
        joined = jnp.concatenate([kept_a[0], got[0], kept_b[0], got[1]], 0)
        joined_out[...] = joined
        mixed = dot(joined, w_qkv_ref[...])
        queries = (mixed[:, :width] + b_qv_ref[0:1, :]).astype(BF16)
        queries = (queries.astype(F32) * score_scale).astype(BF16)
        keys = mixed[:, width : 2 * width].astype(BF16)
        values = (mixed[:, 2 * width :] + b_qv_ref[1:2, :]).astype(BF16)
        mixed_out[:, :width] = queries
        mixed_out[:, width : 2 * width] = keys
        mixed_out[:, 2 * width :] = values
        contexts = []
        for pair in range(2):
            seen = live_ref[pair] > 0
            span = slice(pair * length, (pair + 1) * length)
            heads = []
            for block in range(blocks):
                cols = slice(block * duo, (block + 1) * duo)
                scores = dot(split_heads(queries[span, cols]), keys[span, cols], 1, 1)
                scores = jnp.where(seen, scores, -1e30)
                powered = jnp.exp(scores - jnp.max(scores, axis=-1, keepdims=True))
                low_probs = powered * (1.0 / jnp.sum(powered, axis=-1, keepdims=True))
                low_probs = low_probs.astype(BF16)
                probs_out[pair, block] = low_probs
                heads.append(
                    dot(side_by_side(low_probs), split_heads(values[span, cols])).astype(BF16)
                )
            contexts.append(jnp.concatenate(heads, 1))
        context = jnp.concatenate(contexts, 0)
        context_out[...] = context
        pre_one = joined.astype(F32) + dot(context, w_out_ref[...]) + biases_ref[0:1, :]
        normed, root = normal_form(pre_one)
        normed_out[...] = normed.astype(BF16)
        root_out[...] = jnp.broadcast_to(root, root_out.shape)

    start = first // 2

    def by_rows(columns):
        return pl.BlockSpec((2 * length, columns), lambda i, s: (start + i, 0))

    slot = (1, slot_rows, width)
    total = half * length
    return call(
        kernel,
        scalars,
        [rows, rows, received, live, w_qkv, b_qv, w_out, norm_gains, bias_rows],
        [
            pl.BlockSpec(slot, lambda i, s: (kept_slot(s, first + 2 * i, half), 0, 0)),
            pl.BlockSpec(slot, lambda i, s: (kept_slot(s, first + 2 * i + 1, half), 0, 0)),
            pl.BlockSpec((2, slot_rows, width), lambda i, s: (i, 0, 0)),
            pl.BlockSpec((2, 1, length), lambda i, s: (start + i, 0, 0)),
            whole(w_qkv),
            whole(b_qv),
            whole(w_out),
            whole(norm_gains),
            whole(bias_rows),
        ],
        [
            by_rows(width),
            by_rows(3 * width),
            pl.BlockSpec((2, blocks, 2 * length, length), lambda i, s: (start + i, 0, 0, 0)),
            by_rows(width),
            by_rows(width),
            by_rows(128),
        ],
        [
            jax.ShapeDtypeStruct((total, width), BF16),
            jax.ShapeDtypeStruct((total, 3 * width), BF16),
            jax.ShapeDtypeStruct((half, blocks, 2 * length, length), BF16),
            jax.ShapeDtypeStruct((total, width), BF16),
            jax.ShapeDtypeStruct((total, width), BF16),
            jax.ShapeDtypeStruct((total, 128), F32),
        ],
        (pairs // 2,),
        "attention_forward",
        pairs * length * width * width * 10,
        into=into,
        after=after,
        moved=12 * 2**20,
    )


def spread(grad, out_pairs, scalars_ref, base, shard, first_row, places):
    core = scalars_ref[base + 1]
    for j in range(places):
        row = (first_row ^ j) * 2
        for out, which in ((out_pairs[0], 1 - core), (out_pairs[1], core)):
            out[j] = grad[pl.ds(pl.multiple_of((row + which) * shard, 16), shard), :]


def feed_forward(scalars, normed, cot, far_cot, weights, half, shards, base, after=()):
    w_in, b_in, w_back, norm_gains, bias_rows = weights
    slot_rows, width = cot.shape[1:]
    inner_width = w_in.shape[1]
    length = 2 * slot_rows
    rows = 2 * length
    height = half * length
    steps = half // 2
    chunk = 768
    chunks = inner_width // chunk
    shard = inner_width // shards
    places = shards // 2
    part = 4 * shard
    parts = inner_width // part
    left = width // 2

    def kernel(
        scalars_ref,
        normed_ref,
        cot_a,
        cot_b,
        cot_far,
        w_in_hbm,
        b_in_ref,
        w_back_hbm,
        gains_ref,
        biases_ref,
        slope_out,
        branch_out,
        kept_out,
        far_out,
        sums_out,
        send_a,
        keep_a,
        send_b,
        keep_b,
        w_in_ref,
        w_back_ref,
        held,
        acts,
        branches,
        grad_a,
        grad_b,
        sems,
    ):
        step = pl.program_id(0)

        def fetch_in(j):
            cols = pl.ds(j * chunk, chunk)
            return pltpu.make_async_copy(
                w_in_hbm.at[:, cols], w_in_ref.at[:, cols], sems.at[0, j]
            )

        def fetch_back(j):
            cols = pl.ds(j * chunk, chunk)
            return pltpu.make_async_copy(w_back_hbm.at[cols], w_back_ref.at[cols], sems.at[1, j])

        @pl.when(step == 0)
        def _():
            sums_out[...] = jnp.zeros_like(sums_out)
            for j in range(chunks):
                fetch_in(j).start()
                fetch_back(j).start()

        def close(pre_two, row):
            scaled, root = normal_form(pre_two)
            output = (scaled * gains_ref[1:2, :] + biases_ref[3:4, :]).astype(BF16)
            for i in range(2):
                kept_out[i] = output[i * length : i * length + slot_rows]
                far_out[i] = output[i * length + slot_rows : (i + 1) * length]
            here = jnp.concatenate([cot_a[0], cot_far[0], cot_b[0], cot_far[1]], 0).astype(F32)
            d_two = normal_back(here * gains_ref[1:2, :], scaled, root)
            low = d_two.astype(BF16)
            branch_out[...] = low
            branches[pl.ds(row, rows)] = low
            return jnp.concatenate([row_sum(here * scaled), row_sum(here), row_sum(d_two)], 0)

        def forward(first):
            hidden = normed_ref[...].astype(F32) * gains_ref[0:1, :] + biases_ref[1:2, :]
            low_hidden = hidden.astype(BF16)
            total = hidden + biases_ref[2:3, :]
            for j in range(chunks):
                cols = slice(j * chunk, (j + 1) * chunk)
                if first:
                    fetch_in(j).wait()
                inner = dot(low_hidden, w_in_ref[:, cols]) + b_in_ref[:, cols]
                normal = 0.5 + 0.5 * lax.erf(inner * (0.5**0.5))
                low_act = (inner * normal).astype(BF16)
                density = jnp.exp(inner * inner * -0.5) * 0.3989422804014327
                acts[pl.ds(step * rows, rows), cols] = low_act
                slope_out[:, cols] = (normal + inner * density).astype(BF16)
                if first:
                    fetch_back(j).wait()
                total = total + dot(low_act, w_back_ref[cols, :])
            return total

        @pl.when(step == 0)
        def _():
            held[...] = forward(True)

        @pl.when((step > 0) & (step < steps))
        def _():
            before = held[...]
            held[...] = forward(False)
            sums_out[0:3, :] += close(before, (step - 1) * rows)

        @pl.when(step == steps)
        def _():
            sums_out[0:3, :] += close(held[...], (step - 1) * rows)

        @pl.when(step >= steps)
        def _():
            start = pl.multiple_of((step - steps) * part, 128)
            grad = dot(acts[:, pl.ds(start, part)], branches[...], 0, 0).astype(BF16)
            grad_a[...] = grad[:, :left]
            grad_b[...] = grad[:, left:]
            first_row = scalars_ref[base + 2] & 1
            spread(grad_a, (send_a, keep_a), scalars_ref, base, shard, first_row, 2)
            spread(grad_b, (send_b, keep_b), scalars_ref, base, shard, first_row, 2)

    def ahead(i):
        return jnp.minimum(i, steps - 1)

    def behind(i):
        return jnp.clip(i - 1, 0, steps - 1)

    def slot(j):
        return pl.BlockSpec(
            (1, slot_rows, width), lambda i, s: (kept_slot(s, 2 * behind(i) + j, half), 0, 0)
        )

    duo = pl.BlockSpec((2, slot_rows, width), lambda i, s: (behind(i), 0, 0))
    grads = []
    for columns in (left, left, width - left, width - left):
        grads.append(
            pl.BlockSpec(
                (2, shard, columns),
                lambda i, s: ((s[base + 2] >> 1) ^ jnp.maximum(i - steps, 0), 0, 0),
            )
        )
    return call(
        kernel,
        scalars,
        [normed, cot, cot, far_cot, w_in, b_in, w_back, norm_gains, bias_rows],
        [
            pl.BlockSpec((rows, width), lambda i, s: (ahead(i), 0)),
            slot(0),
            slot(1),
            duo,
            ANY,
            whole(b_in),
            ANY,
            whole(norm_gains),
            whole(bias_rows),
        ],
        [
            pl.BlockSpec((rows, inner_width), lambda i, s: (ahead(i), 0)),
            pl.BlockSpec((rows, width), lambda i, s: (behind(i), 0)),
            duo,
            duo,
            pl.BlockSpec((8, width), lambda i, s: (0, 0)),
        ]
        + grads,
        [
            jax.ShapeDtypeStruct((height, inner_width), BF16),
            jax.ShapeDtypeStruct((height, width), BF16),
            jax.ShapeDtypeStruct((half, slot_rows, width), BF16),
            jax.ShapeDtypeStruct((half, slot_rows, width), BF16),
            jax.ShapeDtypeStruct((8, width), F32),
            jax.ShapeDtypeStruct((places, shard, left), BF16),
            jax.ShapeDtypeStruct((places, shard, left), BF16),
            jax.ShapeDtypeStruct((places, shard, width - left), BF16),
            jax.ShapeDtypeStruct((places, shard, width - left), BF16),
        ],
        (steps + parts,),
        "feed_forward",
        height * width * inner_width * 6,
        after=after,
        scratch=[
            pltpu.VMEM((width, inner_width), BF16),
            pltpu.VMEM((inner_width, width), BF16),
            pltpu.VMEM((rows, width), F32),
            pltpu.VMEM((height, inner_width), BF16),
            pltpu.VMEM((height, width), BF16),
            pltpu.VMEM((part, left), BF16),
            pltpu.VMEM((part, width - left), BF16),
            pltpu.SemaphoreType.DMA((2, chunks)),
        ],
        moved=28 * 2**20,
    )


def feed_backward(scalars, branch, slope, normed, root, context, weights, shards, base, after=()):
    w_in, w_back, norm_gains, bias_rows = weights
    total, width = branch.shape
    inner_width = slope.shape[1]
    chunk = 768
    steps = inner_width // chunk
    turn = steps // 2
    shard = width // shards
    places = shards // 2
    piece = 128

    def kernel(
        scalars_ref,
        branch_ref,
        slope_ref,
        normed_ref,
        root_ref,
        context_ref,
        w_in_ref,
        w_back_ref,
        gains_ref,
        biases_ref,
        low_attn_out,
        sums_out,
        inner_sum_out,
        send_a,
        keep_a,
        send_b,
        keep_b,
        send_out,
        keep_out,
        held,
        low_hidden,
        grad,
    ):
        step = pl.program_id(0)
        place = scalars_ref[base + 2]

        @pl.when(step == 0)
        def _():
            hidden = normed_ref[...].astype(F32) * gains_ref[0:1, :] + biases_ref[1:2, :]
            low_hidden[...] = hidden.astype(BF16)
            held[...] = branch_ref[...].astype(F32)

        sums = jnp.zeros((1, chunk), F32)
        lows = []
        for r in range(0, total, 256):
            span = slice(r, r + 256)
            d_inner = dot(branch_ref[span], w_back_ref[...], 1, 1) * slope_ref[span].astype(F32)
            sums = sums + row_sum(d_inner)
            low = d_inner.astype(BF16)
            lows.append(low)
            held[span] += dot(low, w_in_ref[...], 1, 1)
        inner_sum_out[...] = jnp.broadcast_to(sums, inner_sum_out.shape)
        grad[...] = dot(low_hidden[...], jnp.concatenate(lows, 0), 0, 0).astype(BF16)

        @pl.when(step < turn)
        def _():
            spread(grad, (send_a, keep_a), scalars_ref, base, shard, place, places)

        @pl.when(step >= turn)
        def _():
            spread(grad, (send_b, keep_b), scalars_ref, base, shard, place, places)

        @pl.when(step == steps - 1)
        def _():
            sums = [jnp.zeros((1, width), F32)] * 3
            lows = []
            for i in range(total // piece):
                span = slice(i * piece, (i + 1) * piece)
                d_hidden, scaled = held[span], normed_ref[span].astype(F32)
                d_one = normal_back(d_hidden * gains_ref[0:1, :], scaled, root_ref[span, 0:1])
                lows.append(d_one.astype(BF16))
                low_attn_out[span] = lows[-1]
                for j, term in enumerate((d_hidden * scaled, d_hidden, d_one)):
                    sums[j] = sums[j] + row_sum(term)
            sums_out[...] = jnp.concatenate(sums + [jnp.zeros((5, width), F32)], 0)
            grad[:, :width] = dot(context_ref[...], jnp.concatenate(lows, 0), 0, 0).astype(BF16)
            spread(grad, (send_out, keep_out), scalars_ref, base, shard, place, places)

    half_a = pl.BlockSpec((places, shard, chunk), lambda i, s: (0, 0, jnp.minimum(i, turn - 1)))
    half_b = pl.BlockSpec((places, shard, chunk), lambda i, s: (0, 0, jnp.maximum(i - turn, 0)))
    outer = pl.BlockSpec((places, shard, width), lambda i, s: (0, 0, 0))
    shape_a = jax.ShapeDtypeStruct((places, shard, turn * chunk), BF16)
    shape_b = jax.ShapeDtypeStruct((places, shard, inner_width - turn * chunk), BF16)
    shape_out = jax.ShapeDtypeStruct((places, shard, width), BF16)
    return call(
        kernel,
        scalars,
        [branch, slope, normed, root, context, w_in, w_back, norm_gains, bias_rows],
        [
            whole(branch),
            pl.BlockSpec((total, chunk), lambda i, s: (0, i)),
            whole(normed),
            whole(root),
            whole(context),
            pl.BlockSpec((width, chunk), lambda i, s: (0, i)),
            pl.BlockSpec((chunk, width), lambda i, s: (i, 0)),
            whole(norm_gains),
            whole(bias_rows),
        ],
        [
            pl.BlockSpec((total, width), lambda i, s: (0, 0)),
            pl.BlockSpec((8, width), lambda i, s: (0, 0)),
            pl.BlockSpec((8, chunk), lambda i, s: (0, i)),
            half_a,
            half_a,
            half_b,
            half_b,
            outer,
            outer,
        ],
        [
            jax.ShapeDtypeStruct((total, width), BF16),
            jax.ShapeDtypeStruct((8, width), F32),
            jax.ShapeDtypeStruct((8, inner_width), F32),
            shape_a,
            shape_a,
            shape_b,
            shape_b,
            shape_out,
            shape_out,
        ],
        (steps,),
        "feed_backward",
        total * width * inner_width * 6,
        after=after,
        scratch=[
            pltpu.VMEM((total, width), F32),
            pltpu.VMEM((total, width), BF16),
            pltpu.VMEM((width, chunk), BF16),
        ],
        moved=26 * 2**20,
    )


def attention_backward(scalars, kept, weights, part, parts, shards, base, into=(), after=()):
    low_attn, mixed, probs, joined = kept
    w_out, w_qkv = weights
    total, width = low_attn.shape
    pairs, blocks, _, length = probs.shape
    duo = width // blocks
    slot_rows = length // 2
    score_scale = (width // HEADS) ** (-0.5)
    steps = pairs // 2 // parts
    start = part * steps
    last = part == parts - 1
    before = start * 2 * length
    shard = width // shards
    places = shards // 2
    earlier = [into[0]] if last else []

    def kernel(
        scalars_ref,
        low_attn_ref,
        mixed_ref,
        probs_ref,
        w_out_ref,
        w_qkv_ref,
        *refs,
    ):
        if last:
            joined_ref, earlier_ref = refs[:2]
            refs = refs[2:]
        d_mixed_out, kept_out, far_out, sums_out = refs[:4]
        step = pl.program_id(0)

        @pl.when(step == 0)
        def _():
            sums_out[...] = jnp.zeros_like(sums_out)

        d_context = dot(low_attn_ref[...], w_out_ref[...], 1, 1).astype(BF16)
        for pair in range(2):
            span = slice(pair * length, (pair + 1) * length)
            for block in range(blocks):
                cols = slice(block * duo, (block + 1) * duo)
                key_cols = slice(width + block * duo, width + (block + 1) * duo)
                value_cols = slice(2 * width + block * duo, 2 * width + (block + 1) * duo)
                queries = split_heads(mixed_ref[span, cols])
                keys = mixed_ref[span, key_cols]
                values = mixed_ref[span, value_cols]
                d_heads = split_heads(d_context[span, cols])
                low_probs = probs_ref[pair, block]
                wide = low_probs.astype(F32)
                d_probs = dot(d_heads, values, 1, 1)
                d_scores = wide * (d_probs - jnp.sum(wide * d_probs, axis=-1, keepdims=True))
                d_scores = d_scores.astype(BF16)
                d_queries = dot(side_by_side(d_scores), split_heads(keys)) * score_scale
                d_mixed_out[span, cols] = d_queries.astype(BF16)
                d_mixed_out[span, key_cols] = dot(d_scores, queries, 0, 0).astype(BF16)
                d_mixed_out[span, value_cols] = dot(low_probs, d_heads, 0, 0).astype(BF16)
        d_mixed = d_mixed_out[...]
        sums_out[0:1, :] += row_sum(d_mixed[:, :width].astype(F32))
        sums_out[1:2, :] += row_sum(d_mixed[:, 2 * width :].astype(F32))
        d_rows = low_attn_ref[...].astype(F32) + dot(d_mixed, w_qkv_ref[...], 1, 1)
        d_rows = d_rows.astype(BF16)
        for i in range(2):
            kept_out[i] = d_rows[i * length : i * length + slot_rows]
            far_out[i] = d_rows[i * length + slot_rows : (i + 1) * length]
        if last:
            grads, (held, grad) = refs[4:10], refs[10:]
            held[pl.ds(step * 2 * length, 2 * length)] = d_mixed

            @pl.when(step == steps - 1)
            def _():
                for i in range(3):
                    cols = slice(i * width, (i + 1) * width)
                    total_grad = dot(joined_ref[:before], earlier_ref[:, cols], 0, 0)
                    total_grad = total_grad + dot(joined_ref[before:], held[:, cols], 0, 0)
                    grad[...] = total_grad.astype(BF16)
                    spread(
                        grad,
                        grads[2 * i : 2 * i + 2],
                        scalars_ref,
                        base,
                        shard,
                        scalars_ref[base + 2],
                        places,
                    )

    def by_rows(columns):
        return pl.BlockSpec((2 * length, columns), lambda i, s: (start + i, 0))

    two = pl.BlockSpec((2, slot_rows, width), lambda i, s: (start + i, 0, 0))
    operands = [low_attn, mixed, probs, w_out, w_qkv]
    in_specs = [
        by_rows(width),
        by_rows(3 * width),
        pl.BlockSpec((2, blocks, 2 * length, length), lambda i, s: (start + i, 0, 0, 0)),
        whole(w_out),
        whole(w_qkv),
    ]
    out_specs = [by_rows(3 * width), two, two, pl.BlockSpec((8, width), lambda i, s: (0, 0))]
    out_shape = [
        jax.ShapeDtypeStruct((total, 3 * width), BF16),
        jax.ShapeDtypeStruct((pairs, slot_rows, width), BF16),
        jax.ShapeDtypeStruct((pairs, slot_rows, width), BF16),
        jax.ShapeDtypeStruct((8, width), F32),
    ]
    scratch = []
    if last:
        operands += [joined, into[0]]
        in_specs += [
            whole(joined),
            pl.BlockSpec((before, 3 * width), lambda i, s: (0, 0), pipeline_mode=pl.Buffered(1)),
        ]
        out_specs[0] = by_rows(3 * width)
        out_specs += [pl.BlockSpec((places, shard, width), lambda i, s: (0, 0, 0))] * 6
        out_shape += [jax.ShapeDtypeStruct((places, shard, width), BF16)] * 6
        scratch = [
            pltpu.VMEM((steps * 2 * length, 3 * width), BF16),
            pltpu.VMEM((width, width), BF16),
        ]
        out_specs[0] = pl.BlockSpec((2 * length, 3 * width), lambda i, s: (0, 0))
        out_shape[0] = jax.ShapeDtypeStruct((2 * length, 3 * width), BF16)
    return call(
        kernel,
        scalars,
        operands,
        in_specs,
        out_specs,
        out_shape,
        (steps,),
        "attention_backward",
        total // parts * width * width * 20,
        into=into[1:],
        into_first=1,
        after=after,
        scratch=scratch,
        moved=12 * 2**20,
    )


def added(parts):
    total = parts[0].astype(F32)
    for part in parts[1:]:
        total = total + part.astype(F32)
    return total.astype(BF16)


class Shards:
    def __init__(self, send, keep, order):
        places, self.shard, self.width = send.shape
        bits = places.bit_length() - 1
        self.shape = (2,) * bits + (self.shard, self.width)
        self.order = list(order)
        self.left = list(range(bits))[::-1]
        self.mine = None
        self.held = [keep.reshape(self.shape)]
        self.coming = flipped(send, "dp", 1).reshape(self.shape)

    def step(self, after=None):
        coming = self.coming
        if after is not None:
            coming, _ = lax.optimization_barrier((coming, after))
        self.held.append(coming)
        if not self.order:
            self.mine = lax.optimization_barrier(added(self.held))
            self.coming = flipped(self.mine, "mod", 1)
            return self.mine
        bit = self.order.pop(0)
        dim = self.left.index(bit)
        away = added([lax.index_in_dim(part, 1, dim, keepdims=False) for part in self.held])
        self.held = [lax.index_in_dim(part, 0, dim, keepdims=False) for part in self.held]
        self.left.remove(bit)
        self.coming = flipped(away, "dp", 2 << bit)
        return away

    def result(self):
        return self.mine.astype(F32) + self.coming.astype(F32)


def reduce_plain(send, keep):
    total = jnp.stack([keep, send], 1)
    total = total.reshape(-1, total.shape[-1]).astype(F32)
    share = lax.psum_scatter(total, "dp", scatter_dimension=0, tiled=True)
    return lax.psum(share.astype(BF16), "mod").astype(F32)


def sum_everywhere(value):
    shards = lax.axis_size("dp")
    if shards & (shards - 1):
        return lax.psum(value, ("mod", "dp"))
    mask = 1
    while mask < shards:
        value = value + flipped(value, "dp", mask)
        mask *= 2
    return value + flipped(value, "mod", 1)


def body(
    layer_rows,
    cotangent,
    row_live,
    partner,
    w_qkv,
    b_qv,
    w_out,
    norm_gains,
    bias_rows,
    w_in,
    b_in,
    w_back,
):
    side = lax.axis_index("mod")
    place = lax.axis_index("dp")
    shards = lax.axis_size("dp")
    groups = partner.shape[1]
    aligned = shards >= 8 and shards & (shards - 1) == 0 and (layer_rows.shape[2] // shards) % 16 == 0
    layout = shards if aligned else 16
    half = groups // 2
    width = layer_rows.shape[2]
    slot_rows = layer_rows.shape[1] // groups
    inner_width = w_in.shape[1]
    slots = (groups, slot_rows, width)
    rows = layer_rows[0].reshape(slots)
    cot = cotangent[0].reshape(slots)
    spot = place if aligned else 0 * place
    scalars = jnp.concatenate(
        [partner[0], jnp.stack([side, spot & 1, spot >> 1]).astype(jnp.int32)]
    )
    cut = half // 2
    sent_a = gather_sent(scalars, rows, half, 0, cut)
    got_a = flipped(sent_a, "mod", 1)
    sent_b = gather_sent(scalars, rows, half, cut, cut, [sent_a])
    got_b = flipped(sent_b, "mod", 1)
    sent_cot = gather_sent(scalars, cot, half, 0, half, [sent_b])
    far_cot = flipped(sent_cot, "mod", 1)

    live = row_live.reshape(2, groups, slot_rows)
    words_live = lax.dynamic_slice_in_dim(live[0], side * half, half, 0)
    region_live = live[1][lax.dynamic_slice_in_dim(partner[0], side * half, half, 0)]
    is_first = side == 0
    seen = jnp.concatenate(
        [
            jnp.where(is_first, words_live, region_live),
            jnp.where(is_first, region_live, words_live),
        ],
        1,
    )[:, None, :]

    heads_weights = (w_qkv, b_qv, w_out, norm_gains, bias_rows)
    first_part = attention_forward(
        scalars, rows, got_a, seen, heads_weights, 0, half, after=[sent_cot]
    )
    joined, mixed, probs, context, normed, root = attention_forward(
        scalars, rows, got_b, seen, heads_weights, cut, half, into=first_part
    )
    feed_weights = (w_in, b_in.reshape(1, inner_width), w_back, norm_gains, bias_rows)
    slope, branch, out_kept, out_far, sums_two, *grads = feed_forward(
        scalars, normed, cot, far_cot, feed_weights, half, layout, groups
    )
    back_weights = (w_in, w_back, norm_gains, bias_rows)
    bits = (layout // 2).bit_length() - 1
    order = list(range(bits))
    other = order[1:] + order[:1]

    def travel(send, keep, steps):
        return Shards(send, keep, steps) if aligned else (send, keep)

    def steps_of(pieces, after):
        return [piece.step(after) for piece in pieces] if aligned else []

    back = [travel(*grads[0:2], order), travel(*grads[2:4], order)]
    sent = steps_of(back[:1], grads[0]) + steps_of(back[1:], grads[0])
    out_back = flipped(out_far, "mod", 1)
    low_attn, sums_one, inner_sum, *grads = feed_backward(
        scalars, branch, slope, normed, root, context, back_weights, layout, groups, after=sent
    )
    inner = [travel(*grads[0:2], order), travel(*grads[2:4], order)]
    outer = travel(*grads[4:6], other)
    sent = steps_of(back, low_attn) + steps_of(inner, low_attn) + steps_of([outer], low_attn)
    attn_kept = (low_attn, mixed, probs, joined)
    attn_weights = (w_out, w_qkv)
    *first_part, sums_qv_a = attention_backward(
        scalars, attn_kept, attn_weights, 0, 2, layout, groups, after=sent
    )
    sent = steps_of(back + [outer], sums_qv_a)
    _, d_kept, d_far, sums_qv_b, *grads = attention_backward(
        scalars, attn_kept, attn_weights, 1, 2, layout, groups, into=first_part, after=sent
    )
    qkv = [
        travel(*grads[0:2], order),
        travel(*grads[2:4], other),
        travel(*grads[4:6], order),
    ]
    d_back = flipped(d_far, "mod", 1)
    pieces = back + inner + [outer] + qkv
    if aligned:
        steps_of(back + inner + [outer], sums_qv_b)
        while any(piece.mine is None for piece in pieces):
            for piece in pieces:
                if piece.mine is None:
                    piece.step()
        done = [piece.result() for piece in pieces]
    else:
        done = [reduce_plain(*piece) for piece in pieces]
    grad_back = jnp.concatenate(done[0:2], 1)
    grad_in = jnp.concatenate(done[2:4], 1)
    grad_out = done[4]
    grad_qkv = jnp.concatenate(done[5:], 1)

    sums_qv = sums_qv_a + sums_qv_b
    small = jnp.concatenate(
        [
            sums_qv[0:2],
            sums_one[0:1],
            sums_two[0:1],
            sums_one[2:3],
            sums_one[1:2],
            sums_two[2:3],
            sums_two[1:2],
            inner_sum[0].reshape(-1, width),
        ],
        0,
    )
    small = sum_everywhere(small)
    shard = width // shards
    rows_small = lax.dynamic_slice_in_dim(small[:8], place * shard, shard, 1)
    inner_shard = inner_width // shards
    grad_b_in = lax.dynamic_slice_in_dim(small[8:].reshape(-1), place * inner_shard, inner_shard)

    out_rows = scatter_home(scalars, out_kept, out_back, half).reshape(1, -1, width)
    grad_rows = scatter_home(scalars, d_kept, d_back, half).reshape(1, -1, width)
    return (
        out_rows,
        grad_rows,
        grad_qkv,
        rows_small[0:2],
        grad_out,
        rows_small[2:4],
        rows_small[4:8],
        grad_in,
        grad_b_in,
        grad_back,
    )


def solution(mesh):
    return jax.shard_map(
        body,
        mesh=mesh,
        in_specs=(
            P("mod", "dp", None),
            P("mod", "dp", None),
            P(None, "dp"),
            P("dp", None),
            P(),
            P(),
            P(),
            P(),
            P(),
            P(),
            P(),
            P(),
        ),
        out_specs=(
            P("mod", "dp", None),
            P("mod", "dp", None),
            P("dp", None),
            P(None, "dp"),
            P("dp", None),
            P(None, "dp"),
            P(None, "dp"),
            P("dp", None),
            P("dp"),
            P("dp", None),
        ),
        check_vma=False,
    )
```

```python
import functools

import jax
import jax.numpy as jnp
import numpy as np
from jax import lax
from jax.experimental import pallas as pl
from jax.experimental.pallas import tpu as pltpu
from jax.sharding import PartitionSpec as P

HEADS = 12
EPSILON = 1e-12
F32 = jnp.float32
BF16 = jnp.bfloat16
VMEM_LIMIT = 56 * 2**20


def dot(left, right, left_dim=1, right_dim=0):
    return lax.dot_general(
        left, right, (((left_dim,), (right_dim,)), ((), ())), preferred_element_type=F32
    )


def flipped(value, axis, mask):
    pairs = [(source, source ^ mask) for source in range(lax.axis_size(axis))]
    return lax.ppermute(value, axis, pairs)


def params(limit=VMEM_LIMIT):
    return pltpu.CompilerParams(vmem_limit_bytes=limit)


def kept_slot(scalars, pair, half):
    groups = 2 * half
    side = scalars[groups]
    place = side * half + pair
    return jnp.where(side == 0, place, scalars[place])


def sent_slot(scalars, pair, half):
    groups = 2 * half
    side = scalars[groups]
    place = (1 - side) * half + pair
    return jnp.where(side == 0, place, scalars[place])


ANY = pl.BlockSpec(memory_space=pl.ANY)
LINE = []


def call(kernel, scalars, operands, in_specs, out_specs, out_shape, grid, name, **more):
    after = LINE[-1:]
    into = list(more.get("into", ()))
    into_first = more.get("into_first", 0)
    scratch = list(more.get("scratch", ()))
    taken, spare, given = len(operands), len(into) + len(after), len(out_shape)

    def wrapped(scalars_ref, *refs):
        outs = refs[taken + spare :]
        kernel(scalars_ref, *refs[:taken], *outs[:given], *outs[given + 1 :])

    outs = pl.pallas_call(
        wrapped,
        grid_spec=pltpu.PrefetchScalarGridSpec(
            num_scalar_prefetch=1,
            grid=grid,
            in_specs=list(in_specs) + [ANY] * spare,
            out_specs=list(out_specs) + [ANY],
            scratch_shapes=scratch,
        ),
        out_shape=list(out_shape) + [jax.ShapeDtypeStruct((8, 128), F32)],
        input_output_aliases={1 + taken + i: i + into_first for i in range(len(into))},
        compiler_params=params(more.get("limit", VMEM_LIMIT)),
        cost_estimate=pl.CostEstimate(flops=1, bytes_accessed=1, transcendentals=0),
        name=name,
    )(scalars, *operands, *into, *after)
    LINE.append(outs[-1])
    return list(outs[:-1])


def gather_sent(scalars, rows, half, first, count):
    slot_rows, width = rows.shape[1:]

    def kernel(scalars_ref, rows_ref, out, sems):
        copies = [
            pltpu.make_async_copy(
                rows_ref.at[sent_slot(scalars_ref, first + i, half)], out.at[i], sems.at[i]
            )
            for i in range(count)
        ]
        for copy in copies:
            copy.start()
        for copy in copies:
            copy.wait()

    shape = (count, slot_rows, width)
    return call(
        kernel,
        scalars,
        [rows],
        [ANY],
        [pl.BlockSpec(shape, lambda i, s: (0, 0, 0))],
        [jax.ShapeDtypeStruct(shape, rows.dtype)],
        (1,),
        "gather_sent",
        scratch=[pltpu.SemaphoreType.DMA((count,))],
        limit=8 * 2**20,
    )[0]


def scatter_home(scalars, kept, back, half):
    slot_rows, width = kept.shape[1:]

    def kernel(scalars_ref, kept_ref, back_ref, out, sems):
        copies = []
        for i in range(half):
            copies.append(
                pltpu.make_async_copy(
                    kept_ref.at[i], out.at[kept_slot(scalars_ref, i, half)], sems.at[0, i]
                )
            )
            copies.append(
                pltpu.make_async_copy(
                    back_ref.at[i], out.at[sent_slot(scalars_ref, i, half)], sems.at[1, i]
                )
            )
        for copy in copies:
            copy.start()
        for copy in copies:
            copy.wait()

    shape = (2 * half, slot_rows, width)
    return call(
        kernel,
        scalars,
        [kept, back],
        [ANY, ANY],
        [pl.BlockSpec(shape, lambda i, s: (0, 0, 0))],
        [jax.ShapeDtypeStruct(shape, kept.dtype)],
        (1,),
        "scatter_home",
        scratch=[pltpu.SemaphoreType.DMA((2, half))],
        limit=8 * 2**20,
    )[0]


def split_heads(value):
    low = lax.broadcasted_iota(jnp.int32, value.shape, 1) < value.shape[1] // 2
    zero = jnp.zeros_like(value)
    return jnp.concatenate([jnp.where(low, value, zero), jnp.where(low, zero, value)], 0)


def side_by_side(value):
    rows = value.shape[0] // 2
    return jnp.concatenate([value[:rows], value[rows:]], 1)


def row_sum(value):
    return jnp.sum(value, axis=0, keepdims=True)


def normal_form(value):
    centered = value - jnp.mean(value, axis=-1, keepdims=True)
    root = lax.rsqrt(jnp.mean(centered * centered, axis=-1, keepdims=True) + EPSILON)
    return centered * root, root


def normal_back(lifted, normed, root):
    return root * (
        lifted
        - jnp.mean(lifted, axis=-1, keepdims=True)
        - normed * jnp.mean(lifted * normed, axis=-1, keepdims=True)
    )


def whole(array):
    return pl.BlockSpec(
        array.shape, lambda *_: (0,) * array.ndim, pipeline_mode=pl.Buffered(1)
    )


def attention_forward(
    scalars, rows, received, live, weights, first, half, into=()
):
    w_qkv, b_qv, w_out, norm_gains, bias_rows = weights
    slot_rows, width = rows.shape[1:]
    pairs = received.shape[0]
    length = 2 * slot_rows
    duo = 2 * width // HEADS
    blocks = width // duo
    score_scale = (width // HEADS) ** (-0.5)

    def kernel(
        scalars_ref,
        kept_a,
        kept_b,
        got,
        live_ref,
        w_qkv_ref,
        b_qv_ref,
        w_out_ref,
        gains_ref,
        biases_ref,
        joined_out,
        mixed_out,
        probs_out,
        context_out,
        normed_out,
        root_out,
    ):
        joined = jnp.concatenate([kept_a[0], got[0], kept_b[0], got[1]], 0)
        joined_out[...] = joined
        mixed = dot(joined, w_qkv_ref[...])
        queries = (mixed[:, :width] + b_qv_ref[0:1, :]).astype(BF16)
        queries = (queries.astype(F32) * score_scale).astype(BF16)
        keys = mixed[:, width : 2 * width].astype(BF16)
        values = (mixed[:, 2 * width :] + b_qv_ref[1:2, :]).astype(BF16)
        mixed_out[:, :width] = queries
        mixed_out[:, width : 2 * width] = keys
        mixed_out[:, 2 * width :] = values
        contexts = []
        for pair in range(2):
            seen = live_ref[pair] > 0
            span = slice(pair * length, (pair + 1) * length)
            heads = []
            for block in range(blocks):
                cols = slice(block * duo, (block + 1) * duo)
                scores = dot(split_heads(queries[span, cols]), keys[span, cols], 1, 1)
                scores = jnp.where(seen, scores, -1e30)
                powered = jnp.exp(scores - jnp.max(scores, axis=-1, keepdims=True))
                low_probs = powered * (1.0 / jnp.sum(powered, axis=-1, keepdims=True))
                low_probs = low_probs.astype(BF16)
                probs_out[pair, block] = low_probs
                heads.append(
                    dot(side_by_side(low_probs), split_heads(values[span, cols])).astype(BF16)
                )
            contexts.append(jnp.concatenate(heads, 1))
        context = jnp.concatenate(contexts, 0)
        context_out[...] = context
        pre_one = joined.astype(F32) + dot(context, w_out_ref[...]) + biases_ref[0:1, :]
        normed, root = normal_form(pre_one)
        normed_out[...] = normed.astype(BF16)
        root_out[...] = jnp.broadcast_to(root, root_out.shape)

    start = first // 2

    def by_rows(columns):
        return pl.BlockSpec((2 * length, columns), lambda i, s: (start + i, 0))

    slot = (1, slot_rows, width)
    total = half * length
    return call(
        kernel,
        scalars,
        [rows, rows, received, live, w_qkv, b_qv, w_out, norm_gains, bias_rows],
        [
            pl.BlockSpec(slot, lambda i, s: (kept_slot(s, first + 2 * i, half), 0, 0)),
            pl.BlockSpec(slot, lambda i, s: (kept_slot(s, first + 2 * i + 1, half), 0, 0)),
            pl.BlockSpec((2, slot_rows, width), lambda i, s: (i, 0, 0)),
            pl.BlockSpec((2, 1, length), lambda i, s: (start + i, 0, 0)),
            whole(w_qkv),
            whole(b_qv),
            whole(w_out),
            whole(norm_gains),
            whole(bias_rows),
        ],
        [
            by_rows(width),
            by_rows(3 * width),
            pl.BlockSpec((2, blocks, 2 * length, length), lambda i, s: (start + i, 0, 0, 0)),
            by_rows(width),
            by_rows(width),
            by_rows(128),
        ],
        [
            jax.ShapeDtypeStruct((total, width), BF16),
            jax.ShapeDtypeStruct((total, 3 * width), BF16),
            jax.ShapeDtypeStruct((half, blocks, 2 * length, length), BF16),
            jax.ShapeDtypeStruct((total, width), BF16),
            jax.ShapeDtypeStruct((total, width), BF16),
            jax.ShapeDtypeStruct((total, 128), F32),
        ],
        (pairs // 2,),
        "attention_forward",
        into=into,
    )


def spread(grad, out_pairs, scalars_ref, base, shard, first_row, places):
    core = scalars_ref[base + 1]
    for j in range(places):
        row = (first_row ^ j) * 2
        for out, which in ((out_pairs[0], 1 - core), (out_pairs[1], core)):
            out[j] = grad[pl.ds(pl.multiple_of((row + which) * shard, 16), shard), :]


def feed_forward(scalars, normed, cot, far_cot, weights, half, shards, base):
    w_in, b_in, w_back, norm_gains, bias_rows = weights
    slot_rows, width = cot.shape[1:]
    inner_width = w_in.shape[1]
    length = 2 * slot_rows
    rows = 2 * length
    height = half * length
    steps = half // 2
    chunk = 768
    chunks = inner_width // chunk
    shard = inner_width // shards
    places = shards // 2
    part = 4 * shard
    parts = inner_width // part
    left = width // 2

    def kernel(
        scalars_ref,
        normed_ref,
        cot_a,
        cot_b,
        cot_far,
        w_in_hbm,
        b_in_ref,
        w_back_hbm,
        gains_ref,
        biases_ref,
        slope_out,
        branch_out,
        kept_out,
        far_out,
        sums_out,
        send_a,
        keep_a,
        send_b,
        keep_b,
        w_in_ref,
        w_back_ref,
        held,
        acts,
        branches,
        grad_a,
        grad_b,
        sems,
    ):
        step = pl.program_id(0)

        def fetch_in(j):
            cols = pl.ds(j * chunk, chunk)
            return pltpu.make_async_copy(
                w_in_hbm.at[:, cols], w_in_ref.at[:, cols], sems.at[0, j]
            )

        def fetch_back(j):
            cols = pl.ds(j * chunk, chunk)
            return pltpu.make_async_copy(w_back_hbm.at[cols], w_back_ref.at[cols], sems.at[1, j])

        @pl.when(step == 0)
        def _():
            sums_out[...] = jnp.zeros_like(sums_out)
            for j in range(chunks):
                fetch_in(j).start()
                fetch_back(j).start()

        def close(pre_two, row):
            scaled, root = normal_form(pre_two)
            output = (scaled * gains_ref[1:2, :] + biases_ref[3:4, :]).astype(BF16)
            for i in range(2):
                kept_out[i] = output[i * length : i * length + slot_rows]
                far_out[i] = output[i * length + slot_rows : (i + 1) * length]
            here = jnp.concatenate([cot_a[0], cot_far[0], cot_b[0], cot_far[1]], 0).astype(F32)
            d_two = normal_back(here * gains_ref[1:2, :], scaled, root)
            low = d_two.astype(BF16)
            branch_out[...] = low
            branches[pl.ds(row, rows)] = low
            return jnp.concatenate([row_sum(here * scaled), row_sum(here), row_sum(d_two)], 0)

        def forward(first):
            hidden = normed_ref[...].astype(F32) * gains_ref[0:1, :] + biases_ref[1:2, :]
            low_hidden = hidden.astype(BF16)
            total = hidden + biases_ref[2:3, :]
            for j in range(chunks):
                cols = slice(j * chunk, (j + 1) * chunk)
                if first:
                    fetch_in(j).wait()
                inner = dot(low_hidden, w_in_ref[:, cols]) + b_in_ref[:, cols]
                normal = 0.5 + 0.5 * lax.erf(inner * (0.5**0.5))
                low_act = (inner * normal).astype(BF16)
                density = jnp.exp(inner * inner * -0.5) * 0.3989422804014327
                acts[pl.ds(step * rows, rows), cols] = low_act
                slope_out[:, cols] = (normal + inner * density).astype(BF16)
                if first:
                    fetch_back(j).wait()
                total = total + dot(low_act, w_back_ref[cols, :])
            return total

        @pl.when(step == 0)
        def _():
            held[...] = forward(True)

        @pl.when((step > 0) & (step < steps))
        def _():
            before = held[...]
            held[...] = forward(False)
            sums_out[0:3, :] += close(before, (step - 1) * rows)

        @pl.when(step == steps)
        def _():
            sums_out[0:3, :] += close(held[...], (step - 1) * rows)

        @pl.when(step >= steps)
        def _():
            start = pl.multiple_of((step - steps) * part, 128)
            grad = dot(acts[:, pl.ds(start, part)], branches[...], 0, 0).astype(BF16)
            grad_a[...] = grad[:, :left]
            grad_b[...] = grad[:, left:]
            first_row = scalars_ref[base + 2] & 1
            spread(grad_a, (send_a, keep_a), scalars_ref, base, shard, first_row, 2)
            spread(grad_b, (send_b, keep_b), scalars_ref, base, shard, first_row, 2)

    def ahead(i):
        return jnp.minimum(i, steps - 1)

    def behind(i):
        return jnp.clip(i - 1, 0, steps - 1)

    def slot(j):
        return pl.BlockSpec(
            (1, slot_rows, width), lambda i, s: (kept_slot(s, 2 * behind(i) + j, half), 0, 0)
        )

    duo = pl.BlockSpec((2, slot_rows, width), lambda i, s: (behind(i), 0, 0))
    grads = []
    for columns in (left, left, width - left, width - left):
        grads.append(
            pl.BlockSpec(
                (2, shard, columns),
                lambda i, s: ((s[base + 2] >> 1) ^ jnp.maximum(i - steps, 0), 0, 0),
            )
        )
    return call(
        kernel,
        scalars,
        [normed, cot, cot, far_cot, w_in, b_in, w_back, norm_gains, bias_rows],
        [
            pl.BlockSpec((rows, width), lambda i, s: (ahead(i), 0)),
            slot(0),
            slot(1),
            duo,
            ANY,
            whole(b_in),
            ANY,
            whole(norm_gains),
            whole(bias_rows),
        ],
        [
            pl.BlockSpec((rows, inner_width), lambda i, s: (ahead(i), 0)),
            pl.BlockSpec((rows, width), lambda i, s: (behind(i), 0)),
            duo,
            duo,
            pl.BlockSpec((8, width), lambda i, s: (0, 0)),
        ]
        + grads,
        [
            jax.ShapeDtypeStruct((height, inner_width), BF16),
            jax.ShapeDtypeStruct((height, width), BF16),
            jax.ShapeDtypeStruct((half, slot_rows, width), BF16),
            jax.ShapeDtypeStruct((half, slot_rows, width), BF16),
            jax.ShapeDtypeStruct((8, width), F32),
            jax.ShapeDtypeStruct((places, shard, left), BF16),
            jax.ShapeDtypeStruct((places, shard, left), BF16),
            jax.ShapeDtypeStruct((places, shard, width - left), BF16),
            jax.ShapeDtypeStruct((places, shard, width - left), BF16),
        ],
        (steps + parts,),
        "feed_forward",
        scratch=[
            pltpu.VMEM((width, inner_width), BF16),
            pltpu.VMEM((inner_width, width), BF16),
            pltpu.VMEM((rows, width), F32),
            pltpu.VMEM((height, inner_width), BF16),
            pltpu.VMEM((height, width), BF16),
            pltpu.VMEM((part, left), BF16),
            pltpu.VMEM((part, width - left), BF16),
            pltpu.SemaphoreType.DMA((2, chunks)),
        ],
    )


def feed_backward(scalars, branch, slope, normed, root, context, weights, shards, base):
    w_in, w_back, norm_gains, bias_rows = weights
    total, width = branch.shape
    inner_width = slope.shape[1]
    chunk = 768
    steps = inner_width // chunk
    turn = steps // 2
    shard = width // shards
    places = shards // 2
    piece = 128

    def kernel(
        scalars_ref,
        branch_ref,
        slope_ref,
        normed_ref,
        root_ref,
        context_ref,
        w_in_ref,
        w_back_ref,
        gains_ref,
        biases_ref,
        low_attn_out,
        sums_out,
        inner_sum_out,
        send_a,
        keep_a,
        send_b,
        keep_b,
        send_out,
        keep_out,
        held,
        low_hidden,
        grad,
    ):
        step = pl.program_id(0)
        place = scalars_ref[base + 2]

        @pl.when(step == 0)
        def _():
            hidden = normed_ref[...].astype(F32) * gains_ref[0:1, :] + biases_ref[1:2, :]
            low_hidden[...] = hidden.astype(BF16)
            held[...] = branch_ref[...].astype(F32)

        sums = jnp.zeros((1, chunk), F32)
        lows = []
        for r in range(0, total, 256):
            span = slice(r, r + 256)
            d_inner = dot(branch_ref[span], w_back_ref[...], 1, 1) * slope_ref[span].astype(F32)
            sums = sums + row_sum(d_inner)
            low = d_inner.astype(BF16)
            lows.append(low)
            held[span] += dot(low, w_in_ref[...], 1, 1)
        inner_sum_out[...] = jnp.broadcast_to(sums, inner_sum_out.shape)
        grad[...] = dot(low_hidden[...], jnp.concatenate(lows, 0), 0, 0).astype(BF16)

        @pl.when(step < turn)
        def _():
            spread(grad, (send_a, keep_a), scalars_ref, base, shard, place, places)

        @pl.when(step >= turn)
        def _():
            spread(grad, (send_b, keep_b), scalars_ref, base, shard, place, places)

        @pl.when(step == steps - 1)
        def _():
            sums = [jnp.zeros((1, width), F32)] * 3
            lows = []
            for i in range(total // piece):
                span = slice(i * piece, (i + 1) * piece)
                d_hidden, scaled = held[span], normed_ref[span].astype(F32)
                d_one = normal_back(d_hidden * gains_ref[0:1, :], scaled, root_ref[span, 0:1])
                lows.append(d_one.astype(BF16))
                low_attn_out[span] = lows[-1]
                for j, term in enumerate((d_hidden * scaled, d_hidden, d_one)):
                    sums[j] = sums[j] + row_sum(term)
            sums_out[...] = jnp.concatenate(sums + [jnp.zeros((5, width), F32)], 0)
            grad[:, :width] = dot(context_ref[...], jnp.concatenate(lows, 0), 0, 0).astype(BF16)
            spread(grad, (send_out, keep_out), scalars_ref, base, shard, place, places)

    half_a = pl.BlockSpec((places, shard, chunk), lambda i, s: (0, 0, jnp.minimum(i, turn - 1)))
    half_b = pl.BlockSpec((places, shard, chunk), lambda i, s: (0, 0, jnp.maximum(i - turn, 0)))
    outer = pl.BlockSpec((places, shard, width), lambda i, s: (0, 0, 0))
    shape_a = jax.ShapeDtypeStruct((places, shard, turn * chunk), BF16)
    shape_b = jax.ShapeDtypeStruct((places, shard, inner_width - turn * chunk), BF16)
    shape_out = jax.ShapeDtypeStruct((places, shard, width), BF16)
    return call(
        kernel,
        scalars,
        [branch, slope, normed, root, context, w_in, w_back, norm_gains, bias_rows],
        [
            whole(branch),
            pl.BlockSpec((total, chunk), lambda i, s: (0, i)),
            whole(normed),
            whole(root),
            whole(context),
            pl.BlockSpec((width, chunk), lambda i, s: (0, i)),
            pl.BlockSpec((chunk, width), lambda i, s: (i, 0)),
            whole(norm_gains),
            whole(bias_rows),
        ],
        [
            pl.BlockSpec((total, width), lambda i, s: (0, 0)),
            pl.BlockSpec((8, width), lambda i, s: (0, 0)),
            pl.BlockSpec((8, chunk), lambda i, s: (0, i)),
            half_a,
            half_a,
            half_b,
            half_b,
            outer,
            outer,
        ],
        [
            jax.ShapeDtypeStruct((total, width), BF16),
            jax.ShapeDtypeStruct((8, width), F32),
            jax.ShapeDtypeStruct((8, inner_width), F32),
            shape_a,
            shape_a,
            shape_b,
            shape_b,
            shape_out,
            shape_out,
        ],
        (steps,),
        "feed_backward",
        scratch=[
            pltpu.VMEM((total, width), F32),
            pltpu.VMEM((total, width), BF16),
            pltpu.VMEM((width, chunk), BF16),
        ],
    )


def attention_backward(scalars, kept, weights, part, parts, shards, base, into=()):
    low_attn, mixed, probs, joined = kept
    w_out, w_qkv = weights
    total, width = low_attn.shape
    pairs, blocks, _, length = probs.shape
    duo = width // blocks
    slot_rows = length // 2
    score_scale = (width // HEADS) ** (-0.5)
    steps = pairs // 2 // parts
    start = part * steps
    last = part == parts - 1
    before = start * 2 * length
    shard = width // shards
    places = shards // 2
    earlier = [into[0]] if last else []

    def kernel(
        scalars_ref,
        low_attn_ref,
        mixed_ref,
        probs_ref,
        w_out_ref,
        w_qkv_ref,
        *refs,
    ):
        if last:
            joined_ref, earlier_ref = refs[:2]
            refs = refs[2:]
        d_mixed_out, kept_out, far_out, sums_out = refs[:4]
        step = pl.program_id(0)

        @pl.when(step == 0)
        def _():
            sums_out[...] = jnp.zeros_like(sums_out)

        d_context = dot(low_attn_ref[...], w_out_ref[...], 1, 1).astype(BF16)
        for pair in range(2):
            span = slice(pair * length, (pair + 1) * length)
            for block in range(blocks):
                cols = slice(block * duo, (block + 1) * duo)
                key_cols = slice(width + block * duo, width + (block + 1) * duo)
                value_cols = slice(2 * width + block * duo, 2 * width + (block + 1) * duo)
                queries = split_heads(mixed_ref[span, cols])
                keys = mixed_ref[span, key_cols]
                values = mixed_ref[span, value_cols]
                d_heads = split_heads(d_context[span, cols])
                low_probs = probs_ref[pair, block]
                wide = low_probs.astype(F32)
                d_probs = dot(d_heads, values, 1, 1)
                d_scores = wide * (d_probs - jnp.sum(wide * d_probs, axis=-1, keepdims=True))
                d_scores = d_scores.astype(BF16)
                d_queries = dot(side_by_side(d_scores), split_heads(keys)) * score_scale
                d_mixed_out[span, cols] = d_queries.astype(BF16)
                d_mixed_out[span, key_cols] = dot(d_scores, queries, 0, 0).astype(BF16)
                d_mixed_out[span, value_cols] = dot(low_probs, d_heads, 0, 0).astype(BF16)
        d_mixed = d_mixed_out[...]
        sums_out[0:1, :] += row_sum(d_mixed[:, :width].astype(F32))
        sums_out[1:2, :] += row_sum(d_mixed[:, 2 * width :].astype(F32))
        d_rows = low_attn_ref[...].astype(F32) + dot(d_mixed, w_qkv_ref[...], 1, 1)
        d_rows = d_rows.astype(BF16)
        for i in range(2):
            kept_out[i] = d_rows[i * length : i * length + slot_rows]
            far_out[i] = d_rows[i * length + slot_rows : (i + 1) * length]
        if last:
            grads, (held, grad) = refs[4:10], refs[10:]
            held[pl.ds(step * 2 * length, 2 * length)] = d_mixed

            @pl.when(step == steps - 1)
            def _():
                for i in range(3):
                    cols = slice(i * width, (i + 1) * width)
                    total_grad = dot(joined_ref[:before], earlier_ref[:, cols], 0, 0)
                    total_grad = total_grad + dot(joined_ref[before:], held[:, cols], 0, 0)
                    grad[...] = total_grad.astype(BF16)
                    spread(
                        grad,
                        grads[2 * i : 2 * i + 2],
                        scalars_ref,
                        base,
                        shard,
                        scalars_ref[base + 2],
                        places,
                    )

    def by_rows(columns):
        return pl.BlockSpec((2 * length, columns), lambda i, s: (start + i, 0))

    two = pl.BlockSpec((2, slot_rows, width), lambda i, s: (start + i, 0, 0))
    operands = [low_attn, mixed, probs, w_out, w_qkv]
    in_specs = [
        by_rows(width),
        by_rows(3 * width),
        pl.BlockSpec((2, blocks, 2 * length, length), lambda i, s: (start + i, 0, 0, 0)),
        whole(w_out),
        whole(w_qkv),
    ]
    out_specs = [by_rows(3 * width), two, two, pl.BlockSpec((8, width), lambda i, s: (0, 0))]
    out_shape = [
        jax.ShapeDtypeStruct((total, 3 * width), BF16),
        jax.ShapeDtypeStruct((pairs, slot_rows, width), BF16),
        jax.ShapeDtypeStruct((pairs, slot_rows, width), BF16),
        jax.ShapeDtypeStruct((8, width), F32),
    ]
    scratch = []
    if last:
        operands += [joined, into[0]]
        in_specs += [
            whole(joined),
            pl.BlockSpec((before, 3 * width), lambda i, s: (0, 0), pipeline_mode=pl.Buffered(1)),
        ]
        out_specs[0] = by_rows(3 * width)
        out_specs += [pl.BlockSpec((places, shard, width), lambda i, s: (0, 0, 0))] * 6
        out_shape += [jax.ShapeDtypeStruct((places, shard, width), BF16)] * 6
        scratch = [
            pltpu.VMEM((steps * 2 * length, 3 * width), BF16),
            pltpu.VMEM((width, width), BF16),
        ]
        out_specs[0] = pl.BlockSpec((2 * length, 3 * width), lambda i, s: (0, 0))
        out_shape[0] = jax.ShapeDtypeStruct((2 * length, 3 * width), BF16)
    return call(
        kernel,
        scalars,
        operands,
        in_specs,
        out_specs,
        out_shape,
        (steps,),
        "attention_backward",
        into=into[1:],
        into_first=1,
        scratch=scratch,
    )


class Shards:
    def __init__(self, send, keep, order):
        places, self.shard, self.width = send.shape
        bits = places.bit_length() - 1
        self.order = list(order)
        self.places = list(range(bits))[::-1]
        shape = (2,) * bits + (self.shard, self.width)
        self.held = [(keep.reshape(shape), self.places)]
        self.coming = flipped(send, "dp", 1).reshape(shape)
        self.done = ()
        self.mine = None

    def plan(self):
        self.held.append((self.coming, self.places))
        bit = self.order[0] if self.order else None
        rest = [each for each in self.places if each != bit]
        operands, specs, entries = [], [], []
        for array, dims in self.held:
            place = tuple(1 if dim == bit else 0 for dim in dims)
            block = tuple(2 if dim in rest else 1 for dim in dims)
            operands.append(array)
            specs.append(
                pl.BlockSpec(
                    block + (self.shard, self.width), lambda i, s, place=place: place + (0, 0)
                )
            )
            entries.append([rest.index(dim) if dim in rest else None for dim in dims])
        shape = (2,) * len(rest) + (self.shard, self.width)
        return operands, specs, entries, shape

    def sent(self, total):
        if self.order:
            bit = self.order.pop(0)
            self.places = [each for each in self.places if each != bit]
            self.coming = flipped(total, "dp", 2 << bit)
        else:
            self.mine = total
            self.coming = flipped(total, "mod", 1)


class Everywhere:
    def __init__(self, mine, masks):
        self.masks = list(masks)
        self.send(mine)

    def send(self, mine):
        self.mine = mine
        if self.masks:
            self.coming = flipped(mine, "dp", self.masks.pop(0))
        else:
            self.coming = flipped(mine, "mod", 1)


def advance(scalars, pieces, extra=None):
    plans = [piece.plan() for piece in pieces]
    operands = [array for plan in plans for array in plan[0]]
    in_specs = [spec for plan in plans for spec in plan[1]]
    shapes = [plan[3] for plan in plans]
    out_shape = [jax.ShapeDtypeStruct(shape, BF16) for shape in shapes]
    if extra is not None:
        operands += [extra.mine, extra.coming]
        in_specs += [whole(extra.mine)] * 2
        out_shape.append(jax.ShapeDtypeStruct(extra.mine.shape, F32))

    def kernel(scalars_ref, *refs):
        ins, outs = refs[: len(operands)], refs[len(operands) :]
        at = 0
        for plan, out in zip(plans, outs):
            entries, shape = plan[2], plan[3]
            for index in np.ndindex(shape[:-2]):
                total = None
                for n, dims in enumerate(entries):
                    where = tuple(0 if dim is None else index[dim] for dim in dims)
                    term = ins[at + n][where].astype(F32)
                    total = term if total is None else total + term
                out[index] = total.astype(BF16)
            at += len(entries)
        if extra is not None:
            outs[-1][...] = ins[at][...] + ins[at + 1][...]

    def full(shape):
        return pl.BlockSpec(shape, lambda i, s: (0,) * len(shape))

    totals = call(
        kernel,
        scalars,
        operands,
        in_specs,
        [full(shape.shape) for shape in out_shape],
        out_shape,
        (1,),
        "advance",
    )
    for piece, total in zip(pieces, totals):
        piece.sent(total)
    if extra is not None:
        extra.send(totals[-1])


def finish(scalars, pieces, extra=None):
    operands, widths = [], []
    for piece in pieces:
        operands += [piece.mine, piece.coming]
        widths.append(piece.width)
    if extra is not None:
        operands += [extra.mine, extra.coming]
    shape = (pieces[0].shard, sum(widths))
    out_shape = [jax.ShapeDtypeStruct(shape, F32)]
    if extra is not None:
        out_shape.append(jax.ShapeDtypeStruct(extra.mine.shape, F32))

    def kernel(scalars_ref, *refs):
        out = refs[len(operands)]
        first = 0
        for n, width in enumerate(widths):
            out[:, first : first + width] = refs[2 * n][...].astype(F32) + refs[
                2 * n + 1
            ][...].astype(F32)
            first += width
        if extra is not None:
            refs[-1][...] = refs[2 * len(widths)][...] + refs[2 * len(widths) + 1][...]

    return call(
        kernel,
        scalars,
        operands,
        [whole(array) for array in operands],
        [pl.BlockSpec(each.shape, lambda i, s: (0, 0)) for each in out_shape],
        out_shape,
        (1,),
        "finish",
    )


def pack_small(scalars, sums_qv_a, sums_qv_b, sums_one, sums_two, inner_sum):
    width = sums_one.shape[1]
    count = inner_sum.shape[1] // width

    def kernel(scalars_ref, qv_a, qv_b, one, two, inner, out):
        out[0:2] = qv_a[0:2] + qv_b[0:2]
        out[2:3] = one[0:1]
        out[3:4] = two[0:1]
        out[4:5] = one[2:3]
        out[5:6] = one[1:2]
        out[6:7] = two[2:3]
        out[7:8] = two[1:2]
        for i in range(count):
            out[8 + i : 9 + i] = inner[0:1, i * width : (i + 1) * width]

    operands = [sums_qv_a, sums_qv_b, sums_one, sums_two, inner_sum]
    shape = (8 + count, width)
    return call(
        kernel,
        scalars,
        operands,
        [whole(array) for array in operands],
        [pl.BlockSpec(shape, lambda i, s: (0, 0))],
        [jax.ShapeDtypeStruct(shape, F32)],
        (1,),
        "pack_small",
    )[0]


def reduce_plain(send, keep):
    total = jnp.stack([keep, send], 1)
    total = total.reshape(-1, total.shape[-1]).astype(F32)
    share = lax.psum_scatter(total, "dp", scatter_dimension=0, tiled=True)
    return lax.psum(share.astype(BF16), "mod").astype(F32)


def body(
    layer_rows,
    cotangent,
    row_live,
    partner,
    w_qkv,
    b_qv,
    w_out,
    norm_gains,
    bias_rows,
    w_in,
    b_in,
    w_back,
):
    side = lax.axis_index("mod")
    place = lax.axis_index("dp")
    shards = lax.axis_size("dp")
    groups = partner.shape[1]
    aligned = shards == 16 and (layer_rows.shape[2] // shards) % 16 == 0
    layout = shards if aligned else 16
    half = groups // 2
    width = layer_rows.shape[2]
    slot_rows = layer_rows.shape[1] // groups
    inner_width = w_in.shape[1]
    slots = (groups, slot_rows, width)
    rows = layer_rows[0].reshape(slots)
    cot = cotangent[0].reshape(slots)
    spot = place if aligned else 0 * place
    scalars = jnp.concatenate(
        [partner[0], jnp.stack([side, spot & 1, spot >> 1]).astype(jnp.int32)]
    )
    cut = half // 2
    LINE.clear()
    sent_a = gather_sent(scalars, rows, half, 0, cut)
    got_a = flipped(sent_a, "mod", 1)
    sent_b = gather_sent(scalars, rows, half, cut, cut)
    got_b = flipped(sent_b, "mod", 1)
    sent_cot = gather_sent(scalars, cot, half, 0, half)
    far_cot = flipped(sent_cot, "mod", 1)

    live = row_live.reshape(2, groups, slot_rows)
    words_live = lax.dynamic_slice_in_dim(live[0], side * half, half, 0)
    region_live = live[1][lax.dynamic_slice_in_dim(partner[0], side * half, half, 0)]
    is_first = side == 0
    seen = jnp.concatenate(
        [
            jnp.where(is_first, words_live, region_live),
            jnp.where(is_first, region_live, words_live),
        ],
        1,
    )[:, None, :]

    heads_weights = (w_qkv, b_qv, w_out, norm_gains, bias_rows)
    first_part = attention_forward(scalars, rows, got_a, seen, heads_weights, 0, half)
    joined, mixed, probs, context, normed, root = attention_forward(
        scalars, rows, got_b, seen, heads_weights, cut, half, into=first_part
    )
    feed_weights = (w_in, b_in.reshape(1, inner_width), w_back, norm_gains, bias_rows)
    slope, branch, out_kept, out_far, sums_two, *back = feed_forward(
        scalars, normed, cot, far_cot, feed_weights, half, layout, groups
    )
    out_back = flipped(out_far, "mod", 1)
    back_weights = (w_in, w_back, norm_gains, bias_rows)
    attn_weights = (w_out, w_qkv)
    bits = (layout // 2).bit_length() - 1
    order = list(range(bits))
    other = order[1:] + order[:1]
    if aligned:
        back_a, back_b = Shards(*back[:2], order), Shards(*back[2:], order)
        advance(scalars, [back_a])
        advance(scalars, [back_b])
    low_attn, sums_one, inner_sum, *inner = feed_backward(
        scalars, branch, slope, normed, root, context, back_weights, layout, groups
    )
    if aligned:
        inner_a, inner_b = Shards(*inner[:2], order), Shards(*inner[2:4], order)
        outer = Shards(*inner[4:], other)
    out_rows = scatter_home(scalars, out_kept, out_back, half).reshape(1, -1, width)
    if aligned:
        advance(scalars, [inner_a])
        advance(scalars, [inner_b, outer])
        advance(scalars, [back_a, back_b])
    attn_kept = (low_attn, mixed, probs, joined)
    *first_part, sums_qv_a = attention_backward(
        scalars, attn_kept, attn_weights, 0, 2, layout, groups
    )
    if aligned:
        advance(scalars, [back_a, back_b, outer])
    _, d_kept, d_far, sums_qv_b, *qkv = attention_backward(
        scalars, attn_kept, attn_weights, 1, 2, layout, groups, into=first_part
    )
    d_back = flipped(d_far, "mod", 1)
    small = pack_small(scalars, sums_qv_a, sums_qv_b, sums_one, sums_two, inner_sum)
    if aligned:
        qkv_a, qkv_b = Shards(*qkv[:2], order), Shards(*qkv[2:4], other)
        qkv_c = Shards(*qkv[4:], order)
        small = Everywhere(small, [1] + [2 << bit for bit in order])
        advance(scalars, [inner_a, inner_b, back_a, back_b, outer])
        advance(scalars, [qkv_a, qkv_b, qkv_c], small)
        advance(scalars, [inner_a, inner_b, outer])
        (grad_back,) = finish(scalars, [back_a, back_b])
        advance(scalars, [qkv_a, qkv_b, qkv_c], small)
        advance(scalars, [inner_a, inner_b])
        grad_rows = scatter_home(scalars, d_kept, d_back, half).reshape(1, -1, width)
        advance(scalars, [qkv_a, qkv_b, qkv_c], small)
        (grad_out,) = finish(scalars, [outer])
        (grad_in,) = finish(scalars, [inner_a, inner_b])
        advance(scalars, [qkv_a, qkv_b, qkv_c], small)
        grad_qkv, small = finish(scalars, [qkv_a, qkv_b, qkv_c], small)
    else:
        grad_back = jnp.concatenate([reduce_plain(*back[:2]), reduce_plain(*back[2:])], 1)
        grad_in = jnp.concatenate([reduce_plain(*inner[:2]), reduce_plain(*inner[2:4])], 1)
        grad_out = reduce_plain(*inner[4:])
        grad_qkv = jnp.concatenate([reduce_plain(*qkv[i : i + 2]) for i in (0, 2, 4)], 1)
        grad_rows = scatter_home(scalars, d_kept, d_back, half).reshape(1, -1, width)
        small = lax.psum(small, ("mod", "dp"))

    shard = width // shards
    rows_small = lax.dynamic_slice_in_dim(small[:8], place * shard, shard, 1)
    inner_shard = inner_width // shards
    grad_b_in = lax.dynamic_slice_in_dim(small[8:].reshape(-1), place * inner_shard, inner_shard)

    return (
        out_rows,
        grad_rows,
        grad_qkv,
        rows_small[0:2],
        grad_out,
        rows_small[2:4],
        rows_small[4:8],
        grad_in,
        grad_b_in,
        grad_back,
    )


def solution(mesh):
    return jax.shard_map(
        body,
        mesh=mesh,
        in_specs=(
            P("mod", "dp", None),
            P("mod", "dp", None),
            P(None, "dp"),
            P("dp", None),
            P(),
            P(),
            P(),
            P(),
            P(),
            P(),
            P(),
            P(),
        ),
        out_specs=(
            P("mod", "dp", None),
            P("mod", "dp", None),
            P("dp", None),
            P(None, "dp"),
            P("dp", None),
            P(None, "dp"),
            P(None, "dp"),
            P("dp", None),
            P("dp"),
            P("dp", None),
        ),
        check_vma=False,
    )
```

```python
import functools

import jax
import jax.numpy as jnp
from jax import lax
from jax.experimental import pallas as pl
from jax.experimental.pallas import tpu as pltpu
from jax.sharding import PartitionSpec as P

HEADS = 12
EPSILON = 1e-12
F32 = jnp.float32
BF16 = jnp.bfloat16
VMEM_LIMIT = 62 * 2**20


def dot(left, right, left_dim=1, right_dim=0):
    return lax.dot_general(
        left, right, (((left_dim,), (right_dim,)), ((), ())), preferred_element_type=F32
    )


def flipped(value, axis, mask):
    pairs = [(source, source ^ mask) for source in range(lax.axis_size(axis))]
    return lax.ppermute(value, axis, pairs)


def params(limit=VMEM_LIMIT):
    return pltpu.CompilerParams(vmem_limit_bytes=limit)


def kept_slot(scalars, pair, half):
    groups = 2 * half
    side = scalars[groups]
    place = side * half + pair
    return jnp.where(side == 0, place, scalars[place])


def sent_slot(scalars, pair, half):
    groups = 2 * half
    side = scalars[groups]
    place = (1 - side) * half + pair
    return jnp.where(side == 0, place, scalars[place])


ANY = pl.BlockSpec(memory_space=pl.ANY)
LINE = []


def call(kernel, scalars, operands, in_specs, out_specs, out_shape, grid, name, **more):
    after = LINE[-1:]
    into = list(more.get("into", ()))
    into_first = more.get("into_first", 0)
    scratch = list(more.get("scratch", ()))
    taken, spare, given = len(operands), len(into) + len(after), len(out_shape)

    def wrapped(scalars_ref, *refs):
        outs = refs[taken + spare :]
        kernel(scalars_ref, *refs[:taken], *outs[:given], *outs[given + 1 :])

    outs = pl.pallas_call(
        wrapped,
        grid_spec=pltpu.PrefetchScalarGridSpec(
            num_scalar_prefetch=1,
            grid=grid,
            in_specs=list(in_specs) + [ANY] * spare,
            out_specs=list(out_specs) + [ANY],
            scratch_shapes=scratch,
        ),
        out_shape=list(out_shape) + [jax.ShapeDtypeStruct((8, 128), F32)],
        input_output_aliases={1 + taken + i: i + into_first for i in range(len(into))},
        compiler_params=params(more.get("limit", VMEM_LIMIT)),
        cost_estimate=pl.CostEstimate(flops=1, bytes_accessed=1, transcendentals=0),
        name=name,
    )(scalars, *operands, *into, *after)
    LINE.append(outs[-1])
    return list(outs[:-1])


def gather_sent(scalars, rows, half, first, count):
    slot_rows, width = rows.shape[1:]

    def kernel(scalars_ref, rows_ref, out, sems):
        copies = [
            pltpu.make_async_copy(
                rows_ref.at[sent_slot(scalars_ref, first + i, half)], out.at[i], sems.at[i]
            )
            for i in range(count)
        ]
        for copy in copies:
            copy.start()
        for copy in copies:
            copy.wait()

    shape = (count, slot_rows, width)
    return call(
        kernel,
        scalars,
        [rows],
        [ANY],
        [pl.BlockSpec(shape, lambda i, s: (0, 0, 0))],
        [jax.ShapeDtypeStruct(shape, rows.dtype)],
        (1,),
        "gather_sent",
        scratch=[pltpu.SemaphoreType.DMA((count,))],
    )[0]


def scatter_home(scalars, kept, back, half):
    slot_rows, width = kept.shape[1:]

    def kernel(scalars_ref, kept_ref, back_ref, out, sems):
        copies = []
        for i in range(half):
            copies.append(
                pltpu.make_async_copy(
                    kept_ref.at[i], out.at[kept_slot(scalars_ref, i, half)], sems.at[0, i]
                )
            )
            copies.append(
                pltpu.make_async_copy(
                    back_ref.at[i], out.at[sent_slot(scalars_ref, i, half)], sems.at[1, i]
                )
            )
        for copy in copies:
            copy.start()
        for copy in copies:
            copy.wait()

    shape = (2 * half, slot_rows, width)
    return call(
        kernel,
        scalars,
        [kept, back],
        [ANY, ANY],
        [pl.BlockSpec(shape, lambda i, s: (0, 0, 0))],
        [jax.ShapeDtypeStruct(shape, kept.dtype)],
        (1,),
        "scatter_home",
        scratch=[pltpu.SemaphoreType.DMA((2, half))],
    )[0]


def split_heads(value):
    low = lax.broadcasted_iota(jnp.int32, value.shape, 1) < value.shape[1] // 2
    zero = jnp.zeros_like(value)
    return jnp.concatenate([jnp.where(low, value, zero), jnp.where(low, zero, value)], 0)


def side_by_side(value):
    rows = value.shape[0] // 2
    return jnp.concatenate([value[:rows], value[rows:]], 1)


def row_sum(value):
    return jnp.sum(value, axis=0, keepdims=True)


def normal_form(value):
    centered = value - jnp.mean(value, axis=-1, keepdims=True)
    root = lax.rsqrt(jnp.mean(centered * centered, axis=-1, keepdims=True) + EPSILON)
    return centered * root, root


def normal_back(lifted, normed, root):
    return root * (
        lifted
        - jnp.mean(lifted, axis=-1, keepdims=True)
        - normed * jnp.mean(lifted * normed, axis=-1, keepdims=True)
    )


def whole(array):
    return pl.BlockSpec(
        array.shape, lambda *_: (0,) * array.ndim, pipeline_mode=pl.Buffered(1)
    )


def attention_forward(
    scalars, rows, received, live, weights, first, half, into=()
):
    w_qkv, b_qv, w_out, norm_gains, bias_rows = weights
    slot_rows, width = rows.shape[1:]
    pairs = received.shape[0]
    length = 2 * slot_rows
    duo = 2 * width // HEADS
    blocks = width // duo
    score_scale = (width // HEADS) ** (-0.5)

    def kernel(
        scalars_ref,
        kept_a,
        kept_b,
        got,
        live_ref,
        w_qkv_ref,
        b_qv_ref,
        w_out_ref,
        gains_ref,
        biases_ref,
        joined_out,
        mixed_out,
        probs_out,
        context_out,
        normed_out,
        root_out,
    ):
        joined = jnp.concatenate([kept_a[0], got[0], kept_b[0], got[1]], 0)
        joined_out[...] = joined
        mixed = dot(joined, w_qkv_ref[...])
        queries = (mixed[:, :width] + b_qv_ref[0:1, :]).astype(BF16)
        queries = (queries.astype(F32) * score_scale).astype(BF16)
        keys = mixed[:, width : 2 * width].astype(BF16)
        values = (mixed[:, 2 * width :] + b_qv_ref[1:2, :]).astype(BF16)
        mixed_out[:, :width] = queries
        mixed_out[:, width : 2 * width] = keys
        mixed_out[:, 2 * width :] = values
        contexts = []
        for pair in range(2):
            seen = live_ref[pair] > 0
            span = slice(pair * length, (pair + 1) * length)
            heads = []
            for block in range(blocks):
                cols = slice(block * duo, (block + 1) * duo)
                scores = dot(split_heads(queries[span, cols]), keys[span, cols], 1, 1)
                scores = jnp.where(seen, scores, -1e30)
                powered = jnp.exp(scores - jnp.max(scores, axis=-1, keepdims=True))
                low_probs = powered * (1.0 / jnp.sum(powered, axis=-1, keepdims=True))
                low_probs = low_probs.astype(BF16)
                probs_out[pair, block] = low_probs
                heads.append(
                    dot(side_by_side(low_probs), split_heads(values[span, cols])).astype(BF16)
                )
            contexts.append(jnp.concatenate(heads, 1))
        context = jnp.concatenate(contexts, 0)
        context_out[...] = context
        pre_one = joined.astype(F32) + dot(context, w_out_ref[...]) + biases_ref[0:1, :]
        normed, root = normal_form(pre_one)
        normed_out[...] = normed.astype(BF16)
        root_out[...] = jnp.broadcast_to(root, root_out.shape)

    start = first // 2

    def by_rows(columns):
        return pl.BlockSpec((2 * length, columns), lambda i, s: (start + i, 0))

    slot = (1, slot_rows, width)
    total = half * length
    return call(
        kernel,
        scalars,
        [rows, rows, received, live, w_qkv, b_qv, w_out, norm_gains, bias_rows],
        [
            pl.BlockSpec(slot, lambda i, s: (kept_slot(s, first + 2 * i, half), 0, 0)),
            pl.BlockSpec(slot, lambda i, s: (kept_slot(s, first + 2 * i + 1, half), 0, 0)),
            pl.BlockSpec((2, slot_rows, width), lambda i, s: (i, 0, 0)),
            pl.BlockSpec((2, 1, length), lambda i, s: (start + i, 0, 0)),
            whole(w_qkv),
            whole(b_qv),
            whole(w_out),
            whole(norm_gains),
            whole(bias_rows),
        ],
        [
            by_rows(width),
            by_rows(3 * width),
            pl.BlockSpec((2, blocks, 2 * length, length), lambda i, s: (start + i, 0, 0, 0)),
            by_rows(width),
            by_rows(width),
            by_rows(128),
        ],
        [
            jax.ShapeDtypeStruct((total, width), BF16),
            jax.ShapeDtypeStruct((total, 3 * width), BF16),
            jax.ShapeDtypeStruct((half, blocks, 2 * length, length), BF16),
            jax.ShapeDtypeStruct((total, width), BF16),
            jax.ShapeDtypeStruct((total, width), BF16),
            jax.ShapeDtypeStruct((total, 128), F32),
        ],
        (pairs // 2,),
        "attention_forward",
        into=into,
    )


def spread(grad, out_pairs, scalars_ref, base, shard, first_row, places):
    core = scalars_ref[base + 1]
    for j in range(places):
        row = (first_row ^ j) * 2
        for out, which in ((out_pairs[0], 1 - core), (out_pairs[1], core)):
            out[j] = grad[pl.ds(pl.multiple_of((row + which) * shard, 16), shard), :]


def feed_forward(scalars, normed, cot, far_cot, weights, half, shards, base):
    w_in, b_in, w_back, norm_gains, bias_rows = weights
    slot_rows, width = cot.shape[1:]
    inner_width = w_in.shape[1]
    length = 2 * slot_rows
    rows = 2 * length
    height = half * length
    steps = half // 2
    chunk = 768
    chunks = inner_width // chunk
    shard = inner_width // shards
    places = shards // 2
    part = 4 * shard
    parts = inner_width // part

    def kernel(
        scalars_ref,
        normed_ref,
        cot_a,
        cot_b,
        cot_far,
        w_in_hbm,
        b_in_ref,
        w_back_hbm,
        gains_ref,
        biases_ref,
        slope_out,
        branch_out,
        kept_out,
        far_out,
        sums_out,
        send,
        keep,
        w_in_ref,
        w_back_ref,
        held,
        acts,
        branches,
        grad,
        sems,
    ):
        step = pl.program_id(0)

        def fetch_in(j):
            cols = pl.ds(j * chunk, chunk)
            return pltpu.make_async_copy(
                w_in_hbm.at[:, cols], w_in_ref.at[:, cols], sems.at[0, j]
            )

        def fetch_back(j):
            cols = pl.ds(j * chunk, chunk)
            return pltpu.make_async_copy(w_back_hbm.at[cols], w_back_ref.at[cols], sems.at[1, j])

        @pl.when(step == 0)
        def _():
            sums_out[...] = jnp.zeros_like(sums_out)
            for j in range(chunks):
                fetch_in(j).start()
                fetch_back(j).start()

        def close(pre_two, row):
            scaled, root = normal_form(pre_two)
            output = (scaled * gains_ref[1:2, :] + biases_ref[3:4, :]).astype(BF16)
            for i in range(2):
                kept_out[i] = output[i * length : i * length + slot_rows]
                far_out[i] = output[i * length + slot_rows : (i + 1) * length]
            here = jnp.concatenate([cot_a[0], cot_far[0], cot_b[0], cot_far[1]], 0).astype(F32)
            d_two = normal_back(here * gains_ref[1:2, :], scaled, root)
            low = d_two.astype(BF16)
            branch_out[...] = low
            branches[pl.ds(row, rows)] = low
            return jnp.concatenate([row_sum(here * scaled), row_sum(here), row_sum(d_two)], 0)

        def forward(first):
            hidden = normed_ref[...].astype(F32) * gains_ref[0:1, :] + biases_ref[1:2, :]
            low_hidden = hidden.astype(BF16)
            total = hidden + biases_ref[2:3, :]
            for j in range(chunks):
                cols = slice(j * chunk, (j + 1) * chunk)
                if first:
                    fetch_in(j).wait()
                inner = dot(low_hidden, w_in_ref[:, cols]) + b_in_ref[:, cols]
                normal = 0.5 + 0.5 * lax.erf(inner * (0.5**0.5))
                low_act = (inner * normal).astype(BF16)
                density = jnp.exp(inner * inner * -0.5) * 0.3989422804014327
                acts[pl.ds(step * rows, rows), cols] = low_act
                slope_out[:, cols] = (normal + inner * density).astype(BF16)
                if first:
                    fetch_back(j).wait()
                total = total + dot(low_act, w_back_ref[cols, :])
            return total

        @pl.when(step == 0)
        def _():
            held[...] = forward(True)

        @pl.when((step > 0) & (step < steps))
        def _():
            before = held[...]
            held[...] = forward(False)
            sums_out[0:3, :] += close(before, (step - 1) * rows)

        @pl.when(step == steps)
        def _():
            sums_out[0:3, :] += close(held[...], (step - 1) * rows)

        @pl.when(step >= steps)
        def _():
            start = pl.multiple_of((step - steps) * part, 128)
            grad[...] = dot(acts[:, pl.ds(start, part)], branches[...], 0, 0).astype(BF16)
            spread(grad, (send, keep), scalars_ref, base, shard, scalars_ref[base + 2] & 1, 2)

    def ahead(i):
        return jnp.minimum(i, steps - 1)

    def behind(i):
        return jnp.clip(i - 1, 0, steps - 1)

    def slot(j):
        return pl.BlockSpec(
            (1, slot_rows, width), lambda i, s: (kept_slot(s, 2 * behind(i) + j, half), 0, 0)
        )

    duo = pl.BlockSpec((2, slot_rows, width), lambda i, s: (behind(i), 0, 0))
    grads = pl.BlockSpec(
        (2, shard, width), lambda i, s: ((s[base + 2] >> 1) ^ jnp.maximum(i - steps, 0), 0, 0)
    )
    return call(
        kernel,
        scalars,
        [normed, cot, cot, far_cot, w_in, b_in, w_back, norm_gains, bias_rows],
        [
            pl.BlockSpec((rows, width), lambda i, s: (ahead(i), 0)),
            slot(0),
            slot(1),
            duo,
            ANY,
            whole(b_in),
            ANY,
            whole(norm_gains),
            whole(bias_rows),
        ],
        [
            pl.BlockSpec((rows, inner_width), lambda i, s: (ahead(i), 0)),
            pl.BlockSpec((rows, width), lambda i, s: (behind(i), 0)),
            duo,
            duo,
            pl.BlockSpec((8, width), lambda i, s: (0, 0)),
            grads,
            grads,
        ],
        [
            jax.ShapeDtypeStruct((height, inner_width), BF16),
            jax.ShapeDtypeStruct((height, width), BF16),
            jax.ShapeDtypeStruct((half, slot_rows, width), BF16),
            jax.ShapeDtypeStruct((half, slot_rows, width), BF16),
            jax.ShapeDtypeStruct((8, width), F32),
            jax.ShapeDtypeStruct((places, shard, width), BF16),
            jax.ShapeDtypeStruct((places, shard, width), BF16),
        ],
        (steps + parts,),
        "feed_forward",
        scratch=[
            pltpu.VMEM((width, inner_width), BF16),
            pltpu.VMEM((inner_width, width), BF16),
            pltpu.VMEM((rows, width), F32),
            pltpu.VMEM((height, inner_width), BF16),
            pltpu.VMEM((height, width), BF16),
            pltpu.VMEM((part, width), BF16),
            pltpu.SemaphoreType.DMA((2, chunks)),
        ],
    )


def feed_backward(scalars, branch, slope, normed, root, context, weights, shards, base):
    w_in, w_back, norm_gains, bias_rows = weights
    total, width = branch.shape
    inner_width = slope.shape[1]
    chunk = 768
    steps = inner_width // chunk
    turn = steps // 2
    shard = width // shards
    places = shards // 2
    piece = 128

    def kernel(
        scalars_ref,
        branch_ref,
        slope_ref,
        normed_ref,
        root_ref,
        context_ref,
        w_in_ref,
        w_back_ref,
        gains_ref,
        biases_ref,
        low_attn_out,
        sums_out,
        inner_sum_out,
        send_a,
        keep_a,
        send_b,
        keep_b,
        held,
        low_hidden,
        grad,
    ):
        step = pl.program_id(0)
        place = scalars_ref[base + 2]

        @pl.when(step == 0)
        def _():
            hidden = normed_ref[...].astype(F32) * gains_ref[0:1, :] + biases_ref[1:2, :]
            low_hidden[...] = hidden.astype(BF16)
            held[...] = branch_ref[...].astype(F32)

        sums = jnp.zeros((1, chunk), F32)
        lows = []
        for r in range(0, total, 256):
            span = slice(r, r + 256)
            d_inner = dot(branch_ref[span], w_back_ref[...], 1, 1) * slope_ref[span].astype(F32)
            sums = sums + row_sum(d_inner)
            low = d_inner.astype(BF16)
            lows.append(low)
            held[span] += dot(low, w_in_ref[...], 1, 1)
        inner_sum_out[...] = jnp.broadcast_to(sums, inner_sum_out.shape)
        grad[...] = dot(low_hidden[...], jnp.concatenate(lows, 0), 0, 0).astype(BF16)

        @pl.when(step < turn)
        def _():
            spread(grad, (send_a, keep_a), scalars_ref, base, shard, place, places)

        for j in range(turn):

            @pl.when(step == turn + j)
            def _():
                cols = pl.ds(j * chunk, chunk)
                outs = (send_b.at[:, :, cols], keep_b.at[:, :, cols])
                spread(grad, outs, scalars_ref, base, shard, place, places)

        @pl.when(step == steps - 1)
        def _():
            sums = [jnp.zeros((1, width), F32)] * 3
            lows = []
            for i in range(total // piece):
                span = slice(i * piece, (i + 1) * piece)
                d_hidden, scaled = held[span], normed_ref[span].astype(F32)
                d_one = normal_back(d_hidden * gains_ref[0:1, :], scaled, root_ref[span, 0:1])
                lows.append(d_one.astype(BF16))
                low_attn_out[span] = lows[-1]
                for j, term in enumerate((d_hidden * scaled, d_hidden, d_one)):
                    sums[j] = sums[j] + row_sum(term)
            sums_out[...] = jnp.concatenate(sums + [jnp.zeros((5, width), F32)], 0)
            grad[:, :width] = dot(context_ref[...], jnp.concatenate(lows, 0), 0, 0).astype(BF16)
            cols = pl.ds(turn * chunk, width)
            outs = (send_b.at[:, :, cols], keep_b.at[:, :, cols])
            spread(grad, outs, scalars_ref, base, shard, place, places)

    half_a = pl.BlockSpec((places, shard, chunk), lambda i, s: (0, 0, jnp.minimum(i, turn - 1)))
    wide = (steps - turn) * chunk + width
    half_b = pl.BlockSpec((places, shard, wide), lambda i, s: (0, 0, 0))
    shape_a = jax.ShapeDtypeStruct((places, shard, turn * chunk), BF16)
    shape_b = jax.ShapeDtypeStruct((places, shard, wide), BF16)
    return call(
        kernel,
        scalars,
        [branch, slope, normed, root, context, w_in, w_back, norm_gains, bias_rows],
        [
            whole(branch),
            pl.BlockSpec((total, chunk), lambda i, s: (0, i)),
            whole(normed),
            whole(root),
            whole(context),
            pl.BlockSpec((width, chunk), lambda i, s: (0, i)),
            pl.BlockSpec((chunk, width), lambda i, s: (i, 0)),
            whole(norm_gains),
            whole(bias_rows),
        ],
        [
            pl.BlockSpec((total, width), lambda i, s: (0, 0)),
            pl.BlockSpec((8, width), lambda i, s: (0, 0)),
            pl.BlockSpec((8, chunk), lambda i, s: (0, i)),
            half_a,
            half_a,
            half_b,
            half_b,
        ],
        [
            jax.ShapeDtypeStruct((total, width), BF16),
            jax.ShapeDtypeStruct((8, width), F32),
            jax.ShapeDtypeStruct((8, inner_width), F32),
            shape_a,
            shape_a,
            shape_b,
            shape_b,
        ],
        (steps,),
        "feed_backward",
        scratch=[
            pltpu.VMEM((total, width), F32),
            pltpu.VMEM((total, width), BF16),
            pltpu.VMEM((width, chunk), BF16),
        ],
    )


def attention_backward(scalars, kept, weights, part, parts, shards, base, into=(), sums=()):
    low_attn, mixed, probs, joined = kept
    w_out, w_qkv = weights
    total, width = low_attn.shape
    pairs, blocks, _, length = probs.shape
    duo = width // blocks
    slot_rows = length // 2
    score_scale = (width // HEADS) ** (-0.5)
    steps = pairs // 2 // parts
    start = part * steps
    last = part == parts - 1
    before = start * 2 * length
    shard = width // shards
    places = shards // 2
    turn = 3 * width // 2

    def kernel(
        scalars_ref,
        low_attn_ref,
        mixed_ref,
        probs_ref,
        w_out_ref,
        w_qkv_ref,
        *refs,
    ):
        if last:
            joined_ref, earlier_ref, early_ref, sums_ref = refs[:4]
            refs = refs[4:]
        d_mixed_out, kept_out, far_out, sums_out = refs[:4]
        step = pl.program_id(0)

        @pl.when(step == 0)
        def _():
            sums_out[...] = jnp.zeros_like(sums_out)

        d_context = dot(low_attn_ref[...], w_out_ref[...], 1, 1).astype(BF16)
        for pair in range(2):
            span = slice(pair * length, (pair + 1) * length)
            d_heads, d_probs, d_scores = [], [], []
            for block in range(blocks):
                cols = slice(block * duo, (block + 1) * duo)
                values = mixed_ref[span, 2 * width + block * duo : 2 * width + (block + 1) * duo]
                d_heads.append(split_heads(d_context[span, cols]))
                d_probs.append(dot(d_heads[block], values, 1, 1))
            for block in range(blocks):
                wide = probs_ref[pair, block].astype(F32)
                mean = jnp.sum(wide * d_probs[block], axis=-1, keepdims=True)
                d_scores.append((wide * (d_probs[block] - mean)).astype(BF16))
            for block in range(blocks):
                cols = slice(block * duo, (block + 1) * duo)
                key_cols = slice(width + block * duo, width + (block + 1) * duo)
                value_cols = slice(2 * width + block * duo, 2 * width + (block + 1) * duo)
                queries = split_heads(mixed_ref[span, cols])
                keys = split_heads(mixed_ref[span, key_cols])
                d_queries = dot(side_by_side(d_scores[block]), keys) * score_scale
                d_mixed_out[span, cols] = d_queries.astype(BF16)
                d_mixed_out[span, key_cols] = dot(d_scores[block], queries, 0, 0).astype(BF16)
                d_mixed_out[span, value_cols] = dot(
                    probs_ref[pair, block], d_heads[block], 0, 0
                ).astype(BF16)
        d_mixed = d_mixed_out[...]
        sums_out[0:1, :] += row_sum(d_mixed[:, :width].astype(F32))
        sums_out[1:2, :] += row_sum(d_mixed[:, 2 * width :].astype(F32))
        d_rows = low_attn_ref[...].astype(F32) + dot(d_mixed, w_qkv_ref[...], 1, 1)
        d_rows = d_rows.astype(BF16)
        for i in range(2):
            kept_out[i] = d_rows[i * length : i * length + slot_rows]
            far_out[i] = d_rows[i * length + slot_rows : (i + 1) * length]
        if last:
            grads, (held, grad) = refs[4:8], refs[8:]
            held[pl.ds(step * 2 * length, 2 * length)] = d_mixed
            place = scalars_ref[base + 2]

            @pl.when(step == steps - 1)
            def _():
                for i in range(3):
                    cols = slice(i * width, (i + 1) * width)
                    total_grad = dot(joined_ref[:before], earlier_ref[:, cols], 0, 0)
                    total_grad = total_grad + dot(joined_ref[before:], held[:, cols], 0, 0)
                    grad[...] = total_grad.astype(BF16)
                    for at in range(0, width, width // 2):
                        column = i * width + at
                        piece, column = divmod(column, turn)
                        outs = [
                            each.at[:, :, pl.ds(column, width // 2)]
                            for each in grads[2 * piece : 2 * piece + 2]
                        ]
                        taken = grad.at[:, pl.ds(at, width // 2)]
                        spread(taken, outs, scalars_ref, base, shard, place, places)
                small = early_ref[...]
                known = sums_ref[0:2] + sums_out[0:2]
                small = jnp.concatenate([known, small[2:], jnp.zeros((112, width), F32)], 0)
                grad[:, :128] = small.T.astype(BF16)
                outs = [each.at[:, :, pl.ds(turn, 128)] for each in grads[2:]]
                spread(grad.at[:, pl.ds(0, 128)], outs, scalars_ref, base, shard, place, places)

    def by_rows(columns):
        return pl.BlockSpec((2 * length, columns), lambda i, s: (start + i, 0))

    two = pl.BlockSpec((2, slot_rows, width), lambda i, s: (start + i, 0, 0))
    operands = [low_attn, mixed, probs, w_out, w_qkv]
    in_specs = [
        by_rows(width),
        by_rows(3 * width),
        pl.BlockSpec((2, blocks, 2 * length, length), lambda i, s: (start + i, 0, 0, 0)),
        whole(w_out),
        whole(w_qkv),
    ]
    out_specs = [by_rows(3 * width), two, two, pl.BlockSpec((8, width), lambda i, s: (0, 0))]
    out_shape = [
        jax.ShapeDtypeStruct((total, 3 * width), BF16),
        jax.ShapeDtypeStruct((pairs, slot_rows, width), BF16),
        jax.ShapeDtypeStruct((pairs, slot_rows, width), BF16),
        jax.ShapeDtypeStruct((8, width), F32),
    ]
    scratch = []
    if last:
        operands += [joined, into[0], *sums]
        in_specs += [
            whole(joined),
            pl.BlockSpec((before, 3 * width), lambda i, s: (0, 0), pipeline_mode=pl.Buffered(1)),
            whole(sums[0]),
            whole(sums[1]),
        ]
        for columns in (turn, turn, turn + 128, turn + 128):
            out_specs.append(pl.BlockSpec((places, shard, columns), lambda i, s: (0, 0, 0)))
            out_shape.append(jax.ShapeDtypeStruct((places, shard, columns), BF16))
        scratch = [
            pltpu.VMEM((steps * 2 * length, 3 * width), BF16),
            pltpu.VMEM((width, width), BF16),
        ]
        out_specs[0] = pl.BlockSpec((2 * length, 3 * width), lambda i, s: (0, 0))
        out_shape[0] = jax.ShapeDtypeStruct((2 * length, 3 * width), BF16)
    return call(
        kernel,
        scalars,
        operands,
        in_specs,
        out_specs,
        out_shape,
        (steps,),
        "attention_backward",
        into=into[1:],
        into_first=1,
        scratch=scratch,
    )


def added(parts):
    total = parts[0].astype(F32)
    for part in parts[1:]:
        total = total + part.astype(F32)
    return total.astype(BF16)


def in_turn(value):
    return lax.optimization_barrier((value, LINE[-1]))[0]


class Shards:
    def __init__(self, send, keep, order):
        places, shard, width = send.shape
        bits = places.bit_length() - 1
        self.order = list(order)
        self.halved = "mod" in self.order
        self.places = list(range(bits))[::-1]
        shape = (2,) * bits + (shard, width)
        self.held = [keep.reshape(shape)]
        self.coming = flipped(send, "dp", 1).reshape(shape)

    def step(self):
        self.held.append(in_turn(self.coming))
        if not self.order:
            self.mine = lax.optimization_barrier(added(self.held))
            self.coming = flipped(self.mine, "mod", 1)
            LINE.append(self.mine)
            return
        bit = self.order.pop(0)
        if bit == "mod":
            side, columns = lax.axis_index("mod"), self.held[0].shape[-1] // 2

            def part(array, which):
                return lax.dynamic_slice_in_dim(array, which * columns, columns, array.ndim - 1)

            away = added([part(array, 1 - side) for array in self.held])
            self.held = [part(array, side) for array in self.held]
            self.coming = flipped(away, "mod", 1)
        else:
            dim = self.places.index(bit)
            away = added([lax.index_in_dim(part, 1, dim, keepdims=False) for part in self.held])
            self.held = [lax.index_in_dim(part, 0, dim, keepdims=False) for part in self.held]
            self.places.remove(bit)
            self.coming = flipped(away, "dp", 2 << bit)
        LINE.append(away)

    def result(self):
        coming = in_turn(self.coming)
        if self.halved:
            first = lax.axis_index("mod") == 0
            total = jnp.concatenate(
                [jnp.where(first, self.mine, coming), jnp.where(first, coming, self.mine)], 1
            ).astype(F32)
        else:
            total = self.mine.astype(F32) + coming.astype(F32)
        return total


def reduce_plain(send, keep):
    total = jnp.stack([keep, send], 1)
    total = total.reshape(-1, total.shape[-1]).astype(F32)
    share = lax.psum_scatter(total, "dp", scatter_dimension=0, tiled=True)
    return lax.psum(share.astype(BF16), "mod").astype(F32)


def body(
    layer_rows,
    cotangent,
    row_live,
    partner,
    w_qkv,
    b_qv,
    w_out,
    norm_gains,
    bias_rows,
    w_in,
    b_in,
    w_back,
):
    side = lax.axis_index("mod")
    place = lax.axis_index("dp")
    shards = lax.axis_size("dp")
    groups = partner.shape[1]
    aligned = shards == 16 and (layer_rows.shape[2] // shards) % 16 == 0
    layout = shards if aligned else 16
    half = groups // 2
    width = layer_rows.shape[2]
    slot_rows = layer_rows.shape[1] // groups
    inner_width = w_in.shape[1]
    slots = (groups, slot_rows, width)
    rows = layer_rows[0].reshape(slots)
    cot = cotangent[0].reshape(slots)
    spot = place if aligned else 0 * place
    scalars = jnp.concatenate(
        [partner[0], jnp.stack([side, spot & 1, spot >> 1]).astype(jnp.int32)]
    )
    cut = half // 2
    LINE.clear()
    sent_a = gather_sent(scalars, rows, half, 0, cut)
    got_a = flipped(sent_a, "mod", 1)
    sent_b = gather_sent(scalars, rows, half, cut, cut)
    got_b = flipped(sent_b, "mod", 1)
    sent_cot = gather_sent(scalars, cot, half, 0, half)
    far_cot = flipped(sent_cot, "mod", 1)

    live = row_live.reshape(2, groups, slot_rows)
    words_live = lax.dynamic_slice_in_dim(live[0], side * half, half, 0)
    region_live = live[1][lax.dynamic_slice_in_dim(partner[0], side * half, half, 0)]
    is_first = side == 0
    seen = jnp.concatenate(
        [
            jnp.where(is_first, words_live, region_live),
            jnp.where(is_first, region_live, words_live),
        ],
        1,
    )[:, None, :]

    heads_weights = (w_qkv, b_qv, w_out, norm_gains, bias_rows)
    first_part = attention_forward(scalars, rows, got_a, seen, heads_weights, 0, half)
    joined, mixed, probs, context, normed, root = attention_forward(
        scalars, rows, got_b, seen, heads_weights, cut, half, into=first_part
    )
    feed_weights = (w_in, b_in.reshape(1, inner_width), w_back, norm_gains, bias_rows)
    slope, branch, out_kept, out_far, sums_two, *back = feed_forward(
        scalars, normed, cot, far_cot, feed_weights, half, layout, groups
    )
    out_back = flipped(out_far, "mod", 1)
    back_weights = (w_in, w_back, norm_gains, bias_rows)
    attn_weights = (w_out, w_qkv)
    if aligned:
        back = Shards(*back, [0, 1, 2])
        back.step()
    low_attn, sums_one, inner_sum, *inner = feed_backward(
        scalars, branch, slope, normed, root, context, back_weights, layout, groups
    )
    shard = width // shards
    count = inner_width // width
    early = jnp.concatenate(
        [
            jnp.zeros((2, width), F32),
            sums_one[0:1],
            sums_two[0:1],
            sums_one[2:3],
            sums_one[1:2],
            sums_two[2:3],
            sums_two[1:2],
            inner_sum[0].reshape(shards, count, shard).transpose(1, 0, 2).reshape(count, width),
            jnp.zeros((8 - count, width), F32),
        ],
        0,
    )
    if aligned:
        inner_a, inner_b = Shards(*inner[:2], [0, 1, 2]), Shards(*inner[2:], ["mod", 0, 1, 2])
    out_rows = scatter_home(scalars, out_kept, out_back, half).reshape(1, -1, width)
    if aligned:
        inner_a.step()
        inner_b.step()
        back.step()
    attn_kept = (low_attn, mixed, probs, joined)
    *first_part, sums_qv = attention_backward(
        scalars, attn_kept, attn_weights, 0, 2, layout, groups
    )
    if aligned:
        back.step()
    _, d_kept, d_far, _, *qkv = attention_backward(
        scalars, attn_kept, attn_weights, 1, 2, layout, groups, first_part, (early, sums_qv)
    )
    d_back = flipped(d_far, "mod", 1)
    if aligned:
        qkv_a, qkv_b = Shards(*qkv[:2], [0, 1, 2]), Shards(*qkv[2:], [1, 2, 0])
        back.step()
        inner_a.step()
        inner_b.step()
        qkv_a.step()
        qkv_b.step()
        grad_back = back.result()
        inner_b.step()
        inner_a.step()
        qkv_a.step()
        qkv_b.step()
        grad_rows = scatter_home(scalars, d_kept, d_back, half).reshape(1, -1, width)
        inner_b.step()
        inner_a.step()
        qkv_a.step()
        qkv_b.step()
        inner_b.step()
        qkv_a.step()
        qkv_b.step()
        inner_a, inner_b = inner_a.result(), inner_b.result()
        qkv_a, qkv_b = qkv_a.result(), qkv_b.result()
    else:
        grad_back = reduce_plain(*back)
        inner_a, inner_b = reduce_plain(*inner[:2]), reduce_plain(*inner[2:])
        qkv_a, qkv_b = reduce_plain(*qkv[:2]), reduce_plain(*qkv[2:])
        grad_rows = scatter_home(scalars, d_kept, d_back, half).reshape(1, -1, width)
    turn = inner_width - inner_a.shape[1]
    grad_in = jnp.concatenate([inner_a, inner_b[:, :turn]], 1)
    grad_out = inner_b[:, turn:]
    turn = qkv_a.shape[1]
    grad_qkv = jnp.concatenate([qkv_a, qkv_b[:, :turn]], 1)
    small = qkv_b[:, turn : turn + 16].T
    return (
        out_rows,
        grad_rows,
        grad_qkv,
        small[0:2],
        grad_out,
        small[2:4],
        small[4:8],
        grad_in,
        small[8 : 8 + count].reshape(-1),
        grad_back,
    )


def solution(mesh):
    return jax.shard_map(
        body,
        mesh=mesh,
        in_specs=(
            P("mod", "dp", None),
            P("mod", "dp", None),
            P(None, "dp"),
            P("dp", None),
            P(),
            P(),
            P(),
            P(),
            P(),
            P(),
            P(),
            P(),
        ),
        out_specs=(
            P("mod", "dp", None),
            P("mod", "dp", None),
            P("dp", None),
            P(None, "dp"),
            P("dp", None),
            P(None, "dp"),
            P(None, "dp"),
            P("dp", None),
            P("dp"),
            P("dp", None),
        ),
        check_vma=False,
    )
```

```python
import functools

import jax
import jax.numpy as jnp
from jax import lax
from jax.experimental import pallas as pl
from jax.experimental.pallas import tpu as pltpu
from jax.sharding import PartitionSpec as P

HEADS = 12
EPSILON = 1e-12
F32 = jnp.float32
BF16 = jnp.bfloat16
VMEM_LIMIT = 62 * 2**20


def dot(left, right, left_dim=1, right_dim=0):
    return lax.dot_general(
        left, right, (((left_dim,), (right_dim,)), ((), ())), preferred_element_type=F32
    )


def flipped(value, axis, mask):
    pairs = [(source, source ^ mask) for source in range(lax.axis_size(axis))]
    return lax.ppermute(value, axis, pairs)


def params(limit=VMEM_LIMIT):
    return pltpu.CompilerParams(vmem_limit_bytes=limit)


def kept_slot(scalars, pair, half):
    groups = 2 * half
    side = scalars[groups]
    place = side * half + pair
    return jnp.where(side == 0, place, scalars[place])


def sent_slot(scalars, pair, half):
    groups = 2 * half
    side = scalars[groups]
    place = (1 - side) * half + pair
    return jnp.where(side == 0, place, scalars[place])


ANY = pl.BlockSpec(memory_space=pl.ANY)
LINE = []


def call(kernel, scalars, operands, in_specs, out_specs, out_shape, grid, name, **more):
    after = LINE[-1:]
    into = list(more.get("into", ()))
    into_first = more.get("into_first", 0)
    scratch = list(more.get("scratch", ()))
    taken, spare, given = len(operands), len(into) + len(after), len(out_shape)

    def wrapped(scalars_ref, *refs):
        outs = refs[taken + spare :]
        kernel(scalars_ref, *refs[:taken], *outs[:given], *outs[given + 1 :])

    outs = pl.pallas_call(
        wrapped,
        grid_spec=pltpu.PrefetchScalarGridSpec(
            num_scalar_prefetch=1,
            grid=grid,
            in_specs=list(in_specs) + [ANY] * spare,
            out_specs=list(out_specs) + [ANY],
            scratch_shapes=scratch,
        ),
        out_shape=list(out_shape) + [jax.ShapeDtypeStruct((8, 128), F32)],
        input_output_aliases={1 + taken + i: i + into_first for i in range(len(into))},
        compiler_params=params(more.get("limit", VMEM_LIMIT)),
        cost_estimate=pl.CostEstimate(
            flops=more.get("work", 4 * 10**9), bytes_accessed=2**20, transcendentals=0
        ),
        name=name,
    )(scalars, *operands, *into, *after)
    LINE.append(outs[-1])
    return list(outs[:-1])


def gather_sent(scalars, rows, half, first, count):
    slot_rows, width = rows.shape[1:]

    def kernel(scalars_ref, rows_ref, out, sems):
        copies = [
            pltpu.make_async_copy(
                rows_ref.at[sent_slot(scalars_ref, first + i, half)], out.at[i], sems.at[i]
            )
            for i in range(count)
        ]
        for copy in copies:
            copy.start()
        for copy in copies:
            copy.wait()

    shape = (count, slot_rows, width)
    return call(
        kernel,
        scalars,
        [rows],
        [ANY],
        [pl.BlockSpec(shape, lambda i, s: (0, 0, 0))],
        [jax.ShapeDtypeStruct(shape, rows.dtype)],
        (1,),
        "gather_sent",
        work=5 * 10**8,
        scratch=[pltpu.SemaphoreType.DMA((count,))],
    )[0]


def scatter_home(scalars, kept, back, half):
    slot_rows, width = kept.shape[1:]

    def kernel(scalars_ref, kept_ref, back_ref, out, sems):
        copies = []
        for i in range(half):
            copies.append(
                pltpu.make_async_copy(
                    kept_ref.at[i], out.at[kept_slot(scalars_ref, i, half)], sems.at[0, i]
                )
            )
            copies.append(
                pltpu.make_async_copy(
                    back_ref.at[i], out.at[sent_slot(scalars_ref, i, half)], sems.at[1, i]
                )
            )
        for copy in copies:
            copy.start()
        for copy in copies:
            copy.wait()

    shape = (2 * half, slot_rows, width)
    return call(
        kernel,
        scalars,
        [kept, back],
        [ANY, ANY],
        [pl.BlockSpec(shape, lambda i, s: (0, 0, 0))],
        [jax.ShapeDtypeStruct(shape, kept.dtype)],
        (1,),
        "scatter_home",
        work=5 * 10**8,
        scratch=[pltpu.SemaphoreType.DMA((2, half))],
    )[0]


def split_heads(value):
    low = lax.broadcasted_iota(jnp.int32, value.shape, 1) < value.shape[1] // 2
    zero = jnp.zeros_like(value)
    return jnp.concatenate([jnp.where(low, value, zero), jnp.where(low, zero, value)], 0)


def side_by_side(value):
    rows = value.shape[0] // 2
    return jnp.concatenate([value[:rows], value[rows:]], 1)


def row_sum(value):
    return jnp.sum(value, axis=0, keepdims=True)


def normal_form(value):
    centered = value - jnp.mean(value, axis=-1, keepdims=True)
    root = lax.rsqrt(jnp.mean(centered * centered, axis=-1, keepdims=True) + EPSILON)
    return centered * root, root


def normal_back(lifted, normed, root):
    return root * (
        lifted
        - jnp.mean(lifted, axis=-1, keepdims=True)
        - normed * jnp.mean(lifted * normed, axis=-1, keepdims=True)
    )


def whole(array):
    return pl.BlockSpec(
        array.shape, lambda *_: (0,) * array.ndim, pipeline_mode=pl.Buffered(1)
    )


def attention_forward(
    scalars, rows, received, live, weights, first, half, into=()
):
    w_qkv, b_qv, w_out, norm_gains, bias_rows = weights
    slot_rows, width = rows.shape[1:]
    pairs = received.shape[0]
    length = 2 * slot_rows
    duo = 2 * width // HEADS
    blocks = width // duo
    score_scale = (width // HEADS) ** (-0.5)

    def kernel(
        scalars_ref,
        kept_a,
        kept_b,
        got,
        live_ref,
        w_qkv_ref,
        b_qv_ref,
        w_out_ref,
        gains_ref,
        biases_ref,
        joined_out,
        mixed_out,
        probs_out,
        context_out,
        normed_out,
        root_out,
    ):
        joined = jnp.concatenate([kept_a[0], got[0], kept_b[0], got[1]], 0)
        joined_out[...] = joined
        mixed = dot(joined, w_qkv_ref[...])
        queries = (mixed[:, :width] + b_qv_ref[0:1, :]).astype(BF16)
        queries = (queries.astype(F32) * score_scale).astype(BF16)
        keys = mixed[:, width : 2 * width].astype(BF16)
        values = (mixed[:, 2 * width :] + b_qv_ref[1:2, :]).astype(BF16)
        mixed_out[:, :width] = queries
        mixed_out[:, width : 2 * width] = keys
        mixed_out[:, 2 * width :] = values
        contexts = []
        for pair in range(2):
            seen = live_ref[pair] > 0
            span = slice(pair * length, (pair + 1) * length)
            heads = []
            for block in range(blocks):
                cols = slice(block * duo, (block + 1) * duo)
                scores = dot(split_heads(queries[span, cols]), keys[span, cols], 1, 1)
                scores = jnp.where(seen, scores, -1e30)
                powered = jnp.exp(scores - jnp.max(scores, axis=-1, keepdims=True))
                low_probs = powered * (1.0 / jnp.sum(powered, axis=-1, keepdims=True))
                low_probs = low_probs.astype(BF16)
                probs_out[pair, block] = low_probs
                heads.append(
                    dot(side_by_side(low_probs), split_heads(values[span, cols])).astype(BF16)
                )
            contexts.append(jnp.concatenate(heads, 1))
        context = jnp.concatenate(contexts, 0)
        context_out[...] = context
        pre_one = joined.astype(F32) + dot(context, w_out_ref[...]) + biases_ref[0:1, :]
        normed, root = normal_form(pre_one)
        normed_out[...] = normed.astype(BF16)
        root_out[...] = jnp.broadcast_to(root, root_out.shape)

    start = first // 2

    def by_rows(columns):
        return pl.BlockSpec((2 * length, columns), lambda i, s: (start + i, 0))

    slot = (1, slot_rows, width)
    total = half * length
    return call(
        kernel,
        scalars,
        [rows, rows, received, live, w_qkv, b_qv, w_out, norm_gains, bias_rows],
        [
            pl.BlockSpec(slot, lambda i, s: (kept_slot(s, first + 2 * i, half), 0, 0)),
            pl.BlockSpec(slot, lambda i, s: (kept_slot(s, first + 2 * i + 1, half), 0, 0)),
            pl.BlockSpec((2, slot_rows, width), lambda i, s: (i, 0, 0)),
            pl.BlockSpec((2, 1, length), lambda i, s: (start + i, 0, 0)),
            whole(w_qkv),
            whole(b_qv),
            whole(w_out),
            whole(norm_gains),
            whole(bias_rows),
        ],
        [
            by_rows(width),
            by_rows(3 * width),
            pl.BlockSpec((2, blocks, 2 * length, length), lambda i, s: (start + i, 0, 0, 0)),
            by_rows(width),
            by_rows(width),
            by_rows(128),
        ],
        [
            jax.ShapeDtypeStruct((total, width), BF16),
            jax.ShapeDtypeStruct((total, 3 * width), BF16),
            jax.ShapeDtypeStruct((half, blocks, 2 * length, length), BF16),
            jax.ShapeDtypeStruct((total, width), BF16),
            jax.ShapeDtypeStruct((total, width), BF16),
            jax.ShapeDtypeStruct((total, 128), F32),
        ],
        (pairs // 2,),
        "attention_forward",
        into=into,
    )


def place_of(index, order):
    return sum(1 << bit for n, bit in enumerate(order) if index >> (len(order) - 1 - n) & 1)


def spread(grad, outs, scalars_ref, base, shard, order):
    core, place = scalars_ref[base + 1], scalars_ref[base + 2]
    for j in range(2 ** len(order)):
        row = (place ^ place_of(j, order)) * 2
        for out, which in zip(outs, (1 - core, core)):
            out[j] = grad[pl.ds(pl.multiple_of((row + which) * shard, 16), shard), :]


def feed_forward(scalars, normed, cot, far_cot, weights, half, shards, base):
    w_in, b_in, w_back, norm_gains, bias_rows = weights
    slot_rows, width = cot.shape[1:]
    inner_width = w_in.shape[1]
    length = 2 * slot_rows
    rows = 2 * length
    height = half * length
    steps = half // 2
    chunk = 768
    chunks = inner_width // chunk
    shard = inner_width // shards
    places = shards // 2
    part = 4 * shard
    parts = inner_width // part

    def kernel(
        scalars_ref,
        normed_ref,
        cot_a,
        cot_b,
        cot_far,
        w_in_hbm,
        b_in_ref,
        w_back_hbm,
        gains_ref,
        biases_ref,
        slope_out,
        branch_out,
        kept_out,
        far_out,
        sums_out,
        send,
        keep,
        w_in_ref,
        w_back_ref,
        held,
        acts,
        branches,
        grad,
        sems,
    ):
        step = pl.program_id(0)

        def fetch_in(j):
            cols = pl.ds(j * chunk, chunk)
            return pltpu.make_async_copy(
                w_in_hbm.at[:, cols], w_in_ref.at[:, cols], sems.at[0, j]
            )

        def fetch_back(j):
            cols = pl.ds(j * chunk, chunk)
            return pltpu.make_async_copy(w_back_hbm.at[cols], w_back_ref.at[cols], sems.at[1, j])

        @pl.when(step == 0)
        def _():
            sums_out[...] = jnp.zeros_like(sums_out)
            for j in range(chunks):
                fetch_in(j).start()
                fetch_back(j).start()

        def close(pre_two, row):
            scaled, root = normal_form(pre_two)
            output = (scaled * gains_ref[1:2, :] + biases_ref[3:4, :]).astype(BF16)
            for i in range(2):
                kept_out[i] = output[i * length : i * length + slot_rows]
                far_out[i] = output[i * length + slot_rows : (i + 1) * length]
            here = jnp.concatenate([cot_a[0], cot_far[0], cot_b[0], cot_far[1]], 0).astype(F32)
            d_two = normal_back(here * gains_ref[1:2, :], scaled, root)
            low = d_two.astype(BF16)
            branch_out[...] = low
            branches[pl.ds(row, rows)] = low
            return jnp.concatenate([row_sum(here * scaled), row_sum(here), row_sum(d_two)], 0)

        def forward(first):
            hidden = normed_ref[...].astype(F32) * gains_ref[0:1, :] + biases_ref[1:2, :]
            low_hidden = hidden.astype(BF16)
            total = hidden + biases_ref[2:3, :]
            for j in range(chunks):
                cols = slice(j * chunk, (j + 1) * chunk)
                if first:
                    fetch_in(j).wait()
                inner = dot(low_hidden, w_in_ref[:, cols]) + b_in_ref[:, cols]
                normal = 0.5 + 0.5 * lax.erf(inner * (0.5**0.5))
                low_act = (inner * normal).astype(BF16)
                density = jnp.exp(inner * inner * -0.5) * 0.3989422804014327
                acts[pl.ds(step * rows, rows), cols] = low_act
                slope_out[:, cols] = (normal + inner * density).astype(BF16)
                if first:
                    fetch_back(j).wait()
                total = total + dot(low_act, w_back_ref[cols, :])
            return total

        @pl.when(step == 0)
        def _():
            held[...] = forward(True)

        @pl.when((step > 0) & (step < steps))
        def _():
            before = held[...]
            held[...] = forward(False)
            sums_out[0:3, :] += close(before, (step - 1) * rows)

        @pl.when(step == steps)
        def _():
            sums_out[0:3, :] += close(held[...], (step - 1) * rows)

        @pl.when(step >= steps)
        def _():
            start = pl.multiple_of((step - steps) * part, 128)
            grad[...] = dot(acts[:, pl.ds(start, part)], branches[...], 0, 0).astype(BF16)
            core, low = scalars_ref[base + 1], scalars_ref[base + 2] & 1
            for j in range(2):
                for out, which in ((send, 1 - core), (keep, core)):
                    row = ((low ^ j) * 2 + which) * shard
                    out[j, 0] = grad[pl.ds(pl.multiple_of(row, 16), shard), :]

    def ahead(i):
        return jnp.minimum(i, steps - 1)

    def behind(i):
        return jnp.clip(i - 1, 0, steps - 1)

    def slot(j):
        return pl.BlockSpec(
            (1, slot_rows, width), lambda i, s: (kept_slot(s, 2 * behind(i) + j, half), 0, 0)
        )

    duo = pl.BlockSpec((2, slot_rows, width), lambda i, s: (behind(i), 0, 0))

    def entry(i, s):
        apart = (s[base + 2] >> 1) ^ jnp.maximum(i - steps, 0)
        return 0, (apart & 1) * 2 + (apart >> 1), 0, 0

    grads = pl.BlockSpec((2, 1, shard, width), entry)
    return call(
        kernel,
        scalars,
        [normed, cot, cot, far_cot, w_in, b_in, w_back, norm_gains, bias_rows],
        [
            pl.BlockSpec((rows, width), lambda i, s: (ahead(i), 0)),
            slot(0),
            slot(1),
            duo,
            ANY,
            whole(b_in),
            ANY,
            whole(norm_gains),
            whole(bias_rows),
        ],
        [
            pl.BlockSpec((rows, inner_width), lambda i, s: (ahead(i), 0)),
            pl.BlockSpec((rows, width), lambda i, s: (behind(i), 0)),
            duo,
            duo,
            pl.BlockSpec((8, width), lambda i, s: (0, 0)),
            grads,
            grads,
        ],
        [
            jax.ShapeDtypeStruct((height, inner_width), BF16),
            jax.ShapeDtypeStruct((height, width), BF16),
            jax.ShapeDtypeStruct((half, slot_rows, width), BF16),
            jax.ShapeDtypeStruct((half, slot_rows, width), BF16),
            jax.ShapeDtypeStruct((8, width), F32),
            jax.ShapeDtypeStruct((2, places // 2, shard, width), BF16),
            jax.ShapeDtypeStruct((2, places // 2, shard, width), BF16),
        ],
        (steps + parts,),
        "feed_forward",
        scratch=[
            pltpu.VMEM((width, inner_width), BF16),
            pltpu.VMEM((inner_width, width), BF16),
            pltpu.VMEM((rows, width), F32),
            pltpu.VMEM((height, inner_width), BF16),
            pltpu.VMEM((height, width), BF16),
            pltpu.VMEM((part, width), BF16),
            pltpu.SemaphoreType.DMA((2, chunks)),
        ],
    )


def feed_backward(scalars, branch, slope, normed, root, context, weights, shards, base):
    w_in, w_back, norm_gains, bias_rows = weights
    total, width = branch.shape
    inner_width = slope.shape[1]
    chunk = 768
    steps = inner_width // chunk
    turn = steps // 2
    shard = width // shards
    places = shards // 2
    piece = 128

    def kernel(
        scalars_ref,
        branch_ref,
        slope_ref,
        normed_ref,
        root_ref,
        context_ref,
        w_in_ref,
        w_back_ref,
        gains_ref,
        biases_ref,
        low_attn_out,
        sums_out,
        inner_sum_out,
        send_a,
        keep_a,
        send_b,
        keep_b,
        held,
        low_hidden,
        grad,
    ):
        step = pl.program_id(0)

        @pl.when(step == 0)
        def _():
            hidden = normed_ref[...].astype(F32) * gains_ref[0:1, :] + biases_ref[1:2, :]
            low_hidden[...] = hidden.astype(BF16)
            held[...] = branch_ref[...].astype(F32)

        sums = jnp.zeros((1, chunk), F32)
        lows = []
        for r in range(0, total, 256):
            span = slice(r, r + 256)
            d_inner = dot(branch_ref[span], w_back_ref[...], 1, 1) * slope_ref[span].astype(F32)
            sums = sums + row_sum(d_inner)
            low = d_inner.astype(BF16)
            lows.append(low)
            held[span] += dot(low, w_in_ref[...], 1, 1)
        inner_sum_out[...] = jnp.broadcast_to(sums, inner_sum_out.shape)
        grad[...] = dot(low_hidden[...], jnp.concatenate(lows, 0), 0, 0).astype(BF16)

        @pl.when(step < turn)
        def _():
            spread(grad, (send_a, keep_a), scalars_ref, base, shard, (0, 1, 2))

        for j in range(turn):

            @pl.when(step == turn + j)
            def _():
                cols = pl.ds(j * chunk, chunk)
                outs = (send_b.at[:, :, cols], keep_b.at[:, :, cols])
                spread(grad, outs, scalars_ref, base, shard, (0, 1, 2))

        @pl.when(step == steps - 1)
        def _():
            sums = [jnp.zeros((1, width), F32)] * 3
            lows = []
            for i in range(total // piece):
                span = slice(i * piece, (i + 1) * piece)
                d_hidden, scaled = held[span], normed_ref[span].astype(F32)
                d_one = normal_back(d_hidden * gains_ref[0:1, :], scaled, root_ref[span, 0:1])
                lows.append(d_one.astype(BF16))
                low_attn_out[span] = lows[-1]
                for j, term in enumerate((d_hidden * scaled, d_hidden, d_one)):
                    sums[j] = sums[j] + row_sum(term)
            sums_out[...] = jnp.concatenate(sums + [jnp.zeros((5, width), F32)], 0)
            grad[:, :width] = dot(context_ref[...], jnp.concatenate(lows, 0), 0, 0).astype(BF16)
            cols = pl.ds(turn * chunk, width)
            outs = (send_b.at[:, :, cols], keep_b.at[:, :, cols])
            spread(grad, outs, scalars_ref, base, shard, (0, 1, 2))

    half_a = pl.BlockSpec((places, shard, chunk), lambda i, s: (0, 0, jnp.minimum(i, turn - 1)))
    wide = (steps - turn) * chunk + width
    half_b = pl.BlockSpec((places, shard, wide), lambda i, s: (0, 0, 0))
    shape_a = jax.ShapeDtypeStruct((places, shard, turn * chunk), BF16)
    shape_b = jax.ShapeDtypeStruct((places, shard, wide), BF16)
    return call(
        kernel,
        scalars,
        [branch, slope, normed, root, context, w_in, w_back, norm_gains, bias_rows],
        [
            whole(branch),
            pl.BlockSpec((total, chunk), lambda i, s: (0, i)),
            whole(normed),
            whole(root),
            whole(context),
            pl.BlockSpec((width, chunk), lambda i, s: (0, i)),
            pl.BlockSpec((chunk, width), lambda i, s: (i, 0)),
            whole(norm_gains),
            whole(bias_rows),
        ],
        [
            pl.BlockSpec((total, width), lambda i, s: (0, 0)),
            pl.BlockSpec((8, width), lambda i, s: (0, 0)),
            pl.BlockSpec((8, chunk), lambda i, s: (0, i)),
            half_a,
            half_a,
            half_b,
            half_b,
        ],
        [
            jax.ShapeDtypeStruct((total, width), BF16),
            jax.ShapeDtypeStruct((8, width), F32),
            jax.ShapeDtypeStruct((8, inner_width), F32),
            shape_a,
            shape_a,
            shape_b,
            shape_b,
        ],
        (steps,),
        "feed_backward",
        scratch=[
            pltpu.VMEM((total, width), F32),
            pltpu.VMEM((total, width), BF16),
            pltpu.VMEM((width, chunk), BF16),
        ],
    )


def attention_backward(scalars, kept, weights, part, shards, base, order, earlier=(), sums=()):
    low_attn, mixed, probs, joined = kept
    w_out, w_qkv = weights
    total, width = low_attn.shape
    pairs, blocks, _, length = probs.shape
    duo = width // blocks
    mine = blocks // 2
    span_cols = mine * duo
    slot_rows = length // 2
    score_scale = (width // HEADS) ** (-0.5)
    steps = pairs // 2
    shard = width // shards
    places = shards // 2
    last = part == 1
    columns = 3 * span_cols + (128 if last else 0)

    def kernel(
        scalars_ref,
        low_attn_ref,
        queries_ref,
        keys_ref,
        values_ref,
        probs_ref,
        joined_ref,
        w_out_ref,
        *refs,
    ):
        if last:
            w_qkv_ref, earlier_ref, one, two, inner, sums_ref = refs[:6]
            kept_out, far_out, sums_out, send, keep, held, grad = refs[6:]
        else:
            d_mixed_out, sums_out, send, keep, held, grad = refs
        step = pl.program_id(0)

        @pl.when(step == 0)
        def _():
            sums_out[...] = jnp.zeros_like(sums_out)

        d_context = dot(low_attn_ref[...], w_out_ref[...], 1, 1).astype(BF16)
        rows = []
        for pair in range(2):
            span = slice(pair * length, (pair + 1) * length)
            d_heads, d_probs, d_scores = [], [], []
            for block in range(mine):
                cols = slice(block * duo, (block + 1) * duo)
                d_heads.append(split_heads(d_context[span, cols]))
                d_probs.append(dot(d_heads[block], values_ref[span, cols], 1, 1))
            for block in range(mine):
                wide = probs_ref[pair, block].astype(F32)
                mean = jnp.sum(wide * d_probs[block], axis=-1, keepdims=True)
                d_scores.append((wide * (d_probs[block] - mean)).astype(BF16))
            d_queries, d_keys, d_values = [], [], []
            for block in range(mine):
                cols = slice(block * duo, (block + 1) * duo)
                queries = split_heads(queries_ref[span, cols])
                keys = split_heads(keys_ref[span, cols])
                scaled = dot(side_by_side(d_scores[block]), keys) * score_scale
                d_queries.append(scaled.astype(BF16))
                d_keys.append(dot(d_scores[block], queries, 0, 0).astype(BF16))
                d_values.append(dot(probs_ref[pair, block], d_heads[block], 0, 0).astype(BF16))
            rows.append(jnp.concatenate(d_queries + d_keys + d_values, 1))
        d_mixed = jnp.concatenate(rows, 0)
        held[pl.ds(pl.multiple_of(step * 2 * length, 2 * length), 2 * length)] = d_mixed
        sums_out[0:1, :] += row_sum(d_mixed[:, :span_cols].astype(F32))
        sums_out[1:2, :] += row_sum(d_mixed[:, 2 * span_cols :].astype(F32))
        if last:
            d_rows = low_attn_ref[...].astype(F32)
            for third in range(3):
                cols = slice(third * span_cols, (third + 1) * span_cols)
                full = jnp.concatenate([earlier_ref[:, cols], d_mixed[:, cols]], 1)
                d_rows = d_rows + dot(full, w_qkv_ref[:, third * width : (third + 1) * width], 1, 1)
            d_rows = d_rows.astype(BF16)
            for i in range(2):
                kept_out[i] = d_rows[i * length : i * length + slot_rows]
                far_out[i] = d_rows[i * length + slot_rows : (i + 1) * length]
        else:
            d_mixed_out[...] = d_mixed

        @pl.when(step == steps - 1)
        def _():
            grad[:, : 3 * span_cols] = dot(joined_ref[...], held[...], 0, 0).astype(BF16)
            if last:
                first, second = sums_ref[0:2, :], sums_out[0:2, :]
                small = [jnp.concatenate([first, second], 1), one[0:1], two[0:1]]
                small += [one[2:3], one[1:2], two[2:3], two[1:2], inner[...]]
                small.append(jnp.zeros((120 - inner.shape[0], width), F32))
                grad[:, 3 * span_cols :] = jnp.concatenate(small, 0).T.astype(BF16)
            spread(grad, (send, keep), scalars_ref, base, shard, order)

    def by_rows(count, at=0):
        return pl.BlockSpec((2 * length, count), lambda i, s: (i, at))

    two_slots = pl.BlockSpec((2, slot_rows, width), lambda i, s: (i, 0, 0))
    operands = [low_attn, mixed, mixed, mixed, probs, joined, w_out]
    in_specs = [
        by_rows(width),
        by_rows(span_cols, part),
        by_rows(span_cols, 2 + part),
        by_rows(span_cols, 4 + part),
        pl.BlockSpec((2, mine, 2 * length, length), lambda i, s: (i, part, 0, 0)),
        whole(joined),
        pl.BlockSpec((span_cols, width), lambda i, s: (part, 0), pipeline_mode=pl.Buffered(1)),
    ]
    grads = pl.BlockSpec((places, shard, columns), lambda i, s: (0, 0, 0))
    out_specs = [pl.BlockSpec((8, span_cols), lambda i, s: (0, 0)), grads, grads]
    out_shape = [
        jax.ShapeDtypeStruct((8, span_cols), F32),
        jax.ShapeDtypeStruct((places, shard, columns), BF16),
        jax.ShapeDtypeStruct((places, shard, columns), BF16),
    ]
    if last:
        operands += [w_qkv, earlier, *sums]
        in_specs += [whole(w_qkv), by_rows(3 * span_cols)]
        in_specs += [whole(each) for each in sums]
        out_specs = [two_slots, two_slots] + out_specs
        out_shape = [jax.ShapeDtypeStruct((pairs, slot_rows, width), BF16)] * 2 + out_shape
    else:
        out_specs = [by_rows(3 * span_cols)] + out_specs
        out_shape = [jax.ShapeDtypeStruct((total, 3 * span_cols), BF16)] + out_shape
    return call(
        kernel,
        scalars,
        operands,
        in_specs,
        out_specs,
        out_shape,
        (steps,),
        "attention_backward",
        scratch=[
            pltpu.VMEM((total, 3 * span_cols), BF16),
            pltpu.VMEM((width, columns), BF16),
        ],
    )


def in_turn(value):
    return lax.optimization_barrier((value, LINE[-1]))[0]


class Shards:
    def __init__(self, send, keep, order):
        shard, width = send.shape[-2:]
        self.order = list(order)
        self.halved = "mod" in self.order
        bits = len(self.order) - self.halved
        self.side = lax.axis_index("mod")
        self.held = [(keep.reshape((2**bits, shard, width)), False)]
        self.coming = flipped(send, "dp", 1).reshape((2**bits, shard, width))

    def total(self, first, count, side):
        total = None
        for array, halved in self.held:
            columns = array.shape[-1] // 2
            array = lax.slice_in_dim(array, first, first + count, axis=0)
            if self.halved and not halved:
                array = lax.dynamic_slice_in_dim(array, side * columns, columns, 2)
            array = array.astype(F32)
            total = array if total is None else total + array
        return total.astype(BF16)

    def step(self):
        halved = self.halved and len(self.held) > 1
        self.held.append((in_turn(self.coming), halved))
        count = self.coming.shape[0]
        if not self.order:
            self.mine = lax.optimization_barrier(self.total(0, 1, self.side)[0])
            self.coming = flipped(self.mine, "mod", 1)
            LINE.append(self.mine)
            return
        bit = self.order.pop(0)
        if bit == "mod":
            away = self.total(0, count, 1 - self.side)
            self.coming = flipped(away, "mod", 1)
        else:
            away = self.total(count // 2, count // 2, self.side)
            self.coming = flipped(away, "dp", 2 << bit)
        LINE.append(away)

    def result(self):
        coming = in_turn(self.coming)
        if self.halved:
            first = lax.axis_index("mod") == 0
            total = jnp.concatenate(
                [jnp.where(first, self.mine, coming), jnp.where(first, coming, self.mine)], 1
            ).astype(F32)
        else:
            total = self.mine.astype(F32) + coming.astype(F32)
        return total


def reduce_plain(send, keep, order):
    shard, columns = send.shape[-2:]
    total = jnp.stack([keep.reshape(-1, shard, columns), send.reshape(-1, shard, columns)], 1)
    places = [place_of(j, order) for j in range(total.shape[0])]
    total = jnp.stack([total[places.index(j)] for j in range(total.shape[0])])
    total = total.reshape(-1, columns).astype(F32)
    share = lax.psum_scatter(total, "dp", scatter_dimension=0, tiled=True)
    return lax.psum(share.astype(BF16), "mod").astype(F32)


def body(
    layer_rows,
    cotangent,
    row_live,
    partner,
    w_qkv,
    b_qv,
    w_out,
    norm_gains,
    bias_rows,
    w_in,
    b_in,
    w_back,
):
    side = lax.axis_index("mod")
    place = lax.axis_index("dp")
    shards = lax.axis_size("dp")
    groups = partner.shape[1]
    aligned = shards == 16 and (layer_rows.shape[2] // shards) % 16 == 0
    layout = shards if aligned else 16
    half = groups // 2
    width = layer_rows.shape[2]
    slot_rows = layer_rows.shape[1] // groups
    inner_width = w_in.shape[1]
    slots = (groups, slot_rows, width)
    rows = layer_rows[0].reshape(slots)
    cot = cotangent[0].reshape(slots)
    spot = place if aligned else 0 * place
    scalars = jnp.concatenate(
        [partner[0], jnp.stack([side, spot & 1, spot >> 1]).astype(jnp.int32)]
    )
    cut = half // 2
    LINE.clear()
    sent_a = gather_sent(scalars, rows, half, 0, cut)
    got_a = flipped(sent_a, "mod", 1)
    sent_b = gather_sent(scalars, rows, half, cut, cut)
    got_b = flipped(sent_b, "mod", 1)
    sent_cot = gather_sent(scalars, cot, half, 0, half)
    far_cot = flipped(sent_cot, "mod", 1)

    live = row_live.reshape(2, groups, slot_rows)
    words_live = lax.dynamic_slice_in_dim(live[0], side * half, half, 0)
    region_live = live[1][lax.dynamic_slice_in_dim(partner[0], side * half, half, 0)]
    is_first = side == 0
    seen = jnp.concatenate(
        [
            jnp.where(is_first, words_live, region_live),
            jnp.where(is_first, region_live, words_live),
        ],
        1,
    )[:, None, :]

    heads_weights = (w_qkv, b_qv, w_out, norm_gains, bias_rows)
    first_part = attention_forward(scalars, rows, got_a, seen, heads_weights, 0, half)
    joined, mixed, probs, context, normed, root = attention_forward(
        scalars, rows, got_b, seen, heads_weights, cut, half, into=first_part
    )
    feed_weights = (w_in, b_in.reshape(1, inner_width), w_back, norm_gains, bias_rows)
    slope, branch, out_kept, out_far, sums_two, *back = feed_forward(
        scalars, normed, cot, far_cot, feed_weights, half, layout, groups
    )
    out_back = flipped(out_far, "mod", 1)
    back_weights = (w_in, w_back, norm_gains, bias_rows)
    attn_weights = (w_out, w_qkv)
    paths = ((0, 1, 2), ("mod", 0, 1, 2), (0, 1, 2), (1, 2, 0))
    if aligned:
        back = Shards(*back, paths[0])
        back.step()
    low_attn, sums_one, inner_sum, *inner = feed_backward(
        scalars, branch, slope, normed, root, context, back_weights, layout, groups
    )
    shard = width // shards
    count = inner_width // width
    inner_sum = inner_sum[0].reshape(shards, count, shard).transpose(1, 0, 2).reshape(count, width)
    if aligned:
        inner_a, inner_b = Shards(*inner[:2], paths[0]), Shards(*inner[2:], paths[1])
        back.step()
    out_rows = scatter_home(scalars, out_kept, out_back, half).reshape(1, -1, width)
    if aligned:
        inner_a.step()
        inner_b.step()
    attn_kept = (low_attn, mixed, probs, joined)
    d_mixed, sums_qv, *qkv_a = attention_backward(
        scalars, attn_kept, attn_weights, 0, layout, groups, paths[2]
    )
    if aligned:
        qkv_a = Shards(*qkv_a, paths[2])
        back.step()
        inner_a.step()
        inner_b.step()
        qkv_a.step()
    sums = (sums_one, sums_two, inner_sum, sums_qv)
    d_kept, d_far, _, *qkv_b = attention_backward(
        scalars, attn_kept, attn_weights, 1, layout, groups, paths[3], d_mixed, sums
    )
    d_back = flipped(d_far, "mod", 1)
    if aligned:
        qkv_b = Shards(*qkv_b, paths[3])
        back.step()
        inner_a.step()
        inner_b.step()
        qkv_a.step()
        qkv_b.step()
        grad_back = back.result()
        inner_a.step()
        inner_b.step()
        qkv_a.step()
        qkv_b.step()
        grad_rows = scatter_home(scalars, d_kept, d_back, half).reshape(1, -1, width)
        inner_b.step()
        qkv_a.step()
        qkv_b.step()
        inner_a, inner_b, qkv_a = inner_a.result(), inner_b.result(), qkv_a.result()
        qkv_b.step()
        qkv_b = qkv_b.result()
    else:
        grad_back = reduce_plain(*back, paths[0])
        inner_a = reduce_plain(*inner[:2], (0, 1, 2))
        inner_b = reduce_plain(*inner[2:], (0, 1, 2))
        qkv_a, qkv_b = reduce_plain(*qkv_a, paths[2]), reduce_plain(*qkv_b, paths[3])
        grad_rows = scatter_home(scalars, d_kept, d_back, half).reshape(1, -1, width)
    turn = inner_width - inner_a.shape[1]
    grad_in = jnp.concatenate([inner_a, inner_b[:, :turn]], 1)
    grad_out = inner_b[:, turn:]
    turn = qkv_a.shape[1] // 3
    thirds = []
    for third in range(3):
        cols = slice(third * turn, (third + 1) * turn)
        thirds += [qkv_a[:, cols], qkv_b[:, cols]]
    grad_qkv = jnp.concatenate(thirds, 1)
    small = qkv_b[:, 3 * turn : 3 * turn + 16].T
    return (
        out_rows,
        grad_rows,
        grad_qkv,
        small[0:2],
        grad_out,
        small[2:4],
        small[4:8],
        grad_in,
        small[8 : 8 + count].reshape(-1),
        grad_back,
    )


def solution(mesh):
    return jax.shard_map(
        body,
        mesh=mesh,
        in_specs=(
            P("mod", "dp", None),
            P("mod", "dp", None),
            P(None, "dp"),
            P("dp", None),
            P(),
            P(),
            P(),
            P(),
            P(),
            P(),
            P(),
            P(),
        ),
        out_specs=(
            P("mod", "dp", None),
            P("mod", "dp", None),
            P("dp", None),
            P(None, "dp"),
            P("dp", None),
            P(None, "dp"),
            P(None, "dp"),
            P("dp", None),
            P("dp"),
            P("dp", None),
        ),
        check_vma=False,
    )
```

```python
import functools

import jax
import jax.numpy as jnp
from jax import lax
from jax.experimental import pallas as pl
from jax.experimental.pallas import tpu as pltpu
from jax.sharding import PartitionSpec as P

HEADS = 12
EPSILON = 1e-12
F32 = jnp.float32
BF16 = jnp.bfloat16
VMEM_LIMIT = 255 * 2**18


def dot(left, right, left_dim=1, right_dim=0):
    return lax.dot_general(
        left, right, (((left_dim,), (right_dim,)), ((), ())), preferred_element_type=F32
    )


def flipped(value, axis, mask):
    pairs = [(source, source ^ mask) for source in range(lax.axis_size(axis))]
    return lax.ppermute(value, axis, pairs)


def params(limit=VMEM_LIMIT):
    return pltpu.CompilerParams(vmem_limit_bytes=limit)


def kept_slot(scalars, pair, half):
    groups = 2 * half
    side = scalars[groups]
    place = side * half + pair
    return jnp.where(side == 0, place, scalars[place])


def sent_slot(scalars, pair, half):
    groups = 2 * half
    side = scalars[groups]
    place = (1 - side) * half + pair
    return jnp.where(side == 0, place, scalars[place])


ANY = pl.BlockSpec(memory_space=pl.ANY)
LINE = []


def call(kernel, scalars, operands, in_specs, out_specs, out_shape, grid, name, **more):
    after = list(LINE)
    into = list(more.get("into", ()))
    into_first = more.get("into_first", 0)
    scratch = list(more.get("scratch", ()))
    taken, spare, given = len(operands), len(into) + len(after), len(out_shape)

    def wrapped(scalars_ref, *refs):
        outs = refs[taken + spare :]
        kernel(scalars_ref, *refs[:taken], *outs[:given], *outs[given + 1 :])

    outs = pl.pallas_call(
        wrapped,
        grid_spec=pltpu.PrefetchScalarGridSpec(
            num_scalar_prefetch=1,
            grid=grid,
            in_specs=list(in_specs) + [ANY] * spare,
            out_specs=list(out_specs) + [ANY],
            scratch_shapes=scratch,
        ),
        out_shape=list(out_shape) + [jax.ShapeDtypeStruct((8, 128), F32)],
        input_output_aliases={1 + taken + i: i + into_first for i in range(len(into))},
        compiler_params=params(more.get("limit", VMEM_LIMIT)),
        cost_estimate=pl.CostEstimate(
            flops=more.get("work", 4 * 10**9), bytes_accessed=2**20, transcendentals=0
        ),
        name=name,
    )(scalars, *operands, *into, *after)
    LINE[:] = [outs[-1]]
    return list(outs[:-1])


def gather_sent(partner, rows, half, first, count):
    slot_rows, width = rows.shape[1:]

    def kernel(partner_ref, rows_ref, out, sems):
        side = lax.axis_index("mod")
        copies = []
        for i in range(count):
            place = (1 - side) * half + first + i
            slot = jnp.where(side == 0, place, partner_ref[place])
            copies.append(pltpu.make_async_copy(rows_ref.at[slot], out.at[i], sems.at[i]))
        for copy in copies:
            copy.start()
        for copy in copies:
            copy.wait()

    shape = (count, slot_rows, width)
    return call(
        kernel,
        partner,
        [rows],
        [ANY],
        [pl.BlockSpec(shape, lambda i, s: (0, 0, 0))],
        [jax.ShapeDtypeStruct(shape, rows.dtype)],
        (1,),
        "gather_sent",
        work=5 * 10**8,
        scratch=[pltpu.SemaphoreType.DMA((count,))],
    )[0]


def scatter_home(scalars, kept, back, half):
    slot_rows, width = kept.shape[1:]

    def kernel(scalars_ref, kept_ref, back_ref, out, sems):
        copies = []
        for i in range(half):
            copies.append(
                pltpu.make_async_copy(
                    kept_ref.at[i], out.at[kept_slot(scalars_ref, i, half)], sems.at[0, i]
                )
            )
            copies.append(
                pltpu.make_async_copy(
                    back_ref.at[i], out.at[sent_slot(scalars_ref, i, half)], sems.at[1, i]
                )
            )
        for copy in copies:
            copy.start()
        for copy in copies:
            copy.wait()

    shape = (2 * half, slot_rows, width)
    return call(
        kernel,
        scalars,
        [kept, back],
        [ANY, ANY],
        [pl.BlockSpec(shape, lambda i, s: (0, 0, 0))],
        [jax.ShapeDtypeStruct(shape, kept.dtype)],
        (1,),
        "scatter_home",
        work=2 * 10**10,
        scratch=[pltpu.SemaphoreType.DMA((2, half))],
    )[0]


def parts_of(blocks):
    early = 2 * blocks // 3
    return (0, early), (early, blocks - early)


def split_heads(value):
    low = lax.broadcasted_iota(jnp.int32, value.shape, 1) < value.shape[1] // 2
    zero = jnp.zeros_like(value)
    return jnp.concatenate([jnp.where(low, value, zero), jnp.where(low, zero, value)], 0)


def side_by_side(value):
    rows = value.shape[0] // 2
    return jnp.concatenate([value[:rows], value[rows:]], 1)


def row_sum(value):
    return jnp.sum(value, axis=0, keepdims=True)


def normal_form(value):
    centered = value - jnp.mean(value, axis=-1, keepdims=True)
    root = lax.rsqrt(jnp.mean(centered * centered, axis=-1, keepdims=True) + EPSILON)
    return centered * root, root


def normal_back(lifted, normed, root):
    return root * (
        lifted
        - jnp.mean(lifted, axis=-1, keepdims=True)
        - normed * jnp.mean(lifted * normed, axis=-1, keepdims=True)
    )


def whole(array):
    return pl.BlockSpec(
        array.shape, lambda *_: (0,) * array.ndim, pipeline_mode=pl.Buffered(1)
    )


def attention_forward(scalars, rows, received, live, weights):
    w_qkv, b_qv, w_out, norm_gains, bias_rows = weights
    slot_rows, width = rows.shape[1:]
    pairs = half = rows.shape[0] // 2
    turn = received[0].shape[0] // 2
    length = 2 * slot_rows
    duo = 2 * width // HEADS
    blocks = width // duo
    score_scale = (width // HEADS) ** (-0.5)

    def kernel(
        scalars_ref,
        kept_a,
        kept_b,
        got_a,
        got_b,
        live_ref,
        w_qkv_ref,
        b_qv_ref,
        w_out_ref,
        gains_ref,
        biases_ref,
        joined_out,
        mixed_out,
        probs_out,
        context_out,
        normed_out,
        root_out,
    ):
        got = jnp.where(pl.program_id(0) < turn, got_a[...], got_b[...])
        joined = jnp.concatenate([kept_a[0], got[0], kept_b[0], got[1]], 0)
        joined_out[...] = joined
        mixed = dot(joined, w_qkv_ref[...])
        queries = (mixed[:, :width] + b_qv_ref[0:1, :]).astype(BF16)
        queries = (queries.astype(F32) * score_scale).astype(BF16)
        keys = mixed[:, width : 2 * width].astype(BF16)
        values = (mixed[:, 2 * width :] + b_qv_ref[1:2, :]).astype(BF16)
        for first_block, count in parts_of(blocks):
            cols = slice(first_block * duo, (first_block + count) * duo)
            at = 3 * first_block * duo
            for value in (queries, keys, values):
                mixed_out[:, at : at + count * duo] = value[:, cols]
                at += count * duo
        contexts = []
        for pair in range(2):
            seen = live_ref[pair] > 0
            span = slice(pair * length, (pair + 1) * length)
            heads = []
            for block in range(blocks):
                cols = slice(block * duo, (block + 1) * duo)
                scores = dot(split_heads(queries[span, cols]), keys[span, cols], 1, 1)
                scores = jnp.where(seen, scores, -1e30)
                powered = jnp.exp(scores - jnp.max(scores, axis=-1, keepdims=True))
                low_probs = powered * (1.0 / jnp.sum(powered, axis=-1, keepdims=True))
                low_probs = low_probs.astype(BF16)
                probs_out[pair, block] = low_probs
                heads.append(
                    dot(side_by_side(low_probs), split_heads(values[span, cols])).astype(BF16)
                )
            contexts.append(jnp.concatenate(heads, 1))
        context = jnp.concatenate(contexts, 0)
        context_out[...] = context
        pre_one = joined.astype(F32) + dot(context, w_out_ref[...]) + biases_ref[0:1, :]
        normed, root = normal_form(pre_one)
        normed_out[...] = normed.astype(BF16)
        root_out[...] = jnp.broadcast_to(root, root_out.shape)

    def by_rows(columns):
        return pl.BlockSpec((2 * length, columns), lambda i, s: (i, 0))

    slot = (1, slot_rows, width)
    two = (2, slot_rows, width)
    total = half * length
    return call(
        kernel,
        scalars,
        [rows, rows, *received, live, w_qkv, b_qv, w_out, norm_gains, bias_rows],
        [
            pl.BlockSpec(slot, lambda i, s: (kept_slot(s, 2 * i, half), 0, 0)),
            pl.BlockSpec(slot, lambda i, s: (kept_slot(s, 2 * i + 1, half), 0, 0)),
            pl.BlockSpec(two, lambda i, s: (jnp.minimum(i, turn - 1), 0, 0)),
            pl.BlockSpec(two, lambda i, s: (jnp.maximum(i - turn, 0), 0, 0)),
            pl.BlockSpec((2, 1, length), lambda i, s: (i, 0, 0)),
            whole(w_qkv),
            whole(b_qv),
            whole(w_out),
            whole(norm_gains),
            whole(bias_rows),
        ],
        [
            by_rows(width),
            by_rows(3 * width),
            pl.BlockSpec((2, blocks, 2 * length, length), lambda i, s: (i, 0, 0, 0)),
            by_rows(width),
            by_rows(width),
            by_rows(128),
        ],
        [
            jax.ShapeDtypeStruct((total, width), BF16),
            jax.ShapeDtypeStruct((total, 3 * width), BF16),
            jax.ShapeDtypeStruct((half, blocks, 2 * length, length), BF16),
            jax.ShapeDtypeStruct((total, width), BF16),
            jax.ShapeDtypeStruct((total, width), BF16),
            jax.ShapeDtypeStruct((total, 128), F32),
        ],
        (pairs // 2,),
        "attention_forward",
        work=4 * 10**10,
    )


def place_of(index, order):
    return sum(1 << bit for n, bit in enumerate(order) if index >> (len(order) - 1 - n) & 1)


def spread(grad, outs, scalars_ref, base, shard, order):
    core, place = scalars_ref[base + 1], scalars_ref[base + 2]
    for j in range(2 ** len(order)):
        row = (place ^ place_of(j, order)) * 2
        for out, which in zip(outs, (1 - core, core)):
            out[j] = grad[pl.ds(pl.multiple_of((row + which) * shard, 16), shard), :]


def feed_forward(scalars, normed, cot, far_cot, weights, half, shards, base):
    w_in, b_in, w_back, norm_gains, bias_rows = weights
    slot_rows, width = cot.shape[1:]
    inner_width = w_in.shape[1]
    length = 2 * slot_rows
    rows = 2 * length
    height = half * length
    steps = half // 2
    chunk = 768
    chunks = inner_width // chunk
    shard = inner_width // shards
    places = shards // 2
    part = 4 * shard
    parts = inner_width // part

    def kernel(
        scalars_ref,
        normed_ref,
        cot_a,
        cot_b,
        cot_far,
        w_in_hbm,
        b_in_ref,
        w_back_hbm,
        gains_ref,
        biases_ref,
        slope_out,
        branch_out,
        kept_out,
        far_out,
        sums_out,
        send,
        keep,
        w_in_ref,
        w_back_ref,
        held,
        acts,
        branches,
        grad,
        sems,
    ):
        step = pl.program_id(0)

        def fetch_in(j):
            cols = pl.ds(j * chunk, chunk)
            return pltpu.make_async_copy(
                w_in_hbm.at[:, cols], w_in_ref.at[:, cols], sems.at[0, j]
            )

        def fetch_back(j):
            cols = pl.ds(j * chunk, chunk)
            return pltpu.make_async_copy(w_back_hbm.at[cols], w_back_ref.at[cols], sems.at[1, j])

        @pl.when(step == 0)
        def _():
            sums_out[...] = jnp.zeros_like(sums_out)
            for j in range(chunks):
                fetch_in(j).start()
                fetch_back(j).start()

        def close(pre_two, row):
            scaled, root = normal_form(pre_two)
            output = (scaled * gains_ref[1:2, :] + biases_ref[3:4, :]).astype(BF16)
            for i in range(2):
                kept_out[i] = output[i * length : i * length + slot_rows]
                far_out[i] = output[i * length + slot_rows : (i + 1) * length]
            here = jnp.concatenate([cot_a[0], cot_far[0], cot_b[0], cot_far[1]], 0).astype(F32)
            d_two = normal_back(here * gains_ref[1:2, :], scaled, root)
            low = d_two.astype(BF16)
            branch_out[...] = low
            branches[pl.ds(row, rows)] = low
            return jnp.concatenate([row_sum(here * scaled), row_sum(here), row_sum(d_two)], 0)

        def forward(first):
            hidden = normed_ref[...].astype(F32) * gains_ref[0:1, :] + biases_ref[1:2, :]
            low_hidden = hidden.astype(BF16)
            total = hidden + biases_ref[2:3, :]
            for j in range(chunks):
                cols = slice(j * chunk, (j + 1) * chunk)
                if first:
                    fetch_in(j).wait()
                inner = dot(low_hidden, w_in_ref[:, cols]) + b_in_ref[:, cols]
                normal = 0.5 + 0.5 * lax.erf(inner * (0.5**0.5))
                low_act = (inner * normal).astype(BF16)
                density = jnp.exp(inner * inner * -0.5) * 0.3989422804014327
                acts[pl.ds(step * rows, rows), cols] = low_act
                slope_out[:, cols] = (normal + inner * density).astype(BF16)
                if first:
                    fetch_back(j).wait()
                total = total + dot(low_act, w_back_ref[cols, :])
            return total

        @pl.when(step == 0)
        def _():
            held[...] = forward(True)

        @pl.when((step > 0) & (step < steps))
        def _():
            before = held[...]
            held[...] = forward(False)
            sums_out[0:3, :] += close(before, (step - 1) * rows)

        @pl.when(step == steps)
        def _():
            sums_out[0:3, :] += close(held[...], (step - 1) * rows)

        @pl.when(step >= steps)
        def _():
            start = pl.multiple_of((step - steps) * part, 128)
            grad[...] = dot(acts[:, pl.ds(start, part)], branches[...], 0, 0).astype(BF16)
            core, low = scalars_ref[base + 1], scalars_ref[base + 2] & 1
            for j in range(2):
                for out, which in ((send, 1 - core), (keep, core)):
                    row = ((low ^ j) * 2 + which) * shard
                    out[j, 0] = grad[pl.ds(pl.multiple_of(row, 16), shard), :]

    def ahead(i):
        return jnp.minimum(i, steps - 1)

    def behind(i):
        return jnp.clip(i - 1, 0, steps - 1)

    def slot(j):
        return pl.BlockSpec(
            (1, slot_rows, width), lambda i, s: (kept_slot(s, 2 * behind(i) + j, half), 0, 0)
        )

    duo = pl.BlockSpec((2, slot_rows, width), lambda i, s: (behind(i), 0, 0))

    def entry(i, s):
        apart = (s[base + 2] >> 1) ^ jnp.maximum(i - steps, 0)
        return 0, (apart & 1) * 2 + (apart >> 1), 0, 0

    grads = pl.BlockSpec((2, 1, shard, width), entry)
    return call(
        kernel,
        scalars,
        [normed, cot, cot, far_cot, w_in, b_in, w_back, norm_gains, bias_rows],
        [
            pl.BlockSpec((rows, width), lambda i, s: (ahead(i), 0)),
            slot(0),
            slot(1),
            duo,
            ANY,
            whole(b_in),
            ANY,
            whole(norm_gains),
            whole(bias_rows),
        ],
        [
            pl.BlockSpec((rows, inner_width), lambda i, s: (ahead(i), 0)),
            pl.BlockSpec((rows, width), lambda i, s: (behind(i), 0)),
            duo,
            duo,
            pl.BlockSpec((8, width), lambda i, s: (0, 0)),
            grads,
            grads,
        ],
        [
            jax.ShapeDtypeStruct((height, inner_width), BF16),
            jax.ShapeDtypeStruct((height, width), BF16),
            jax.ShapeDtypeStruct((half, slot_rows, width), BF16),
            jax.ShapeDtypeStruct((half, slot_rows, width), BF16),
            jax.ShapeDtypeStruct((8, width), F32),
            jax.ShapeDtypeStruct((2, places // 2, shard, width), BF16),
            jax.ShapeDtypeStruct((2, places // 2, shard, width), BF16),
        ],
        (steps + parts,),
        "feed_forward",
        scratch=[
            pltpu.VMEM((width, inner_width), BF16),
            pltpu.VMEM((inner_width, width), BF16),
            pltpu.VMEM((rows, width), F32),
            pltpu.VMEM((height, inner_width), BF16),
            pltpu.VMEM((height, width), BF16),
            pltpu.VMEM((part, width), BF16),
            pltpu.SemaphoreType.DMA((2, chunks)),
        ],
    )


def feed_backward(scalars, branch, slope, normed, root, context, weights, shards, base, orders):
    w_in, w_back, norm_gains, bias_rows = weights
    total, width = branch.shape
    inner_width = slope.shape[1]
    chunk = 768
    steps = inner_width // chunk
    turn = steps // 2
    shard = width // shards
    places = shards // 2
    piece = 128

    def kernel(
        scalars_ref,
        branch_ref,
        slope_ref,
        normed_ref,
        root_ref,
        context_ref,
        w_in_ref,
        w_back_ref,
        gains_ref,
        biases_ref,
        low_attn_out,
        sums_out,
        inner_sum_out,
        send_a,
        keep_a,
        send_b,
        keep_b,
        held,
        low_hidden,
        grad,
    ):
        step = pl.program_id(0)

        @pl.when(step == 0)
        def _():
            hidden = normed_ref[...].astype(F32) * gains_ref[0:1, :] + biases_ref[1:2, :]
            low_hidden[...] = hidden.astype(BF16)
            held[...] = branch_ref[...].astype(F32)

        @pl.when(step < steps)
        def _():
            sums = jnp.zeros((1, chunk), F32)
            lows = []
            for r in range(0, total, 256):
                span = slice(r, r + 256)
                d_inner = dot(branch_ref[span], w_back_ref[...], 1, 1)
                d_inner = d_inner * slope_ref[span].astype(F32)
                sums = sums + row_sum(d_inner)
                low = d_inner.astype(BF16)
                lows.append(low)
                held[span] += dot(low, w_in_ref[...], 1, 1)
            inner_sum_out[...] = jnp.broadcast_to(sums, inner_sum_out.shape)
            grad[...] = dot(low_hidden[...], jnp.concatenate(lows, 0), 0, 0).astype(BF16)

        @pl.when(step == steps)
        def _():
            sums = [jnp.zeros((1, width), F32)] * 3
            lows = []
            for i in range(total // piece):
                span = slice(i * piece, (i + 1) * piece)
                d_hidden, scaled = held[span], normed_ref[span].astype(F32)
                d_one = normal_back(d_hidden * gains_ref[0:1, :], scaled, root_ref[span, 0:1])
                lows.append(d_one.astype(BF16))
                low_attn_out[span] = lows[-1]
                for j, term in enumerate((d_hidden * scaled, d_hidden, d_one)):
                    sums[j] = sums[j] + row_sum(term)
            sums_out[...] = jnp.concatenate(sums + [jnp.zeros((5, width), F32)], 0)
            grad[...] = dot(context_ref[...], jnp.concatenate(lows, 0), 0, 0).astype(BF16)

        @pl.when(step < turn)
        def _():
            spread(grad, (send_a, keep_a), scalars_ref, base, shard, orders[0])

        @pl.when(step >= turn)
        def _():
            spread(grad, (send_b, keep_b), scalars_ref, base, shard, orders[1])

    def now(i):
        return jnp.minimum(i, steps - 1)

    half_a = pl.BlockSpec((places, shard, chunk), lambda i, s: (0, 0, jnp.minimum(i, turn - 1)))
    half_b = pl.BlockSpec((places, shard, chunk), lambda i, s: (0, 0, jnp.maximum(i - turn, 0)))
    shape_a = jax.ShapeDtypeStruct((places, shard, turn * chunk), BF16)
    shape_b = jax.ShapeDtypeStruct((places, shard, (steps + 1 - turn) * chunk), BF16)
    return call(
        kernel,
        scalars,
        [branch, slope, normed, root, context, w_in, w_back, norm_gains, bias_rows],
        [
            whole(branch),
            pl.BlockSpec((total, chunk), lambda i, s: (0, now(i))),
            whole(normed),
            whole(root),
            whole(context),
            pl.BlockSpec((width, chunk), lambda i, s: (0, now(i))),
            pl.BlockSpec((chunk, width), lambda i, s: (now(i), 0)),
            whole(norm_gains),
            whole(bias_rows),
        ],
        [
            pl.BlockSpec((total, width), lambda i, s: (0, 0)),
            pl.BlockSpec((8, width), lambda i, s: (0, 0)),
            pl.BlockSpec((8, chunk), lambda i, s: (0, now(i))),
            half_a,
            half_a,
            half_b,
            half_b,
        ],
        [
            jax.ShapeDtypeStruct((total, width), BF16),
            jax.ShapeDtypeStruct((8, width), F32),
            jax.ShapeDtypeStruct((8, inner_width), F32),
            shape_a,
            shape_a,
            shape_b,
            shape_b,
        ],
        (steps + 1,),
        "feed_backward",
        scratch=[
            pltpu.VMEM((total, width), F32),
            pltpu.VMEM((total, width), BF16),
            pltpu.VMEM((width, chunk), BF16),
        ],
    )


def attention_backward(scalars, kept, weights, part, shards, base, order, earlier=(), sums=()):
    low_attn, mixed, probs, joined = kept
    w_out, w_qkv = weights
    total, width = low_attn.shape
    pairs, blocks, _, length = probs.shape
    duo = width // blocks
    first_block, mine = parts_of(blocks)[part]
    span_cols = mine * duo
    slot_rows = length // 2
    score_scale = (width // HEADS) ** (-0.5)
    steps = pairs // 2
    shard = width // shards
    places = shards // 2
    last = part == 1
    columns = 3 * span_cols + (128 if last else 0)

    def kernel(
        scalars_ref,
        low_attn_ref,
        mixed_ref,
        probs_ref,
        joined_ref,
        w_out_ref,
        *refs,
    ):
        if last:
            w_qkv_ref, earlier_ref, one, two, inner, sums_ref = refs[:6]
            kept_out, far_out, sums_out, send, keep, held, grad = refs[6:]
        else:
            d_mixed_out, sums_out, send, keep, held, grad = refs
        step = pl.program_id(0)

        @pl.when(step == 0)
        def _():
            sums_out[...] = jnp.zeros_like(sums_out)

        d_context = dot(low_attn_ref[...], w_out_ref[...], 1, 1).astype(BF16)
        rows = []
        for pair in range(2):
            span = slice(pair * length, (pair + 1) * length)
            d_heads, d_probs, d_scores = [], [], []
            for block in range(mine):
                cols = slice(block * duo, (block + 1) * duo)
                values = mixed_ref[span, 2 * span_cols + block * duo : 2 * span_cols + (block + 1) * duo]
                d_heads.append(split_heads(d_context[span, cols]))
                d_probs.append(dot(d_heads[block], values, 1, 1))
            for block in range(mine):
                wide = probs_ref[pair, block].astype(F32)
                mean = jnp.sum(wide * d_probs[block], axis=-1, keepdims=True)
                d_scores.append((wide * (d_probs[block] - mean)).astype(BF16))
            d_queries, d_keys, d_values = [], [], []
            for block in range(mine):
                cols = slice(block * duo, (block + 1) * duo)
                queries = split_heads(mixed_ref[span, cols])
                keys = mixed_ref[span, span_cols + block * duo : span_cols + (block + 1) * duo]
                keys = split_heads(keys)
                scaled = dot(side_by_side(d_scores[block]), keys) * score_scale
                d_queries.append(scaled.astype(BF16))
                d_keys.append(dot(d_scores[block], queries, 0, 0).astype(BF16))
                d_values.append(dot(probs_ref[pair, block], d_heads[block], 0, 0).astype(BF16))
            rows.append(jnp.concatenate(d_queries + d_keys + d_values, 1))
        d_mixed = jnp.concatenate(rows, 0)
        held[pl.ds(pl.multiple_of(step * 2 * length, 2 * length), 2 * length)] = d_mixed
        sums_out[0:1, :] += row_sum(d_mixed[:, :span_cols].astype(F32))
        sums_out[1:2, :] += row_sum(d_mixed[:, 2 * span_cols :].astype(F32))
        if last:
            d_rows = low_attn_ref[...].astype(F32)
            for third in range(3):
                before = earlier_ref.shape[1] // 3
                before = earlier_ref[:, third * before : (third + 1) * before]
                full = d_mixed[:, third * span_cols : (third + 1) * span_cols]
                full = jnp.concatenate([before, full], 1)
                d_rows = d_rows + dot(full, w_qkv_ref[:, third * width : (third + 1) * width], 1, 1)
            d_rows = d_rows.astype(BF16)
            for i in range(2):
                kept_out[i] = d_rows[i * length : i * length + slot_rows]
                far_out[i] = d_rows[i * length + slot_rows : (i + 1) * length]
        else:
            d_mixed_out[...] = d_mixed

        @pl.when(step == steps - 1)
        def _():
            grad[:, : 3 * span_cols] = dot(joined_ref[...], held[...], 0, 0).astype(BF16)
            if last:
                first, second = sums_ref[0:2, :], sums_out[0:2, :]
                small = [jnp.concatenate([first, second], 1), one[0:1], two[0:1]]
                small += [one[2:3], one[1:2], two[2:3], two[1:2], inner[...]]
                small.append(jnp.zeros((120 - inner.shape[0], width), F32))
                grad[:, 3 * span_cols :] = jnp.concatenate(small, 0).T.astype(BF16)
            spread(grad, (send, keep), scalars_ref, base, shard, order)

    def by_rows(count, at=0):
        return pl.BlockSpec((2 * length, count), lambda i, s: (i, at))

    two_slots = pl.BlockSpec((2, slot_rows, width), lambda i, s: (i, 0, 0))
    operands = [low_attn, mixed, probs, joined, w_out]
    in_specs = [
        by_rows(width),
        by_rows(3 * span_cols, first_block // mine),
        pl.BlockSpec((2, mine, 2 * length, length), lambda i, s: (i, first_block // mine, 0, 0)),
        whole(joined),
        pl.BlockSpec(
            (span_cols, width), lambda i, s: (first_block // mine, 0), pipeline_mode=pl.Buffered(1)
        ),
    ]
    grads = pl.BlockSpec((places, shard, columns), lambda i, s: (0, 0, 0))
    out_specs = [pl.BlockSpec((8, span_cols), lambda i, s: (0, 0)), grads, grads]
    out_shape = [
        jax.ShapeDtypeStruct((8, span_cols), F32),
        jax.ShapeDtypeStruct((places, shard, columns), BF16),
        jax.ShapeDtypeStruct((places, shard, columns), BF16),
    ]
    if last:
        operands += [w_qkv, earlier, *sums]
        in_specs += [whole(w_qkv), by_rows(earlier.shape[1])]
        in_specs += [whole(each) for each in sums]
        out_specs = [two_slots, two_slots] + out_specs
        out_shape = [jax.ShapeDtypeStruct((pairs, slot_rows, width), BF16)] * 2 + out_shape
    else:
        out_specs = [by_rows(3 * span_cols)] + out_specs
        out_shape = [jax.ShapeDtypeStruct((total, 3 * span_cols), BF16)] + out_shape
    return call(
        kernel,
        scalars,
        operands,
        in_specs,
        out_specs,
        out_shape,
        (steps,),
        "attention_backward",
        scratch=[
            pltpu.VMEM((total, 3 * span_cols), BF16),
            pltpu.VMEM((width, columns), BF16),
        ],
    )


def in_turn(value):
    value, *rest = lax.optimization_barrier((value, *LINE))
    LINE[:] = rest[:1]
    return value


def pause(scalars):
    def kernel(scalars_ref):
        del scalars_ref

    call(kernel, scalars, [], [], [], [], (1,), "pause", work=2 * 10**10)


class Shards:
    def __init__(self, send, keep, order):
        shard, width = send.shape[-2:]
        self.order = list(order)
        shape = (2 ** len(self.order), shard, width)
        self.held = [keep.reshape(shape)]
        self.coming = flipped(send, "dp", 1).reshape(shape)

    def step(self):
        self.held.append(in_turn(self.coming))
        count = self.coming.shape[0]
        first = count // 2 if self.order else 0
        total = None
        for array in self.held:
            array = lax.slice_in_dim(array, first, count, axis=0).astype(F32)
            total = array if total is None else total + array
        total = total.astype(BF16)
        if self.order:
            self.coming = flipped(total, "dp", 2 << self.order.pop(0))
        else:
            self.mine = lax.optimization_barrier(total[0])
            self.coming = flipped(self.mine, "mod", 1)
        LINE.append(total)

    def result(self):
        return self.mine.astype(F32) + in_turn(self.coming).astype(F32)


def finish_qkv(scalars, early, late, width, count):
    shard = early.mine.shape[0]
    widths = (early.mine.shape[1] // 3, (late.mine.shape[1] - 128) // 3)

    def kernel(scalars_ref, mine_a, coming_a, mine_b, coming_b, qkv, b_qv, gains, biases, inner):
        parts = [
            mine[...].astype(F32) + coming[...].astype(F32)
            for mine, coming in ((mine_a, coming_a), (mine_b, coming_b))
        ]
        at = 0
        for third in range(3):
            for part, columns in zip(parts, widths):
                qkv[:, at : at + columns] = part[:, third * columns : (third + 1) * columns]
                at += columns
        small = jnp.concatenate([parts[1][:, 3 * widths[1] :], jnp.zeros((128 - shard, 128), F32)], 0)
        small = small.T[:, :shard]
        b_qv[...] = small[0:2]
        gains[...] = small[2:4]
        biases[...] = small[4:8]
        inner[...] = small[8 : 8 + count]

    operands = [early.mine, early.coming, late.mine, late.coming]
    shapes = ((shard, 3 * width), (2, shard), (2, shard), (4, shard), (count, shard))
    return call(
        kernel,
        scalars,
        operands,
        [whole(array) for array in operands],
        [pl.BlockSpec(shape, lambda i, s: (0, 0)) for shape in shapes],
        [jax.ShapeDtypeStruct(shape, F32) for shape in shapes],
        (1,),
        "finish_qkv",
    )


def reduce_plain(send, keep, order):
    shard, columns = send.shape[-2:]
    total = jnp.stack([keep.reshape(-1, shard, columns), send.reshape(-1, shard, columns)], 1)
    places = [place_of(j, order) for j in range(total.shape[0])]
    total = jnp.stack([total[places.index(j)] for j in range(total.shape[0])])
    total = total.reshape(-1, columns).astype(F32)
    share = lax.psum_scatter(total, "dp", scatter_dimension=0, tiled=True)
    return lax.psum(share.astype(BF16), "mod").astype(F32)


def body(
    layer_rows,
    cotangent,
    row_live,
    partner,
    w_qkv,
    b_qv,
    w_out,
    norm_gains,
    bias_rows,
    w_in,
    b_in,
    w_back,
):
    side = lax.axis_index("mod")
    place = lax.axis_index("dp")
    shards = lax.axis_size("dp")
    groups = partner.shape[1]
    aligned = shards == 16 and (layer_rows.shape[2] // shards) % 16 == 0
    layout = shards if aligned else 16
    half = groups // 2
    width = layer_rows.shape[2]
    slot_rows = layer_rows.shape[1] // groups
    inner_width = w_in.shape[1]
    slots = (groups, slot_rows, width)
    rows = layer_rows[0].reshape(slots)
    cot = cotangent[0].reshape(slots)
    spot = place if aligned else 0 * place
    scalars = jnp.concatenate(
        [partner[0], jnp.stack([side, spot & 1, spot >> 1]).astype(jnp.int32)]
    )
    cut = half // 2
    LINE.clear()
    sent = gather_sent(partner[0], rows, half, 0, cut)
    got_a = flipped(sent, "mod", 1)
    sent = gather_sent(partner[0], rows, half, cut, half - cut)
    got_b = flipped(sent, "mod", 1)
    sent_cot = gather_sent(partner[0], cot, half, 0, half)
    got_a, sent_cot = lax.optimization_barrier((got_a, sent_cot))
    far_cot = flipped(sent_cot, "mod", 1)

    live = row_live.reshape(2, groups, slot_rows)
    words_live = lax.dynamic_slice_in_dim(live[0], side * half, half, 0)
    region_live = live[1][lax.dynamic_slice_in_dim(partner[0], side * half, half, 0)]
    is_first = side == 0
    seen = jnp.concatenate(
        [
            jnp.where(is_first, words_live, region_live),
            jnp.where(is_first, region_live, words_live),
        ],
        1,
    )[:, None, :]

    heads_weights = (w_qkv, b_qv, w_out, norm_gains, bias_rows)
    joined, mixed, probs, context, normed, root = attention_forward(
        scalars, rows, (got_a, got_b), seen, heads_weights
    )
    feed_weights = (w_in, b_in.reshape(1, inner_width), w_back, norm_gains, bias_rows)
    slope, branch, out_kept, out_far, sums_two, *back = feed_forward(
        scalars, normed, cot, far_cot, feed_weights, half, layout, groups
    )
    out_back = flipped(out_far, "mod", 1)
    back_weights = (w_in, w_back, norm_gains, bias_rows)
    attn_weights = (w_out, w_qkv)
    path, other = (0, 1, 2), (1, 0, 2)
    if aligned:
        back = Shards(*back, path)
        back.step()
    low_attn, sums_one, inner_sum, *inner = feed_backward(
        scalars,
        branch,
        slope,
        normed,
        root,
        context,
        back_weights,
        layout,
        groups,
        (other, path),
    )
    shard = width // shards
    count = inner_width // width
    inner_sum = inner_sum[0].reshape(shards, count, shard).transpose(1, 0, 2).reshape(count, width)
    if aligned:
        back.step()
        out_back = in_turn(out_back)
        pause(scalars)
        inner_a, inner_b = Shards(*inner[:2], other), Shards(*inner[2:], path)
        inner_a.step()
        inner_b.step()
    attn_kept = (low_attn, mixed, probs, joined)
    d_mixed, sums_qv, *qkv_a = attention_backward(
        scalars, attn_kept, attn_weights, 0, layout, groups, path
    )
    if aligned:
        back.step()
        inner_a.step()
        inner_b.step()
        pause(scalars)
        qkv_a = Shards(*qkv_a, path)
        qkv_a.step()
    sums = (sums_one, sums_two, inner_sum, sums_qv)
    d_kept, d_far, _, *qkv_b = attention_backward(
        scalars, attn_kept, attn_weights, 1, layout, groups, path, d_mixed, sums
    )
    d_back = flipped(d_far, "mod", 1)
    if aligned:
        qkv_b = Shards(*qkv_b, path)
        inner_b.step()
        qkv_b.step()
        qkv_a.step()
        inner_a.step()
        back.step()
        out_rows = scatter_home(scalars, out_kept, out_back, half).reshape(1, -1, width)
        qkv_b.step()
        qkv_a.step()
        inner_b.step()
        qkv_b.step()
        inner_a.step()
        grad_back = back.result()
        grad_rows = scatter_home(scalars, d_kept, d_back, half).reshape(1, -1, width)
        qkv_a.step()
        qkv_b.step()
        inner_a, inner_b = inner_a.result(), inner_b.result()
        grad_qkv, *small = finish_qkv(scalars, qkv_a, qkv_b, width, count)
    else:
        out_rows = scatter_home(scalars, out_kept, out_back, half).reshape(1, -1, width)
        grad_back = reduce_plain(*back, path)
        inner_a, inner_b = reduce_plain(*inner[:2], other), reduce_plain(*inner[2:], path)
        qkv_a, qkv_b = reduce_plain(*qkv_a, path), reduce_plain(*qkv_b, path)
        grad_rows = scatter_home(scalars, d_kept, d_back, half).reshape(1, -1, width)
        columns = (qkv_a.shape[1] // 3, (qkv_b.shape[1] - 128) // 3)
        thirds = []
        for third in range(3):
            for part, wide in zip((qkv_a, qkv_b), columns):
                thirds.append(part[:, third * wide : (third + 1) * wide])
        grad_qkv = jnp.concatenate(thirds, 1)
        small = qkv_b[:, 3 * columns[1] :].T
        small = small[0:2], small[2:4], small[4:8], small[8 : 8 + count]
    turn = inner_width - inner_a.shape[1]
    return (
        out_rows,
        grad_rows,
        grad_qkv,
        small[0],
        inner_b[:, turn:],
        small[1],
        small[2],
        jnp.concatenate([inner_a, inner_b[:, :turn]], 1),
        small[3].reshape(-1),
        grad_back,
    )


def solution(mesh):
    return jax.shard_map(
        body,
        mesh=mesh,
        in_specs=(
            P("mod", "dp", None),
            P("mod", "dp", None),
            P(None, "dp"),
            P("dp", None),
            P(),
            P(),
            P(),
            P(),
            P(),
            P(),
            P(),
            P(),
        ),
        out_specs=(
            P("mod", "dp", None),
            P("mod", "dp", None),
            P("dp", None),
            P(None, "dp"),
            P("dp", None),
            P(None, "dp"),
            P(None, "dp"),
            P("dp", None),
            P("dp"),
            P("dp", None),
        ),
        check_vma=False,
    )
```

```python
import functools

import jax
import jax.numpy as jnp
from jax import lax
from jax.experimental import pallas as pl
from jax.experimental.pallas import tpu as pltpu
from jax.sharding import PartitionSpec as P

HEADS = 12
EPSILON = 1e-12
F32 = jnp.float32
BF16 = jnp.bfloat16
VMEM_LIMIT = 26 * 2**20


def dot(left, right, left_dim=1, right_dim=0):
    return lax.dot_general(
        left, right, (((left_dim,), (right_dim,)), ((), ())), preferred_element_type=F32
    )


def flipped(value, axis, mask):
    pairs = [(source, source ^ mask) for source in range(lax.axis_size(axis))]
    return lax.ppermute(value, axis, pairs)


def params(limit=VMEM_LIMIT):
    return pltpu.CompilerParams(vmem_limit_bytes=limit)


def kept_slot(scalars, pair, half):
    groups = 2 * half
    side = scalars[groups]
    place = side * half + pair
    return jnp.where(side == 0, place, scalars[place])


def sent_slot(scalars, pair, half):
    groups = 2 * half
    side = scalars[groups]
    place = (1 - side) * half + pair
    return jnp.where(side == 0, place, scalars[place])


ANY = pl.BlockSpec(memory_space=pl.ANY)
RESIDENT = pl.BlockSpec(memory_space=pltpu.VMEM)
LINE = []


def call(kernel, scalars, operands, in_specs, out_specs, out_shape, grid, name, **more):
    after = list(LINE)
    scratch = list(more.get("scratch", ()))
    taken, given = len(operands), len(out_shape)

    def wrapped(scalars_ref, *refs):
        outs = refs[taken + len(after) :]
        kernel(scalars_ref, *refs[:taken], *outs[:given], *outs[given + 1 :])

    placed = [
        pltpu.with_memory_space_constraint(array, pltpu.VMEM if spec is RESIDENT else pltpu.HBM)
        for array, spec in zip(operands + after, list(in_specs) + [ANY] * len(after))
    ]
    shapes = [
        pltpu.VMEM(shape.shape, shape.dtype) if spec is RESIDENT else shape
        for shape, spec in zip(out_shape, out_specs)
    ]
    outs = pl.pallas_call(
        wrapped,
        grid_spec=pltpu.PrefetchScalarGridSpec(
            num_scalar_prefetch=1,
            grid=grid,
            in_specs=list(in_specs) + [ANY] * len(after),
            out_specs=list(out_specs) + [ANY],
            scratch_shapes=scratch,
        ),
        out_shape=shapes + [jax.ShapeDtypeStruct((8, 128), F32)],
        compiler_params=params(more.get("limit", VMEM_LIMIT)),
        cost_estimate=pl.CostEstimate(
            flops=more.get("work", 4 * 10**9), bytes_accessed=2**20, transcendentals=0
        ),
        name=name,
    )(scalars, *placed)
    LINE[:] = [outs[-1]]
    return list(outs[:-1])


def fetch(scalars, arrays):
    count = len(arrays)

    def kernel(scalars_ref, *refs):
        sems = refs[-1]
        copies = [
            pltpu.make_async_copy(refs[i], refs[count + i], sems.at[i]) for i in range(count)
        ]
        for copy in copies:
            copy.start()
        for copy in copies:
            copy.wait()

    return call(
        kernel,
        scalars,
        list(arrays),
        [ANY] * count,
        [RESIDENT] * count,
        [jax.ShapeDtypeStruct(array.shape, array.dtype) for array in arrays],
        (1,),
        "fetch",
        work=10**7,
        scratch=[pltpu.SemaphoreType.DMA((count,))],
    )


def gather_sent(partner, rows, half, first, count):
    slot_rows, width = rows.shape[1:]

    def kernel(partner_ref, rows_ref, out, sems):
        side = lax.axis_index("mod")
        copies = []
        for i in range(count):
            place = (1 - side) * half + first + i
            slot = jnp.where(side == 0, place, partner_ref[place])
            copies.append(pltpu.make_async_copy(rows_ref.at[slot], out.at[i], sems.at[i]))
        for copy in copies:
            copy.start()
        for copy in copies:
            copy.wait()

    shape = (count, slot_rows, width)
    return call(
        kernel,
        partner,
        [rows],
        [ANY],
        [pl.BlockSpec(shape, lambda i, s: (0, 0, 0))],
        [jax.ShapeDtypeStruct(shape, rows.dtype)],
        (1,),
        "gather_sent",
        work=10**7,
        scratch=[pltpu.SemaphoreType.DMA((count,))],
    )[0]


def scatter_home(scalars, kept, back, half):
    slot_rows, width = kept.shape[1:]

    def kernel(scalars_ref, kept_ref, back_ref, out, sems):
        copies = []
        for i in range(half):
            copies.append(
                pltpu.make_async_copy(
                    kept_ref.at[i], out.at[kept_slot(scalars_ref, i, half)], sems.at[0, i]
                )
            )
            copies.append(
                pltpu.make_async_copy(
                    back_ref.at[i], out.at[sent_slot(scalars_ref, i, half)], sems.at[1, i]
                )
            )
        for copy in copies:
            copy.start()
        for copy in copies:
            copy.wait()

    shape = (2 * half, slot_rows, width)
    return call(
        kernel,
        scalars,
        [kept, back],
        [ANY, ANY],
        [pl.BlockSpec(shape, lambda i, s: (0, 0, 0))],
        [jax.ShapeDtypeStruct(shape, kept.dtype)],
        (1,),
        "scatter_home",
        work=2 * 10**10,
        scratch=[pltpu.SemaphoreType.DMA((2, half))],
    )[0]


def parts_of(blocks):
    early = 2 * blocks // 3
    return (0, early), (early, blocks - early)


def split_heads(value):
    low = lax.broadcasted_iota(jnp.int32, value.shape, 1) < value.shape[1] // 2
    zero = jnp.zeros_like(value)
    return jnp.concatenate([jnp.where(low, value, zero), jnp.where(low, zero, value)], 0)


def side_by_side(value):
    rows = value.shape[0] // 2
    return jnp.concatenate([value[:rows], value[rows:]], 1)


def row_sum(value):
    return jnp.sum(value, axis=0, keepdims=True)


def normal_form(value):
    centered = value - jnp.mean(value, axis=-1, keepdims=True)
    root = lax.rsqrt(jnp.mean(centered * centered, axis=-1, keepdims=True) + EPSILON)
    return centered * root, root


def normal_back(lifted, normed, root):
    return root * (
        lifted
        - jnp.mean(lifted, axis=-1, keepdims=True)
        - normed * jnp.mean(lifted * normed, axis=-1, keepdims=True)
    )


def whole(array):
    return pl.BlockSpec(
        array.shape, lambda *_: (0,) * array.ndim, pipeline_mode=pl.Buffered(1)
    )


def attention_forward(scalars, rows, received, live, weights):
    w_qkv, b_qv, w_out, norm_gains, bias_rows = weights
    slot_rows, width = rows.shape[1:]
    pairs = half = rows.shape[0] // 2
    turn = received[0].shape[0] // 2
    length = 2 * slot_rows
    duo = 2 * width // HEADS
    blocks = width // duo
    score_scale = (width // HEADS) ** (-0.5)

    def kernel(
        scalars_ref,
        kept_a,
        kept_b,
        got_a,
        got_b,
        live_ref,
        w_qkv_ref,
        b_qv_ref,
        w_out_ref,
        gains_ref,
        biases_ref,
        joined_out,
        mixed_out,
        probs_out,
        context_out,
        normed_out,
        root_out,
    ):
        step = pl.program_id(0)
        rows_here = pl.ds(pl.multiple_of(step * 2 * length, 2 * length), 2 * length)
        got = jnp.where(step < turn, got_a[...], got_b[...])
        joined = jnp.concatenate([kept_a[0], got[0], kept_b[0], got[1]], 0)
        joined_out[rows_here] = joined
        mixed = dot(joined, w_qkv_ref[...])
        queries = (mixed[:, :width] + b_qv_ref[0:1, :]).astype(BF16)
        queries = (queries.astype(F32) * score_scale).astype(BF16)
        keys = mixed[:, width : 2 * width].astype(BF16)
        values = (mixed[:, 2 * width :] + b_qv_ref[1:2, :]).astype(BF16)
        for first_block, count in parts_of(blocks):
            cols = slice(first_block * duo, (first_block + count) * duo)
            at = 3 * first_block * duo
            for value in (queries, keys, values):
                mixed_out[rows_here, at : at + count * duo] = value[:, cols]
                at += count * duo
        contexts = []
        for pair in range(2):
            seen = live_ref[pair] > 0
            span = slice(pair * length, (pair + 1) * length)
            heads = []
            for block in range(blocks):
                cols = slice(block * duo, (block + 1) * duo)
                scores = dot(split_heads(queries[span, cols]), keys[span, cols], 1, 1)
                scores = jnp.where(seen, scores, -1e30)
                powered = jnp.exp(scores - jnp.max(scores, axis=-1, keepdims=True))
                low_probs = powered * (1.0 / jnp.sum(powered, axis=-1, keepdims=True))
                low_probs = low_probs.astype(BF16)
                probs_out[2 * step + pair, block] = low_probs
                heads.append(
                    dot(side_by_side(low_probs), split_heads(values[span, cols])).astype(BF16)
                )
            contexts.append(jnp.concatenate(heads, 1))
        context = jnp.concatenate(contexts, 0)
        context_out[rows_here] = context
        pre_one = joined.astype(F32) + dot(context, w_out_ref[...]) + biases_ref[0:1, :]
        normed, root = normal_form(pre_one)
        normed_out[rows_here] = normed.astype(BF16)
        root_out[rows_here] = jnp.broadcast_to(root, (2 * length, 128))

    slot = (1, slot_rows, width)
    two = (2, slot_rows, width)
    total = half * length
    return call(
        kernel,
        scalars,
        [rows, rows, *received, live, w_qkv, b_qv, w_out, norm_gains, bias_rows],
        [
            pl.BlockSpec(slot, lambda i, s: (kept_slot(s, 2 * i, half), 0, 0)),
            pl.BlockSpec(slot, lambda i, s: (kept_slot(s, 2 * i + 1, half), 0, 0)),
            pl.BlockSpec(two, lambda i, s: (jnp.minimum(i, turn - 1), 0, 0)),
            pl.BlockSpec(two, lambda i, s: (jnp.maximum(i - turn, 0), 0, 0)),
            pl.BlockSpec((2, 1, length), lambda i, s: (i, 0, 0)),
            RESIDENT,
            whole(b_qv),
            RESIDENT,
            whole(norm_gains),
            whole(bias_rows),
        ],
        [RESIDENT] * 6,
        [
            jax.ShapeDtypeStruct((total, width), BF16),
            jax.ShapeDtypeStruct((total, 3 * width), BF16),
            jax.ShapeDtypeStruct((half, blocks, 2 * length, length), BF16),
            jax.ShapeDtypeStruct((total, width), BF16),
            jax.ShapeDtypeStruct((total, width), BF16),
            jax.ShapeDtypeStruct((total, 128), F32),
        ],
        (pairs // 2,),
        "attention_forward",
        work=4 * 10**10,
    )


def place_of(index, order):
    return sum(1 << bit for n, bit in enumerate(order) if index >> (len(order) - 1 - n) & 1)


def spread(grad, outs, scalars_ref, base, shard, order):
    core, place = scalars_ref[base + 1], scalars_ref[base + 2]
    for j in range(2 ** len(order)):
        row = (place ^ place_of(j, order)) * 2
        for out, which in zip(outs, (1 - core, core)):
            out[j] = grad[pl.ds(pl.multiple_of((row + which) * shard, 16), shard), :]


def feed_forward(scalars, normed, cot, far_cot, weights, half, shards, base):
    w_in, b_in, w_back, norm_gains, bias_rows = weights
    slot_rows, width = cot.shape[1:]
    inner_width = w_in.shape[1]
    length = 2 * slot_rows
    rows = 2 * length
    height = half * length
    steps = half // 2
    chunk = 768
    chunks = inner_width // chunk
    shard = inner_width // shards
    places = shards // 2
    part = 4 * shard
    parts = inner_width // part

    def kernel(
        scalars_ref,
        normed_ref,
        cot_a,
        cot_b,
        cot_far,
        w_in_ref,
        b_in_ref,
        w_back_ref,
        gains_ref,
        biases_ref,
        slope_out,
        branch_out,
        kept_out,
        far_out,
        sums_out,
        send,
        keep,
        held,
        acts,
        grad,
    ):
        step = pl.program_id(0)

        @pl.when(step == 0)
        def _():
            sums_out[...] = jnp.zeros_like(sums_out)

        def close(pre_two, row):
            scaled, root = normal_form(pre_two)
            output = (scaled * gains_ref[1:2, :] + biases_ref[3:4, :]).astype(BF16)
            for i in range(2):
                kept_out[i] = output[i * length : i * length + slot_rows]
                far_out[i] = output[i * length + slot_rows : (i + 1) * length]
            here = jnp.concatenate([cot_a[0], cot_far[0], cot_b[0], cot_far[1]], 0).astype(F32)
            d_two = normal_back(here * gains_ref[1:2, :], scaled, root)
            low = d_two.astype(BF16)
            branch_out[pl.ds(pl.multiple_of(row, rows), rows)] = low
            return jnp.concatenate([row_sum(here * scaled), row_sum(here), row_sum(d_two)], 0)

        def forward():
            here = pl.ds(pl.multiple_of(step * rows, rows), rows)
            hidden = normed_ref[here].astype(F32) * gains_ref[0:1, :] + biases_ref[1:2, :]
            low_hidden = hidden.astype(BF16)
            total = hidden + biases_ref[2:3, :]
            for j in range(chunks):
                cols = slice(j * chunk, (j + 1) * chunk)
                inner = dot(low_hidden, w_in_ref[:, cols]) + b_in_ref[:, cols]
                normal = 0.5 + 0.5 * lax.erf(inner * (0.5**0.5))
                low_act = (inner * normal).astype(BF16)
                density = jnp.exp(inner * inner * -0.5) * 0.3989422804014327
                acts[here, cols] = low_act
                slope_out[here, cols] = (normal + inner * density).astype(BF16)
                total = total + dot(low_act, w_back_ref[cols, :])
            return total

        @pl.when(step == 0)
        def _():
            held[...] = forward()

        @pl.when((step > 0) & (step < steps))
        def _():
            before = held[...]
            held[...] = forward()
            sums_out[0:3, :] += close(before, (step - 1) * rows)

        @pl.when(step == steps)
        def _():
            sums_out[0:3, :] += close(held[...], (step - 1) * rows)

        @pl.when(step >= steps)
        def _():
            start = pl.multiple_of((step - steps) * part, 128)
            grad[...] = dot(acts[:, pl.ds(start, part)], branch_out[...], 0, 0).astype(BF16)
            core, low = scalars_ref[base + 1], scalars_ref[base + 2] & 1
            for j in range(2):
                for out, which in ((send, 1 - core), (keep, core)):
                    row = ((low ^ j) * 2 + which) * shard
                    out[j, 0] = grad[pl.ds(pl.multiple_of(row, 16), shard), :]

    def behind(i):
        return jnp.clip(i - 1, 0, steps - 1)

    def slot(j):
        return pl.BlockSpec(
            (1, slot_rows, width), lambda i, s: (kept_slot(s, 2 * behind(i) + j, half), 0, 0)
        )

    duo = pl.BlockSpec((2, slot_rows, width), lambda i, s: (behind(i), 0, 0))

    def entry(i, s):
        apart = (s[base + 2] >> 1) ^ jnp.maximum(i - steps, 0)
        return 0, (apart & 1) * 2 + (apart >> 1), 0, 0

    grads = pl.BlockSpec((2, 1, shard, width), entry)
    return call(
        kernel,
        scalars,
        [normed, cot, cot, far_cot, w_in, b_in, w_back, norm_gains, bias_rows],
        [
            RESIDENT,
            slot(0),
            slot(1),
            duo,
            RESIDENT,
            whole(b_in),
            RESIDENT,
            whole(norm_gains),
            whole(bias_rows),
        ],
        [
            RESIDENT,
            RESIDENT,
            duo,
            duo,
            pl.BlockSpec((8, width), lambda i, s: (0, 0)),
            grads,
            grads,
        ],
        [
            jax.ShapeDtypeStruct((height, inner_width), BF16),
            jax.ShapeDtypeStruct((height, width), BF16),
            jax.ShapeDtypeStruct((half, slot_rows, width), BF16),
            jax.ShapeDtypeStruct((half, slot_rows, width), BF16),
            jax.ShapeDtypeStruct((8, width), F32),
            jax.ShapeDtypeStruct((2, places // 2, shard, width), BF16),
            jax.ShapeDtypeStruct((2, places // 2, shard, width), BF16),
        ],
        (steps + parts,),
        "feed_forward",
        scratch=[
            pltpu.VMEM((rows, width), F32),
            pltpu.VMEM((height, inner_width), BF16),
            pltpu.VMEM((part, width), BF16),
        ],
    )


def feed_backward(scalars, branch, slope, normed, root, context, weights, shards, base, orders):
    w_in, w_back, norm_gains, bias_rows = weights
    total, width = branch.shape
    inner_width = slope.shape[1]
    chunk = 768
    steps = inner_width // chunk
    turn = steps // 2
    shard = width // shards
    places = shards // 2
    piece = 128

    def kernel(
        scalars_ref,
        branch_ref,
        slope_ref,
        normed_ref,
        root_ref,
        context_ref,
        w_in_ref,
        w_back_ref,
        gains_ref,
        biases_ref,
        low_attn_out,
        sums_out,
        inner_sum_out,
        send_a,
        keep_a,
        send_b,
        keep_b,
        held,
        low_hidden,
        grad,
    ):
        step = pl.program_id(0)

        @pl.when(step == 0)
        def _():
            hidden = normed_ref[...].astype(F32) * gains_ref[0:1, :] + biases_ref[1:2, :]
            low_hidden[...] = hidden.astype(BF16)
            held[...] = branch_ref[...].astype(F32)

        @pl.when(step < steps)
        def _():
            cols = pl.ds(pl.multiple_of(step * chunk, chunk), chunk)
            sums = jnp.zeros((1, chunk), F32)
            lows = []
            for r in range(0, total, 256):
                span = slice(r, r + 256)
                d_inner = dot(branch_ref[span], w_back_ref[cols, :], 1, 1)
                d_inner = d_inner * slope_ref[span, cols].astype(F32)
                sums = sums + row_sum(d_inner)
                low = d_inner.astype(BF16)
                lows.append(low)
                held[span] += dot(low, w_in_ref[:, cols], 1, 1)
            inner_sum_out[...] = jnp.broadcast_to(sums, inner_sum_out.shape)
            grad[...] = dot(low_hidden[...], jnp.concatenate(lows, 0), 0, 0).astype(BF16)

        @pl.when(step == steps)
        def _():
            sums = [jnp.zeros((1, width), F32)] * 3
            lows = []
            for i in range(total // piece):
                span = slice(i * piece, (i + 1) * piece)
                d_hidden, scaled = held[span], normed_ref[span].astype(F32)
                d_one = normal_back(d_hidden * gains_ref[0:1, :], scaled, root_ref[span, 0:1])
                lows.append(d_one.astype(BF16))
                low_attn_out[span] = lows[-1]
                for j, term in enumerate((d_hidden * scaled, d_hidden, d_one)):
                    sums[j] = sums[j] + row_sum(term)
            sums_out[...] = jnp.concatenate(sums + [jnp.zeros((5, width), F32)], 0)
            grad[...] = dot(context_ref[...], jnp.concatenate(lows, 0), 0, 0).astype(BF16)

        @pl.when(step < turn)
        def _():
            spread(grad, (send_a, keep_a), scalars_ref, base, shard, orders[0])

        @pl.when(step >= turn)
        def _():
            spread(grad, (send_b, keep_b), scalars_ref, base, shard, orders[1])

    def now(i):
        return jnp.minimum(i, steps - 1)

    half_a = pl.BlockSpec((places, shard, chunk), lambda i, s: (0, 0, jnp.minimum(i, turn - 1)))
    half_b = pl.BlockSpec((places, shard, chunk), lambda i, s: (0, 0, jnp.maximum(i - turn, 0)))
    shape_a = jax.ShapeDtypeStruct((places, shard, turn * chunk), BF16)
    shape_b = jax.ShapeDtypeStruct((places, shard, (steps + 1 - turn) * chunk), BF16)
    return call(
        kernel,
        scalars,
        [branch, slope, normed, root, context, w_in, w_back, norm_gains, bias_rows],
        [
            RESIDENT,
            RESIDENT,
            RESIDENT,
            RESIDENT,
            RESIDENT,
            RESIDENT,
            RESIDENT,
            whole(norm_gains),
            whole(bias_rows),
        ],
        [
            RESIDENT,
            pl.BlockSpec((8, width), lambda i, s: (0, 0)),
            pl.BlockSpec((8, chunk), lambda i, s: (0, now(i))),
            half_a,
            half_a,
            half_b,
            half_b,
        ],
        [
            jax.ShapeDtypeStruct((total, width), BF16),
            jax.ShapeDtypeStruct((8, width), F32),
            jax.ShapeDtypeStruct((8, inner_width), F32),
            shape_a,
            shape_a,
            shape_b,
            shape_b,
        ],
        (steps + 1,),
        "feed_backward",
        scratch=[
            pltpu.VMEM((total, width), F32),
            pltpu.VMEM((total, width), BF16),
            pltpu.VMEM((width, chunk), BF16),
        ],
    )


def attention_backward(scalars, kept, weights, part, shards, base, order, earlier=(), sums=()):
    low_attn, mixed, probs, joined = kept
    w_out, w_qkv = weights
    total, width = low_attn.shape
    pairs, blocks, _, length = probs.shape
    duo = width // blocks
    first_block, mine = parts_of(blocks)[part]
    span_cols = mine * duo
    slot_rows = length // 2
    score_scale = (width // HEADS) ** (-0.5)
    steps = pairs // 2
    shard = width // shards
    places = shards // 2
    last = part == 1
    columns = 3 * span_cols + (128 if last else 0)

    def kernel(
        scalars_ref,
        low_attn_ref,
        mixed_ref,
        probs_ref,
        joined_ref,
        w_out_ref,
        *refs,
    ):
        if last:
            w_qkv_ref, earlier_ref, one, two, inner, sums_ref = refs[:6]
            kept_out, far_out, sums_out, send, keep, held, grad = refs[6:]
        else:
            held, sums_out, send, keep, grad = refs
        step = pl.program_id(0)

        @pl.when(step == 0)
        def _():
            sums_out[...] = jnp.zeros_like(sums_out)

        here = pl.ds(pl.multiple_of(step * 2 * length, 2 * length), 2 * length)
        low_attn = low_attn_ref[here]
        w_out_rows = slice(first_block * duo, (first_block + mine) * duo)
        d_context = dot(low_attn, w_out_ref[w_out_rows, :], 1, 1).astype(BF16)
        at = 3 * first_block * duo
        mixed = mixed_ref[here, at : at + 3 * span_cols]
        rows = []
        for pair in range(2):
            span = slice(pair * length, (pair + 1) * length)
            chosen = [probs_ref[2 * step + pair, first_block + block] for block in range(mine)]
            parts = []
            for third in range(3):
                first = third * span_cols
                parts.append(
                    [
                        mixed[span, first + block * duo : first + (block + 1) * duo]
                        for block in range(mine)
                    ]
                )
            queries, keys, values = parts
            d_heads, d_probs, d_scores = [], [], []
            for block in range(mine):
                cols = slice(block * duo, (block + 1) * duo)
                d_heads.append(split_heads(d_context[span, cols]))
                d_probs.append(dot(d_heads[block], values[block], 1, 1))
            for block in range(mine):
                wide = chosen[block].astype(F32)
                mean = jnp.sum(wide * d_probs[block], axis=-1, keepdims=True)
                d_scores.append((wide * (d_probs[block] - mean)).astype(BF16))
            d_queries, d_keys, d_values = [], [], []
            for block in range(mine):
                scaled = dot(side_by_side(d_scores[block]), split_heads(keys[block])) * score_scale
                d_queries.append(scaled.astype(BF16))
                d_keys.append(dot(d_scores[block], split_heads(queries[block]), 0, 0).astype(BF16))
                d_values.append(dot(chosen[block], d_heads[block], 0, 0).astype(BF16))
            rows.append(jnp.concatenate(d_queries + d_keys + d_values, 1))
        d_mixed = jnp.concatenate(rows, 0)
        held[here] = d_mixed
        sums_out[0:1, :] += row_sum(d_mixed[:, :span_cols].astype(F32))
        sums_out[1:2, :] += row_sum(d_mixed[:, 2 * span_cols :].astype(F32))
        if last:
            d_rows = low_attn.astype(F32)
            before = earlier_ref.shape[1] // 3
            for third in range(3):
                full = [
                    earlier_ref[here, third * before : (third + 1) * before],
                    d_mixed[:, third * span_cols : (third + 1) * span_cols],
                ]
                cols = slice(third * width, (third + 1) * width)
                d_rows = d_rows + dot(jnp.concatenate(full, 1), w_qkv_ref[:, cols], 1, 1)
            d_rows = d_rows.astype(BF16)
            for i in range(2):
                kept_out[i] = d_rows[i * length : i * length + slot_rows]
                far_out[i] = d_rows[i * length + slot_rows : (i + 1) * length]

        @pl.when(step == steps - 1)
        def _():
            grad[:, : 3 * span_cols] = dot(joined_ref[...], held[...], 0, 0).astype(BF16)
            if last:
                first, second = sums_ref[0:2, :], sums_out[0:2, :]
                small = [jnp.concatenate([first, second], 1), one[0:1], two[0:1]]
                small += [one[2:3], one[1:2], two[2:3], two[1:2], inner[...]]
                small.append(jnp.zeros((120 - inner.shape[0], width), F32))
                grad[:, 3 * span_cols :] = jnp.concatenate(small, 0).T.astype(BF16)
            spread(grad, (send, keep), scalars_ref, base, shard, order)

    two_slots = pl.BlockSpec((2, slot_rows, width), lambda i, s: (i, 0, 0))
    operands = [low_attn, mixed, probs, joined, w_out]
    in_specs = [RESIDENT] * 5
    grads = pl.BlockSpec((places, shard, columns), lambda i, s: (0, 0, 0))
    out_specs = [pl.BlockSpec((8, span_cols), lambda i, s: (0, 0)), grads, grads]
    out_shape = [
        jax.ShapeDtypeStruct((8, span_cols), F32),
        jax.ShapeDtypeStruct((places, shard, columns), BF16),
        jax.ShapeDtypeStruct((places, shard, columns), BF16),
    ]
    if last:
        operands += [w_qkv, earlier, *sums]
        in_specs += [RESIDENT, RESIDENT]
        in_specs += [whole(each) for each in sums]
        out_specs = [two_slots, two_slots] + out_specs
        out_shape = [jax.ShapeDtypeStruct((pairs, slot_rows, width), BF16)] * 2 + out_shape
    else:
        out_specs = [RESIDENT] + out_specs
        out_shape = [jax.ShapeDtypeStruct((total, 3 * span_cols), BF16)] + out_shape
    return call(
        kernel,
        scalars,
        operands,
        in_specs,
        out_specs,
        out_shape,
        (steps,),
        "attention_backward",
        scratch=[pltpu.VMEM((total, 3 * span_cols), BF16)] * last
        + [pltpu.VMEM((width, columns), BF16)],
    )


def in_turn(value):
    value, *rest = lax.optimization_barrier((value, *LINE))
    LINE[:] = rest[:1]
    return value


def pause(scalars):
    def kernel(scalars_ref):
        del scalars_ref

    call(kernel, scalars, [], [], [], [], (1,), "pause", work=2 * 10**10)


class Shards:
    def __init__(self, send, keep, order):
        shard, width = send.shape[-2:]
        self.order = list(order)
        shape = (2 ** len(self.order), shard, width)
        self.held = [keep.reshape(shape)]
        self.coming = flipped(send, "dp", 1).reshape(shape)

    def step(self):
        self.held.append(in_turn(self.coming))
        count = self.coming.shape[0]
        first = count // 2 if self.order else 0
        total = None
        for array in self.held:
            array = lax.slice_in_dim(array, first, count, axis=0).astype(F32)
            total = array if total is None else total + array
        total = total.astype(BF16)
        if self.order:
            self.coming = flipped(total, "dp", 2 << self.order.pop(0))
        else:
            self.mine = lax.optimization_barrier(total[0])
            self.coming = flipped(self.mine, "mod", 1)
        LINE.append(total)

    def result(self):
        return self.mine.astype(F32) + in_turn(self.coming).astype(F32)


def finish_qkv(scalars, early, late, width, count):
    shard = early.mine.shape[0]
    widths = (early.mine.shape[1] // 3, (late.mine.shape[1] - 128) // 3)

    def kernel(scalars_ref, mine_a, coming_a, mine_b, coming_b, qkv, b_qv, gains, biases, inner):
        parts = [
            mine[...].astype(F32) + coming[...].astype(F32)
            for mine, coming in ((mine_a, coming_a), (mine_b, coming_b))
        ]
        at = 0
        for third in range(3):
            for part, columns in zip(parts, widths):
                qkv[:, at : at + columns] = part[:, third * columns : (third + 1) * columns]
                at += columns
        small = jnp.concatenate([parts[1][:, 3 * widths[1] :], jnp.zeros((128 - shard, 128), F32)], 0)
        small = small.T[:, :shard]
        b_qv[...] = small[0:2]
        gains[...] = small[2:4]
        biases[...] = small[4:8]
        inner[...] = small[8 : 8 + count]

    operands = [early.mine, early.coming, late.mine, late.coming]
    shapes = ((shard, 3 * width), (2, shard), (2, shard), (4, shard), (count, shard))
    return call(
        kernel,
        scalars,
        operands,
        [whole(array) for array in operands],
        [pl.BlockSpec(shape, lambda i, s: (0, 0)) for shape in shapes],
        [jax.ShapeDtypeStruct(shape, F32) for shape in shapes],
        (1,),
        "finish_qkv",
    )


def reduce_plain(send, keep, order):
    shard, columns = send.shape[-2:]
    total = jnp.stack([keep.reshape(-1, shard, columns), send.reshape(-1, shard, columns)], 1)
    places = [place_of(j, order) for j in range(total.shape[0])]
    total = jnp.stack([total[places.index(j)] for j in range(total.shape[0])])
    total = total.reshape(-1, columns).astype(F32)
    share = lax.psum_scatter(total, "dp", scatter_dimension=0, tiled=True)
    return lax.psum(share.astype(BF16), "mod").astype(F32)


def body(
    layer_rows,
    cotangent,
    row_live,
    partner,
    w_qkv,
    b_qv,
    w_out,
    norm_gains,
    bias_rows,
    w_in,
    b_in,
    w_back,
):
    side = lax.axis_index("mod")
    place = lax.axis_index("dp")
    shards = lax.axis_size("dp")
    groups = partner.shape[1]
    aligned = shards == 16 and (layer_rows.shape[2] // shards) % 16 == 0
    layout = shards if aligned else 16
    half = groups // 2
    width = layer_rows.shape[2]
    slot_rows = layer_rows.shape[1] // groups
    inner_width = w_in.shape[1]
    slots = (groups, slot_rows, width)
    rows = layer_rows[0].reshape(slots)
    cot = cotangent[0].reshape(slots)
    cut = half // 2
    LINE.clear()
    sent = gather_sent(partner[0], rows, half, 0, cut)
    got_a = flipped(sent, "mod", 1)
    sent = gather_sent(partner[0], rows, half, cut, half - cut)
    got_b = flipped(sent, "mod", 1)
    sent_cot = gather_sent(partner[0], cot, half, 0, half)
    got_a, sent_cot, row_live, partner = lax.optimization_barrier(
        (got_a, sent_cot, row_live, partner)
    )
    far_cot = flipped(sent_cot, "mod", 1)
    spot = place if aligned else 0 * place
    scalars = jnp.concatenate(
        [partner[0], jnp.stack([side, spot & 1, spot >> 1]).astype(jnp.int32)]
    )

    live = row_live.reshape(2, groups, slot_rows)
    words_live = lax.dynamic_slice_in_dim(live[0], side * half, half, 0)
    region_live = live[1][lax.dynamic_slice_in_dim(partner[0], side * half, half, 0)]
    is_first = side == 0
    seen = jnp.concatenate(
        [
            jnp.where(is_first, words_live, region_live),
            jnp.where(is_first, region_live, words_live),
        ],
        1,
    )[:, None, :]

    w_qkv, w_out, w_in, w_back = fetch(scalars, (w_qkv, w_out, w_in, w_back))
    heads_weights = (w_qkv, b_qv, w_out, norm_gains, bias_rows)
    joined, mixed, probs, context, normed, root = attention_forward(
        scalars, rows, (got_a, got_b), seen, heads_weights
    )
    feed_weights = (w_in, b_in.reshape(1, inner_width), w_back, norm_gains, bias_rows)
    slope, branch, out_kept, out_far, sums_two, *back = feed_forward(
        scalars, normed, cot, far_cot, feed_weights, half, layout, groups
    )
    out_back = flipped(out_far, "mod", 1)
    back_weights = (w_in, w_back, norm_gains, bias_rows)
    attn_weights = (w_out, w_qkv)
    path, other = (0, 1, 2), (1, 0, 2)
    if aligned:
        back = Shards(*back, path)
        back.step()
    low_attn, sums_one, inner_sum, *inner = feed_backward(
        scalars,
        branch,
        slope,
        normed,
        root,
        context,
        back_weights,
        layout,
        groups,
        (other, path),
    )
    shard = width // shards
    count = inner_width // width
    inner_sum = inner_sum[0].reshape(shards, count, shard).transpose(1, 0, 2).reshape(count, width)
    if aligned:
        back.step()
        out_back = in_turn(out_back)
        pause(scalars)
        inner_a, inner_b = Shards(*inner[:2], other), Shards(*inner[2:], path)
        inner_a.step()
        inner_b.step()
    attn_kept = (low_attn, mixed, probs, joined)
    d_mixed, sums_qv, *qkv_a = attention_backward(
        scalars, attn_kept, attn_weights, 0, layout, groups, path
    )
    if aligned:
        back.step()
        inner_a.step()
        inner_b.step()
        pause(scalars)
        qkv_a = Shards(*qkv_a, path)
        qkv_a.step()
    sums = (sums_one, sums_two, inner_sum, sums_qv)
    d_kept, d_far, _, *qkv_b = attention_backward(
        scalars, attn_kept, attn_weights, 1, layout, groups, path, d_mixed, sums
    )
    d_back = flipped(d_far, "mod", 1)
    if aligned:
        qkv_b = Shards(*qkv_b, path)
        inner_b.step()
        qkv_b.step()
        qkv_a.step()
        inner_a.step()
        back.step()
        out_rows = scatter_home(scalars, out_kept, out_back, half).reshape(1, -1, width)
        qkv_b.step()
        qkv_a.step()
        inner_b.step()
        qkv_b.step()
        inner_a.step()
        grad_back = back.result()
        grad_rows = scatter_home(scalars, d_kept, d_back, half).reshape(1, -1, width)
        qkv_a.step()
        qkv_b.step()
        inner_a, inner_b = inner_a.result(), inner_b.result()
        grad_qkv, *small = finish_qkv(scalars, qkv_a, qkv_b, width, count)
    else:
        out_rows = scatter_home(scalars, out_kept, out_back, half).reshape(1, -1, width)
        grad_back = reduce_plain(*back, path)
        inner_a, inner_b = reduce_plain(*inner[:2], other), reduce_plain(*inner[2:], path)
        qkv_a, qkv_b = reduce_plain(*qkv_a, path), reduce_plain(*qkv_b, path)
        grad_rows = scatter_home(scalars, d_kept, d_back, half).reshape(1, -1, width)
        columns = (qkv_a.shape[1] // 3, (qkv_b.shape[1] - 128) // 3)
        thirds = []
        for third in range(3):
            for part, wide in zip((qkv_a, qkv_b), columns):
                thirds.append(part[:, third * wide : (third + 1) * wide])
        grad_qkv = jnp.concatenate(thirds, 1)
        small = qkv_b[:, 3 * columns[1] :].T
        small = small[0:2], small[2:4], small[4:8], small[8 : 8 + count]
    turn = inner_width - inner_a.shape[1]
    return (
        out_rows,
        grad_rows,
        grad_qkv,
        small[0],
        inner_b[:, turn:],
        small[1],
        small[2],
        jnp.concatenate([inner_a, inner_b[:, :turn]], 1),
        small[3].reshape(-1),
        grad_back,
    )


def solution(mesh):
    return jax.shard_map(
        body,
        mesh=mesh,
        in_specs=(
            P("mod", "dp", None),
            P("mod", "dp", None),
            P(None, "dp"),
            P("dp", None),
            P(),
            P(),
            P(),
            P(),
            P(),
            P(),
            P(),
            P(),
        ),
        out_specs=(
            P("mod", "dp", None),
            P("mod", "dp", None),
            P("dp", None),
            P(None, "dp"),
            P("dp", None),
            P(None, "dp"),
            P(None, "dp"),
            P("dp", None),
            P("dp"),
            P("dp", None),
        ),
        check_vma=False,
    )
```

```python
import functools

import jax
import jax.numpy as jnp
from jax import lax
from jax.experimental import pallas as pl
from jax.experimental.pallas import tpu as pltpu
from jax.sharding import PartitionSpec as P

HEADS = 12
EPSILON = 1e-12
F32 = jnp.float32
BF16 = jnp.bfloat16
VMEM_LIMIT = 26 * 2**20


def dot(left, right, left_dim=1, right_dim=0):
    return lax.dot_general(
        left, right, (((left_dim,), (right_dim,)), ((), ())), preferred_element_type=F32
    )


def flipped(value, axis, mask):
    pairs = [(source, source ^ mask) for source in range(lax.axis_size(axis))]
    return lax.ppermute(value, axis, pairs)


def params(limit=VMEM_LIMIT):
    return pltpu.CompilerParams(vmem_limit_bytes=limit)


def kept_slot(scalars, pair, half):
    groups = 2 * half
    side = scalars[groups]
    place = side * half + pair
    return jnp.where(side == 0, place, scalars[place])


def sent_slot(scalars, pair, half):
    groups = 2 * half
    side = scalars[groups]
    place = (1 - side) * half + pair
    return jnp.where(side == 0, place, scalars[place])


ANY = pl.BlockSpec(memory_space=pl.ANY)
RESIDENT = pl.BlockSpec(memory_space=pltpu.VMEM)
LINE = []


def call(kernel, scalars, operands, in_specs, out_specs, out_shape, grid, name, **more):
    after = LINE[1:]
    if LINE:
        after.append(pltpu.with_memory_space_constraint(LINE[0], pltpu.HBM))
    scratch = list(more.get("scratch", ()))
    taken, given = len(operands), len(out_shape)

    def wrapped(scalars_ref, *refs):
        outs = refs[taken + len(after) :]
        kernel(scalars_ref, *refs[:taken], *outs[:given], *outs[given + 1 :])

    placed = []
    for i, (array, spec) in enumerate(zip(operands, in_specs)):
        if i not in more.get("anywhere", ()):
            space = pltpu.VMEM if spec is RESIDENT else pltpu.HBM
            array = pltpu.with_memory_space_constraint(array, space)
        placed.append(array)
    shapes = [
        (pltpu.VMEM if spec is RESIDENT else pltpu.HBM)(shape.shape, shape.dtype)
        for shape, spec in zip(out_shape, out_specs)
    ]
    outs = pl.pallas_call(
        wrapped,
        grid_spec=pltpu.PrefetchScalarGridSpec(
            num_scalar_prefetch=1,
            grid=grid,
            in_specs=list(in_specs) + [ANY] * len(after),
            out_specs=list(out_specs) + [ANY],
            scratch_shapes=scratch,
        ),
        out_shape=shapes + [pltpu.HBM((8, 128), F32)],
        compiler_params=params(more.get("limit", VMEM_LIMIT)),
        cost_estimate=pl.CostEstimate(
            flops=more.get("work", 4 * 10**9), bytes_accessed=2**20, transcendentals=0
        ),
        name=name,
    )(scalars, *placed, *after)
    LINE[:] = [outs[-1]]
    return list(outs[:-1])


def fetch(scalars, arrays):
    count = len(arrays)

    def kernel(scalars_ref, *refs):
        sems = refs[-1]
        copies = [
            pltpu.make_async_copy(refs[i], refs[count + i], sems.at[i]) for i in range(count)
        ]
        for copy in copies:
            copy.start()
        for copy in copies:
            copy.wait()

    return call(
        kernel,
        scalars,
        list(arrays),
        [ANY] * count,
        [RESIDENT] * count,
        [jax.ShapeDtypeStruct(array.shape, array.dtype) for array in arrays],
        (1,),
        "fetch",
        work=10**7,
        scratch=[pltpu.SemaphoreType.DMA((count,))],
    )


def gather_sent(partner, rows, half, first, count):
    slot_rows, width = rows.shape[1:]

    partner = pltpu.with_memory_space_constraint(partner, pltpu.HBM)

    def kernel(partner_ref, rows_ref, out, sems):
        side = lax.axis_index("mod")
        copies = []
        for i in range(count):
            place = (1 - side) * half + first + i
            slot = jnp.where(side == 0, place, partner_ref[place])
            copies.append(pltpu.make_async_copy(rows_ref.at[slot], out.at[i], sems.at[i]))
        for copy in copies:
            copy.start()
        for copy in copies:
            copy.wait()

    shape = (count, slot_rows, width)
    return call(
        kernel,
        partner,
        [rows],
        [ANY],
        [pl.BlockSpec(shape, lambda i, s: (0, 0, 0))],
        [jax.ShapeDtypeStruct(shape, rows.dtype)],
        (1,),
        "gather_sent",
        work=10**7,
        scratch=[pltpu.SemaphoreType.DMA((count,))],
    )[0]


def scatter_home(scalars, kept, back, half):
    slot_rows, width = kept.shape[1:]

    def kernel(scalars_ref, kept_ref, back_ref, out, sems):
        copies = []
        for i in range(half):
            copies.append(
                pltpu.make_async_copy(
                    kept_ref.at[i], out.at[kept_slot(scalars_ref, i, half)], sems.at[0, i]
                )
            )
            copies.append(
                pltpu.make_async_copy(
                    back_ref.at[i], out.at[sent_slot(scalars_ref, i, half)], sems.at[1, i]
                )
            )
        for copy in copies:
            copy.start()
        for copy in copies:
            copy.wait()

    shape = (2 * half, slot_rows, width)
    return call(
        kernel,
        scalars,
        [kept, back],
        [ANY, ANY],
        [pl.BlockSpec(shape, lambda i, s: (0, 0, 0))],
        [jax.ShapeDtypeStruct(shape, kept.dtype)],
        (1,),
        "scatter_home",
        anywhere=(1,),
        work=10**7,
        scratch=[pltpu.SemaphoreType.DMA((2, half))],
    )[0]


def parts_of(blocks):
    early = 2 * blocks // 3
    return (0, early), (early, blocks - early)


def split_heads(value):
    low = lax.broadcasted_iota(jnp.int32, value.shape, 1) < value.shape[1] // 2
    zero = jnp.zeros_like(value)
    return jnp.concatenate([jnp.where(low, value, zero), jnp.where(low, zero, value)], 0)


def side_by_side(value):
    rows = value.shape[0] // 2
    return jnp.concatenate([value[:rows], value[rows:]], 1)


def row_sum(value):
    return jnp.sum(value, axis=0, keepdims=True)


def normal_form(value):
    centered = value - jnp.mean(value, axis=-1, keepdims=True)
    root = lax.rsqrt(jnp.mean(centered * centered, axis=-1, keepdims=True) + EPSILON)
    return centered * root, root


def normal_back(lifted, normed, root):
    return root * (
        lifted
        - jnp.mean(lifted, axis=-1, keepdims=True)
        - normed * jnp.mean(lifted * normed, axis=-1, keepdims=True)
    )


def whole(array):
    return pl.BlockSpec(
        array.shape, lambda *_: (0,) * array.ndim, pipeline_mode=pl.Buffered(1)
    )


def attention_forward(scalars, rows, received, live, weights):
    w_qkv, b_qv, w_out, norm_gains, bias_rows = weights
    slot_rows, width = rows.shape[1:]
    pairs = half = rows.shape[0] // 2
    turn = received[0].shape[0] // 2
    length = 2 * slot_rows
    duo = 2 * width // HEADS
    blocks = width // duo
    score_scale = (width // HEADS) ** (-0.5)

    def kernel(
        scalars_ref,
        kept_a,
        kept_b,
        got_a,
        got_b,
        live_ref,
        w_qkv_ref,
        b_qv_ref,
        w_out_ref,
        gains_ref,
        biases_ref,
        joined_out,
        mixed_out,
        probs_out,
        context_out,
        normed_out,
        root_out,
    ):
        step = pl.program_id(0)
        rows_here = pl.ds(pl.multiple_of(step * 2 * length, 2 * length), 2 * length)
        got = jnp.where(step < turn, got_a[...], got_b[...])
        joined = jnp.concatenate([kept_a[0], got[0], kept_b[0], got[1]], 0)
        joined_out[rows_here] = joined
        mixed = dot(joined, w_qkv_ref[...])
        queries = (mixed[:, :width] + b_qv_ref[0:1, :]).astype(BF16)
        queries = (queries.astype(F32) * score_scale).astype(BF16)
        keys = mixed[:, width : 2 * width].astype(BF16)
        values = (mixed[:, 2 * width :] + b_qv_ref[1:2, :]).astype(BF16)
        for first_block, count in parts_of(blocks):
            cols = slice(first_block * duo, (first_block + count) * duo)
            at = 3 * first_block * duo
            for value in (queries, keys, values):
                mixed_out[:, at : at + count * duo] = value[:, cols]
                at += count * duo
        contexts = []
        for pair in range(2):
            seen = live_ref[pair] > 0
            span = slice(pair * length, (pair + 1) * length)
            heads = []
            for block in range(blocks):
                cols = slice(block * duo, (block + 1) * duo)
                scores = dot(split_heads(queries[span, cols]), keys[span, cols], 1, 1)
                scores = jnp.where(seen, scores, -1e30)
                powered = jnp.exp(scores - jnp.max(scores, axis=-1, keepdims=True))
                low_probs = powered * (1.0 / jnp.sum(powered, axis=-1, keepdims=True))
                low_probs = low_probs.astype(BF16)
                probs_out[pair, block] = low_probs
                heads.append(
                    dot(side_by_side(low_probs), split_heads(values[span, cols])).astype(BF16)
                )
            contexts.append(jnp.concatenate(heads, 1))
        context = jnp.concatenate(contexts, 0)
        context_out[rows_here] = context
        pre_one = joined.astype(F32) + dot(context, w_out_ref[...]) + biases_ref[0:1, :]
        normed, root = normal_form(pre_one)
        normed_out[rows_here] = normed.astype(BF16)
        root_out[rows_here] = jnp.broadcast_to(root, (2 * length, 128))

    slot = (1, slot_rows, width)
    two = (2, slot_rows, width)
    total = half * length
    return call(
        kernel,
        scalars,
        [rows, rows, *received, live, w_qkv, b_qv, w_out, norm_gains, bias_rows],
        [
            pl.BlockSpec(slot, lambda i, s: (kept_slot(s, 2 * i, half), 0, 0)),
            pl.BlockSpec(slot, lambda i, s: (kept_slot(s, 2 * i + 1, half), 0, 0)),
            pl.BlockSpec(two, lambda i, s: (jnp.minimum(i, turn - 1), 0, 0)),
            pl.BlockSpec(two, lambda i, s: (jnp.maximum(i - turn, 0), 0, 0)),
            pl.BlockSpec((2, 1, length), lambda i, s: (i, 0, 0)),
            RESIDENT,
            whole(b_qv),
            RESIDENT,
            whole(norm_gains),
            whole(bias_rows),
        ],
        [
            RESIDENT,
            pl.BlockSpec((2 * length, 3 * width), lambda i, s: (i, 0)),
            pl.BlockSpec((2, blocks, 2 * length, length), lambda i, s: (i, 0, 0, 0)),
            RESIDENT,
            RESIDENT,
            RESIDENT,
        ],
        [
            jax.ShapeDtypeStruct((total, width), BF16),
            jax.ShapeDtypeStruct((total, 3 * width), BF16),
            jax.ShapeDtypeStruct((half, blocks, 2 * length, length), BF16),
            jax.ShapeDtypeStruct((total, width), BF16),
            jax.ShapeDtypeStruct((total, width), BF16),
            jax.ShapeDtypeStruct((total, 128), F32),
        ],
        (pairs // 2,),
        "attention_forward",
        limit=16 * 2**20,
        work=4 * 10**10,
    )


def place_of(index, order):
    return sum(1 << bit for n, bit in enumerate(order) if index >> (len(order) - 1 - n) & 1)


def spread(grad, outs, scalars_ref, base, shard, order):
    core, place = scalars_ref[base + 1], scalars_ref[base + 2]
    for j in range(2 ** len(order)):
        row = (place ^ place_of(j, order)) * 2
        for out, which in zip(outs, (1 - core, core)):
            out[j] = grad[pl.ds(pl.multiple_of((row + which) * shard, 16), shard), :]


def feed_forward(scalars, normed, cot, far_cot, weights, half, shards, base):
    w_in, b_in, w_back, norm_gains, bias_rows = weights
    slot_rows, width = cot.shape[1:]
    inner_width = w_in.shape[1]
    length = 2 * slot_rows
    rows = 2 * length
    height = half * length
    steps = half // 2
    chunk = 768
    chunks = inner_width // chunk
    shard = inner_width // shards
    places = shards // 2
    part = 4 * shard
    parts = inner_width // part

    def kernel(
        scalars_ref,
        normed_ref,
        cot_a,
        cot_b,
        cot_far,
        w_in_ref,
        b_in_ref,
        w_back_ref,
        gains_ref,
        biases_ref,
        slope_out,
        branch_out,
        kept_out,
        far_out,
        sums_out,
        send,
        keep,
        held,
        acts,
        grad,
    ):
        step = pl.program_id(0)

        @pl.when(step == 0)
        def _():
            sums_out[...] = jnp.zeros_like(sums_out)

        def close(pre_two, row):
            scaled, root = normal_form(pre_two)
            output = (scaled * gains_ref[1:2, :] + biases_ref[3:4, :]).astype(BF16)
            for i in range(2):
                kept_out[i] = output[i * length : i * length + slot_rows]
                far_out[i] = output[i * length + slot_rows : (i + 1) * length]
            here = jnp.concatenate([cot_a[0], cot_far[0], cot_b[0], cot_far[1]], 0).astype(F32)
            d_two = normal_back(here * gains_ref[1:2, :], scaled, root)
            low = d_two.astype(BF16)
            branch_out[pl.ds(pl.multiple_of(row, rows), rows)] = low
            return jnp.concatenate([row_sum(here * scaled), row_sum(here), row_sum(d_two)], 0)

        def forward():
            here = pl.ds(pl.multiple_of(step * rows, rows), rows)
            hidden = normed_ref[here].astype(F32) * gains_ref[0:1, :] + biases_ref[1:2, :]
            low_hidden = hidden.astype(BF16)
            total = hidden + biases_ref[2:3, :]
            for j in range(chunks):
                cols = slice(j * chunk, (j + 1) * chunk)
                inner = dot(low_hidden, w_in_ref[:, cols]) + b_in_ref[:, cols]
                normal = 0.5 + 0.5 * lax.erf(inner * (0.5**0.5))
                low_act = (inner * normal).astype(BF16)
                density = jnp.exp(inner * inner * -0.5) * 0.3989422804014327
                acts[here, cols] = low_act
                slope_out[here, cols] = (normal + inner * density).astype(BF16)
                total = total + dot(low_act, w_back_ref[cols, :])
            return total

        @pl.when(step == 0)
        def _():
            held[...] = forward()

        @pl.when((step > 0) & (step < steps))
        def _():
            before = held[...]
            held[...] = forward()
            sums_out[0:3, :] += close(before, (step - 1) * rows)

        @pl.when(step == steps)
        def _():
            sums_out[0:3, :] += close(held[...], (step - 1) * rows)

        @pl.when(step >= steps)
        def _():
            start = pl.multiple_of((step - steps) * part, 128)
            grad[...] = dot(acts[:, pl.ds(start, part)], branch_out[...], 0, 0).astype(BF16)
            core, low = scalars_ref[base + 1], scalars_ref[base + 2] & 1
            for j in range(2):
                for out, which in ((send, 1 - core), (keep, core)):
                    row = ((low ^ j) * 2 + which) * shard
                    out[j, 0] = grad[pl.ds(pl.multiple_of(row, 16), shard), :]

    def behind(i):
        return jnp.clip(i - 1, 0, steps - 1)

    def slot(j):
        return pl.BlockSpec(
            (1, slot_rows, width), lambda i, s: (kept_slot(s, 2 * behind(i) + j, half), 0, 0)
        )

    duo = pl.BlockSpec((2, slot_rows, width), lambda i, s: (behind(i), 0, 0))

    def entry(i, s):
        apart = (s[base + 2] >> 1) ^ jnp.maximum(i - steps, 0)
        return 0, (apart & 1) * 2 + (apart >> 1), 0, 0

    grads = pl.BlockSpec((2, 1, shard, width), entry)
    return call(
        kernel,
        scalars,
        [normed, cot, cot, far_cot, w_in, b_in, w_back, norm_gains, bias_rows],
        [
            RESIDENT,
            slot(0),
            slot(1),
            duo,
            RESIDENT,
            whole(b_in),
            RESIDENT,
            whole(norm_gains),
            whole(bias_rows),
        ],
        [
            RESIDENT,
            RESIDENT,
            duo,
            duo,
            pl.BlockSpec((8, width), lambda i, s: (0, 0)),
            grads,
            grads,
        ],
        [
            jax.ShapeDtypeStruct((height, inner_width), BF16),
            jax.ShapeDtypeStruct((height, width), BF16),
            jax.ShapeDtypeStruct((half, slot_rows, width), BF16),
            jax.ShapeDtypeStruct((half, slot_rows, width), BF16),
            jax.ShapeDtypeStruct((8, width), F32),
            jax.ShapeDtypeStruct((2, places // 2, shard, width), BF16),
            jax.ShapeDtypeStruct((2, places // 2, shard, width), BF16),
        ],
        (steps + parts,),
        "feed_forward",
        limit=18 * 2**20,
        anywhere=(3,),
        scratch=[
            pltpu.VMEM((rows, width), F32),
            pltpu.VMEM((height, inner_width), BF16),
            pltpu.VMEM((part, width), BF16),
        ],
    )


def feed_backward(scalars, branch, slope, normed, root, context, weights, shards, base, orders):
    w_in, w_back, norm_gains, bias_rows = weights
    total, width = branch.shape
    inner_width = slope.shape[1]
    chunk = 768
    steps = inner_width // chunk
    turn = steps // 2
    shard = width // shards
    places = shards // 2
    piece = 128

    def kernel(
        scalars_ref,
        branch_ref,
        slope_ref,
        normed_ref,
        root_ref,
        context_ref,
        w_in_ref,
        w_back_ref,
        gains_ref,
        biases_ref,
        low_attn_out,
        sums_out,
        inner_sum_out,
        send_a,
        keep_a,
        send_b,
        keep_b,
        held,
        low_hidden,
        grad,
    ):
        step = pl.program_id(0)

        @pl.when(step == 0)
        def _():
            hidden = normed_ref[...].astype(F32) * gains_ref[0:1, :] + biases_ref[1:2, :]
            low_hidden[...] = hidden.astype(BF16)
            held[...] = branch_ref[...].astype(F32)

        @pl.when(step < steps)
        def _():
            cols = pl.ds(pl.multiple_of(step * chunk, chunk), chunk)
            sums = jnp.zeros((1, chunk), F32)
            lows = []
            for r in range(0, total, 256):
                span = slice(r, r + 256)
                d_inner = dot(branch_ref[span], w_back_ref[cols, :], 1, 1)
                d_inner = d_inner * slope_ref[span, cols].astype(F32)
                sums = sums + row_sum(d_inner)
                low = d_inner.astype(BF16)
                lows.append(low)
                held[span] += dot(low, w_in_ref[:, cols], 1, 1)
            inner_sum_out[...] = jnp.broadcast_to(sums, inner_sum_out.shape)
            grad[...] = dot(low_hidden[...], jnp.concatenate(lows, 0), 0, 0).astype(BF16)

        @pl.when(step == steps)
        def _():
            sums = [jnp.zeros((1, width), F32)] * 3
            lows = []
            for i in range(total // piece):
                span = slice(i * piece, (i + 1) * piece)
                d_hidden, scaled = held[span], normed_ref[span].astype(F32)
                d_one = normal_back(d_hidden * gains_ref[0:1, :], scaled, root_ref[span, 0:1])
                lows.append(d_one.astype(BF16))
                low_attn_out[span] = lows[-1]
                for j, term in enumerate((d_hidden * scaled, d_hidden, d_one)):
                    sums[j] = sums[j] + row_sum(term)
            sums_out[...] = jnp.concatenate(sums + [jnp.zeros((5, width), F32)], 0)
            grad[...] = dot(context_ref[...], jnp.concatenate(lows, 0), 0, 0).astype(BF16)

        @pl.when(step < turn)
        def _():
            spread(grad, (send_a, keep_a), scalars_ref, base, shard, orders[0])

        @pl.when(step >= turn)
        def _():
            spread(grad, (send_b, keep_b), scalars_ref, base, shard, orders[1])

    def now(i):
        return jnp.minimum(i, steps - 1)

    half_a = pl.BlockSpec((places, shard, chunk), lambda i, s: (0, 0, jnp.minimum(i, turn - 1)))
    half_b = pl.BlockSpec((places, shard, chunk), lambda i, s: (0, 0, jnp.maximum(i - turn, 0)))
    shape_a = jax.ShapeDtypeStruct((places, shard, turn * chunk), BF16)
    shape_b = jax.ShapeDtypeStruct((places, shard, (steps + 1 - turn) * chunk), BF16)
    return call(
        kernel,
        scalars,
        [branch, slope, normed, root, context, w_in, w_back, norm_gains, bias_rows],
        [
            RESIDENT,
            RESIDENT,
            RESIDENT,
            RESIDENT,
            RESIDENT,
            RESIDENT,
            RESIDENT,
            whole(norm_gains),
            whole(bias_rows),
        ],
        [
            RESIDENT,
            pl.BlockSpec((8, width), lambda i, s: (0, 0)),
            pl.BlockSpec((8, chunk), lambda i, s: (0, now(i))),
            half_a,
            half_a,
            half_b,
            half_b,
        ],
        [
            jax.ShapeDtypeStruct((total, width), BF16),
            jax.ShapeDtypeStruct((8, width), F32),
            jax.ShapeDtypeStruct((8, inner_width), F32),
            shape_a,
            shape_a,
            shape_b,
            shape_b,
        ],
        (steps + 1,),
        "feed_backward",
        limit=21 * 2**20,
        scratch=[
            pltpu.VMEM((total, width), F32),
            pltpu.VMEM((total, width), BF16),
            pltpu.VMEM((width, chunk), BF16),
        ],
    )


def attention_backward(scalars, kept, weights, part, shards, base, order, earlier=(), sums=()):
    low_attn, mixed, probs, joined = kept
    w_out, w_qkv = weights
    total, width = low_attn.shape
    pairs, blocks, _, length = probs.shape
    duo = width // blocks
    first_block, mine = parts_of(blocks)[part]
    span_cols = mine * duo
    slot_rows = length // 2
    score_scale = (width // HEADS) ** (-0.5)
    steps = pairs // 2
    shard = width // shards
    places = shards // 2
    last = part == 1
    columns = 3 * span_cols + (128 if last else 0)

    def kernel(
        scalars_ref,
        low_attn_ref,
        mixed_ref,
        probs_ref,
        joined_ref,
        w_out_ref,
        *refs,
    ):
        if last:
            w_qkv_ref, earlier_ref, one, two, inner, sums_ref = refs[:6]
            kept_out, far_out, sums_out, send, keep, held, grad = refs[6:]
        else:
            held, sums_out, send, keep, grad = refs
        step = pl.program_id(0)

        @pl.when(step == 0)
        def _():
            sums_out[...] = jnp.zeros_like(sums_out)

        here = pl.ds(pl.multiple_of(step * 2 * length, 2 * length), 2 * length)
        low_attn = low_attn_ref[here]
        w_out_rows = slice(first_block * duo, (first_block + mine) * duo)
        d_context = dot(low_attn, w_out_ref[w_out_rows, :], 1, 1).astype(BF16)
        mixed = mixed_ref[...]
        rows = []
        for pair in range(2):
            span = slice(pair * length, (pair + 1) * length)
            chosen = [probs_ref[pair, block] for block in range(mine)]
            parts = []
            for third in range(3):
                first = third * span_cols
                parts.append(
                    [
                        mixed[span, first + block * duo : first + (block + 1) * duo]
                        for block in range(mine)
                    ]
                )
            queries, keys, values = parts
            d_heads, d_probs, d_scores = [], [], []
            for block in range(mine):
                cols = slice(block * duo, (block + 1) * duo)
                d_heads.append(split_heads(d_context[span, cols]))
                d_probs.append(dot(d_heads[block], values[block], 1, 1))
            for block in range(mine):
                wide = chosen[block].astype(F32)
                mean = jnp.sum(wide * d_probs[block], axis=-1, keepdims=True)
                d_scores.append((wide * (d_probs[block] - mean)).astype(BF16))
            d_queries, d_keys, d_values = [], [], []
            for block in range(mine):
                scaled = dot(side_by_side(d_scores[block]), split_heads(keys[block])) * score_scale
                d_queries.append(scaled.astype(BF16))
                d_keys.append(dot(d_scores[block], split_heads(queries[block]), 0, 0).astype(BF16))
                d_values.append(dot(chosen[block], d_heads[block], 0, 0).astype(BF16))
            rows.append(jnp.concatenate(d_queries + d_keys + d_values, 1))
        d_mixed = jnp.concatenate(rows, 0)
        held[here] = d_mixed
        sums_out[0:1, :] += row_sum(d_mixed[:, :span_cols].astype(F32))
        sums_out[1:2, :] += row_sum(d_mixed[:, 2 * span_cols :].astype(F32))
        if last:
            d_rows = low_attn.astype(F32)
            before = earlier_ref.shape[1] // 3
            for third in range(3):
                full = [
                    earlier_ref[here, third * before : (third + 1) * before],
                    d_mixed[:, third * span_cols : (third + 1) * span_cols],
                ]
                cols = slice(third * width, (third + 1) * width)
                d_rows = d_rows + dot(jnp.concatenate(full, 1), w_qkv_ref[:, cols], 1, 1)
            d_rows = d_rows.astype(BF16)
            for i in range(2):
                kept_out[i] = d_rows[i * length : i * length + slot_rows]
                far_out[i] = d_rows[i * length + slot_rows : (i + 1) * length]

        @pl.when(step == steps - 1)
        def _():
            grad[:, : 3 * span_cols] = dot(joined_ref[...], held[...], 0, 0).astype(BF16)
            if last:
                first, second = sums_ref[0:2, :], sums_out[0:2, :]
                count = inner.shape[1] // width
                small = [jnp.concatenate([first, second], 1), one[0:1], two[0:1]]
                small += [one[2:3], one[1:2], two[2:3], two[1:2]]
                for at in range(count):
                    runs = [
                        inner[0:1, (start * count + at) * shard : (start * count + at + 1) * shard]
                        for start in range(shards)
                    ]
                    small.append(jnp.concatenate(runs, 1))
                small.append(jnp.zeros((120 - count, width), F32))
                grad[:, 3 * span_cols :] = jnp.concatenate(small, 0).T.astype(BF16)
            spread(grad, (send, keep), scalars_ref, base, shard, order)

    two_slots = pl.BlockSpec((2, slot_rows, width), lambda i, s: (i, 0, 0))
    operands = [low_attn, mixed, probs, joined, w_out]
    skip = first_block // mine
    in_specs = [
        RESIDENT,
        pl.BlockSpec((2 * length, 3 * span_cols), lambda i, s: (i, skip)),
        pl.BlockSpec((2, mine, 2 * length, length), lambda i, s: (i, skip, 0, 0)),
        RESIDENT,
        RESIDENT,
    ]
    grads = pl.BlockSpec((places, shard, columns), lambda i, s: (0, 0, 0))
    out_specs = [pl.BlockSpec((8, span_cols), lambda i, s: (0, 0)), grads, grads]
    out_shape = [
        jax.ShapeDtypeStruct((8, span_cols), F32),
        jax.ShapeDtypeStruct((places, shard, columns), BF16),
        jax.ShapeDtypeStruct((places, shard, columns), BF16),
    ]
    if last:
        operands += [w_qkv, earlier, *sums]
        in_specs += [RESIDENT, RESIDENT]
        in_specs += [whole(each) for each in sums]
        out_specs = [two_slots, two_slots] + out_specs
        out_shape = [jax.ShapeDtypeStruct((pairs, slot_rows, width), BF16)] * 2 + out_shape
    else:
        out_specs = [RESIDENT] + out_specs
        out_shape = [jax.ShapeDtypeStruct((total, 3 * span_cols), BF16)] + out_shape
    return call(
        kernel,
        scalars,
        operands,
        in_specs,
        out_specs,
        out_shape,
        (steps,),
        "attention_backward",
        limit=16 * 2**20,
        scratch=[pltpu.VMEM((total, 3 * span_cols), BF16)] * last
        + [pltpu.VMEM((width, columns), BF16)],
    )


def in_turn(value):
    value, *rest = lax.optimization_barrier((value, *LINE))
    LINE[:] = rest[:1]
    return value


def pause(scalars):
    def kernel(scalars_ref):
        del scalars_ref

    call(kernel, scalars, [], [], [], [], (1,), "pause", work=2 * 10**10)


class Shards:
    def __init__(self, send, keep, order):
        shard, width = send.shape[-2:]
        self.order = list(order)
        shape = (2 ** len(self.order), shard, width)
        self.held = [keep.reshape(shape)]
        self.coming = flipped(send, "dp", 1).reshape(shape)

    def step(self):
        self.held.append(in_turn(self.coming))
        count = self.coming.shape[0]
        first = count // 2 if self.order else 0
        total = None
        for array in self.held:
            array = lax.slice_in_dim(array, first, count, axis=0).astype(F32)
            total = array if total is None else total + array
        total = total.astype(BF16)
        if self.order:
            self.coming = flipped(total, "dp", 2 << self.order.pop(0))
        else:
            self.mine = lax.optimization_barrier(total[0])
            self.coming = flipped(self.mine, "mod", 1)
        LINE.append(total)

    def result(self):
        return self.mine.astype(F32) + in_turn(self.coming).astype(F32)


def finish_qkv(scalars, early, late, width, count):
    shard = early.mine.shape[0]
    widths = (early.mine.shape[1] // 3, (late.mine.shape[1] - 128) // 3)

    def kernel(scalars_ref, mine_a, coming_a, mine_b, coming_b, qkv, b_qv, gains, biases, inner):
        parts = [
            mine[...].astype(F32) + coming[...].astype(F32)
            for mine, coming in ((mine_a, coming_a), (mine_b, coming_b))
        ]
        at = 0
        for third in range(3):
            for part, columns in zip(parts, widths):
                qkv[:, at : at + columns] = part[:, third * columns : (third + 1) * columns]
                at += columns
        small = jnp.concatenate([parts[1][:, 3 * widths[1] :], jnp.zeros((128 - shard, 128), F32)], 0)
        small = small.T[:, :shard]
        b_qv[...] = small[0:2]
        gains[...] = small[2:4]
        biases[...] = small[4:8]
        inner[...] = small[8 : 8 + count]

    operands = [early.mine, early.coming, late.mine, late.coming]
    shapes = ((shard, 3 * width), (2, shard), (2, shard), (4, shard), (count, shard))
    return call(
        kernel,
        scalars,
        operands,
        [whole(array) for array in operands],
        [pl.BlockSpec(shape, lambda i, s: (0, 0)) for shape in shapes],
        [jax.ShapeDtypeStruct(shape, F32) for shape in shapes],
        (1,),
        "finish_qkv",
        anywhere=(0, 1, 2, 3),
    )


def reduce_plain(send, keep, order):
    shard, columns = send.shape[-2:]
    total = jnp.stack([keep.reshape(-1, shard, columns), send.reshape(-1, shard, columns)], 1)
    places = [place_of(j, order) for j in range(total.shape[0])]
    total = jnp.stack([total[places.index(j)] for j in range(total.shape[0])])
    total = total.reshape(-1, columns).astype(F32)
    share = lax.psum_scatter(total, "dp", scatter_dimension=0, tiled=True)
    return lax.psum(share.astype(BF16), "mod").astype(F32)


def body(
    layer_rows,
    cotangent,
    row_live,
    partner,
    w_qkv,
    b_qv,
    w_out,
    norm_gains,
    bias_rows,
    w_in,
    b_in,
    w_back,
):
    side = lax.axis_index("mod")
    place = lax.axis_index("dp")
    shards = lax.axis_size("dp")
    groups = partner.shape[1]
    aligned = shards == 16 and (layer_rows.shape[2] // shards) % 16 == 0
    layout = shards if aligned else 16
    half = groups // 2
    width = layer_rows.shape[2]
    slot_rows = layer_rows.shape[1] // groups
    inner_width = w_in.shape[1]
    slots = (groups, slot_rows, width)
    rows = layer_rows[0].reshape(slots)
    cot = cotangent[0].reshape(slots)
    cut = half // 2
    LINE.clear()
    sent = gather_sent(partner[0], rows, half, 0, cut)
    got_a = flipped(sent, "mod", 1)
    sent = gather_sent(partner[0], rows, half, cut, half - cut)
    got_b = flipped(sent, "mod", 1)
    sent_cot = gather_sent(partner[0], cot, half, 0, half)
    got_a, sent_cot, row_live, partner = lax.optimization_barrier(
        (got_a, sent_cot, row_live, partner)
    )
    far_cot = flipped(sent_cot, "mod", 1)
    spot = place if aligned else 0 * place
    scalars = jnp.concatenate(
        [partner[0], jnp.stack([side, spot & 1, spot >> 1]).astype(jnp.int32)]
    )

    live = row_live.reshape(2, groups, slot_rows)
    words_live = lax.dynamic_slice_in_dim(live[0], side * half, half, 0)
    region_live = live[1][lax.dynamic_slice_in_dim(partner[0], side * half, half, 0)]
    is_first = side == 0
    seen = jnp.concatenate(
        [
            jnp.where(is_first, words_live, region_live),
            jnp.where(is_first, region_live, words_live),
        ],
        1,
    )[:, None, :]

    w_qkv, w_out, w_in, w_back = fetch(scalars, (w_qkv, w_out, w_in, w_back))
    heads_weights = (w_qkv, b_qv, w_out, norm_gains, bias_rows)
    joined, mixed, probs, context, normed, root = attention_forward(
        scalars, rows, (got_a, got_b), seen, heads_weights
    )
    feed_weights = (w_in, b_in.reshape(1, inner_width), w_back, norm_gains, bias_rows)
    slope, branch, out_kept, out_far, sums_two, *back = feed_forward(
        scalars, normed, cot, far_cot, feed_weights, half, layout, groups
    )
    out_back = flipped(out_far, "mod", 1)
    back_weights = (w_in, w_back, norm_gains, bias_rows)
    attn_weights = (w_out, w_qkv)
    path, other = (0, 1, 2), (1, 0, 2)
    if aligned:
        back = Shards(*back, path)
        back.step()
    low_attn, sums_one, inner_sum, *inner = feed_backward(
        scalars,
        branch,
        slope,
        normed,
        root,
        context,
        back_weights,
        layout,
        groups,
        (path, other),
    )
    shard = width // shards
    count = inner_width // width
    if aligned:
        back.step()
        out_back = in_turn(out_back)
        pause(scalars)
        inner_a, inner_b = Shards(*inner[:2], path), Shards(*inner[2:], other)
        inner_a.step()
        inner_b.step()
    attn_kept = (low_attn, mixed, probs, joined)
    d_mixed, sums_qv, *qkv_a = attention_backward(
        scalars, attn_kept, attn_weights, 0, layout, groups, path
    )
    if aligned:
        back.step()
        inner_a.step()
        pause(scalars)
        qkv_a = Shards(*qkv_a, path)
        qkv_a.step()
    if layout != shards:
        inner_sum = inner_sum.reshape(8, shards, count, shard).transpose(0, 2, 1, 3)
        inner_sum = inner_sum.reshape(8, count, layout, width // layout).transpose(0, 2, 1, 3)
        inner_sum = inner_sum.reshape(8, inner_width)
    sums = (sums_one, sums_two, inner_sum, sums_qv)
    d_kept, d_far, _, *qkv_b = attention_backward(
        scalars, attn_kept, attn_weights, 1, layout, groups, path, d_mixed, sums
    )
    d_back = flipped(d_far, "mod", 1)
    if aligned:
        qkv_b = Shards(*qkv_b, path)
        back.step()
        inner_b.step()
        inner_a.step()
        qkv_b.step()
        qkv_a.step()
        out_rows = scatter_home(scalars, out_kept, out_back, half).reshape(1, -1, width)
        inner_b.step()
        qkv_b.step()
        inner_a.step()
        qkv_a.step()
        grad_back = back.result()
        qkv_b.step()
        inner_b.step()
        grad_rows = scatter_home(scalars, d_kept, d_back, half).reshape(1, -1, width)
        qkv_a.step()
        qkv_b.step()
        inner_a, inner_b = inner_a.result(), inner_b.result()
        grad_qkv, *small = finish_qkv(scalars, qkv_a, qkv_b, width, count)
    else:
        out_rows = scatter_home(scalars, out_kept, out_back, half).reshape(1, -1, width)
        grad_back = reduce_plain(*back, path)
        inner_a, inner_b = reduce_plain(*inner[:2], path), reduce_plain(*inner[2:], other)
        qkv_a, qkv_b = reduce_plain(*qkv_a, path), reduce_plain(*qkv_b, path)
        grad_rows = scatter_home(scalars, d_kept, d_back, half).reshape(1, -1, width)
        columns = (qkv_a.shape[1] // 3, (qkv_b.shape[1] - 128) // 3)
        thirds = []
        for third in range(3):
            for part, wide in zip((qkv_a, qkv_b), columns):
                thirds.append(part[:, third * wide : (third + 1) * wide])
        grad_qkv = jnp.concatenate(thirds, 1)
        small = qkv_b[:, 3 * columns[1] :].T
        small = small[0:2], small[2:4], small[4:8], small[8 : 8 + count]
    turn = inner_width - inner_a.shape[1]
    return (
        out_rows,
        grad_rows,
        grad_qkv,
        small[0],
        inner_b[:, turn:],
        small[1],
        small[2],
        jnp.concatenate([inner_a, inner_b[:, :turn]], 1),
        small[3].reshape(-1),
        grad_back,
    )


def solution(mesh):
    return jax.shard_map(
        body,
        mesh=mesh,
        in_specs=(
            P("mod", "dp", None),
            P("mod", "dp", None),
            P(None, "dp"),
            P("dp", None),
            P(),
            P(),
            P(),
            P(),
            P(),
            P(),
            P(),
            P(),
        ),
        out_specs=(
            P("mod", "dp", None),
            P("mod", "dp", None),
            P("dp", None),
            P(None, "dp"),
            P("dp", None),
            P(None, "dp"),
            P(None, "dp"),
            P("dp", None),
            P("dp"),
            P("dp", None),
        ),
        check_vma=False,
    )
```

```python
import functools

import jax
import jax.numpy as jnp
from jax import lax
from jax.experimental import pallas as pl
from jax.experimental.pallas import tpu as pltpu
from jax.sharding import PartitionSpec as P

HEADS = 12
EPSILON = 1e-12
F32 = jnp.float32
BF16 = jnp.bfloat16
VMEM_LIMIT = 26 * 2**20


def dot(left, right, left_dim=1, right_dim=0):
    return lax.dot_general(
        left, right, (((left_dim,), (right_dim,)), ((), ())), preferred_element_type=F32
    )


def flipped(value, axis, mask):
    pairs = [(source, source ^ mask) for source in range(lax.axis_size(axis))]
    return lax.ppermute(value, axis, pairs)


def params(limit=VMEM_LIMIT):
    return pltpu.CompilerParams(vmem_limit_bytes=limit)


def kept_slot(scalars, pair, half):
    groups = 2 * half
    side = scalars[groups]
    place = side * half + pair
    return jnp.where(side == 0, place, scalars[place])


def sent_slot(scalars, pair, half):
    groups = 2 * half
    side = scalars[groups]
    place = (1 - side) * half + pair
    return jnp.where(side == 0, place, scalars[place])


ANY = pl.BlockSpec(memory_space=pl.ANY)
RESIDENT = pl.BlockSpec(memory_space=pltpu.VMEM)
LINE = []


def call(kernel, scalars, operands, in_specs, out_specs, out_shape, grid, name, **more):
    after = LINE[1:]
    if LINE:
        after.append(pltpu.with_memory_space_constraint(LINE[0], pltpu.HBM))
    scratch = list(more.get("scratch", ()))
    taken, given = len(operands), len(out_shape)

    def wrapped(scalars_ref, *refs):
        outs = refs[taken + len(after) :]
        kernel(scalars_ref, *refs[:taken], *outs[:given], *outs[given + 1 :])

    placed = []
    for i, (array, spec) in enumerate(zip(operands, in_specs)):
        if i not in more.get("anywhere", ()):
            space = pltpu.VMEM if spec is RESIDENT else pltpu.HBM
            array = pltpu.with_memory_space_constraint(array, space)
        placed.append(array)
    shapes = [
        (pltpu.VMEM if spec is RESIDENT else pltpu.HBM)(shape.shape, shape.dtype)
        for shape, spec in zip(out_shape, out_specs)
    ]
    outs = pl.pallas_call(
        wrapped,
        grid_spec=pltpu.PrefetchScalarGridSpec(
            num_scalar_prefetch=1,
            grid=grid,
            in_specs=list(in_specs) + [ANY] * len(after),
            out_specs=list(out_specs) + [ANY],
            scratch_shapes=scratch,
        ),
        out_shape=shapes + [pltpu.HBM((8, 128), F32)],
        compiler_params=params(more.get("limit", VMEM_LIMIT)),
        cost_estimate=pl.CostEstimate(
            flops=more.get("work", 4 * 10**9), bytes_accessed=2**20, transcendentals=0
        ),
        name=name,
    )(scalars, *placed, *after)
    LINE[:] = [outs[-1]]
    return list(outs[:-1])


def fetch(scalars, arrays):
    count = len(arrays)

    def kernel(scalars_ref, *refs):
        sems = refs[-1]
        copies = [
            pltpu.make_async_copy(refs[i], refs[count + i], sems.at[i]) for i in range(count)
        ]
        for copy in copies:
            copy.start()
        for copy in copies:
            copy.wait()

    return call(
        kernel,
        scalars,
        list(arrays),
        [ANY] * count,
        [RESIDENT] * count,
        [jax.ShapeDtypeStruct(array.shape, array.dtype) for array in arrays],
        (1,),
        "fetch",
        work=10**7,
        scratch=[pltpu.SemaphoreType.DMA((count,))],
    )


def gather_sent(partner, rows, half, first, count):
    slot_rows, width = rows.shape[1:]

    partner = pltpu.with_memory_space_constraint(partner, pltpu.HBM)

    def kernel(partner_ref, rows_ref, out, sems):
        side = lax.axis_index("mod")
        copies = []
        for i in range(count):
            place = (1 - side) * half + first + i
            slot = jnp.where(side == 0, place, partner_ref[place])
            copies.append(pltpu.make_async_copy(rows_ref.at[slot], out.at[i], sems.at[i]))
        for copy in copies:
            copy.start()
        for copy in copies:
            copy.wait()

    shape = (count, slot_rows, width)
    return call(
        kernel,
        partner,
        [rows],
        [ANY],
        [pl.BlockSpec(shape, lambda i, s: (0, 0, 0))],
        [jax.ShapeDtypeStruct(shape, rows.dtype)],
        (1,),
        "gather_sent",
        work=10**7,
        scratch=[pltpu.SemaphoreType.DMA((count,))],
    )[0]


def scatter_home(scalars, kept, back, half):
    slot_rows, width = kept.shape[1:]

    def kernel(scalars_ref, kept_ref, back_ref, out, sems):
        copies = []
        for i in range(half):
            copies.append(
                pltpu.make_async_copy(
                    kept_ref.at[i], out.at[kept_slot(scalars_ref, i, half)], sems.at[0, i]
                )
            )
            copies.append(
                pltpu.make_async_copy(
                    back_ref.at[i], out.at[sent_slot(scalars_ref, i, half)], sems.at[1, i]
                )
            )
        for copy in copies:
            copy.start()
        for copy in copies:
            copy.wait()

    shape = (2 * half, slot_rows, width)
    return call(
        kernel,
        scalars,
        [kept, back],
        [ANY, ANY],
        [pl.BlockSpec(shape, lambda i, s: (0, 0, 0))],
        [jax.ShapeDtypeStruct(shape, kept.dtype)],
        (1,),
        "scatter_home",
        anywhere=(1,),
        work=2 * 10**10,
        scratch=[pltpu.SemaphoreType.DMA((2, half))],
    )[0]


def parts_of(blocks):
    early = 2 * blocks // 3
    return (0, early), (early, blocks - early)


def split_heads(value):
    low = lax.broadcasted_iota(jnp.int32, value.shape, 1) < value.shape[1] // 2
    zero = jnp.zeros_like(value)
    return jnp.concatenate([jnp.where(low, value, zero), jnp.where(low, zero, value)], 0)


def side_by_side(value):
    rows = value.shape[0] // 2
    return jnp.concatenate([value[:rows], value[rows:]], 1)


def row_sum(value):
    return jnp.sum(value, axis=0, keepdims=True)


def normal_form(value):
    centered = value - jnp.mean(value, axis=-1, keepdims=True)
    root = lax.rsqrt(jnp.mean(centered * centered, axis=-1, keepdims=True) + EPSILON)
    return centered * root, root


def normal_back(lifted, normed, root):
    return root * (
        lifted
        - jnp.mean(lifted, axis=-1, keepdims=True)
        - normed * jnp.mean(lifted * normed, axis=-1, keepdims=True)
    )


def whole(array):
    return pl.BlockSpec(
        array.shape, lambda *_: (0,) * array.ndim, pipeline_mode=pl.Buffered(1)
    )


def attention_forward(scalars, rows, received, live, weights):
    w_qkv, b_qv, w_out, norm_gains, bias_rows = weights
    slot_rows, width = rows.shape[1:]
    pairs = half = rows.shape[0] // 2
    turn = received[0].shape[0] // 2
    length = 2 * slot_rows
    duo = 2 * width // HEADS
    blocks = width // duo
    score_scale = (width // HEADS) ** (-0.5)

    def kernel(
        scalars_ref,
        kept_a,
        kept_b,
        got_a,
        got_b,
        live_ref,
        w_qkv_ref,
        b_qv_ref,
        w_out_ref,
        gains_ref,
        biases_ref,
        joined_out,
        mixed_out,
        probs_out,
        context_out,
        normed_out,
        root_out,
    ):
        step = pl.program_id(0)
        rows_here = pl.ds(pl.multiple_of(step * 2 * length, 2 * length), 2 * length)
        got = jnp.where(step < turn, got_a[...], got_b[...])
        joined = jnp.concatenate([kept_a[0], got[0], kept_b[0], got[1]], 0)
        joined_out[rows_here] = joined
        mixed = dot(joined, w_qkv_ref[...])
        queries = (mixed[:, :width] + b_qv_ref[0:1, :]).astype(BF16)
        queries = (queries.astype(F32) * score_scale).astype(BF16)
        keys = mixed[:, width : 2 * width].astype(BF16)
        values = (mixed[:, 2 * width :] + b_qv_ref[1:2, :]).astype(BF16)
        for first_block, count in parts_of(blocks):
            cols = slice(first_block * duo, (first_block + count) * duo)
            at = 3 * first_block * duo
            for value in (queries, keys, values):
                mixed_out[:, at : at + count * duo] = value[:, cols]
                at += count * duo
        contexts = []
        for pair in range(2):
            seen = live_ref[pair] > 0
            span = slice(pair * length, (pair + 1) * length)
            heads = []
            for block in range(blocks):
                cols = slice(block * duo, (block + 1) * duo)
                scores = dot(split_heads(queries[span, cols]), keys[span, cols], 1, 1)
                scores = jnp.where(seen, scores, -1e30)
                powered = jnp.exp(scores - jnp.max(scores, axis=-1, keepdims=True))
                low_probs = powered * (1.0 / jnp.sum(powered, axis=-1, keepdims=True))
                low_probs = low_probs.astype(BF16)
                probs_out[pair, block] = low_probs
                heads.append(
                    dot(side_by_side(low_probs), split_heads(values[span, cols])).astype(BF16)
                )
            contexts.append(jnp.concatenate(heads, 1))
        context = jnp.concatenate(contexts, 0)
        context_out[rows_here] = context
        pre_one = joined.astype(F32) + dot(context, w_out_ref[...]) + biases_ref[0:1, :]
        normed, root = normal_form(pre_one)
        normed_out[rows_here] = normed.astype(BF16)
        root_out[rows_here] = jnp.broadcast_to(root, (2 * length, 128))

    slot = (1, slot_rows, width)
    two = (2, slot_rows, width)
    total = half * length
    return call(
        kernel,
        scalars,
        [rows, rows, *received, live, w_qkv, b_qv, w_out, norm_gains, bias_rows],
        [
            pl.BlockSpec(slot, lambda i, s: (kept_slot(s, 2 * i, half), 0, 0)),
            pl.BlockSpec(slot, lambda i, s: (kept_slot(s, 2 * i + 1, half), 0, 0)),
            pl.BlockSpec(two, lambda i, s: (jnp.minimum(i, turn - 1), 0, 0)),
            pl.BlockSpec(two, lambda i, s: (jnp.maximum(i - turn, 0), 0, 0)),
            pl.BlockSpec((2, 1, length), lambda i, s: (i, 0, 0)),
            RESIDENT,
            whole(b_qv),
            RESIDENT,
            whole(norm_gains),
            whole(bias_rows),
        ],
        [
            RESIDENT,
            pl.BlockSpec((2 * length, 3 * width), lambda i, s: (i, 0)),
            pl.BlockSpec((2, blocks, 2 * length, length), lambda i, s: (i, 0, 0, 0)),
            RESIDENT,
            RESIDENT,
            RESIDENT,
        ],
        [
            jax.ShapeDtypeStruct((total, width), BF16),
            jax.ShapeDtypeStruct((total, 3 * width), BF16),
            jax.ShapeDtypeStruct((half, blocks, 2 * length, length), BF16),
            jax.ShapeDtypeStruct((total, width), BF16),
            jax.ShapeDtypeStruct((total, width), BF16),
            jax.ShapeDtypeStruct((total, 128), F32),
        ],
        (pairs // 2,),
        "attention_forward",
        limit=16 * 2**20,
        work=4 * 10**10,
    )


def place_of(index, order):
    return sum(1 << bit for n, bit in enumerate(order) if index >> (len(order) - 1 - n) & 1)


def spread(grad, outs, scalars_ref, base, shard, order):
    core, place = scalars_ref[base + 1], scalars_ref[base + 2]
    count = 2 ** len(order)
    for j in range(count):
        row = (place ^ place_of(j, order)) * 2
        for out, which in zip(outs, (1 - core, core)):
            if isinstance(out, tuple):
                out = out[2 * j // count].at[j % (count // 2)]
            else:
                out = out.at[j]
            out[...] = grad[pl.ds(pl.multiple_of((row + which) * shard, 16), shard), :]


def feed_forward(scalars, normed, cot, far_cot, weights, half, shards, base):
    w_in, b_in, w_back, norm_gains, bias_rows = weights
    slot_rows, width = cot.shape[1:]
    inner_width = w_in.shape[1]
    length = 2 * slot_rows
    rows = 2 * length
    height = half * length
    steps = half // 2
    chunk = 768
    chunks = inner_width // chunk
    shard = inner_width // shards
    places = shards // 2
    part = 4 * shard
    parts = inner_width // part

    def kernel(
        scalars_ref,
        normed_ref,
        cot_a,
        cot_b,
        cot_far,
        w_in_ref,
        b_in_ref,
        w_back_ref,
        gains_ref,
        biases_ref,
        slope_out,
        branch_out,
        kept_out,
        far_out,
        sums_out,
        near,
        away,
        keep,
        held,
        acts,
        grad,
    ):
        step = pl.program_id(0)

        @pl.when(step == 0)
        def _():
            sums_out[...] = jnp.zeros_like(sums_out)

        def close(pre_two, row):
            scaled, root = normal_form(pre_two)
            output = (scaled * gains_ref[1:2, :] + biases_ref[3:4, :]).astype(BF16)
            for i in range(2):
                kept_out[i] = output[i * length : i * length + slot_rows]
                far_out[i] = output[i * length + slot_rows : (i + 1) * length]
            here = jnp.concatenate([cot_a[0], cot_far[0], cot_b[0], cot_far[1]], 0).astype(F32)
            d_two = normal_back(here * gains_ref[1:2, :], scaled, root)
            low = d_two.astype(BF16)
            branch_out[pl.ds(pl.multiple_of(row, rows), rows)] = low
            return jnp.concatenate([row_sum(here * scaled), row_sum(here), row_sum(d_two)], 0)

        def forward():
            here = pl.ds(pl.multiple_of(step * rows, rows), rows)
            hidden = normed_ref[here].astype(F32) * gains_ref[0:1, :] + biases_ref[1:2, :]
            low_hidden = hidden.astype(BF16)
            total = hidden + biases_ref[2:3, :]
            for j in range(chunks):
                cols = slice(j * chunk, (j + 1) * chunk)
                inner = dot(low_hidden, w_in_ref[:, cols]) + b_in_ref[:, cols]
                normal = 0.5 + 0.5 * lax.erf(inner * (0.5**0.5))
                low_act = (inner * normal).astype(BF16)
                density = jnp.exp(inner * inner * -0.5) * 0.3989422804014327
                acts[here, cols] = low_act
                slope_out[here, cols] = (normal + inner * density).astype(BF16)
                total = total + dot(low_act, w_back_ref[cols, :])
            return total

        @pl.when(step == 0)
        def _():
            held[...] = forward()

        @pl.when((step > 0) & (step < steps))
        def _():
            before = held[...]
            held[...] = forward()
            sums_out[0:3, :] += close(before, (step - 1) * rows)

        @pl.when(step == steps)
        def _():
            sums_out[0:3, :] += close(held[...], (step - 1) * rows)

        @pl.when(step >= steps)
        def _():
            start = pl.multiple_of((step - steps) * part, 128)
            grad[...] = dot(acts[:, pl.ds(start, part)], branch_out[...], 0, 0).astype(BF16)
            core, low = scalars_ref[base + 1], scalars_ref[base + 2] & 1
            for j in range(2):
                for out, which in (((near, away)[j].at[0, 0], 1 - core), (keep.at[j, 0], core)):
                    row = ((low ^ j) * 2 + which) * shard
                    out[...] = grad[pl.ds(pl.multiple_of(row, 16), shard), :]

    def behind(i):
        return jnp.clip(i - 1, 0, steps - 1)

    def slot(j):
        return pl.BlockSpec(
            (1, slot_rows, width), lambda i, s: (kept_slot(s, 2 * behind(i) + j, half), 0, 0)
        )

    duo = pl.BlockSpec((2, slot_rows, width), lambda i, s: (behind(i), 0, 0))

    def entry(i, s):
        apart = (s[base + 2] >> 1) ^ jnp.maximum(i - steps, 0)
        return 0, (apart & 1) * 2 + (apart >> 1), 0, 0

    grads = [pl.BlockSpec((count, 1, shard, width), entry) for count in (1, 1, 2)]
    return call(
        kernel,
        scalars,
        [normed, cot, cot, far_cot, w_in, b_in, w_back, norm_gains, bias_rows],
        [
            RESIDENT,
            slot(0),
            slot(1),
            duo,
            RESIDENT,
            whole(b_in),
            RESIDENT,
            whole(norm_gains),
            whole(bias_rows),
        ],
        [
            RESIDENT,
            RESIDENT,
            duo,
            duo,
            pl.BlockSpec((8, width), lambda i, s: (0, 0)),
            *grads,
        ],
        [
            jax.ShapeDtypeStruct((height, inner_width), BF16),
            jax.ShapeDtypeStruct((height, width), BF16),
            jax.ShapeDtypeStruct((half, slot_rows, width), BF16),
            jax.ShapeDtypeStruct((half, slot_rows, width), BF16),
            jax.ShapeDtypeStruct((8, width), F32),
            jax.ShapeDtypeStruct((1, places // 2, shard, width), BF16),
            jax.ShapeDtypeStruct((1, places // 2, shard, width), BF16),
            jax.ShapeDtypeStruct((2, places // 2, shard, width), BF16),
        ],
        (steps + parts,),
        "feed_forward",
        limit=18 * 2**20,
        anywhere=(3,),
        scratch=[
            pltpu.VMEM((rows, width), F32),
            pltpu.VMEM((height, inner_width), BF16),
            pltpu.VMEM((part, width), BF16),
        ],
    )


def feed_backward(scalars, branch, slope, normed, root, weights, shards, base, order):
    w_in, w_back, norm_gains, bias_rows = weights
    total, width = branch.shape
    inner_width = slope.shape[1]
    chunk = 768
    steps = inner_width // chunk
    shard = width // shards
    places = shards // 2
    piece = 128

    def kernel(
        scalars_ref,
        branch_ref,
        slope_ref,
        normed_ref,
        root_ref,
        w_in_ref,
        w_back_ref,
        gains_ref,
        biases_ref,
        low_attn_out,
        sums_out,
        inner_sum_out,
        send,
        keep,
        held,
        low_hidden,
        grad,
    ):
        step = pl.program_id(0)

        @pl.when(step == 0)
        def _():
            hidden = normed_ref[...].astype(F32) * gains_ref[0:1, :] + biases_ref[1:2, :]
            low_hidden[...] = hidden.astype(BF16)
            held[...] = branch_ref[...].astype(F32)

        cols = pl.ds(pl.multiple_of(step * chunk, chunk), chunk)
        sums = jnp.zeros((1, chunk), F32)
        lows = []
        for r in range(0, total, 512):
            span = slice(r, r + 512)
            d_inner = dot(branch_ref[span], w_back_ref[cols, :], 1, 1)
            d_inner = d_inner * slope_ref[span, cols].astype(F32)
            sums = sums + row_sum(d_inner)
            low = d_inner.astype(BF16)
            lows.append(low)
            held[span] += dot(low, w_in_ref[:, cols], 1, 1)
        inner_sum_out[...] = jnp.broadcast_to(sums, inner_sum_out.shape)
        grad[...] = dot(low_hidden[...], jnp.concatenate(lows, 0), 0, 0).astype(BF16)

        spread(grad, (send, keep), scalars_ref, base, shard, order)

        @pl.when(step == steps - 1)
        def _():
            sums = [jnp.zeros((1, width), F32)] * 3
            for i in range(total // piece):
                span = slice(i * piece, (i + 1) * piece)
                d_hidden, scaled = held[span], normed_ref[span].astype(F32)
                d_one = normal_back(d_hidden * gains_ref[0:1, :], scaled, root_ref[span, 0:1])
                low_attn_out[span] = d_one.astype(BF16)
                for j, term in enumerate((d_hidden * scaled, d_hidden, d_one)):
                    sums[j] = sums[j] + row_sum(term)
            sums_out[...] = jnp.concatenate(sums + [jnp.zeros((5, width), F32)], 0)
    grads = pl.BlockSpec(
        (places, shard, chunk), lambda i, s: (0, 0, i ^ (s[base + 3] * (steps // 2)))
    )
    shape = jax.ShapeDtypeStruct((places, shard, inner_width), BF16)
    return call(
        kernel,
        scalars,
        [branch, slope, normed, root, w_in, w_back, norm_gains, bias_rows],
        [
            RESIDENT,
            RESIDENT,
            RESIDENT,
            RESIDENT,
            RESIDENT,
            RESIDENT,
            whole(norm_gains),
            whole(bias_rows),
        ],
        [
            RESIDENT,
            pl.BlockSpec((8, width), lambda i, s: (0, 0)),
            pl.BlockSpec((8, chunk), lambda i, s: (0, i)),
            grads,
            grads,
        ],
        [
            jax.ShapeDtypeStruct((total, width), BF16),
            jax.ShapeDtypeStruct((8, width), F32),
            jax.ShapeDtypeStruct((8, inner_width), F32),
            shape,
            shape,
        ],
        (steps,),
        "feed_backward",
        limit=21 * 2**20,
        scratch=[
            pltpu.VMEM((total, width), F32),
            pltpu.VMEM((total, width), BF16),
            pltpu.VMEM((width, chunk), BF16),
        ],
    )


def attention_backward(scalars, kept, weights, part, shards, base, order, earlier=(), sums=()):
    low_attn, mixed, probs, joined, context = kept
    w_out, w_qkv = weights
    total, width = low_attn.shape
    pairs, blocks, _, length = probs.shape
    duo = width // blocks
    first_block, mine = parts_of(blocks)[part]
    span_cols = mine * duo
    slot_rows = length // 2
    score_scale = (width // HEADS) ** (-0.5)
    steps = pairs // 2
    shard = width // shards
    places = shards // 2
    last = part == 1
    columns = 3 * span_cols + (128 if last else width)

    def kernel(
        scalars_ref,
        low_attn_ref,
        mixed_ref,
        probs_ref,
        joined_ref,
        w_out_ref,
        *refs,
    ):
        if last:
            w_qkv_ref, earlier_ref, one, two, inner, sums_ref = refs[:6]
            kept_out, far_out, sums_out, near, away, keep, held, grad = refs[6:]
        else:
            context_ref, held, sums_out, near, away, keep, grad = refs
        step = pl.program_id(0)

        @pl.when(step == 0)
        def _():
            sums_out[...] = jnp.zeros_like(sums_out)

        here = pl.ds(pl.multiple_of(step * 2 * length, 2 * length), 2 * length)
        low_attn = low_attn_ref[here]
        w_out_rows = slice(first_block * duo, (first_block + mine) * duo)
        d_context = dot(low_attn, w_out_ref[w_out_rows, :], 1, 1).astype(BF16)
        mixed = mixed_ref[...]
        rows = []
        for pair in range(2):
            span = slice(pair * length, (pair + 1) * length)
            chosen = [probs_ref[pair, block] for block in range(mine)]
            parts = []
            for third in range(3):
                first = third * span_cols
                parts.append(
                    [
                        mixed[span, first + block * duo : first + (block + 1) * duo]
                        for block in range(mine)
                    ]
                )
            queries, keys, values = parts
            d_heads, d_probs, d_scores = [], [], []
            for block in range(mine):
                cols = slice(block * duo, (block + 1) * duo)
                d_heads.append(split_heads(d_context[span, cols]))
                d_probs.append(dot(d_heads[block], values[block], 1, 1))
            for block in range(mine):
                wide = chosen[block].astype(F32)
                mean = jnp.sum(wide * d_probs[block], axis=-1, keepdims=True)
                d_scores.append((wide * (d_probs[block] - mean)).astype(BF16))
            d_queries, d_keys, d_values = [], [], []
            for block in range(mine):
                scaled = dot(side_by_side(d_scores[block]), split_heads(keys[block])) * score_scale
                d_queries.append(scaled.astype(BF16))
                d_keys.append(dot(d_scores[block], split_heads(queries[block]), 0, 0).astype(BF16))
                d_values.append(dot(chosen[block], d_heads[block], 0, 0).astype(BF16))
            rows.append(jnp.concatenate(d_queries + d_keys + d_values, 1))
        d_mixed = jnp.concatenate(rows, 0)
        held[here] = d_mixed
        sums_out[0:1, :] += row_sum(d_mixed[:, :span_cols].astype(F32))
        sums_out[1:2, :] += row_sum(d_mixed[:, 2 * span_cols :].astype(F32))
        if last:
            d_rows = low_attn.astype(F32)
            before = earlier_ref.shape[1] // 3
            for third in range(3):
                full = [
                    earlier_ref[here, third * before : (third + 1) * before],
                    d_mixed[:, third * span_cols : (third + 1) * span_cols],
                ]
                cols = slice(third * width, (third + 1) * width)
                d_rows = d_rows + dot(jnp.concatenate(full, 1), w_qkv_ref[:, cols], 1, 1)
            d_rows = d_rows.astype(BF16)
            for i in range(2):
                kept_out[i] = d_rows[i * length : i * length + slot_rows]
                far_out[i] = d_rows[i * length + slot_rows : (i + 1) * length]

        @pl.when(step == steps - 1)
        def _():
            grad[:, : 3 * span_cols] = dot(joined_ref[...], held[...], 0, 0).astype(BF16)
            if last:
                first, second = sums_ref[0:2, :], sums_out[0:2, :]
                count = inner.shape[1] // width
                small = [jnp.concatenate([first, second], 1), one[0:1], two[0:1]]
                small += [one[2:3], one[1:2], two[2:3], two[1:2]]
                for at in range(count):
                    runs = [
                        inner[0:1, (start * count + at) * shard : (start * count + at + 1) * shard]
                        for start in range(shards)
                    ]
                    small.append(jnp.concatenate(runs, 1))
                small.append(jnp.zeros((120 - count, width), F32))
                grad[:, 3 * span_cols :] = jnp.concatenate(small, 0).T.astype(BF16)
            else:
                outer = dot(context_ref[...], low_attn_ref[...], 0, 0)
                grad[:, 3 * span_cols :] = outer.astype(BF16)
            spread(grad, ((near, away), keep), scalars_ref, base, shard, order)

    two_slots = pl.BlockSpec((2, slot_rows, width), lambda i, s: (i, 0, 0))
    operands = [low_attn, mixed, probs, joined, w_out]
    skip = first_block // mine
    in_specs = [
        RESIDENT,
        pl.BlockSpec((2 * length, 3 * span_cols), lambda i, s: (i, skip)),
        pl.BlockSpec((2, mine, 2 * length, length), lambda i, s: (i, skip, 0, 0)),
        RESIDENT,
        RESIDENT,
    ]
    out_specs = [pl.BlockSpec((8, span_cols), lambda i, s: (0, 0))]
    out_shape = [jax.ShapeDtypeStruct((8, span_cols), F32)]
    for entries in (places // 2, places // 2, places):
        shape = (entries, shard, columns)
        out_specs.append(pl.BlockSpec(shape, lambda i, s: (0, 0, 0)))
        out_shape.append(jax.ShapeDtypeStruct(shape, BF16))
    if last:
        operands += [w_qkv, earlier, *sums]
        in_specs += [RESIDENT, RESIDENT]
        in_specs += [whole(each) for each in sums]
        out_specs = [two_slots, two_slots] + out_specs
        out_shape = [jax.ShapeDtypeStruct((pairs, slot_rows, width), BF16)] * 2 + out_shape
    else:
        operands.append(context)
        in_specs.append(RESIDENT)
        out_specs = [RESIDENT] + out_specs
        out_shape = [jax.ShapeDtypeStruct((total, 3 * span_cols), BF16)] + out_shape
    return call(
        kernel,
        scalars,
        operands,
        in_specs,
        out_specs,
        out_shape,
        (steps,),
        "attention_backward",
        limit=16 * 2**20,
        scratch=[pltpu.VMEM((total, 3 * span_cols), BF16)] * last
        + [pltpu.VMEM((width, columns), BF16)],
    )


def in_turn(value):
    value, *rest = lax.optimization_barrier((value, *LINE))
    LINE[:] = rest[:1]
    return value


def pause(scalars):
    def kernel(scalars_ref):
        del scalars_ref

    call(kernel, scalars, [], [], [], [], (1,), "pause", work=2 * 10**10)


class Shards:
    def __init__(self, *arrays, order):
        *sends, keep = arrays
        shard, width = keep.shape[-2:]
        self.order = list(order)
        self.columns = width // 2 if "mod" in self.order else width
        count = 2 ** sum(step != "mod" for step in self.order)
        self.held = [(0, keep.reshape((count, shard, width)))]
        self.count = count
        shape = (count // len(sends), shard, width)
        self.coming = []
        for i in range(len(sends))[::-1]:
            self.coming.append((i * shape[0], flipped(sends[i], "dp", 1).reshape(shape)))

    def step(self):
        bit = self.order.pop(0) if self.order else None
        count = self.count
        first = count // 2 if bit in (0, 1, 2) else 0
        column = self.columns if bit == "mod" else 0
        late = []
        for at, array in self.coming:
            if at + array.shape[0] > first:
                self.held.append((at, in_turn(array)))
            else:
                late.append((at, array))
        total = None
        for at, array in self.held:
            if at >= count or at + array.shape[0] <= first:
                continue
            array = lax.slice_in_dim(array, first - at if first > at else 0, count - at, axis=0)
            array = lax.slice_in_dim(array, column, column + self.columns, axis=2)
            array = array.astype(F32)
            total = array if total is None else total + array
        total = total.astype(BF16)
        if bit is None:
            self.mine = lax.optimization_barrier(total[0])
            self.coming = flipped(self.mine, "mod", 1)
        elif bit == "mod":
            self.coming = late + [(0, flipped(total, "mod", 1))]
        else:
            self.coming = late + [(0, flipped(total, "dp", 2 << bit))]
            self.count = first
        LINE.append(total)

    def result(self):
        return self.mine.astype(F32) + in_turn(self.coming).astype(F32)


def finish(scalars, inner, early, late, width, inner_width, base):
    pieces = [inner, early, late]
    shard = early.mine.shape[0]
    count = inner_width // width
    turn = inner.mine.shape[1]
    widths = ((early.mine.shape[1] - width) // 3, (late.mine.shape[1] - 128) // 3)

    def kernel(scalars_ref, *refs):
        ins, (grad_in, grad_out, qkv, b_qv, gains, biases, b_in) = refs[:6], refs[6:]
        first = scalars_ref[base + 3] == 0
        grad_in[:, :turn] = jnp.where(first, ins[0][...], ins[1][...]).astype(F32)
        grad_in[:, turn:] = jnp.where(first, ins[1][...], ins[0][...]).astype(F32)
        parts = [ins[2 * i][...].astype(F32) + ins[2 * i + 1][...].astype(F32) for i in (1, 2)]
        grad_out[...] = parts[0][:, 3 * widths[0] :]
        at = 0
        for third in range(3):
            for part, columns in zip(parts, widths):
                qkv[:, at : at + columns] = part[:, third * columns : (third + 1) * columns]
                at += columns
        small = jnp.concatenate([parts[1][:, 3 * widths[1] :], jnp.zeros((128 - shard, 128), F32)], 0)
        small = small.T[:, :shard]
        b_qv[...] = small[0:2]
        gains[...] = small[2:4]
        biases[...] = small[4:8]
        b_in[...] = small[8 : 8 + count]

    operands = [each for piece in pieces for each in (piece.mine, piece.coming)]
    shapes = [(shard, inner_width), (shard, width), (shard, 3 * width)]
    shapes += [(2, shard), (2, shard), (4, shard), (count, shard)]
    return call(
        kernel,
        scalars,
        operands,
        [whole(array) for array in operands],
        [pl.BlockSpec(shape, lambda i, s: (0, 0)) for shape in shapes],
        [jax.ShapeDtypeStruct(shape, F32) for shape in shapes],
        (1,),
        "finish",
        anywhere=range(6),
    )


def reduce_plain(*arrays, order):
    *sends, keep = arrays
    shard, columns = keep.shape[-2:]
    send = jnp.concatenate([each.reshape(-1, shard, columns) for each in sends], 0)
    total = jnp.stack([keep.reshape(-1, shard, columns), send.reshape(-1, shard, columns)], 1)
    places = [place_of(j, order) for j in range(total.shape[0])]
    total = jnp.stack([total[places.index(j)] for j in range(total.shape[0])])
    total = total.reshape(-1, columns).astype(F32)
    share = lax.psum_scatter(total, "dp", scatter_dimension=0, tiled=True)
    return lax.psum(share.astype(BF16), "mod").astype(F32)


def body(
    layer_rows,
    cotangent,
    row_live,
    partner,
    w_qkv,
    b_qv,
    w_out,
    norm_gains,
    bias_rows,
    w_in,
    b_in,
    w_back,
):
    side = lax.axis_index("mod")
    place = lax.axis_index("dp")
    shards = lax.axis_size("dp")
    groups = partner.shape[1]
    aligned = shards == 16 and (layer_rows.shape[2] // shards) % 16 == 0
    layout = shards if aligned else 16
    half = groups // 2
    width = layer_rows.shape[2]
    slot_rows = layer_rows.shape[1] // groups
    inner_width = w_in.shape[1]
    slots = (groups, slot_rows, width)
    rows = layer_rows[0].reshape(slots)
    cot = cotangent[0].reshape(slots)
    cut = half // 2
    LINE.clear()
    sent = gather_sent(partner[0], rows, half, 0, cut)
    got_a = flipped(sent, "mod", 1)
    sent = gather_sent(partner[0], rows, half, cut, half - cut)
    got_b = flipped(sent, "mod", 1)
    sent_cot = gather_sent(partner[0], cot, half, 0, half)
    got_a, sent_cot, row_live, partner = lax.optimization_barrier(
        (got_a, sent_cot, row_live, partner)
    )
    far_cot = flipped(sent_cot, "mod", 1)
    spot = place if aligned else 0 * place
    scalars = jnp.concatenate(
        [partner[0], jnp.stack([side, spot & 1, spot >> 1, side * aligned]).astype(jnp.int32)]
    )

    live = row_live.reshape(2, groups, slot_rows)
    words_live = lax.dynamic_slice_in_dim(live[0], side * half, half, 0)
    region_live = live[1][lax.dynamic_slice_in_dim(partner[0], side * half, half, 0)]
    is_first = side == 0
    seen = jnp.concatenate(
        [
            jnp.where(is_first, words_live, region_live),
            jnp.where(is_first, region_live, words_live),
        ],
        1,
    )[:, None, :]

    w_qkv, w_out, w_in, w_back = fetch(scalars, (w_qkv, w_out, w_in, w_back))
    heads_weights = (w_qkv, b_qv, w_out, norm_gains, bias_rows)
    joined, mixed, probs, context, normed, root = attention_forward(
        scalars, rows, (got_a, got_b), seen, heads_weights
    )
    feed_weights = (w_in, b_in.reshape(1, inner_width), w_back, norm_gains, bias_rows)
    slope, branch, out_kept, out_far, sums_two, *back = feed_forward(
        scalars, normed, cot, far_cot, feed_weights, half, layout, groups
    )
    out_back = flipped(out_far, "mod", 1)
    back_weights = (w_in, w_back, norm_gains, bias_rows)
    attn_weights = (w_out, w_qkv)
    path = (0, 1, 2)
    if aligned:
        back = Shards(*back, order=path)
        back.step()
    low_attn, sums_one, inner_sum, *inner = feed_backward(
        scalars, branch, slope, normed, root, back_weights, layout, groups, path
    )
    shard = width // shards
    count = inner_width // width
    if aligned:
        back.step()
        out_back = in_turn(out_back)
        pause(scalars)
        inner = Shards(*inner, order=("mod", 0, 1, 2))
        inner.step()
    attn_kept = (low_attn, mixed, probs, joined, context)
    d_mixed, sums_qv, *qkv_a = attention_backward(
        scalars, attn_kept, attn_weights, 0, layout, groups, path
    )
    if aligned:
        back.step()
        out_rows = scatter_home(scalars, out_kept, out_back, half).reshape(1, -1, width)
        qkv_a = Shards(*qkv_a, order=path)
        qkv_a.step()
    if layout != shards:
        inner_sum = inner_sum.reshape(8, shards, count, shard).transpose(0, 2, 1, 3)
        inner_sum = inner_sum.reshape(8, count, layout, width // layout).transpose(0, 2, 1, 3)
        inner_sum = inner_sum.reshape(8, inner_width)
    sums = (sums_one, sums_two, inner_sum, sums_qv)
    d_kept, d_far, _, *qkv_b = attention_backward(
        scalars, attn_kept, attn_weights, 1, layout, groups, path, d_mixed, sums
    )
    d_back = flipped(d_far, "mod", 1)
    if aligned:
        qkv_b = Shards(*qkv_b, order=path)
        inner.step()
        back.step()
        qkv_a.step()
        qkv_b.step()
        inner.step()
        pause(scalars)
        qkv_a.step()
        qkv_b.step()
        grad_back = back.result()
        inner.step()
        pause(scalars)
        qkv_a.step()
        qkv_b.step()
        inner.step()
        grad_rows = scatter_home(scalars, d_kept, d_back, half).reshape(1, -1, width)
        qkv_b.step()
        grad_in, grad_out, grad_qkv, *small = finish(
            scalars, inner, qkv_a, qkv_b, width, inner_width, groups
        )
    else:
        out_rows = scatter_home(scalars, out_kept, out_back, half).reshape(1, -1, width)
        grad_back = reduce_plain(*back, order=path)
        grad_in = reduce_plain(*inner, order=path)
        qkv_a, qkv_b = reduce_plain(*qkv_a, order=path), reduce_plain(*qkv_b, order=path)
        grad_rows = scatter_home(scalars, d_kept, d_back, half).reshape(1, -1, width)
        columns = ((qkv_a.shape[1] - width) // 3, (qkv_b.shape[1] - 128) // 3)
        thirds = []
        for third in range(3):
            for part, wide in zip((qkv_a, qkv_b), columns):
                thirds.append(part[:, third * wide : (third + 1) * wide])
        grad_qkv = jnp.concatenate(thirds, 1)
        small = qkv_b[:, 3 * columns[1] :].T
        small = small[0:2], small[2:4], small[4:8], small[8 : 8 + count]
        grad_out = qkv_a[:, 3 * columns[0] :]
    return (
        out_rows,
        grad_rows,
        grad_qkv,
        small[0],
        grad_out,
        small[1],
        small[2],
        grad_in,
        small[3].reshape(-1),
        grad_back,
    )


def solution(mesh):
    return jax.shard_map(
        body,
        mesh=mesh,
        in_specs=(
            P("mod", "dp", None),
            P("mod", "dp", None),
            P(None, "dp"),
            P("dp", None),
            P(),
            P(),
            P(),
            P(),
            P(),
            P(),
            P(),
            P(),
        ),
        out_specs=(
            P("mod", "dp", None),
            P("mod", "dp", None),
            P("dp", None),
            P(None, "dp"),
            P("dp", None),
            P(None, "dp"),
            P(None, "dp"),
            P("dp", None),
            P("dp"),
            P("dp", None),
        ),
        check_vma=False,
    )
```

```python
import functools

import jax
import jax.numpy as jnp
from jax import lax
from jax.experimental import pallas as pl
from jax.experimental.pallas import tpu as pltpu
from jax.sharding import PartitionSpec as P

HEADS = 12
EPSILON = 1e-12
F32 = jnp.float32
BF16 = jnp.bfloat16
VMEM_LIMIT = 26 * 2**20


def dot(left, right, left_dim=1, right_dim=0):
    return lax.dot_general(
        left, right, (((left_dim,), (right_dim,)), ((), ())), preferred_element_type=F32
    )


def flipped(value, axis, mask):
    pairs = [(source, source ^ mask) for source in range(lax.axis_size(axis))]
    return lax.ppermute(value, axis, pairs)


def params(limit=VMEM_LIMIT):
    return pltpu.CompilerParams(vmem_limit_bytes=limit)


def kept_slot(scalars, pair, half):
    groups = 2 * half
    side = scalars[groups]
    place = side * half + pair
    return jnp.where(side == 0, place, scalars[place])


def sent_slot(scalars, pair, half):
    groups = 2 * half
    side = scalars[groups]
    place = (1 - side) * half + pair
    return jnp.where(side == 0, place, scalars[place])


ANY = pl.BlockSpec(memory_space=pl.ANY)
RESIDENT = pl.BlockSpec(memory_space=pltpu.VMEM)
LINE = []


def call(kernel, scalars, operands, in_specs, out_specs, out_shape, grid, name, **more):
    after = LINE[1:]
    if LINE:
        after.append(pltpu.with_memory_space_constraint(LINE[0], pltpu.HBM))
    scratch = list(more.get("scratch", ()))
    taken, given = len(operands), len(out_shape)

    def wrapped(scalars_ref, *refs):
        outs = refs[taken + len(after) :]
        kernel(scalars_ref, *refs[:taken], *outs[:given], *outs[given + 1 :])

    placed = []
    for i, (array, spec) in enumerate(zip(operands, in_specs)):
        if i not in more.get("anywhere", ()):
            space = pltpu.VMEM if spec is RESIDENT else pltpu.HBM
            array = pltpu.with_memory_space_constraint(array, space)
        placed.append(array)
    shapes = [
        (pltpu.VMEM if spec is RESIDENT else pltpu.HBM)(shape.shape, shape.dtype)
        for shape, spec in zip(out_shape, out_specs)
    ]
    outs = pl.pallas_call(
        wrapped,
        grid_spec=pltpu.PrefetchScalarGridSpec(
            num_scalar_prefetch=1,
            grid=grid,
            in_specs=list(in_specs) + [ANY] * len(after),
            out_specs=list(out_specs) + [ANY],
            scratch_shapes=scratch,
        ),
        out_shape=shapes + [pltpu.HBM((8, 128), F32)],
        compiler_params=params(more.get("limit", VMEM_LIMIT)),
        cost_estimate=pl.CostEstimate(
            flops=more.get("work", 4 * 10**9), bytes_accessed=2**20, transcendentals=0
        ),
        name=name,
    )(scalars, *placed, *after)
    LINE[:] = [outs[-1]]
    return list(outs[:-1])


def fetch(scalars, arrays):
    count = len(arrays)

    def kernel(scalars_ref, *refs):
        sems = refs[-1]
        copies = [
            pltpu.make_async_copy(refs[i], refs[count + i], sems.at[i]) for i in range(count)
        ]
        for copy in copies:
            copy.start()
        for copy in copies:
            copy.wait()

    return call(
        kernel,
        scalars,
        list(arrays),
        [ANY] * count,
        [RESIDENT] * count,
        [jax.ShapeDtypeStruct(array.shape, array.dtype) for array in arrays],
        (1,),
        "fetch",
        work=10**7,
        scratch=[pltpu.SemaphoreType.DMA((count,))],
    )


def gather_sent(partner, rows, half, first, count):
    slot_rows, width = rows.shape[1:]

    partner = pltpu.with_memory_space_constraint(partner, pltpu.HBM)

    def kernel(partner_ref, rows_ref, out, sems):
        side = lax.axis_index("mod")
        copies = []
        for i in range(count):
            place = (1 - side) * half + first + i
            slot = jnp.where(side == 0, place, partner_ref[place])
            copies.append(pltpu.make_async_copy(rows_ref.at[slot], out.at[i], sems.at[i]))
        for copy in copies:
            copy.start()
        for copy in copies:
            copy.wait()

    shape = (count, slot_rows, width)
    return call(
        kernel,
        partner,
        [rows],
        [ANY],
        [pl.BlockSpec(shape, lambda i, s: (0, 0, 0))],
        [jax.ShapeDtypeStruct(shape, rows.dtype)],
        (1,),
        "gather_sent",
        work=10**7,
        scratch=[pltpu.SemaphoreType.DMA((count,))],
    )[0]


def scatter_home(scalars, kept, back, half):
    slot_rows, width = kept.shape[1:]

    def kernel(scalars_ref, kept_ref, back_ref, out, sems):
        copies = []
        for i in range(half):
            copies.append(
                pltpu.make_async_copy(
                    kept_ref.at[i], out.at[kept_slot(scalars_ref, i, half)], sems.at[0, i]
                )
            )
            copies.append(
                pltpu.make_async_copy(
                    back_ref.at[i], out.at[sent_slot(scalars_ref, i, half)], sems.at[1, i]
                )
            )
        for copy in copies:
            copy.start()
        for copy in copies:
            copy.wait()

    shape = (2 * half, slot_rows, width)
    return call(
        kernel,
        scalars,
        [kept, back],
        [ANY, ANY],
        [pl.BlockSpec(shape, lambda i, s: (0, 0, 0))],
        [jax.ShapeDtypeStruct(shape, kept.dtype)],
        (1,),
        "scatter_home",
        anywhere=(1,),
        work=2 * 10**10,
        scratch=[pltpu.SemaphoreType.DMA((2, half))],
    )[0]


def parts_of(blocks):
    early = 2 * blocks // 3
    return (0, early), (early, blocks - early)


def split_heads(value):
    low = lax.broadcasted_iota(jnp.int32, value.shape, 1) < value.shape[1] // 2
    zero = jnp.zeros_like(value)
    return jnp.concatenate([jnp.where(low, value, zero), jnp.where(low, zero, value)], 0)


def side_by_side(value):
    rows = value.shape[0] // 2
    return jnp.concatenate([value[:rows], value[rows:]], 1)


def row_sum(value):
    return jnp.sum(value, axis=0, keepdims=True)


def normal_form(value):
    centered = value - jnp.mean(value, axis=-1, keepdims=True)
    root = lax.rsqrt(jnp.mean(centered * centered, axis=-1, keepdims=True) + EPSILON)
    return centered * root, root


def normal_back(lifted, normed, root):
    return root * (
        lifted
        - jnp.mean(lifted, axis=-1, keepdims=True)
        - normed * jnp.mean(lifted * normed, axis=-1, keepdims=True)
    )


def whole(array):
    return pl.BlockSpec(
        array.shape, lambda *_: (0,) * array.ndim, pipeline_mode=pl.Buffered(1)
    )


def attention_forward(scalars, rows, received, live, weights):
    w_qkv, b_qv, w_out, norm_gains, bias_rows = weights
    slot_rows, width = rows.shape[1:]
    pairs = half = rows.shape[0] // 2
    turn = received[0].shape[0] // 2
    length = 2 * slot_rows
    duo = 2 * width // HEADS
    blocks = width // duo
    score_scale = (width // HEADS) ** (-0.5)

    def kernel(
        scalars_ref,
        kept_a,
        kept_b,
        got_a,
        got_b,
        live_ref,
        w_qkv_ref,
        b_qv_ref,
        w_out_ref,
        gains_ref,
        biases_ref,
        joined_out,
        mixed_out,
        probs_out,
        context_out,
        normed_out,
        root_out,
    ):
        step = pl.program_id(0)
        rows_here = pl.ds(pl.multiple_of(step * 2 * length, 2 * length), 2 * length)
        got = jnp.where(step < turn, got_a[...], got_b[...])
        joined = jnp.concatenate([kept_a[0], got[0], kept_b[0], got[1]], 0)
        joined_out[rows_here] = joined
        mixed = dot(joined, w_qkv_ref[...])
        queries = (mixed[:, :width] + b_qv_ref[0:1, :]).astype(BF16)
        queries = (queries.astype(F32) * score_scale).astype(BF16)
        keys = mixed[:, width : 2 * width].astype(BF16)
        values = (mixed[:, 2 * width :] + b_qv_ref[1:2, :]).astype(BF16)
        for first_block, count in parts_of(blocks):
            cols = slice(first_block * duo, (first_block + count) * duo)
            at = 3 * first_block * duo
            for value in (queries, keys, values):
                mixed_out[:, at : at + count * duo] = value[:, cols]
                at += count * duo
        contexts = []
        for pair in range(2):
            seen = live_ref[pair] > 0
            span = slice(pair * length, (pair + 1) * length)
            heads = []
            for block in range(blocks):
                cols = slice(block * duo, (block + 1) * duo)
                scores = dot(split_heads(queries[span, cols]), keys[span, cols], 1, 1)
                scores = jnp.where(seen, scores, -1e30)
                powered = jnp.exp(scores - jnp.max(scores, axis=-1, keepdims=True))
                low_probs = powered * (1.0 / jnp.sum(powered, axis=-1, keepdims=True))
                low_probs = low_probs.astype(BF16)
                probs_out[pair, block] = low_probs
                heads.append(
                    dot(side_by_side(low_probs), split_heads(values[span, cols])).astype(BF16)
                )
            contexts.append(jnp.concatenate(heads, 1))
        context = jnp.concatenate(contexts, 0)
        context_out[rows_here] = context
        pre_one = joined.astype(F32) + dot(context, w_out_ref[...]) + biases_ref[0:1, :]
        normed, root = normal_form(pre_one)
        normed_out[rows_here] = normed.astype(BF16)
        root_out[rows_here] = jnp.broadcast_to(root, (2 * length, 128))

    slot = (1, slot_rows, width)
    two = (2, slot_rows, width)
    total = half * length
    return call(
        kernel,
        scalars,
        [rows, rows, *received, live, w_qkv, b_qv, w_out, norm_gains, bias_rows],
        [
            pl.BlockSpec(slot, lambda i, s: (kept_slot(s, 2 * i, half), 0, 0)),
            pl.BlockSpec(slot, lambda i, s: (kept_slot(s, 2 * i + 1, half), 0, 0)),
            pl.BlockSpec(two, lambda i, s: (jnp.minimum(i, turn - 1), 0, 0)),
            pl.BlockSpec(two, lambda i, s: (jnp.maximum(i - turn, 0), 0, 0)),
            pl.BlockSpec((2, 1, length), lambda i, s: (i, 0, 0)),
            RESIDENT,
            whole(b_qv),
            RESIDENT,
            whole(norm_gains),
            whole(bias_rows),
        ],
        [
            RESIDENT,
            pl.BlockSpec((2 * length, 3 * width), lambda i, s: (i, 0)),
            pl.BlockSpec((2, blocks, 2 * length, length), lambda i, s: (i, 0, 0, 0)),
            RESIDENT,
            RESIDENT,
            RESIDENT,
        ],
        [
            jax.ShapeDtypeStruct((total, width), BF16),
            jax.ShapeDtypeStruct((total, 3 * width), BF16),
            jax.ShapeDtypeStruct((half, blocks, 2 * length, length), BF16),
            jax.ShapeDtypeStruct((total, width), BF16),
            jax.ShapeDtypeStruct((total, width), BF16),
            jax.ShapeDtypeStruct((total, 128), F32),
        ],
        (pairs // 2,),
        "attention_forward",
        limit=16 * 2**20,
        work=4 * 10**10,
    )


def place_of(index, order):
    return sum(1 << bit for n, bit in enumerate(order) if index >> (len(order) - 1 - n) & 1)


def spread(grad, outs, scalars_ref, base, shard, order):
    core, place = scalars_ref[base + 1], scalars_ref[base + 2]
    count = 2 ** len(order)
    for j in range(count):
        row = (place ^ place_of(j, order)) * 2
        for out, which in zip(outs, (1 - core, core)):
            if isinstance(out, tuple):
                out = out[2 * j // count].at[j % (count // 2)]
            else:
                out = out.at[j]
            out[...] = grad[pl.ds(pl.multiple_of((row + which) * shard, 16), shard), :]


def feed_forward(scalars, normed, cot, far_cot, weights, half, shards, base):
    w_in, b_in, w_back, norm_gains, bias_rows = weights
    slot_rows, width = cot.shape[1:]
    inner_width = w_in.shape[1]
    length = 2 * slot_rows
    rows = 2 * length
    height = half * length
    steps = half // 2
    chunk = 768
    chunks = inner_width // chunk
    shard = inner_width // shards
    places = shards // 2
    part = 4 * shard
    parts = inner_width // part

    def kernel(
        scalars_ref,
        normed_ref,
        cot_a,
        cot_b,
        cot_far,
        w_in_ref,
        b_in_ref,
        w_back_ref,
        gains_ref,
        biases_ref,
        slope_out,
        branch_out,
        kept_out,
        far_out,
        sums_out,
        near,
        away,
        keep,
        held,
        acts,
        grad,
    ):
        step = pl.program_id(0)

        @pl.when(step == 0)
        def _():
            sums_out[...] = jnp.zeros_like(sums_out)

        def close(pre_two, row):
            scaled, root = normal_form(pre_two)
            output = (scaled * gains_ref[1:2, :] + biases_ref[3:4, :]).astype(BF16)
            for i in range(2):
                kept_out[i] = output[i * length : i * length + slot_rows]
                far_out[i] = output[i * length + slot_rows : (i + 1) * length]
            here = jnp.concatenate([cot_a[0], cot_far[0], cot_b[0], cot_far[1]], 0).astype(F32)
            d_two = normal_back(here * gains_ref[1:2, :], scaled, root)
            low = d_two.astype(BF16)
            branch_out[pl.ds(pl.multiple_of(row, rows), rows)] = low
            return jnp.concatenate([row_sum(here * scaled), row_sum(here), row_sum(d_two)], 0)

        def forward():
            here = pl.ds(pl.multiple_of(step * rows, rows), rows)
            hidden = normed_ref[here].astype(F32) * gains_ref[0:1, :] + biases_ref[1:2, :]
            low_hidden = hidden.astype(BF16)
            total = hidden + biases_ref[2:3, :]
            for j in range(chunks):
                cols = slice(j * chunk, (j + 1) * chunk)
                inner = dot(low_hidden, w_in_ref[:, cols]) + b_in_ref[:, cols]
                normal = 0.5 + 0.5 * lax.erf(inner * (0.5**0.5))
                low_act = (inner * normal).astype(BF16)
                density = jnp.exp(inner * inner * -0.5) * 0.3989422804014327
                acts[here, cols] = low_act
                slope_out[here, cols] = (normal + inner * density).astype(BF16)
                total = total + dot(low_act, w_back_ref[cols, :])
            return total

        @pl.when(step == 0)
        def _():
            held[...] = forward()

        @pl.when((step > 0) & (step < steps))
        def _():
            before = held[...]
            held[...] = forward()
            sums_out[0:3, :] += close(before, (step - 1) * rows)

        @pl.when(step == steps)
        def _():
            sums_out[0:3, :] += close(held[...], (step - 1) * rows)

        @pl.when(step >= steps)
        def _():
            start = pl.multiple_of((step - steps) * part, 128)
            grad[...] = dot(acts[:, pl.ds(start, part)], branch_out[...], 0, 0).astype(BF16)
            core, low = scalars_ref[base + 1], scalars_ref[base + 2] & 1
            for j in range(2):
                for out, which in (((near, away)[j].at[0, 0], 1 - core), (keep.at[j, 0], core)):
                    row = ((low ^ j) * 2 + which) * shard
                    out[...] = grad[pl.ds(pl.multiple_of(row, 16), shard), :]

    def behind(i):
        return jnp.clip(i - 1, 0, steps - 1)

    def slot(j):
        return pl.BlockSpec(
            (1, slot_rows, width), lambda i, s: (kept_slot(s, 2 * behind(i) + j, half), 0, 0)
        )

    duo = pl.BlockSpec((2, slot_rows, width), lambda i, s: (behind(i), 0, 0))

    def entry(i, s):
        apart = (s[base + 2] >> 1) ^ jnp.maximum(i - steps, 0)
        return 0, (apart & 1) * 2 + (apart >> 1), 0, 0

    grads = [pl.BlockSpec((count, 1, shard, width), entry) for count in (1, 1, 2)]
    return call(
        kernel,
        scalars,
        [normed, cot, cot, far_cot, w_in, b_in, w_back, norm_gains, bias_rows],
        [
            RESIDENT,
            slot(0),
            slot(1),
            duo,
            RESIDENT,
            whole(b_in),
            RESIDENT,
            whole(norm_gains),
            whole(bias_rows),
        ],
        [
            RESIDENT,
            RESIDENT,
            duo,
            duo,
            pl.BlockSpec((8, width), lambda i, s: (0, 0)),
            *grads,
        ],
        [
            jax.ShapeDtypeStruct((height, inner_width), BF16),
            jax.ShapeDtypeStruct((height, width), BF16),
            jax.ShapeDtypeStruct((half, slot_rows, width), BF16),
            jax.ShapeDtypeStruct((half, slot_rows, width), BF16),
            jax.ShapeDtypeStruct((8, width), F32),
            jax.ShapeDtypeStruct((1, places // 2, shard, width), BF16),
            jax.ShapeDtypeStruct((1, places // 2, shard, width), BF16),
            jax.ShapeDtypeStruct((2, places // 2, shard, width), BF16),
        ],
        (steps + parts,),
        "feed_forward",
        limit=18 * 2**20,
        anywhere=(3,),
        scratch=[
            pltpu.VMEM((rows, width), F32),
            pltpu.VMEM((height, inner_width), BF16),
            pltpu.VMEM((part, width), BF16),
        ],
    )


def feed_backward(scalars, branch, slope, normed, root, weights, shards, base, order):
    w_in, w_back, norm_gains, bias_rows = weights
    total, width = branch.shape
    inner_width = slope.shape[1]
    chunk = 768
    steps = inner_width // chunk
    shard = width // shards
    places = shards // 2
    piece = 128

    def kernel(
        scalars_ref,
        branch_ref,
        slope_ref,
        normed_ref,
        root_ref,
        w_in_ref,
        w_back_ref,
        gains_ref,
        biases_ref,
        low_attn_out,
        sums_out,
        inner_sum_out,
        send,
        keep,
        held,
        low_hidden,
        grad,
    ):
        step = pl.program_id(0)

        @pl.when(step == 0)
        def _():
            hidden = normed_ref[...].astype(F32) * gains_ref[0:1, :] + biases_ref[1:2, :]
            low_hidden[...] = hidden.astype(BF16)
            held[...] = branch_ref[...].astype(F32)

        cols = pl.ds(pl.multiple_of(step * chunk, chunk), chunk)
        sums = jnp.zeros((1, chunk), F32)
        lows = []
        for r in range(0, total, 512):
            span = slice(r, r + 512)
            d_inner = dot(branch_ref[span], w_back_ref[cols, :], 1, 1)
            d_inner = d_inner * slope_ref[span, cols].astype(F32)
            sums = sums + row_sum(d_inner)
            low = d_inner.astype(BF16)
            lows.append(low)
            held[span] += dot(low, w_in_ref[:, cols], 1, 1)
        inner_sum_out[...] = jnp.broadcast_to(sums, inner_sum_out.shape)
        grad[...] = dot(low_hidden[...], jnp.concatenate(lows, 0), 0, 0).astype(BF16)

        spread(grad, (send, keep), scalars_ref, base, shard, order)

        @pl.when(step == steps - 1)
        def _():
            sums = [jnp.zeros((1, width), F32)] * 3
            for i in range(total // piece):
                span = slice(i * piece, (i + 1) * piece)
                d_hidden, scaled = held[span], normed_ref[span].astype(F32)
                d_one = normal_back(d_hidden * gains_ref[0:1, :], scaled, root_ref[span, 0:1])
                low_attn_out[span] = d_one.astype(BF16)
                for j, term in enumerate((d_hidden * scaled, d_hidden, d_one)):
                    sums[j] = sums[j] + row_sum(term)
            sums_out[...] = jnp.concatenate(sums + [jnp.zeros((5, width), F32)], 0)
    grads = pl.BlockSpec(
        (places, shard, chunk), lambda i, s: (0, 0, i ^ (s[base + 3] * (steps // 2)))
    )
    shape = jax.ShapeDtypeStruct((places, shard, inner_width), BF16)
    return call(
        kernel,
        scalars,
        [branch, slope, normed, root, w_in, w_back, norm_gains, bias_rows],
        [
            RESIDENT,
            RESIDENT,
            RESIDENT,
            RESIDENT,
            RESIDENT,
            RESIDENT,
            whole(norm_gains),
            whole(bias_rows),
        ],
        [
            RESIDENT,
            pl.BlockSpec((8, width), lambda i, s: (0, 0)),
            pl.BlockSpec((8, chunk), lambda i, s: (0, i)),
            grads,
            grads,
        ],
        [
            jax.ShapeDtypeStruct((total, width), BF16),
            jax.ShapeDtypeStruct((8, width), F32),
            jax.ShapeDtypeStruct((8, inner_width), F32),
            shape,
            shape,
        ],
        (steps,),
        "feed_backward",
        limit=21 * 2**20,
        scratch=[
            pltpu.VMEM((total, width), F32),
            pltpu.VMEM((total, width), BF16),
            pltpu.VMEM((width, chunk), BF16),
        ],
    )


def attention_backward(scalars, kept, weights, part, shards, base, order, earlier=(), sums=()):
    low_attn, mixed, probs, joined, context = kept
    w_out, w_qkv = weights
    total, width = low_attn.shape
    pairs, blocks, _, length = probs.shape
    duo = width // blocks
    first_block, mine = parts_of(blocks)[part]
    span_cols = mine * duo
    slot_rows = length // 2
    score_scale = (width // HEADS) ** (-0.5)
    steps = pairs // 2
    shard = width // shards
    places = shards // 2
    last = part == 1
    columns = 3 * span_cols + (128 if last else width)

    def kernel(
        scalars_ref,
        low_attn_ref,
        mixed_ref,
        probs_ref,
        joined_ref,
        w_out_ref,
        *refs,
    ):
        if last:
            w_qkv_ref, earlier_ref, one, two, inner, sums_ref = refs[:6]
            kept_out, far_out, sums_out, near, away, keep, held, grad = refs[6:]
        else:
            context_ref, held, sums_out, near, away, keep, grad = refs
        step = pl.program_id(0)

        @pl.when(step == 0)
        def _():
            sums_out[...] = jnp.zeros_like(sums_out)

        here = pl.ds(pl.multiple_of(step * 2 * length, 2 * length), 2 * length)
        low_attn = low_attn_ref[here]
        w_out_rows = slice(first_block * duo, (first_block + mine) * duo)
        d_context = dot(low_attn, w_out_ref[w_out_rows, :], 1, 1).astype(BF16)
        mixed = mixed_ref[...]
        rows = []
        for pair in range(2):
            span = slice(pair * length, (pair + 1) * length)
            chosen = [probs_ref[pair, block] for block in range(mine)]
            parts = []
            for third in range(3):
                first = third * span_cols
                parts.append(
                    [
                        mixed[span, first + block * duo : first + (block + 1) * duo]
                        for block in range(mine)
                    ]
                )
            queries, keys, values = parts
            d_heads, d_probs, d_scores = [], [], []
            for block in range(mine):
                cols = slice(block * duo, (block + 1) * duo)
                d_heads.append(split_heads(d_context[span, cols]))
                d_probs.append(dot(d_heads[block], values[block], 1, 1))
            for block in range(mine):
                wide = chosen[block].astype(F32)
                mean = jnp.sum(wide * d_probs[block], axis=-1, keepdims=True)
                d_scores.append((wide * (d_probs[block] - mean)).astype(BF16))
            d_queries, d_keys, d_values = [], [], []
            for block in range(mine):
                scaled = dot(side_by_side(d_scores[block]), split_heads(keys[block])) * score_scale
                d_queries.append(scaled.astype(BF16))
                d_keys.append(dot(d_scores[block], split_heads(queries[block]), 0, 0).astype(BF16))
                d_values.append(dot(chosen[block], d_heads[block], 0, 0).astype(BF16))
            rows.append(jnp.concatenate(d_queries + d_keys + d_values, 1))
        d_mixed = jnp.concatenate(rows, 0)
        held[here] = d_mixed
        sums_out[0:1, :] += row_sum(d_mixed[:, :span_cols].astype(F32))
        sums_out[1:2, :] += row_sum(d_mixed[:, 2 * span_cols :].astype(F32))
        if last:
            d_rows = low_attn.astype(F32)
            before = earlier_ref.shape[1] // 3
            for third in range(3):
                full = [
                    earlier_ref[here, third * before : (third + 1) * before],
                    d_mixed[:, third * span_cols : (third + 1) * span_cols],
                ]
                cols = slice(third * width, (third + 1) * width)
                d_rows = d_rows + dot(jnp.concatenate(full, 1), w_qkv_ref[:, cols], 1, 1)
            d_rows = d_rows.astype(BF16)
            for i in range(2):
                kept_out[i] = d_rows[i * length : i * length + slot_rows]
                far_out[i] = d_rows[i * length + slot_rows : (i + 1) * length]

        @pl.when(step == steps - 1)
        def _():
            grad[:, : 3 * span_cols] = dot(joined_ref[...], held[...], 0, 0).astype(BF16)
            if last:
                first, second = sums_ref[0:2, :], sums_out[0:2, :]
                count = inner.shape[1] // width
                small = [jnp.concatenate([first, second], 1), one[0:1], two[0:1]]
                small += [one[2:3], one[1:2], two[2:3], two[1:2]]
                for at in range(count):
                    runs = [
                        inner[0:1, (start * count + at) * shard : (start * count + at + 1) * shard]
                        for start in range(shards)
                    ]
                    small.append(jnp.concatenate(runs, 1))
                small.append(jnp.zeros((120 - count, width), F32))
                grad[:, 3 * span_cols :] = jnp.concatenate(small, 0).T.astype(BF16)
            else:
                outer = dot(context_ref[...], low_attn_ref[...], 0, 0)
                grad[:, 3 * span_cols :] = outer.astype(BF16)
            spread(grad, ((near, away), keep), scalars_ref, base, shard, order)

    two_slots = pl.BlockSpec((2, slot_rows, width), lambda i, s: (i, 0, 0))
    operands = [low_attn, mixed, probs, joined, w_out]
    skip = first_block // mine
    in_specs = [
        RESIDENT,
        pl.BlockSpec((2 * length, 3 * span_cols), lambda i, s: (i, skip)),
        pl.BlockSpec((2, mine, 2 * length, length), lambda i, s: (i, skip, 0, 0)),
        RESIDENT,
        RESIDENT,
    ]
    out_specs = [pl.BlockSpec((8, span_cols), lambda i, s: (0, 0))]
    out_shape = [jax.ShapeDtypeStruct((8, span_cols), F32)]
    for entries in (places // 2, places // 2, places):
        shape = (entries, shard, columns)
        out_specs.append(pl.BlockSpec(shape, lambda i, s: (0, 0, 0)))
        out_shape.append(jax.ShapeDtypeStruct(shape, BF16))
    if last:
        operands += [w_qkv, earlier, *sums]
        in_specs += [RESIDENT, RESIDENT]
        in_specs += [whole(each) for each in sums]
        out_specs = [two_slots, two_slots] + out_specs
        out_shape = [jax.ShapeDtypeStruct((pairs, slot_rows, width), BF16)] * 2 + out_shape
    else:
        operands.append(context)
        in_specs.append(RESIDENT)
        out_specs = [RESIDENT] + out_specs
        out_shape = [jax.ShapeDtypeStruct((total, 3 * span_cols), BF16)] + out_shape
    return call(
        kernel,
        scalars,
        operands,
        in_specs,
        out_specs,
        out_shape,
        (steps,),
        "attention_backward",
        limit=16 * 2**20,
        scratch=[pltpu.VMEM((total, 3 * span_cols), BF16)] * last
        + [pltpu.VMEM((width, columns), BF16)],
    )


def in_turn(value):
    value, *rest = lax.optimization_barrier((value, *LINE))
    LINE[:] = rest[:1]
    return value


def pause(scalars):
    def kernel(scalars_ref):
        del scalars_ref

    call(kernel, scalars, [], [], [], [], (1,), "pause", work=2 * 10**10)


class Shards:
    def __init__(self, *arrays, order):
        *sends, keep = arrays
        shard, width = keep.shape[-2:]
        self.order = list(order)
        self.columns = width // 2 if "mod" in self.order else width
        count = 2 ** sum(step != "mod" for step in self.order)
        self.held = [(0, keep.reshape((count, shard, width)))]
        self.count = count
        shape = (count // len(sends), shard, width)
        self.coming = []
        for i in range(len(sends))[::-1]:
            self.coming.append((i * shape[0], flipped(sends[i], "dp", 1).reshape(shape)))

    def step(self):
        bit = self.order.pop(0) if self.order else None
        count = self.count
        first = count // 2 if bit in (0, 1, 2) else 0
        column = self.columns if bit == "mod" else 0
        late = []
        for at, array in self.coming:
            if at + array.shape[0] > first:
                self.held.append((at, in_turn(array)))
            else:
                late.append((at, array))
        total = None
        for at, array in self.held:
            if at >= count or at + array.shape[0] <= first:
                continue
            array = lax.slice_in_dim(array, first - at if first > at else 0, count - at, axis=0)
            array = lax.slice_in_dim(array, column, column + self.columns, axis=2)
            array = array.astype(F32)
            total = array if total is None else total + array
        total = total.astype(BF16)
        if bit is None:
            self.mine = lax.optimization_barrier(total[0])
            self.coming = flipped(self.mine, "mod", 1)
        elif bit == "mod":
            self.coming = late + [(0, flipped(total, "mod", 1))]
        else:
            self.coming = late + [(0, flipped(total, "dp", 2 << bit))]
            self.count = first
        LINE.append(total)

    def result(self):
        return self.mine.astype(F32) + in_turn(self.coming).astype(F32)


def finish(scalars, inner, early, late, width, inner_width, base):
    pieces = [inner, early, late]
    shard = early.mine.shape[0]
    count = inner_width // width
    turn = inner.mine.shape[1]
    widths = ((early.mine.shape[1] - width) // 3, (late.mine.shape[1] - 128) // 3)

    def kernel(scalars_ref, *refs):
        ins, (grad_in, grad_out, qkv, b_qv, gains, biases, b_in) = refs[:6], refs[6:]
        first = scalars_ref[base + 3] == 0
        grad_in[:, :turn] = jnp.where(first, ins[0][...], ins[1][...]).astype(F32)
        grad_in[:, turn:] = jnp.where(first, ins[1][...], ins[0][...]).astype(F32)
        parts = [ins[2 * i][...].astype(F32) + ins[2 * i + 1][...].astype(F32) for i in (1, 2)]
        grad_out[...] = parts[0][:, 3 * widths[0] :]
        at = 0
        for third in range(3):
            for part, columns in zip(parts, widths):
                qkv[:, at : at + columns] = part[:, third * columns : (third + 1) * columns]
                at += columns
        small = jnp.concatenate([parts[1][:, 3 * widths[1] :], jnp.zeros((128 - shard, 128), F32)], 0)
        small = small.T[:, :shard]
        b_qv[...] = small[0:2]
        gains[...] = small[2:4]
        biases[...] = small[4:8]
        b_in[...] = jnp.concatenate([small[8 + i : 9 + i] for i in range(count)], 1)

    operands = [each for piece in pieces for each in (piece.mine, piece.coming)]
    shapes = [(shard, inner_width), (shard, width), (shard, 3 * width)]
    shapes += [(2, shard), (2, shard), (4, shard), (1, count * shard)]
    return call(
        kernel,
        scalars,
        operands,
        [whole(array) for array in operands],
        [pl.BlockSpec(shape, lambda i, s: (0, 0)) for shape in shapes],
        [jax.ShapeDtypeStruct(shape, F32) for shape in shapes],
        (1,),
        "finish",
        anywhere=range(6),
    )


def reduce_plain(*arrays, order):
    *sends, keep = arrays
    shard, columns = keep.shape[-2:]
    send = jnp.concatenate([each.reshape(-1, shard, columns) for each in sends], 0)
    total = jnp.stack([keep.reshape(-1, shard, columns), send.reshape(-1, shard, columns)], 1)
    places = [place_of(j, order) for j in range(total.shape[0])]
    total = jnp.stack([total[places.index(j)] for j in range(total.shape[0])])
    total = total.reshape(-1, columns).astype(F32)
    share = lax.psum_scatter(total, "dp", scatter_dimension=0, tiled=True)
    return lax.psum(share.astype(BF16), "mod").astype(F32)


def body(
    layer_rows,
    cotangent,
    row_live,
    partner,
    w_qkv,
    b_qv,
    w_out,
    norm_gains,
    bias_rows,
    w_in,
    b_in,
    w_back,
):
    side = lax.axis_index("mod")
    place = lax.axis_index("dp")
    shards = lax.axis_size("dp")
    groups = partner.shape[1]
    aligned = shards == 16 and (layer_rows.shape[2] // shards) % 16 == 0
    layout = shards if aligned else 16
    half = groups // 2
    width = layer_rows.shape[2]
    slot_rows = layer_rows.shape[1] // groups
    inner_width = w_in.shape[1]
    slots = (groups, slot_rows, width)
    rows = layer_rows[0].reshape(slots)
    cot = cotangent[0].reshape(slots)
    cut = half // 2
    LINE.clear()
    sent = gather_sent(partner[0], rows, half, 0, cut)
    got_a = flipped(sent, "mod", 1)
    sent = gather_sent(partner[0], rows, half, cut, half - cut)
    got_b = flipped(sent, "mod", 1)
    sent_cot = gather_sent(partner[0], cot, half, 0, half)
    got_a, sent_cot, row_live, partner = lax.optimization_barrier(
        (got_a, sent_cot, row_live, partner)
    )
    far_cot = flipped(sent_cot, "mod", 1)
    spot = place if aligned else 0 * place
    scalars = jnp.concatenate(
        [partner[0], jnp.stack([side, spot & 1, spot >> 1, side * aligned]).astype(jnp.int32)]
    )

    live = row_live.reshape(2, groups, slot_rows)
    words_live = lax.dynamic_slice_in_dim(live[0], side * half, half, 0)
    region_live = live[1][lax.dynamic_slice_in_dim(partner[0], side * half, half, 0)]
    is_first = side == 0
    seen = jnp.concatenate(
        [
            jnp.where(is_first, words_live, region_live),
            jnp.where(is_first, region_live, words_live),
        ],
        1,
    )[:, None, :]

    w_qkv, w_out, w_in, w_back = fetch(scalars, (w_qkv, w_out, w_in, w_back))
    heads_weights = (w_qkv, b_qv, w_out, norm_gains, bias_rows)
    joined, mixed, probs, context, normed, root = attention_forward(
        scalars, rows, (got_a, got_b), seen, heads_weights
    )
    feed_weights = (w_in, b_in.reshape(1, inner_width), w_back, norm_gains, bias_rows)
    slope, branch, out_kept, out_far, sums_two, *back = feed_forward(
        scalars, normed, cot, far_cot, feed_weights, half, layout, groups
    )
    out_back = flipped(out_far, "mod", 1)
    back_weights = (w_in, w_back, norm_gains, bias_rows)
    attn_weights = (w_out, w_qkv)
    path = (0, 1, 2)
    if aligned:
        back = Shards(*back, order=path)
        back.step()
    low_attn, sums_one, inner_sum, *inner = feed_backward(
        scalars, branch, slope, normed, root, back_weights, layout, groups, path
    )
    shard = width // shards
    count = inner_width // width
    if aligned:
        back.step()
        out_back = in_turn(out_back)
        pause(scalars)
        inner = Shards(*inner, order=("mod", 0, 1, 2))
        inner.step()
    attn_kept = (low_attn, mixed, probs, joined, context)
    d_mixed, sums_qv, *qkv_a = attention_backward(
        scalars, attn_kept, attn_weights, 0, layout, groups, path
    )
    if aligned:
        back.step()
        out_rows = scatter_home(scalars, out_kept, out_back, half).reshape(1, -1, width)
        qkv_a = Shards(*qkv_a, order=path)
        qkv_a.step()
    if layout != shards:
        inner_sum = inner_sum.reshape(8, shards, count, shard).transpose(0, 2, 1, 3)
        inner_sum = inner_sum.reshape(8, count, layout, width // layout).transpose(0, 2, 1, 3)
        inner_sum = inner_sum.reshape(8, inner_width)
    sums = (sums_one, sums_two, inner_sum, sums_qv)
    d_kept, d_far, _, *qkv_b = attention_backward(
        scalars, attn_kept, attn_weights, 1, layout, groups, path, d_mixed, sums
    )
    d_back = flipped(d_far, "mod", 1)
    if aligned:
        qkv_b = Shards(*qkv_b, order=path)
        inner.step()
        back.step()
        qkv_a.step()
        qkv_b.step()
        inner.step()
        pause(scalars)
        qkv_a.step()
        qkv_b.step()
        grad_back = back.result()
        inner.step()
        grad_rows = scatter_home(scalars, d_kept, d_back, half).reshape(1, -1, width)
        qkv_a.step()
        qkv_b.step()
        inner.step()
        qkv_b.step()
        grad_in, grad_out, grad_qkv, *small = finish(
            scalars, inner, qkv_a, qkv_b, width, inner_width, groups
        )
    else:
        out_rows = scatter_home(scalars, out_kept, out_back, half).reshape(1, -1, width)
        grad_back = reduce_plain(*back, order=path)
        grad_in = reduce_plain(*inner, order=path)
        qkv_a, qkv_b = reduce_plain(*qkv_a, order=path), reduce_plain(*qkv_b, order=path)
        grad_rows = scatter_home(scalars, d_kept, d_back, half).reshape(1, -1, width)
        columns = ((qkv_a.shape[1] - width) // 3, (qkv_b.shape[1] - 128) // 3)
        thirds = []
        for third in range(3):
            for part, wide in zip((qkv_a, qkv_b), columns):
                thirds.append(part[:, third * wide : (third + 1) * wide])
        grad_qkv = jnp.concatenate(thirds, 1)
        small = qkv_b[:, 3 * columns[1] :].T
        small = small[0:2], small[2:4], small[4:8], small[8 : 8 + count]
        grad_out = qkv_a[:, 3 * columns[0] :]
    return (
        out_rows,
        grad_rows,
        grad_qkv,
        small[0],
        grad_out,
        small[1],
        small[2],
        grad_in,
        small[3].reshape(-1),
        grad_back,
    )


def solution(mesh):
    return jax.shard_map(
        body,
        mesh=mesh,
        in_specs=(
            P("mod", "dp", None),
            P("mod", "dp", None),
            P(None, "dp"),
            P("dp", None),
            P(),
            P(),
            P(),
            P(),
            P(),
            P(),
            P(),
            P(),
        ),
        out_specs=(
            P("mod", "dp", None),
            P("mod", "dp", None),
            P("dp", None),
            P(None, "dp"),
            P("dp", None),
            P(None, "dp"),
            P(None, "dp"),
            P("dp", None),
            P("dp"),
            P("dp", None),
        ),
        check_vma=False,
    )
```

```python
import functools

import jax
import jax.numpy as jnp
from jax import lax
from jax.experimental import pallas as pl
from jax.experimental.pallas import tpu as pltpu
from jax.sharding import PartitionSpec as P

HEADS = 12
EPSILON = 1e-12
F32 = jnp.float32
BF16 = jnp.bfloat16
VMEM_LIMIT = 26 * 2**20


def dot(left, right, left_dim=1, right_dim=0):
    return lax.dot_general(
        left, right, (((left_dim,), (right_dim,)), ((), ())), preferred_element_type=F32
    )


def flipped(value, axis, mask):
    pairs = [(source, source ^ mask) for source in range(lax.axis_size(axis))]
    return lax.ppermute(value, axis, pairs)


def params(limit=VMEM_LIMIT):
    return pltpu.CompilerParams(vmem_limit_bytes=limit)


def kept_slot(scalars, pair, half):
    groups = 2 * half
    side = scalars[groups]
    place = side * half + pair
    return jnp.where(side == 0, place, scalars[place])


def sent_slot(scalars, pair, half):
    groups = 2 * half
    side = scalars[groups]
    place = (1 - side) * half + pair
    return jnp.where(side == 0, place, scalars[place])


ANY = pl.BlockSpec(memory_space=pl.ANY)
RESIDENT = pl.BlockSpec(memory_space=pltpu.VMEM)
LINE = []


def call(kernel, scalars, operands, in_specs, out_specs, out_shape, grid, name, **more):
    after = LINE[1:]
    if LINE:
        after.append(pltpu.with_memory_space_constraint(LINE[0], pltpu.HBM))
    scratch = list(more.get("scratch", ()))
    taken, given = len(operands), len(out_shape)

    def wrapped(scalars_ref, *refs):
        outs = refs[taken + len(after) :]
        kernel(scalars_ref, *refs[:taken], *outs[:given], *outs[given + 1 :])

    placed = []
    for i, (array, spec) in enumerate(zip(operands, in_specs)):
        if i not in more.get("anywhere", ()):
            space = pltpu.VMEM if spec is RESIDENT else pltpu.HBM
            array = pltpu.with_memory_space_constraint(array, space)
        placed.append(array)
    shapes = [
        (pltpu.VMEM if spec is RESIDENT else pltpu.HBM)(shape.shape, shape.dtype)
        for shape, spec in zip(out_shape, out_specs)
    ]
    outs = pl.pallas_call(
        wrapped,
        grid_spec=pltpu.PrefetchScalarGridSpec(
            num_scalar_prefetch=1,
            grid=grid,
            in_specs=list(in_specs) + [ANY] * len(after),
            out_specs=list(out_specs) + [ANY],
            scratch_shapes=scratch,
        ),
        out_shape=shapes + [pltpu.HBM((8, 128), F32)],
        compiler_params=params(more.get("limit", VMEM_LIMIT)),
        cost_estimate=pl.CostEstimate(
            flops=more.get("work", 4 * 10**9), bytes_accessed=2**20, transcendentals=0
        ),
        name=name,
    )(scalars, *placed, *after)
    LINE[:] = [outs[-1]]
    return list(outs[:-1])


def fetch(scalars, arrays):
    count = len(arrays)

    def kernel(scalars_ref, *refs):
        sems = refs[-1]
        copies = [
            pltpu.make_async_copy(refs[i], refs[count + i], sems.at[i]) for i in range(count)
        ]
        for copy in copies:
            copy.start()
        for copy in copies:
            copy.wait()

    return call(
        kernel,
        scalars,
        list(arrays),
        [ANY] * count,
        [RESIDENT] * count,
        [jax.ShapeDtypeStruct(array.shape, array.dtype) for array in arrays],
        (1,),
        "fetch",
        work=10**7,
        scratch=[pltpu.SemaphoreType.DMA((count,))],
    )


def gather_sent(partner, rows, half, first, count):
    slot_rows, width = rows.shape[1:]

    partner = pltpu.with_memory_space_constraint(partner, pltpu.HBM)

    def kernel(partner_ref, rows_ref, out, sems):
        side = lax.axis_index("mod")
        copies = []
        for i in range(count):
            place = (1 - side) * half + first + i
            slot = jnp.where(side == 0, place, partner_ref[place])
            copies.append(pltpu.make_async_copy(rows_ref.at[slot], out.at[i], sems.at[i]))
        for copy in copies:
            copy.start()
        for copy in copies:
            copy.wait()

    shape = (count, slot_rows, width)
    return call(
        kernel,
        partner,
        [rows],
        [ANY],
        [pl.BlockSpec(shape, lambda i, s: (0, 0, 0))],
        [jax.ShapeDtypeStruct(shape, rows.dtype)],
        (1,),
        "gather_sent",
        work=10**7,
        scratch=[pltpu.SemaphoreType.DMA((count,))],
    )[0]


def scatter_home(scalars, kept, back, half):
    slot_rows, width = kept.shape[1:]

    def kernel(scalars_ref, kept_ref, back_ref, out, sems):
        copies = []
        for i in range(half):
            copies.append(
                pltpu.make_async_copy(
                    kept_ref.at[i], out.at[kept_slot(scalars_ref, i, half)], sems.at[0, i]
                )
            )
            copies.append(
                pltpu.make_async_copy(
                    back_ref.at[i], out.at[sent_slot(scalars_ref, i, half)], sems.at[1, i]
                )
            )
        for copy in copies:
            copy.start()
        for copy in copies:
            copy.wait()

    shape = (2 * half, slot_rows, width)
    return call(
        kernel,
        scalars,
        [kept, back],
        [ANY, ANY],
        [pl.BlockSpec(shape, lambda i, s: (0, 0, 0))],
        [jax.ShapeDtypeStruct(shape, kept.dtype)],
        (1,),
        "scatter_home",
        anywhere=(1,),
        work=2 * 10**10,
        scratch=[pltpu.SemaphoreType.DMA((2, half))],
    )[0]


def parts_of(blocks):
    early = blocks // 2
    return (0, early), (early, blocks - early)


def split_heads(value):
    low = lax.broadcasted_iota(jnp.int32, value.shape, 1) < value.shape[1] // 2
    zero = jnp.zeros_like(value)
    return jnp.concatenate([jnp.where(low, value, zero), jnp.where(low, zero, value)], 0)


def side_by_side(value):
    rows = value.shape[0] // 2
    return jnp.concatenate([value[:rows], value[rows:]], 1)


def row_sum(value):
    return jnp.sum(value, axis=0, keepdims=True)


def normal_form(value):
    centered = value - jnp.mean(value, axis=-1, keepdims=True)
    root = lax.rsqrt(jnp.mean(centered * centered, axis=-1, keepdims=True) + EPSILON)
    return centered * root, root


def normal_back(lifted, normed, root):
    return root * (
        lifted
        - jnp.mean(lifted, axis=-1, keepdims=True)
        - normed * jnp.mean(lifted * normed, axis=-1, keepdims=True)
    )


def whole(array):
    return pl.BlockSpec(
        array.shape, lambda *_: (0,) * array.ndim, pipeline_mode=pl.Buffered(1)
    )


def attention_forward(scalars, rows, received, live, weights):
    w_qkv, b_qv, w_out, norm_gains, bias_rows = weights
    slot_rows, width = rows.shape[1:]
    pairs = half = rows.shape[0] // 2
    turn = received[0].shape[0] // 2
    length = 2 * slot_rows
    duo = 2 * width // HEADS
    blocks = width // duo
    score_scale = (width // HEADS) ** (-0.5)

    def kernel(
        scalars_ref,
        kept_a,
        kept_b,
        got_a,
        got_b,
        live_ref,
        w_qkv_ref,
        b_qv_ref,
        w_out_ref,
        gains_ref,
        biases_ref,
        joined_out,
        mixed_out,
        probs_out,
        context_out,
        normed_out,
        root_out,
    ):
        step = pl.program_id(0)
        rows_here = pl.ds(pl.multiple_of(step * 2 * length, 2 * length), 2 * length)
        got = jnp.where(step < turn, got_a[...], got_b[...])
        joined = jnp.concatenate([kept_a[0], got[0], kept_b[0], got[1]], 0)
        joined_out[rows_here] = joined
        mixed = dot(joined, w_qkv_ref[...])
        queries = (mixed[:, :width] + b_qv_ref[0:1, :]).astype(BF16)
        queries = (queries.astype(F32) * score_scale).astype(BF16)
        keys = mixed[:, width : 2 * width].astype(BF16)
        values = (mixed[:, 2 * width :] + b_qv_ref[1:2, :]).astype(BF16)
        for first_block, count in parts_of(blocks):
            cols = slice(first_block * duo, (first_block + count) * duo)
            at = 3 * first_block * duo
            for value in (queries, keys, values):
                mixed_out[:, at : at + count * duo] = value[:, cols]
                at += count * duo
        contexts = []
        for pair in range(2):
            seen = live_ref[pair] > 0
            span = slice(pair * length, (pair + 1) * length)
            heads = []
            for block in range(blocks):
                cols = slice(block * duo, (block + 1) * duo)
                scores = dot(split_heads(queries[span, cols]), keys[span, cols], 1, 1)
                scores = jnp.where(seen, scores, -1e30)
                powered = jnp.exp(scores - jnp.max(scores, axis=-1, keepdims=True))
                low_probs = powered * (1.0 / jnp.sum(powered, axis=-1, keepdims=True))
                low_probs = low_probs.astype(BF16)
                probs_out[pair, block] = low_probs
                heads.append(
                    dot(side_by_side(low_probs), split_heads(values[span, cols])).astype(BF16)
                )
            contexts.append(jnp.concatenate(heads, 1))
        context = jnp.concatenate(contexts, 0)
        context_out[rows_here] = context
        pre_one = joined.astype(F32) + dot(context, w_out_ref[...]) + biases_ref[0:1, :]
        normed, root = normal_form(pre_one)
        normed_out[rows_here] = normed.astype(BF16)
        root_out[rows_here] = jnp.broadcast_to(root, (2 * length, 128))

    slot = (1, slot_rows, width)
    two = (2, slot_rows, width)
    total = half * length
    return call(
        kernel,
        scalars,
        [rows, rows, *received, live, w_qkv, b_qv, w_out, norm_gains, bias_rows],
        [
            pl.BlockSpec(slot, lambda i, s: (kept_slot(s, 2 * i, half), 0, 0)),
            pl.BlockSpec(slot, lambda i, s: (kept_slot(s, 2 * i + 1, half), 0, 0)),
            pl.BlockSpec(two, lambda i, s: (jnp.minimum(i, turn - 1), 0, 0)),
            pl.BlockSpec(two, lambda i, s: (jnp.maximum(i - turn, 0), 0, 0)),
            pl.BlockSpec((2, 1, length), lambda i, s: (i, 0, 0)),
            RESIDENT,
            whole(b_qv),
            RESIDENT,
            whole(norm_gains),
            whole(bias_rows),
        ],
        [
            RESIDENT,
            pl.BlockSpec((2 * length, 3 * width), lambda i, s: (i, 0)),
            pl.BlockSpec((2, blocks, 2 * length, length), lambda i, s: (i, 0, 0, 0)),
            RESIDENT,
            RESIDENT,
            RESIDENT,
        ],
        [
            jax.ShapeDtypeStruct((total, width), BF16),
            jax.ShapeDtypeStruct((total, 3 * width), BF16),
            jax.ShapeDtypeStruct((half, blocks, 2 * length, length), BF16),
            jax.ShapeDtypeStruct((total, width), BF16),
            jax.ShapeDtypeStruct((total, width), BF16),
            jax.ShapeDtypeStruct((total, 128), F32),
        ],
        (pairs // 2,),
        "attention_forward",
        limit=16 * 2**20,
        work=4 * 10**10,
    )


def place_of(index, order):
    return sum(1 << bit for n, bit in enumerate(order) if index >> (len(order) - 1 - n) & 1)


def spread(grad, outs, scalars_ref, base, shard, order):
    core, place = scalars_ref[base + 1], scalars_ref[base + 2]
    count = 2 ** len(order)
    for j in range(count):
        row = (place ^ place_of(j, order)) * 2
        for out, which in zip(outs, (1 - core, core)):
            if isinstance(out, tuple):
                out = out[2 * j // count].at[j % (count // 2)]
            else:
                out = out.at[j]
            out[...] = grad[pl.ds(pl.multiple_of((row + which) * shard, 16), shard), :]


def feed_forward(scalars, normed, cot, far_cot, weights, half, shards, base):
    w_in, b_in, w_back, norm_gains, bias_rows = weights
    slot_rows, width = cot.shape[1:]
    inner_width = w_in.shape[1]
    length = 2 * slot_rows
    rows = 2 * length
    height = half * length
    steps = half // 2
    chunk = 768
    chunks = inner_width // chunk
    shard = inner_width // shards
    places = shards // 2
    part = 4 * shard
    parts = inner_width // part

    def kernel(
        scalars_ref,
        normed_ref,
        cot_a,
        cot_b,
        cot_far,
        w_in_ref,
        b_in_ref,
        w_back_ref,
        gains_ref,
        biases_ref,
        slope_out,
        branch_out,
        kept_out,
        far_out,
        sums_out,
        near,
        away,
        keep,
        held,
        acts,
        grad,
    ):
        step = pl.program_id(0)

        @pl.when(step == 0)
        def _():
            sums_out[...] = jnp.zeros_like(sums_out)

        def close(pre_two, row):
            scaled, root = normal_form(pre_two)
            output = (scaled * gains_ref[1:2, :] + biases_ref[3:4, :]).astype(BF16)
            for i in range(2):
                kept_out[i] = output[i * length : i * length + slot_rows]
                far_out[i] = output[i * length + slot_rows : (i + 1) * length]
            here = jnp.concatenate([cot_a[0], cot_far[0], cot_b[0], cot_far[1]], 0).astype(F32)
            d_two = normal_back(here * gains_ref[1:2, :], scaled, root)
            low = d_two.astype(BF16)
            branch_out[pl.ds(pl.multiple_of(row, rows), rows)] = low
            return jnp.concatenate([row_sum(here * scaled), row_sum(here), row_sum(d_two)], 0)

        def forward():
            here = pl.ds(pl.multiple_of(step * rows, rows), rows)
            hidden = normed_ref[here].astype(F32) * gains_ref[0:1, :] + biases_ref[1:2, :]
            low_hidden = hidden.astype(BF16)
            total = hidden + biases_ref[2:3, :]
            for j in range(chunks):
                cols = slice(j * chunk, (j + 1) * chunk)
                inner = dot(low_hidden, w_in_ref[:, cols]) + b_in_ref[:, cols]
                normal = 0.5 + 0.5 * lax.erf(inner * (0.5**0.5))
                low_act = (inner * normal).astype(BF16)
                density = jnp.exp(inner * inner * -0.5) * 0.3989422804014327
                acts[here, cols] = low_act
                slope_out[here, cols] = (normal + inner * density).astype(BF16)
                total = total + dot(low_act, w_back_ref[cols, :])
            return total

        @pl.when(step == 0)
        def _():
            held[...] = forward()

        @pl.when((step > 0) & (step < steps))
        def _():
            before = held[...]
            held[...] = forward()
            sums_out[0:3, :] += close(before, (step - 1) * rows)

        @pl.when(step == steps)
        def _():
            sums_out[0:3, :] += close(held[...], (step - 1) * rows)

        @pl.when(step >= steps)
        def _():
            start = pl.multiple_of((step - steps) * part, 128)
            grad[...] = dot(acts[:, pl.ds(start, part)], branch_out[...], 0, 0).astype(BF16)
            core, low = scalars_ref[base + 1], scalars_ref[base + 2] & 1
            for j in range(2):
                for out, which in (((near, away)[j].at[0, 0], 1 - core), (keep.at[j, 0], core)):
                    row = ((low ^ j) * 2 + which) * shard
                    out[...] = grad[pl.ds(pl.multiple_of(row, 16), shard), :]

    def behind(i):
        return jnp.clip(i - 1, 0, steps - 1)

    def slot(j):
        return pl.BlockSpec(
            (1, slot_rows, width), lambda i, s: (kept_slot(s, 2 * behind(i) + j, half), 0, 0)
        )

    duo = pl.BlockSpec((2, slot_rows, width), lambda i, s: (behind(i), 0, 0))

    def entry(i, s):
        apart = (s[base + 2] >> 1) ^ jnp.maximum(i - steps, 0)
        return 0, (apart & 1) * 2 + (apart >> 1), 0, 0

    grads = [pl.BlockSpec((count, 1, shard, width), entry) for count in (1, 1, 2)]
    return call(
        kernel,
        scalars,
        [normed, cot, cot, far_cot, w_in, b_in, w_back, norm_gains, bias_rows],
        [
            RESIDENT,
            slot(0),
            slot(1),
            duo,
            RESIDENT,
            whole(b_in),
            RESIDENT,
            whole(norm_gains),
            whole(bias_rows),
        ],
        [
            RESIDENT,
            RESIDENT,
            duo,
            duo,
            pl.BlockSpec((8, width), lambda i, s: (0, 0)),
            *grads,
        ],
        [
            jax.ShapeDtypeStruct((height, inner_width), BF16),
            jax.ShapeDtypeStruct((height, width), BF16),
            jax.ShapeDtypeStruct((half, slot_rows, width), BF16),
            jax.ShapeDtypeStruct((half, slot_rows, width), BF16),
            jax.ShapeDtypeStruct((8, width), F32),
            jax.ShapeDtypeStruct((1, places // 2, shard, width), BF16),
            jax.ShapeDtypeStruct((1, places // 2, shard, width), BF16),
            jax.ShapeDtypeStruct((2, places // 2, shard, width), BF16),
        ],
        (steps + parts,),
        "feed_forward",
        limit=18 * 2**20,
        anywhere=(3,),
        scratch=[
            pltpu.VMEM((rows, width), F32),
            pltpu.VMEM((height, inner_width), BF16),
            pltpu.VMEM((part, width), BF16),
        ],
    )


def feed_backward(scalars, branch, slope, normed, root, weights, shards, base, order):
    w_in, w_back, norm_gains, bias_rows = weights
    total, width = branch.shape
    inner_width = slope.shape[1]
    chunk = 768
    steps = inner_width // chunk
    shard = width // shards
    places = shards // 2
    piece = 128

    def kernel(
        scalars_ref,
        branch_ref,
        slope_ref,
        normed_ref,
        root_ref,
        w_in_ref,
        w_back_ref,
        gains_ref,
        biases_ref,
        low_attn_out,
        sums_out,
        inner_sum_out,
        send,
        keep,
        held,
        low_hidden,
        grad,
    ):
        step = pl.program_id(0)

        @pl.when(step == 0)
        def _():
            hidden = normed_ref[...].astype(F32) * gains_ref[0:1, :] + biases_ref[1:2, :]
            low_hidden[...] = hidden.astype(BF16)
            held[...] = branch_ref[...].astype(F32)

        cols = pl.ds(pl.multiple_of(step * chunk, chunk), chunk)
        sums = jnp.zeros((1, chunk), F32)
        lows = []
        for r in range(0, total, 512):
            span = slice(r, r + 512)
            d_inner = dot(branch_ref[span], w_back_ref[cols, :], 1, 1)
            d_inner = d_inner * slope_ref[span, cols].astype(F32)
            sums = sums + row_sum(d_inner)
            low = d_inner.astype(BF16)
            lows.append(low)
            held[span] += dot(low, w_in_ref[:, cols], 1, 1)
        inner_sum_out[...] = jnp.broadcast_to(sums, inner_sum_out.shape)
        grad[...] = dot(low_hidden[...], jnp.concatenate(lows, 0), 0, 0).astype(BF16)

        spread(grad, (send, keep), scalars_ref, base, shard, order)

        @pl.when(step == steps - 1)
        def _():
            sums = [jnp.zeros((1, width), F32)] * 3
            for i in range(total // piece):
                span = slice(i * piece, (i + 1) * piece)
                d_hidden, scaled = held[span], normed_ref[span].astype(F32)
                d_one = normal_back(d_hidden * gains_ref[0:1, :], scaled, root_ref[span, 0:1])
                low_attn_out[span] = d_one.astype(BF16)
                for j, term in enumerate((d_hidden * scaled, d_hidden, d_one)):
                    sums[j] = sums[j] + row_sum(term)
            sums_out[...] = jnp.concatenate(sums + [jnp.zeros((5, width), F32)], 0)
    grads = pl.BlockSpec(
        (places, shard, chunk), lambda i, s: (0, 0, i ^ (s[base + 3] * (steps // 2)))
    )
    shape = jax.ShapeDtypeStruct((places, shard, inner_width), BF16)
    return call(
        kernel,
        scalars,
        [branch, slope, normed, root, w_in, w_back, norm_gains, bias_rows],
        [
            RESIDENT,
            RESIDENT,
            RESIDENT,
            RESIDENT,
            RESIDENT,
            RESIDENT,
            whole(norm_gains),
            whole(bias_rows),
        ],
        [
            RESIDENT,
            pl.BlockSpec((8, width), lambda i, s: (0, 0)),
            pl.BlockSpec((8, chunk), lambda i, s: (0, i)),
            grads,
            grads,
        ],
        [
            jax.ShapeDtypeStruct((total, width), BF16),
            jax.ShapeDtypeStruct((8, width), F32),
            jax.ShapeDtypeStruct((8, inner_width), F32),
            shape,
            shape,
        ],
        (steps,),
        "feed_backward",
        limit=21 * 2**20,
        scratch=[
            pltpu.VMEM((total, width), F32),
            pltpu.VMEM((total, width), BF16),
            pltpu.VMEM((width, chunk), BF16),
        ],
    )


def attention_backward(scalars, kept, weights, part, shards, base, order, earlier=(), sums=()):
    low_attn, mixed, probs, joined, context = kept
    w_out, w_qkv = weights
    total, width = low_attn.shape
    pairs, blocks, _, length = probs.shape
    duo = width // blocks
    first_block, mine = parts_of(blocks)[part]
    span_cols = mine * duo
    slot_rows = length // 2
    score_scale = (width // HEADS) ** (-0.5)
    steps = pairs // 2
    shard = width // shards
    places = shards // 2
    last = part == 1
    columns = 3 * span_cols + (128 if last else width)

    def kernel(
        scalars_ref,
        low_attn_ref,
        mixed_ref,
        probs_ref,
        joined_ref,
        w_out_ref,
        *refs,
    ):
        if last:
            w_qkv_ref, earlier_ref, one, two, inner, sums_ref = refs[:6]
            kept_out, far_out, sums_out, near, away, keep, held, grad = refs[6:]
        else:
            context_ref, held, sums_out, near, away, keep, grad = refs
        step = pl.program_id(0)

        @pl.when(step == 0)
        def _():
            sums_out[...] = jnp.zeros_like(sums_out)

        here = pl.ds(pl.multiple_of(step * 2 * length, 2 * length), 2 * length)
        low_attn = low_attn_ref[here]
        w_out_rows = slice(first_block * duo, (first_block + mine) * duo)
        d_context = dot(low_attn, w_out_ref[w_out_rows, :], 1, 1).astype(BF16)
        mixed = mixed_ref[...]
        rows = []
        for pair in range(2):
            span = slice(pair * length, (pair + 1) * length)
            chosen = [probs_ref[pair, block] for block in range(mine)]
            parts = []
            for third in range(3):
                first = third * span_cols
                parts.append(
                    [
                        mixed[span, first + block * duo : first + (block + 1) * duo]
                        for block in range(mine)
                    ]
                )
            queries, keys, values = parts
            d_heads, d_probs, d_scores = [], [], []
            for block in range(mine):
                cols = slice(block * duo, (block + 1) * duo)
                d_heads.append(split_heads(d_context[span, cols]))
                d_probs.append(dot(d_heads[block], values[block], 1, 1))
            for block in range(mine):
                wide = chosen[block].astype(F32)
                mean = jnp.sum(wide * d_probs[block], axis=-1, keepdims=True)
                d_scores.append((wide * (d_probs[block] - mean)).astype(BF16))
            d_queries, d_keys, d_values = [], [], []
            for block in range(mine):
                scaled = dot(side_by_side(d_scores[block]), split_heads(keys[block])) * score_scale
                d_queries.append(scaled.astype(BF16))
                d_keys.append(dot(d_scores[block], split_heads(queries[block]), 0, 0).astype(BF16))
                d_values.append(dot(chosen[block], d_heads[block], 0, 0).astype(BF16))
            rows.append(jnp.concatenate(d_queries + d_keys + d_values, 1))
        d_mixed = jnp.concatenate(rows, 0)
        held[here] = d_mixed
        sums_out[0:1, :] += row_sum(d_mixed[:, :span_cols].astype(F32))
        sums_out[1:2, :] += row_sum(d_mixed[:, 2 * span_cols :].astype(F32))
        if last:
            d_rows = low_attn.astype(F32)
            before = earlier_ref.shape[1] // 3
            for third in range(3):
                full = [
                    earlier_ref[here, third * before : (third + 1) * before],
                    d_mixed[:, third * span_cols : (third + 1) * span_cols],
                ]
                cols = slice(third * width, (third + 1) * width)
                d_rows = d_rows + dot(jnp.concatenate(full, 1), w_qkv_ref[:, cols], 1, 1)
            d_rows = d_rows.astype(BF16)
            for i in range(2):
                kept_out[i] = d_rows[i * length : i * length + slot_rows]
                far_out[i] = d_rows[i * length + slot_rows : (i + 1) * length]

        @pl.when(step == steps - 1)
        def _():
            grad[:, : 3 * span_cols] = dot(joined_ref[...], held[...], 0, 0).astype(BF16)
            if last:
                first, second = sums_ref[0:2, :], sums_out[0:2, :]
                count = inner.shape[1] // width
                small = [jnp.concatenate([first, second], 1), one[0:1], two[0:1]]
                small += [one[2:3], one[1:2], two[2:3], two[1:2]]
                for at in range(count):
                    runs = [
                        inner[0:1, (start * count + at) * shard : (start * count + at + 1) * shard]
                        for start in range(shards)
                    ]
                    small.append(jnp.concatenate(runs, 1))
                small.append(jnp.zeros((120 - count, width), F32))
                grad[:, 3 * span_cols :] = jnp.concatenate(small, 0).T.astype(BF16)
            else:
                outer = dot(context_ref[...], low_attn_ref[...], 0, 0)
                grad[:, 3 * span_cols :] = outer.astype(BF16)
            spread(grad, ((near, away), keep), scalars_ref, base, shard, order)

    two_slots = pl.BlockSpec((2, slot_rows, width), lambda i, s: (i, 0, 0))
    operands = [low_attn, mixed, probs, joined, w_out]
    skip = first_block // mine
    in_specs = [
        RESIDENT,
        pl.BlockSpec((2 * length, 3 * span_cols), lambda i, s: (i, skip)),
        pl.BlockSpec((2, mine, 2 * length, length), lambda i, s: (i, skip, 0, 0)),
        RESIDENT,
        RESIDENT,
    ]
    out_specs = [pl.BlockSpec((8, span_cols), lambda i, s: (0, 0))]
    out_shape = [jax.ShapeDtypeStruct((8, span_cols), F32)]
    for entries in (places // 2, places // 2, places):
        shape = (entries, shard, columns)
        out_specs.append(pl.BlockSpec(shape, lambda i, s: (0, 0, 0)))
        out_shape.append(jax.ShapeDtypeStruct(shape, BF16))
    if last:
        operands += [w_qkv, earlier, *sums]
        in_specs += [RESIDENT, RESIDENT]
        in_specs += [whole(each) for each in sums]
        out_specs = [two_slots, two_slots] + out_specs
        out_shape = [jax.ShapeDtypeStruct((pairs, slot_rows, width), BF16)] * 2 + out_shape
    else:
        operands.append(context)
        in_specs.append(RESIDENT)
        out_specs = [RESIDENT] + out_specs
        out_shape = [jax.ShapeDtypeStruct((total, 3 * span_cols), BF16)] + out_shape
    return call(
        kernel,
        scalars,
        operands,
        in_specs,
        out_specs,
        out_shape,
        (steps,),
        "attention_backward",
        limit=16 * 2**20,
        scratch=[pltpu.VMEM((total, 3 * span_cols), BF16)] * last
        + [pltpu.VMEM((width, columns), BF16)],
    )


def in_turn(value):
    value, *rest = lax.optimization_barrier((value, *LINE))
    LINE[:] = rest[:1]
    return value


def pause(scalars):
    def kernel(scalars_ref):
        del scalars_ref

    call(kernel, scalars, [], [], [], [], (1,), "pause", work=2 * 10**10)


class Shards:
    def __init__(self, *arrays, order):
        *sends, keep = arrays
        shard, width = keep.shape[-2:]
        self.order = list(order)
        self.columns = width // 2 if "mod" in self.order else width
        count = 2 ** sum(step != "mod" for step in self.order)
        self.held = [(0, keep.reshape((count, shard, width)))]
        self.count = count
        shape = (count // len(sends), shard, width)
        self.coming = []
        for i in range(len(sends))[::-1]:
            self.coming.append((i * shape[0], flipped(sends[i], "dp", 1).reshape(shape)))

    def step(self):
        bit = self.order.pop(0) if self.order else None
        count = self.count
        first = count // 2 if bit in (0, 1, 2) else 0
        column = self.columns if bit == "mod" else 0
        late = []
        for at, array in self.coming:
            if at + array.shape[0] > first:
                self.held.append((at, in_turn(array)))
            else:
                late.append((at, array))
        total = None
        for at, array in self.held:
            if at >= count or at + array.shape[0] <= first:
                continue
            array = lax.slice_in_dim(array, first - at if first > at else 0, count - at, axis=0)
            array = lax.slice_in_dim(array, column, column + self.columns, axis=2)
            array = array.astype(F32)
            total = array if total is None else total + array
        total = total.astype(BF16)
        if bit is None:
            self.mine = lax.optimization_barrier(total[0])
            self.coming = flipped(self.mine, "mod", 1)
        elif bit == "mod":
            self.coming = late + [(0, flipped(total, "mod", 1))]
        else:
            self.coming = late + [(0, flipped(total, "dp", 2 << bit))]
            self.count = first
        LINE.append(total)

    def result(self):
        return self.mine.astype(F32) + in_turn(self.coming).astype(F32)


def finish(scalars, inner, early, late, width, inner_width, base):
    pieces = [inner, early, late]
    shard = early.mine.shape[0]
    count = inner_width // width
    turn = inner.mine.shape[1]
    widths = ((early.mine.shape[1] - width) // 3, (late.mine.shape[1] - 128) // 3)

    def kernel(scalars_ref, *refs):
        ins, (grad_in, grad_out, qkv, b_qv, gains, biases, b_in) = refs[:6], refs[6:]
        first = scalars_ref[base + 3] == 0
        grad_in[:, :turn] = jnp.where(first, ins[0][...], ins[1][...]).astype(F32)
        grad_in[:, turn:] = jnp.where(first, ins[1][...], ins[0][...]).astype(F32)
        parts = [ins[2 * i][...].astype(F32) + ins[2 * i + 1][...].astype(F32) for i in (1, 2)]
        grad_out[...] = parts[0][:, 3 * widths[0] :]
        at = 0
        for third in range(3):
            for part, columns in zip(parts, widths):
                qkv[:, at : at + columns] = part[:, third * columns : (third + 1) * columns]
                at += columns
        small = jnp.concatenate([parts[1][:, 3 * widths[1] :], jnp.zeros((128 - shard, 128), F32)], 0)
        small = small.T[:, :shard]
        b_qv[...] = small[0:2]
        gains[...] = small[2:4]
        biases[...] = small[4:8]
        b_in[...] = jnp.concatenate([small[8 + i : 9 + i] for i in range(count)], 1)

    operands = [each for piece in pieces for each in (piece.mine, piece.coming)]
    shapes = [(shard, inner_width), (shard, width), (shard, 3 * width)]
    shapes += [(2, shard), (2, shard), (4, shard), (1, count * shard)]
    return call(
        kernel,
        scalars,
        operands,
        [whole(array) for array in operands],
        [pl.BlockSpec(shape, lambda i, s: (0, 0)) for shape in shapes],
        [jax.ShapeDtypeStruct(shape, F32) for shape in shapes],
        (1,),
        "finish",
        anywhere=range(6),
    )


def reduce_plain(*arrays, order):
    *sends, keep = arrays
    shard, columns = keep.shape[-2:]
    send = jnp.concatenate([each.reshape(-1, shard, columns) for each in sends], 0)
    total = jnp.stack([keep.reshape(-1, shard, columns), send.reshape(-1, shard, columns)], 1)
    places = [place_of(j, order) for j in range(total.shape[0])]
    total = jnp.stack([total[places.index(j)] for j in range(total.shape[0])])
    total = total.reshape(-1, columns).astype(F32)
    share = lax.psum_scatter(total, "dp", scatter_dimension=0, tiled=True)
    return lax.psum(share.astype(BF16), "mod").astype(F32)


def body(
    layer_rows,
    cotangent,
    row_live,
    partner,
    w_qkv,
    b_qv,
    w_out,
    norm_gains,
    bias_rows,
    w_in,
    b_in,
    w_back,
):
    side = lax.axis_index("mod")
    place = lax.axis_index("dp")
    shards = lax.axis_size("dp")
    groups = partner.shape[1]
    aligned = shards == 16 and (layer_rows.shape[2] // shards) % 16 == 0
    layout = shards if aligned else 16
    half = groups // 2
    width = layer_rows.shape[2]
    slot_rows = layer_rows.shape[1] // groups
    inner_width = w_in.shape[1]
    slots = (groups, slot_rows, width)
    rows = layer_rows[0].reshape(slots)
    cot = cotangent[0].reshape(slots)
    cut = half // 2
    LINE.clear()
    sent = gather_sent(partner[0], rows, half, 0, cut)
    got_a = flipped(sent, "mod", 1)
    sent = gather_sent(partner[0], rows, half, cut, half - cut)
    got_b = flipped(sent, "mod", 1)
    sent_cot = gather_sent(partner[0], cot, half, 0, half)
    got_a, sent_cot, row_live, partner = lax.optimization_barrier(
        (got_a, sent_cot, row_live, partner)
    )
    far_cot = flipped(sent_cot, "mod", 1)
    spot = place if aligned else 0 * place
    scalars = jnp.concatenate(
        [partner[0], jnp.stack([side, spot & 1, spot >> 1, side * aligned]).astype(jnp.int32)]
    )

    live = row_live.reshape(2, groups, slot_rows)
    words_live = lax.dynamic_slice_in_dim(live[0], side * half, half, 0)
    region_live = live[1][lax.dynamic_slice_in_dim(partner[0], side * half, half, 0)]
    is_first = side == 0
    seen = jnp.concatenate(
        [
            jnp.where(is_first, words_live, region_live),
            jnp.where(is_first, region_live, words_live),
        ],
        1,
    )[:, None, :]

    w_qkv, w_out, w_in, w_back = fetch(scalars, (w_qkv, w_out, w_in, w_back))
    heads_weights = (w_qkv, b_qv, w_out, norm_gains, bias_rows)
    joined, mixed, probs, context, normed, root = attention_forward(
        scalars, rows, (got_a, got_b), seen, heads_weights
    )
    feed_weights = (w_in, b_in.reshape(1, inner_width), w_back, norm_gains, bias_rows)
    slope, branch, out_kept, out_far, sums_two, *back = feed_forward(
        scalars, normed, cot, far_cot, feed_weights, half, layout, groups
    )
    out_back = flipped(out_far, "mod", 1)
    back_weights = (w_in, w_back, norm_gains, bias_rows)
    attn_weights = (w_out, w_qkv)
    path = (0, 1, 2)
    if aligned:
        back = Shards(*back, order=path)
        back.step()
    low_attn, sums_one, inner_sum, *inner = feed_backward(
        scalars, branch, slope, normed, root, back_weights, layout, groups, path
    )
    shard = width // shards
    count = inner_width // width
    if aligned:
        back.step()
        out_back = in_turn(out_back)
        pause(scalars)
        inner = Shards(*inner, order=("mod", 0, 1, 2))
        inner.step()
    attn_kept = (low_attn, mixed, probs, joined, context)
    d_mixed, sums_qv, *qkv_a = attention_backward(
        scalars, attn_kept, attn_weights, 0, layout, groups, path
    )
    if aligned:
        back.step()
        out_rows = scatter_home(scalars, out_kept, out_back, half).reshape(1, -1, width)
        qkv_a = Shards(*qkv_a, order=path)
        qkv_a.step()
    if layout != shards:
        inner_sum = inner_sum.reshape(8, shards, count, shard).transpose(0, 2, 1, 3)
        inner_sum = inner_sum.reshape(8, count, layout, width // layout).transpose(0, 2, 1, 3)
        inner_sum = inner_sum.reshape(8, inner_width)
    sums = (sums_one, sums_two, inner_sum, sums_qv)
    d_kept, d_far, _, *qkv_b = attention_backward(
        scalars, attn_kept, attn_weights, 1, layout, groups, path, d_mixed, sums
    )
    d_back = flipped(d_far, "mod", 1)
    if aligned:
        qkv_b = Shards(*qkv_b, order=path)
        inner.step()
        back.step()
        qkv_a.step()
        qkv_b.step()
        inner.step()
        pause(scalars)
        qkv_a.step()
        qkv_b.step()
        grad_back = back.result()
        inner.step()
        grad_rows = scatter_home(scalars, d_kept, d_back, half).reshape(1, -1, width)
        qkv_a.step()
        qkv_b.step()
        inner.step()
        qkv_b.step()
        grad_in, grad_out, grad_qkv, *small = finish(
            scalars, inner, qkv_a, qkv_b, width, inner_width, groups
        )
    else:
        out_rows = scatter_home(scalars, out_kept, out_back, half).reshape(1, -1, width)
        grad_back = reduce_plain(*back, order=path)
        grad_in = reduce_plain(*inner, order=path)
        qkv_a, qkv_b = reduce_plain(*qkv_a, order=path), reduce_plain(*qkv_b, order=path)
        grad_rows = scatter_home(scalars, d_kept, d_back, half).reshape(1, -1, width)
        columns = ((qkv_a.shape[1] - width) // 3, (qkv_b.shape[1] - 128) // 3)
        thirds = []
        for third in range(3):
            for part, wide in zip((qkv_a, qkv_b), columns):
                thirds.append(part[:, third * wide : (third + 1) * wide])
        grad_qkv = jnp.concatenate(thirds, 1)
        small = qkv_b[:, 3 * columns[1] :].T
        small = small[0:2], small[2:4], small[4:8], small[8 : 8 + count]
        grad_out = qkv_a[:, 3 * columns[0] :]
    return (
        out_rows,
        grad_rows,
        grad_qkv,
        small[0],
        grad_out,
        small[1],
        small[2],
        grad_in,
        small[3].reshape(-1),
        grad_back,
    )


def solution(mesh):
    return jax.shard_map(
        body,
        mesh=mesh,
        in_specs=(
            P("mod", "dp", None),
            P("mod", "dp", None),
            P(None, "dp"),
            P("dp", None),
            P(),
            P(),
            P(),
            P(),
            P(),
            P(),
            P(),
            P(),
        ),
        out_specs=(
            P("mod", "dp", None),
            P("mod", "dp", None),
            P("dp", None),
            P(None, "dp"),
            P("dp", None),
            P(None, "dp"),
            P(None, "dp"),
            P("dp", None),
            P("dp"),
            P("dp", None),
        ),
        check_vma=False,
    )
```

```python
import functools

import jax
import jax.numpy as jnp
from jax import lax
from jax.experimental import pallas as pl
from jax.experimental.pallas import tpu as pltpu
from jax.sharding import PartitionSpec as P

HEADS = 12
EPSILON = 1e-12
F32 = jnp.float32
BF16 = jnp.bfloat16
VMEM_LIMIT = 26 * 2**20


def dot(left, right, left_dim=1, right_dim=0):
    return lax.dot_general(
        left, right, (((left_dim,), (right_dim,)), ((), ())), preferred_element_type=F32
    )


def flipped(value, axis, mask):
    pairs = [(source, source ^ mask) for source in range(lax.axis_size(axis))]
    return lax.ppermute(value, axis, pairs)


def params(limit=VMEM_LIMIT):
    return pltpu.CompilerParams(vmem_limit_bytes=limit)


def kept_slot(scalars, pair, half):
    groups = 2 * half
    side = scalars[groups]
    place = side * half + pair
    return jnp.where(side == 0, place, scalars[place])


def sent_slot(scalars, pair, half):
    groups = 2 * half
    side = scalars[groups]
    place = (1 - side) * half + pair
    return jnp.where(side == 0, place, scalars[place])


ANY = pl.BlockSpec(memory_space=pl.ANY)
RESIDENT = pl.BlockSpec(memory_space=pltpu.VMEM)
LINE = []


def call(kernel, scalars, operands, in_specs, out_specs, out_shape, grid, name, **more):
    after = LINE[1:]
    if LINE:
        after.append(pltpu.with_memory_space_constraint(LINE[0], pltpu.HBM))
    scratch = list(more.get("scratch", ()))
    taken, given = len(operands), len(out_shape)

    def wrapped(scalars_ref, *refs):
        outs = refs[taken + len(after) :]
        kernel(scalars_ref, *refs[:taken], *outs[:given], *outs[given + 1 :])

    placed = []
    for i, (array, spec) in enumerate(zip(operands, in_specs)):
        if i not in more.get("anywhere", ()):
            space = pltpu.VMEM if spec is RESIDENT else pltpu.HBM
            array = pltpu.with_memory_space_constraint(array, space)
        placed.append(array)
    shapes = [
        (pltpu.VMEM if spec is RESIDENT else pltpu.HBM)(shape.shape, shape.dtype)
        for shape, spec in zip(out_shape, out_specs)
    ]
    outs = pl.pallas_call(
        wrapped,
        grid_spec=pltpu.PrefetchScalarGridSpec(
            num_scalar_prefetch=1,
            grid=grid,
            in_specs=list(in_specs) + [ANY] * len(after),
            out_specs=list(out_specs) + [ANY],
            scratch_shapes=scratch,
        ),
        out_shape=shapes + [pltpu.HBM((8, 128), F32)],
        compiler_params=params(more.get("limit", VMEM_LIMIT)),
        cost_estimate=pl.CostEstimate(
            flops=more.get("work", 4 * 10**9), bytes_accessed=2**20, transcendentals=0
        ),
        name=name,
    )(scalars, *placed, *after)
    LINE[:] = [outs[-1]]
    return list(outs[:-1])


def fetch(scalars, arrays):
    count = len(arrays)

    def kernel(scalars_ref, *refs):
        sems = refs[-1]
        copies = [
            pltpu.make_async_copy(refs[i], refs[count + i], sems.at[i]) for i in range(count)
        ]
        for copy in copies:
            copy.start()
        for copy in copies:
            copy.wait()

    return call(
        kernel,
        scalars,
        list(arrays),
        [ANY] * count,
        [RESIDENT] * count,
        [jax.ShapeDtypeStruct(array.shape, array.dtype) for array in arrays],
        (1,),
        "fetch",
        work=10**7,
        scratch=[pltpu.SemaphoreType.DMA((count,))],
    )


def gather_sent(partner, rows, half, first, count):
    slot_rows, width = rows.shape[1:]

    partner = pltpu.with_memory_space_constraint(partner, pltpu.HBM)

    def kernel(partner_ref, rows_ref, out, sems):
        side = lax.axis_index("mod")
        copies = []
        for i in range(count):
            place = (1 - side) * half + first + i
            slot = jnp.where(side == 0, place, partner_ref[place])
            copies.append(pltpu.make_async_copy(rows_ref.at[slot], out.at[i], sems.at[i]))
        for copy in copies:
            copy.start()
        for copy in copies:
            copy.wait()

    shape = (count, slot_rows, width)
    return call(
        kernel,
        partner,
        [rows],
        [ANY],
        [pl.BlockSpec(shape, lambda i, s: (0, 0, 0))],
        [jax.ShapeDtypeStruct(shape, rows.dtype)],
        (1,),
        "gather_sent",
        work=10**7,
        scratch=[pltpu.SemaphoreType.DMA((count,))],
    )[0]


def scatter_home(scalars, kept, back, half):
    slot_rows, width = kept.shape[1:]

    def kernel(scalars_ref, kept_ref, back_ref, out, sems):
        copies = []
        for i in range(half):
            copies.append(
                pltpu.make_async_copy(
                    kept_ref.at[i], out.at[kept_slot(scalars_ref, i, half)], sems.at[0, i]
                )
            )
            copies.append(
                pltpu.make_async_copy(
                    back_ref.at[i], out.at[sent_slot(scalars_ref, i, half)], sems.at[1, i]
                )
            )
        for copy in copies:
            copy.start()
        for copy in copies:
            copy.wait()

    shape = (2 * half, slot_rows, width)
    return call(
        kernel,
        scalars,
        [kept, back],
        [ANY, ANY],
        [pl.BlockSpec(shape, lambda i, s: (0, 0, 0))],
        [jax.ShapeDtypeStruct(shape, kept.dtype)],
        (1,),
        "scatter_home",
        anywhere=(1,),
        work=2 * 10**10,
        scratch=[pltpu.SemaphoreType.DMA((2, half))],
    )[0]


def parts_of(blocks):
    early = blocks // 2
    return (0, early), (early, blocks - early)


def split_heads(value):
    low = lax.broadcasted_iota(jnp.int32, value.shape, 1) < value.shape[1] // 2
    zero = jnp.zeros_like(value)
    return jnp.concatenate([jnp.where(low, value, zero), jnp.where(low, zero, value)], 0)


def side_by_side(value):
    rows = value.shape[0] // 2
    return jnp.concatenate([value[:rows], value[rows:]], 1)


def row_sum(value):
    return jnp.sum(value, axis=0, keepdims=True)


def normal_form(value):
    centered = value - jnp.mean(value, axis=-1, keepdims=True)
    root = lax.rsqrt(jnp.mean(centered * centered, axis=-1, keepdims=True) + EPSILON)
    return centered * root, root


def normal_back(lifted, normed, root):
    return root * (
        lifted
        - jnp.mean(lifted, axis=-1, keepdims=True)
        - normed * jnp.mean(lifted * normed, axis=-1, keepdims=True)
    )


def whole(array):
    return pl.BlockSpec(
        array.shape, lambda *_: (0,) * array.ndim, pipeline_mode=pl.Buffered(1)
    )


def attention_forward(scalars, rows, received, live, weights):
    w_qkv, b_qv, w_out, norm_gains, bias_rows = weights
    slot_rows, width = rows.shape[1:]
    pairs = half = rows.shape[0] // 2
    turn = received[0].shape[0] // 2
    length = 2 * slot_rows
    duo = 2 * width // HEADS
    blocks = width // duo
    score_scale = (width // HEADS) ** (-0.5)

    def kernel(
        scalars_ref,
        kept_a,
        kept_b,
        got_a,
        got_b,
        live_ref,
        w_qkv_ref,
        b_qv_ref,
        w_out_ref,
        gains_ref,
        biases_ref,
        joined_out,
        mixed_out,
        probs_out,
        context_out,
        normed_out,
        root_out,
    ):
        step = pl.program_id(0)
        rows_here = pl.ds(pl.multiple_of(step * 2 * length, 2 * length), 2 * length)
        got = jnp.where(step < turn, got_a[...], got_b[...])
        joined = jnp.concatenate([kept_a[0], got[0], kept_b[0], got[1]], 0)
        joined_out[rows_here] = joined
        mixed = dot(joined, w_qkv_ref[...])
        queries = (mixed[:, :width] + b_qv_ref[0:1, :]).astype(BF16)
        queries = (queries.astype(F32) * score_scale).astype(BF16)
        keys = mixed[:, width : 2 * width].astype(BF16)
        values = (mixed[:, 2 * width :] + b_qv_ref[1:2, :]).astype(BF16)
        for first_block, count in parts_of(blocks):
            cols = slice(first_block * duo, (first_block + count) * duo)
            at = 3 * first_block * duo
            for value in (queries, keys, values):
                mixed_out[:, at : at + count * duo] = value[:, cols]
                at += count * duo
        contexts = []
        for pair in range(2):
            seen = live_ref[pair] > 0
            span = slice(pair * length, (pair + 1) * length)
            heads = []
            for block in range(blocks):
                cols = slice(block * duo, (block + 1) * duo)
                scores = dot(split_heads(queries[span, cols]), keys[span, cols], 1, 1)
                scores = jnp.where(seen, scores, -1e30)
                powered = jnp.exp(scores - jnp.max(scores, axis=-1, keepdims=True))
                low_probs = powered * (1.0 / jnp.sum(powered, axis=-1, keepdims=True))
                low_probs = low_probs.astype(BF16)
                probs_out[pair, block] = low_probs
                heads.append(
                    dot(side_by_side(low_probs), split_heads(values[span, cols])).astype(BF16)
                )
            contexts.append(jnp.concatenate(heads, 1))
        context = jnp.concatenate(contexts, 0)
        context_out[rows_here] = context
        pre_one = joined.astype(F32) + dot(context, w_out_ref[...]) + biases_ref[0:1, :]
        normed, root = normal_form(pre_one)
        normed_out[rows_here] = normed.astype(BF16)
        root_out[rows_here] = jnp.broadcast_to(root, (2 * length, 128))

    slot = (1, slot_rows, width)
    two = (2, slot_rows, width)
    total = half * length
    return call(
        kernel,
        scalars,
        [rows, rows, *received, live, w_qkv, b_qv, w_out, norm_gains, bias_rows],
        [
            pl.BlockSpec(slot, lambda i, s: (kept_slot(s, 2 * i, half), 0, 0)),
            pl.BlockSpec(slot, lambda i, s: (kept_slot(s, 2 * i + 1, half), 0, 0)),
            pl.BlockSpec(two, lambda i, s: (jnp.minimum(i, turn - 1), 0, 0)),
            pl.BlockSpec(two, lambda i, s: (jnp.maximum(i - turn, 0), 0, 0)),
            pl.BlockSpec((2, 1, length), lambda i, s: (i, 0, 0)),
            RESIDENT,
            whole(b_qv),
            RESIDENT,
            whole(norm_gains),
            whole(bias_rows),
        ],
        [
            RESIDENT,
            pl.BlockSpec((2 * length, 3 * width), lambda i, s: (i, 0)),
            pl.BlockSpec((2, blocks, 2 * length, length), lambda i, s: (i, 0, 0, 0)),
            RESIDENT,
            RESIDENT,
            RESIDENT,
        ],
        [
            jax.ShapeDtypeStruct((total, width), BF16),
            jax.ShapeDtypeStruct((total, 3 * width), BF16),
            jax.ShapeDtypeStruct((half, blocks, 2 * length, length), BF16),
            jax.ShapeDtypeStruct((total, width), BF16),
            jax.ShapeDtypeStruct((total, width), BF16),
            jax.ShapeDtypeStruct((total, 128), F32),
        ],
        (pairs // 2,),
        "attention_forward",
        limit=16 * 2**20,
        work=4 * 10**10,
    )


def place_of(index, order):
    return sum(1 << bit for n, bit in enumerate(order) if index >> (len(order) - 1 - n) & 1)


def spread(grad, outs, scalars_ref, base, shard, order):
    core, place = scalars_ref[base + 1], scalars_ref[base + 2]
    count = 2 ** len(order)
    for j in range(count):
        row = (place ^ place_of(j, order)) * 2
        for out, which in zip(outs, (1 - core, core)):
            if isinstance(out, tuple):
                out = out[2 * j // count].at[j % (count // 2)]
            else:
                out = out.at[j]
            out[...] = grad[pl.ds(pl.multiple_of((row + which) * shard, 16), shard), :]


def feed_forward(scalars, normed, cot, far_cot, weights, half, shards, base):
    w_in, b_in, w_back, norm_gains, bias_rows = weights
    slot_rows, width = cot.shape[1:]
    inner_width = w_in.shape[1]
    length = 2 * slot_rows
    rows = 2 * length
    height = half * length
    steps = half // 2
    chunk = 768
    chunks = inner_width // chunk
    shard = inner_width // shards
    places = shards // 2
    part = 4 * shard
    parts = inner_width // part

    def kernel(
        scalars_ref,
        normed_ref,
        cot_a,
        cot_b,
        cot_far,
        w_in_ref,
        b_in_ref,
        w_back_ref,
        gains_ref,
        biases_ref,
        slope_out,
        branch_out,
        kept_out,
        far_out,
        sums_out,
        near,
        away,
        keep,
        held,
        acts,
        grad,
    ):
        step = pl.program_id(0)

        @pl.when(step == 0)
        def _():
            sums_out[...] = jnp.zeros_like(sums_out)

        def close(pre_two, row):
            scaled, root = normal_form(pre_two)
            output = (scaled * gains_ref[1:2, :] + biases_ref[3:4, :]).astype(BF16)
            for i in range(2):
                kept_out[i] = output[i * length : i * length + slot_rows]
                far_out[i] = output[i * length + slot_rows : (i + 1) * length]
            here = jnp.concatenate([cot_a[0], cot_far[0], cot_b[0], cot_far[1]], 0).astype(F32)
            d_two = normal_back(here * gains_ref[1:2, :], scaled, root)
            low = d_two.astype(BF16)
            branch_out[pl.ds(pl.multiple_of(row, rows), rows)] = low
            return jnp.concatenate([row_sum(here * scaled), row_sum(here), row_sum(d_two)], 0)

        def forward():
            here = pl.ds(pl.multiple_of(step * rows, rows), rows)
            hidden = normed_ref[here].astype(F32) * gains_ref[0:1, :] + biases_ref[1:2, :]
            low_hidden = hidden.astype(BF16)
            total = hidden + biases_ref[2:3, :]
            for j in range(chunks):
                cols = slice(j * chunk, (j + 1) * chunk)
                inner = dot(low_hidden, w_in_ref[:, cols]) + b_in_ref[:, cols]
                normal = 0.5 + 0.5 * lax.erf(inner * (0.5**0.5))
                low_act = (inner * normal).astype(BF16)
                density = jnp.exp(inner * inner * -0.5) * 0.3989422804014327
                acts[here, cols] = low_act
                slope_out[here, cols] = (normal + inner * density).astype(BF16)
                total = total + dot(low_act, w_back_ref[cols, :])
            return total

        @pl.when(step == 0)
        def _():
            held[...] = forward()

        @pl.when((step > 0) & (step < steps))
        def _():
            before = held[...]
            held[...] = forward()
            sums_out[0:3, :] += close(before, (step - 1) * rows)

        @pl.when(step == steps)
        def _():
            sums_out[0:3, :] += close(held[...], (step - 1) * rows)

        @pl.when(step >= steps)
        def _():
            start = pl.multiple_of((step - steps) * part, 128)
            grad[...] = dot(acts[:, pl.ds(start, part)], branch_out[...], 0, 0).astype(BF16)
            core, low = scalars_ref[base + 1], scalars_ref[base + 2] & 1
            for j in range(2):
                for out, which in (((near, away)[j].at[0, 0], 1 - core), (keep.at[j, 0], core)):
                    row = ((low ^ j) * 2 + which) * shard
                    out[...] = grad[pl.ds(pl.multiple_of(row, 16), shard), :]

    def behind(i):
        return jnp.clip(i - 1, 0, steps - 1)

    def slot(j):
        return pl.BlockSpec(
            (1, slot_rows, width), lambda i, s: (kept_slot(s, 2 * behind(i) + j, half), 0, 0)
        )

    duo = pl.BlockSpec((2, slot_rows, width), lambda i, s: (behind(i), 0, 0))

    def entry(i, s):
        apart = (s[base + 2] >> 1) ^ jnp.maximum(i - steps, 0)
        return 0, (apart & 1) * 2 + (apart >> 1), 0, 0

    grads = [pl.BlockSpec((count, 1, shard, width), entry) for count in (1, 1, 2)]
    return call(
        kernel,
        scalars,
        [normed, cot, cot, far_cot, w_in, b_in, w_back, norm_gains, bias_rows],
        [
            RESIDENT,
            slot(0),
            slot(1),
            duo,
            RESIDENT,
            whole(b_in),
            RESIDENT,
            whole(norm_gains),
            whole(bias_rows),
        ],
        [
            RESIDENT,
            RESIDENT,
            duo,
            duo,
            pl.BlockSpec((8, width), lambda i, s: (0, 0)),
            *grads,
        ],
        [
            jax.ShapeDtypeStruct((height, inner_width), BF16),
            jax.ShapeDtypeStruct((height, width), BF16),
            jax.ShapeDtypeStruct((half, slot_rows, width), BF16),
            jax.ShapeDtypeStruct((half, slot_rows, width), BF16),
            jax.ShapeDtypeStruct((8, width), F32),
            jax.ShapeDtypeStruct((1, places // 2, shard, width), BF16),
            jax.ShapeDtypeStruct((1, places // 2, shard, width), BF16),
            jax.ShapeDtypeStruct((2, places // 2, shard, width), BF16),
        ],
        (steps + parts,),
        "feed_forward",
        limit=18 * 2**20,
        anywhere=(3,),
        scratch=[
            pltpu.VMEM((rows, width), F32),
            pltpu.VMEM((height, inner_width), BF16),
            pltpu.VMEM((part, width), BF16),
        ],
    )


def feed_backward(scalars, branch, slope, normed, root, context, weights, shards, base, order):
    w_in, w_back, norm_gains, bias_rows = weights
    total, width = branch.shape
    inner_width = slope.shape[1]
    chunk = 768
    steps = inner_width // chunk
    shard = width // shards
    places = shards // 2
    piece = 128

    def kernel(
        scalars_ref,
        branch_ref,
        slope_ref,
        normed_ref,
        root_ref,
        context_ref,
        w_in_ref,
        w_back_ref,
        gains_ref,
        biases_ref,
        low_attn_out,
        outer_out,
        sums_out,
        inner_sum_out,
        send,
        keep,
        held,
        low_hidden,
        grad,
    ):
        step = pl.program_id(0)

        @pl.when(step == 0)
        def _():
            hidden = normed_ref[...].astype(F32) * gains_ref[0:1, :] + biases_ref[1:2, :]
            low_hidden[...] = hidden.astype(BF16)
            held[...] = branch_ref[...].astype(F32)

        cols = pl.ds(pl.multiple_of(step * chunk, chunk), chunk)
        sums = jnp.zeros((1, chunk), F32)
        lows = []
        for r in range(0, total, 512):
            span = slice(r, r + 512)
            d_inner = dot(branch_ref[span], w_back_ref[cols, :], 1, 1)
            d_inner = d_inner * slope_ref[span, cols].astype(F32)
            sums = sums + row_sum(d_inner)
            low = d_inner.astype(BF16)
            lows.append(low)
            held[span] += dot(low, w_in_ref[:, cols], 1, 1)
        inner_sum_out[...] = jnp.broadcast_to(sums, inner_sum_out.shape)
        grad[...] = dot(low_hidden[...], jnp.concatenate(lows, 0), 0, 0).astype(BF16)

        spread(grad, (send, keep), scalars_ref, base, shard, order)

        @pl.when(step == steps - 1)
        def _():
            sums = [jnp.zeros((1, width), F32)] * 3
            for i in range(total // piece):
                span = slice(i * piece, (i + 1) * piece)
                d_hidden, scaled = held[span], normed_ref[span].astype(F32)
                d_one = normal_back(d_hidden * gains_ref[0:1, :], scaled, root_ref[span, 0:1])
                low_attn_out[span] = d_one.astype(BF16)
                for j, term in enumerate((d_hidden * scaled, d_hidden, d_one)):
                    sums[j] = sums[j] + row_sum(term)
            sums_out[...] = jnp.concatenate(sums + [jnp.zeros((5, width), F32)], 0)
            outer_out[...] = dot(context_ref[...], low_attn_out[...], 0, 0).astype(BF16)
    grads = pl.BlockSpec(
        (places, shard, chunk), lambda i, s: (0, 0, i ^ (s[base + 3] * (steps // 2)))
    )
    shape = jax.ShapeDtypeStruct((places, shard, inner_width), BF16)
    return call(
        kernel,
        scalars,
        [branch, slope, normed, root, context, w_in, w_back, norm_gains, bias_rows],
        [
            *[RESIDENT] * 7,
            whole(norm_gains),
            whole(bias_rows),
        ],
        [
            RESIDENT,
            RESIDENT,
            pl.BlockSpec((8, width), lambda i, s: (0, 0)),
            pl.BlockSpec((8, chunk), lambda i, s: (0, i)),
            grads,
            grads,
        ],
        [
            jax.ShapeDtypeStruct((total, width), BF16),
            jax.ShapeDtypeStruct((width, width), BF16),
            jax.ShapeDtypeStruct((8, width), F32),
            jax.ShapeDtypeStruct((8, inner_width), F32),
            shape,
            shape,
        ],
        (steps,),
        "feed_backward",
        limit=20 * 2**20,
        scratch=[
            pltpu.VMEM((total, width), F32),
            pltpu.VMEM((total, width), BF16),
            pltpu.VMEM((width, chunk), BF16),
        ],
    )


def attention_backward(scalars, kept, weights, part, shards, base, order, earlier=(), sums=()):
    low_attn, mixed, probs, joined, outer = kept
    w_out, w_qkv = weights
    total, width = low_attn.shape
    pairs, blocks, _, length = probs.shape
    duo = width // blocks
    first_block, mine = parts_of(blocks)[part]
    span_cols = mine * duo
    slot_rows = length // 2
    score_scale = (width // HEADS) ** (-0.5)
    steps = pairs // 2
    shard = width // shards
    places = shards // 2
    last = part == 1
    columns = 3 * span_cols + (128 if last else width)

    def kernel(
        scalars_ref,
        low_attn_ref,
        mixed_ref,
        probs_ref,
        joined_ref,
        w_out_ref,
        *refs,
    ):
        if last:
            w_qkv_ref, earlier_ref, one, two, inner, sums_ref = refs[:6]
            kept_out, far_out, sums_out, near, away, keep, held, grad = refs[6:]
        else:
            outer_ref, held, sums_out, near, away, keep, grad = refs
        step = pl.program_id(0)

        @pl.when(step == 0)
        def _():
            sums_out[...] = jnp.zeros_like(sums_out)

        here = pl.ds(pl.multiple_of(step * 2 * length, 2 * length), 2 * length)
        low_attn = low_attn_ref[here]
        w_out_rows = slice(first_block * duo, (first_block + mine) * duo)
        d_context = dot(low_attn, w_out_ref[w_out_rows, :], 1, 1).astype(BF16)
        mixed = mixed_ref[...]
        rows = []
        for pair in range(2):
            span = slice(pair * length, (pair + 1) * length)
            chosen = [probs_ref[pair, block] for block in range(mine)]
            parts = []
            for third in range(3):
                first = third * span_cols
                parts.append(
                    [
                        mixed[span, first + block * duo : first + (block + 1) * duo]
                        for block in range(mine)
                    ]
                )
            queries, keys, values = parts
            d_heads, d_probs, d_scores = [], [], []
            for block in range(mine):
                cols = slice(block * duo, (block + 1) * duo)
                d_heads.append(split_heads(d_context[span, cols]))
                d_probs.append(dot(d_heads[block], values[block], 1, 1))
            for block in range(mine):
                wide = chosen[block].astype(F32)
                mean = jnp.sum(wide * d_probs[block], axis=-1, keepdims=True)
                d_scores.append((wide * (d_probs[block] - mean)).astype(BF16))
            d_queries, d_keys, d_values = [], [], []
            for block in range(mine):
                scaled = dot(side_by_side(d_scores[block]), split_heads(keys[block])) * score_scale
                d_queries.append(scaled.astype(BF16))
                d_keys.append(dot(d_scores[block], split_heads(queries[block]), 0, 0).astype(BF16))
                d_values.append(dot(chosen[block], d_heads[block], 0, 0).astype(BF16))
            rows.append(jnp.concatenate(d_queries + d_keys + d_values, 1))
        d_mixed = jnp.concatenate(rows, 0)
        held[here] = d_mixed
        sums_out[0:1, :] += row_sum(d_mixed[:, :span_cols].astype(F32))
        sums_out[1:2, :] += row_sum(d_mixed[:, 2 * span_cols :].astype(F32))
        if last:
            d_rows = low_attn.astype(F32)
            before = earlier_ref.shape[1] // 3
            for third in range(3):
                full = [
                    earlier_ref[here, third * before : (third + 1) * before],
                    d_mixed[:, third * span_cols : (third + 1) * span_cols],
                ]
                cols = slice(third * width, (third + 1) * width)
                d_rows = d_rows + dot(jnp.concatenate(full, 1), w_qkv_ref[:, cols], 1, 1)
            d_rows = d_rows.astype(BF16)
            for i in range(2):
                kept_out[i] = d_rows[i * length : i * length + slot_rows]
                far_out[i] = d_rows[i * length + slot_rows : (i + 1) * length]

        @pl.when(step == steps - 1)
        def _():
            grad[:, : 3 * span_cols] = dot(joined_ref[...], held[...], 0, 0).astype(BF16)
            if last:
                first, second = sums_ref[0:2, :], sums_out[0:2, :]
                count = inner.shape[1] // width
                small = [jnp.concatenate([first, second], 1), one[0:1], two[0:1]]
                small += [one[2:3], one[1:2], two[2:3], two[1:2]]
                for at in range(count):
                    runs = [
                        inner[0:1, (start * count + at) * shard : (start * count + at + 1) * shard]
                        for start in range(shards)
                    ]
                    small.append(jnp.concatenate(runs, 1))
                small.append(jnp.zeros((120 - count, width), F32))
                grad[:, 3 * span_cols :] = jnp.concatenate(small, 0).T.astype(BF16)
            else:
                grad[:, 3 * span_cols :] = outer_ref[...]
            spread(grad, ((near, away), keep), scalars_ref, base, shard, order)

    two_slots = pl.BlockSpec((2, slot_rows, width), lambda i, s: (i, 0, 0))
    operands = [low_attn, mixed, probs, joined, w_out]
    skip = first_block // mine
    in_specs = [
        RESIDENT,
        pl.BlockSpec((2 * length, 3 * span_cols), lambda i, s: (i, skip)),
        pl.BlockSpec((2, mine, 2 * length, length), lambda i, s: (i, skip, 0, 0)),
        RESIDENT,
        RESIDENT,
    ]
    out_specs = [pl.BlockSpec((8, span_cols), lambda i, s: (0, 0))]
    out_shape = [jax.ShapeDtypeStruct((8, span_cols), F32)]
    for entries in (places // 2, places // 2, places):
        shape = (entries, shard, columns)
        out_specs.append(pl.BlockSpec(shape, lambda i, s: (0, 0, 0)))
        out_shape.append(jax.ShapeDtypeStruct(shape, BF16))
    if last:
        operands += [w_qkv, earlier, *sums]
        in_specs += [RESIDENT, RESIDENT]
        in_specs += [whole(each) for each in sums]
        out_specs = [two_slots, two_slots] + out_specs
        out_shape = [jax.ShapeDtypeStruct((pairs, slot_rows, width), BF16)] * 2 + out_shape
    else:
        operands.append(outer)
        in_specs.append(RESIDENT)
        out_specs = [RESIDENT] + out_specs
        out_shape = [jax.ShapeDtypeStruct((total, 3 * span_cols), BF16)] + out_shape
    return call(
        kernel,
        scalars,
        operands,
        in_specs,
        out_specs,
        out_shape,
        (steps,),
        "attention_backward",
        limit=13 * 2**20,
        scratch=[pltpu.VMEM((total, 3 * span_cols), BF16)] * last
        + [pltpu.VMEM((width, columns), BF16)],
    )


def in_turn(value):
    value, *rest = lax.optimization_barrier((value, *LINE))
    LINE[:] = rest[:1]
    return value


def pause(scalars):
    def kernel(scalars_ref):
        del scalars_ref

    call(kernel, scalars, [], [], [], [], (1,), "pause", work=2 * 10**10)


class Shards:
    def __init__(self, *arrays, order):
        *sends, keep = arrays
        shard, width = keep.shape[-2:]
        self.order = list(order)
        self.columns = width // 2 if "mod" in self.order else width
        count = 2 ** sum(step != "mod" for step in self.order)
        self.held = [(0, keep.reshape((count, shard, width)))]
        self.count = count
        shape = (count // len(sends), shard, width)
        self.coming = []
        for i in range(len(sends))[::-1]:
            self.coming.append((i * shape[0], flipped(sends[i], "dp", 1).reshape(shape)))

    def step(self):
        bit = self.order.pop(0) if self.order else None
        count = self.count
        first = count // 2 if bit in (0, 1, 2) else 0
        column = self.columns if bit == "mod" else 0
        late = []
        for at, array in self.coming:
            if at + array.shape[0] > first:
                self.held.append((at, in_turn(array)))
            else:
                late.append((at, array))
        total = None
        for at, array in self.held:
            if at >= count or at + array.shape[0] <= first:
                continue
            array = lax.slice_in_dim(array, first - at if first > at else 0, count - at, axis=0)
            array = lax.slice_in_dim(array, column, column + self.columns, axis=2)
            array = array.astype(F32)
            total = array if total is None else total + array
        total = total.astype(BF16)
        if bit is None:
            self.mine = lax.optimization_barrier(total[0])
            self.coming = flipped(self.mine, "mod", 1)
        elif bit == "mod":
            self.coming = late + [(0, flipped(total, "mod", 1))]
        else:
            self.coming = late + [(0, flipped(total, "dp", 2 << bit))]
            self.count = first
        LINE.append(total)

    def result(self):
        return self.mine.astype(F32) + in_turn(self.coming).astype(F32)


def finish(scalars, inner, early, late, width, inner_width, base):
    pieces = [inner, early, late]
    shard = early.mine.shape[0]
    count = inner_width // width
    turn = inner.mine.shape[1]
    widths = ((early.mine.shape[1] - width) // 3, (late.mine.shape[1] - 128) // 3)

    def kernel(scalars_ref, *refs):
        ins, (grad_in, grad_out, qkv, b_qv, gains, biases, b_in) = refs[:6], refs[6:]
        first = scalars_ref[base + 3] == 0
        grad_in[:, :turn] = jnp.where(first, ins[0][...], ins[1][...]).astype(F32)
        grad_in[:, turn:] = jnp.where(first, ins[1][...], ins[0][...]).astype(F32)
        parts = [ins[2 * i][...].astype(F32) + ins[2 * i + 1][...].astype(F32) for i in (1, 2)]
        grad_out[...] = parts[0][:, 3 * widths[0] :]
        at = 0
        for third in range(3):
            for part, columns in zip(parts, widths):
                qkv[:, at : at + columns] = part[:, third * columns : (third + 1) * columns]
                at += columns
        small = jnp.concatenate([parts[1][:, 3 * widths[1] :], jnp.zeros((128 - shard, 128), F32)], 0)
        small = small.T[:, :shard]
        b_qv[...] = small[0:2]
        gains[...] = small[2:4]
        biases[...] = small[4:8]
        b_in[...] = jnp.concatenate([small[8 + i : 9 + i] for i in range(count)], 1)

    operands = [each for piece in pieces for each in (piece.mine, piece.coming)]
    shapes = [(shard, inner_width), (shard, width), (shard, 3 * width)]
    shapes += [(2, shard), (2, shard), (4, shard), (1, count * shard)]
    return call(
        kernel,
        scalars,
        operands,
        [whole(array) for array in operands],
        [pl.BlockSpec(shape, lambda i, s: (0, 0)) for shape in shapes],
        [jax.ShapeDtypeStruct(shape, F32) for shape in shapes],
        (1,),
        "finish",
        anywhere=range(6),
    )


def reduce_plain(*arrays, order):
    *sends, keep = arrays
    shard, columns = keep.shape[-2:]
    send = jnp.concatenate([each.reshape(-1, shard, columns) for each in sends], 0)
    total = jnp.stack([keep.reshape(-1, shard, columns), send.reshape(-1, shard, columns)], 1)
    places = [place_of(j, order) for j in range(total.shape[0])]
    total = jnp.stack([total[places.index(j)] for j in range(total.shape[0])])
    total = total.reshape(-1, columns).astype(F32)
    share = lax.psum_scatter(total, "dp", scatter_dimension=0, tiled=True)
    return lax.psum(share.astype(BF16), "mod").astype(F32)


def body(
    layer_rows,
    cotangent,
    row_live,
    partner,
    w_qkv,
    b_qv,
    w_out,
    norm_gains,
    bias_rows,
    w_in,
    b_in,
    w_back,
):
    side = lax.axis_index("mod")
    place = lax.axis_index("dp")
    shards = lax.axis_size("dp")
    groups = partner.shape[1]
    aligned = shards == 16 and (layer_rows.shape[2] // shards) % 16 == 0
    layout = shards if aligned else 16
    half = groups // 2
    width = layer_rows.shape[2]
    slot_rows = layer_rows.shape[1] // groups
    inner_width = w_in.shape[1]
    slots = (groups, slot_rows, width)
    rows = layer_rows[0].reshape(slots)
    cot = cotangent[0].reshape(slots)
    cut = half // 2
    LINE.clear()
    sent = gather_sent(partner[0], rows, half, 0, cut)
    got_a = flipped(sent, "mod", 1)
    sent = gather_sent(partner[0], rows, half, cut, half - cut)
    got_b = flipped(sent, "mod", 1)
    sent_cot = gather_sent(partner[0], cot, half, 0, half)
    got_a, sent_cot, row_live, partner = lax.optimization_barrier(
        (got_a, sent_cot, row_live, partner)
    )
    far_cot = flipped(sent_cot, "mod", 1)
    spot = place if aligned else 0 * place
    scalars = jnp.concatenate(
        [partner[0], jnp.stack([side, spot & 1, spot >> 1, side * aligned]).astype(jnp.int32)]
    )

    live = row_live.reshape(2, groups, slot_rows)
    words_live = lax.dynamic_slice_in_dim(live[0], side * half, half, 0)
    region_live = live[1][lax.dynamic_slice_in_dim(partner[0], side * half, half, 0)]
    is_first = side == 0
    seen = jnp.concatenate(
        [
            jnp.where(is_first, words_live, region_live),
            jnp.where(is_first, region_live, words_live),
        ],
        1,
    )[:, None, :]

    w_qkv, w_out, w_in, w_back = fetch(scalars, (w_qkv, w_out, w_in, w_back))
    heads_weights = (w_qkv, b_qv, w_out, norm_gains, bias_rows)
    joined, mixed, probs, context, normed, root = attention_forward(
        scalars, rows, (got_a, got_b), seen, heads_weights
    )
    feed_weights = (w_in, b_in.reshape(1, inner_width), w_back, norm_gains, bias_rows)
    slope, branch, out_kept, out_far, sums_two, *back = feed_forward(
        scalars, normed, cot, far_cot, feed_weights, half, layout, groups
    )
    out_back = flipped(out_far, "mod", 1)
    back_weights = (w_in, w_back, norm_gains, bias_rows)
    attn_weights = (w_out, w_qkv)
    path = (0, 1, 2)
    if aligned:
        back = Shards(*back, order=path)
        back.step()
    low_attn, outer, sums_one, inner_sum, *inner = feed_backward(
        scalars, branch, slope, normed, root, context, back_weights, layout, groups, path
    )
    shard = width // shards
    count = inner_width // width
    if aligned:
        back.step()
        out_back = in_turn(out_back)
        pause(scalars)
        inner = Shards(*inner, order=("mod", 0, 1, 2))
        inner.step()
    attn_kept = (low_attn, mixed, probs, joined, outer)
    d_mixed, sums_qv, *qkv_a = attention_backward(
        scalars, attn_kept, attn_weights, 0, layout, groups, path
    )
    if aligned:
        back.step()
        out_rows = scatter_home(scalars, out_kept, out_back, half).reshape(1, -1, width)
        qkv_a = Shards(*qkv_a, order=path)
        qkv_a.step()
    if layout != shards:
        inner_sum = inner_sum.reshape(8, shards, count, shard).transpose(0, 2, 1, 3)
        inner_sum = inner_sum.reshape(8, count, layout, width // layout).transpose(0, 2, 1, 3)
        inner_sum = inner_sum.reshape(8, inner_width)
    sums = (sums_one, sums_two, inner_sum, sums_qv)
    d_kept, d_far, _, *qkv_b = attention_backward(
        scalars, attn_kept, attn_weights, 1, layout, groups, path, d_mixed, sums
    )
    d_back = flipped(d_far, "mod", 1)
    if aligned:
        qkv_b = Shards(*qkv_b, order=path)
        inner.step()
        back.step()
        qkv_a.step()
        qkv_b.step()
        inner.step()
        pause(scalars)
        qkv_a.step()
        qkv_b.step()
        grad_back = back.result()
        inner.step()
        grad_rows = scatter_home(scalars, d_kept, d_back, half).reshape(1, -1, width)
        qkv_a.step()
        qkv_b.step()
        inner.step()
        qkv_b.step()
        grad_in, grad_out, grad_qkv, *small = finish(
            scalars, inner, qkv_a, qkv_b, width, inner_width, groups
        )
    else:
        out_rows = scatter_home(scalars, out_kept, out_back, half).reshape(1, -1, width)
        grad_back = reduce_plain(*back, order=path)
        grad_in = reduce_plain(*inner, order=path)
        qkv_a, qkv_b = reduce_plain(*qkv_a, order=path), reduce_plain(*qkv_b, order=path)
        grad_rows = scatter_home(scalars, d_kept, d_back, half).reshape(1, -1, width)
        columns = ((qkv_a.shape[1] - width) // 3, (qkv_b.shape[1] - 128) // 3)
        thirds = []
        for third in range(3):
            for part, wide in zip((qkv_a, qkv_b), columns):
                thirds.append(part[:, third * wide : (third + 1) * wide])
        grad_qkv = jnp.concatenate(thirds, 1)
        small = qkv_b[:, 3 * columns[1] :].T
        small = small[0:2], small[2:4], small[4:8], small[8 : 8 + count]
        grad_out = qkv_a[:, 3 * columns[0] :]
    return (
        out_rows,
        grad_rows,
        grad_qkv,
        small[0],
        grad_out,
        small[1],
        small[2],
        grad_in,
        small[3].reshape(-1),
        grad_back,
    )


def solution(mesh):
    return jax.shard_map(
        body,
        mesh=mesh,
        in_specs=(
            P("mod", "dp", None),
            P("mod", "dp", None),
            P(None, "dp"),
            P("dp", None),
            P(),
            P(),
            P(),
            P(),
            P(),
            P(),
            P(),
            P(),
        ),
        out_specs=(
            P("mod", "dp", None),
            P("mod", "dp", None),
            P("dp", None),
            P(None, "dp"),
            P("dp", None),
            P(None, "dp"),
            P(None, "dp"),
            P("dp", None),
            P("dp"),
            P("dp", None),
        ),
        check_vma=False,
    )
```
